32 devices in a mesh: clip: 4 (over x, core), tube: 2 (over y), head: 4 (over z).
Axes of the slice: x: 2, y: 2, z: 4, core: 2. Of those that a mesh axis runs over, the one named last changes fastest.
Arguments:
- tokens: bfloat16 [4, 16, 16, 16, 768], P('clip', None, 'tube'), may hold values from -6 to 6
- token_mask: int32 [4, 16, 16, 16], P('clip', None, 'tube'), may hold values from 0 to 1, as said below
- mask_embed: float32 [768], replicated, may hold values from -5 to 5
- norm_gains: float32 [2, 2, 768], replicated, may hold values from 0.5 to 1.5
- norm_shifts: float32 [2, 2, 768], replicated, may hold values from -2 to 2
- w_qkv: bfloat16 [2, 768, 3, 768], P(None, None, None, 'head'), may hold values from -0.21875 to 0.21875
- b_qv: float32 [2, 2, 768], P(None, None, 'head'), may hold values from -2 to 2
- w_out: bfloat16 [2, 768, 768], P(None, 'head'), may hold values from -0.875 to 0.875
- b_out: float32 [2, 768], replicated, may hold values from -2 to 2
- w_up: bfloat16 [2, 768, 3072], P(None, None, 'head'), may hold values from -0.21875 to 0.21875
- b_up: float32 [2, 3072], P(None, 'head'), may hold values from -2 to 2
- w_down: bfloat16 [2, 3072, 768], P(None, 'head'), may hold values from -0.109375 to 0.109375
- b_down: float32 [2, 768], replicated, may hold values from -2 to 2
- cotangent: bfloat16 [4, 16, 16, 16, 768], P('clip', None, 'tube'), may hold values from -6 to 6
Outputs:
- result: bfloat16 [4, 16, 16, 16, 768], P('clip', None, 'tube')
- grad_tokens: bfloat16 [4, 16, 16, 16, 768], P('clip', None, 'tube')
- grad_mask_embed: float32 [768], replicated
- grad_norm_gains: float32 [2, 2, 768], replicated
- grad_norm_shifts: float32 [2, 2, 768], replicated
- grad_w_qkv: float32 [2, 768, 3, 768], P(None, None, None, 'head')
- grad_b_qv: float32 [2, 2, 768], P(None, None, 'head')
- grad_w_out: float32 [2, 768, 768], P(None, 'head')
- grad_b_out: float32 [2, 768], replicated
- grad_w_up: float32 [2, 768, 3072], P(None, None, 'head')
- grad_b_up: float32 [2, 3072], P(None, 'head')
- grad_w_down: float32 [2, 3072, 768], P(None, 'head')
- grad_b_down: float32 [2, 768], replicated
The draws below stay inside these ranges and needn't reach their ends.
Inputs may be any that keep to these rules, and one draw needn't show every extreme that they name: token_mask is 1 where a token is masked; each clip masks its tokens at a rate of its own between one half and all.
All inputs are finite; a program needn't handle non-finite values.
Results may differ from the reference program's by a relative error of at most 0.03.
Values may be sent and summed in bfloat16 or wider, within the bound.
A program may use at most 256 MiB of HBM per device.

```python
from functools import partial
import jax
import jax.numpy as jnp
from jax import lax

D = 768
HD = 64
FF = 3072
FRAMES = 16
TUBES = 16
TPATCH = 16
HH = 768
CLIPS = 4


def draw_token_mask(key, part):
    key = jax.random.fold_in(key, 5)
    rate_key, cell_key = jax.random.split(key)
    levels = jax.random.randint(rate_key, (CLIPS, 1, 1, 1), 8, 17)
    cells = jax.random.randint(cell_key, (CLIPS, FRAMES, TUBES, TPATCH), 0, 16)
    return (cells < levels).astype(jnp.int32)


def steps_of(stream_key, extent, cuts, smallest, largest):
    def one(position, parts):
        draws = jax.random.uniform(jax.random.fold_in(jax.random.fold_in(stream_key, 6), position), (parts,), jnp.float32, smallest / len(cuts), largest / len(cuts))
        return jnp.repeat(jnp.exp(draws), extent[position] // parts).reshape((-1,) + (1,) * (len(extent) - position - 1))

    gain = one(*cuts[0])
    for cut in cuts[1:]:
        gain = gain * one(*cut)
    return gain


def centred(stream_key, shape, scale, most, shards=(), dtype=jnp.bfloat16):
    gain = steps_of(stream_key, shape, shards, -0.22, 0.18) if shards else 1.0
    values = jax.random.normal(stream_key, shape, jnp.float32) * scale * gain
    return jnp.minimum(jnp.maximum(values, -most), most).astype(dtype)


def setup_inputs(seed: int = 0) -> dict:
    streams_of = jax.random.split(jax.random.key(seed), 15)
    tokens = centred(streams_of[0], (CLIPS, FRAMES, TUBES, TPATCH, D), 1.0, 6.0, ((0, 4), (2, 2)))
    token_mask = draw_token_mask(jax.random.fold_in(streams_of[14], 71), 0)
    mask_embed = centred(streams_of[2], (D,), 1.0, 5.0, (), jnp.float32)
    norm_gains = jnp.clip(1.0 + 0.1 * jax.random.normal(streams_of[3], (2, 2, D), jnp.float32), 0.5, 1.5)
    norm_shifts = centred(streams_of[4], (2, 2, D), 0.3, 2.0, (), jnp.float32)
    w_qkv = centred(streams_of[5], (2, D, 3, HH), D ** -0.5, 0.21875, ((3, 4),))
    b_qv = centred(streams_of[6], (2, 2, HH), 0.3, 2.0, ((2, 4),), jnp.float32)
    w_out = centred(streams_of[7], (2, HH, D), (HH // 16) ** -0.5, 0.875, ((1, 4),))
    b_out = centred(streams_of[8], (2, D), 0.3, 2.0, (), jnp.float32)
    w_up = centred(streams_of[9], (2, D, FF), D ** -0.5, 0.21875, ((2, 4),))
    b_up = centred(streams_of[10], (2, FF), 0.3, 2.0, ((1, 4),), jnp.float32)
    w_down = centred(streams_of[11], (2, FF, D), FF ** -0.5, 0.109375, ((1, 4),))
    b_down = centred(streams_of[12], (2, D), 0.3, 2.0, (), jnp.float32)
    cotangent = centred(streams_of[13], (CLIPS, FRAMES, TUBES, TPATCH, D), 1.0, 6.0, ((0, 4), (2, 2)))
    return {"tokens": tokens, "token_mask": token_mask, "mask_embed": mask_embed, "norm_gains": norm_gains, "norm_shifts": norm_shifts, "w_qkv": w_qkv, "b_qv": b_qv, "w_out": w_out, "b_out": b_out, "w_up": w_up, "b_up": b_up, "w_down": w_down, "b_down": b_down, "cotangent": cotangent}


EPS = 1e-05
HIGHEST = lax.Precision.HIGHEST

@jax.custom_vjp
def low(v):
    return lax.optimization_barrier(v.astype(jnp.bfloat16)).astype(jnp.float32)

@jax.custom_vjp
def low_back(v):
    return v

def low_keep(v):
    return (low(v), None)

def low_pass(kept, grad):
    return (grad,)

def back_keep(v):
    return (v, None)

def back_low(kept, grad):
    return (low(grad),)
low.defvjp(low_keep, low_pass)
low_back.defvjp(back_keep, back_low)

def layer_norm(values, gain_vector, shift_vector):
    centre = values - lax.optimization_barrier(jnp.mean(values, -1, keepdims=True))
    spread = lax.optimization_barrier(jnp.mean(centre * centre, -1, keepdims=True))
    return centre * lax.rsqrt(spread + EPS) * gain_vector + shift_vector

def attend(triple):
    queries, key_rows, value_rows = triple
    scores = low_back(jnp.einsum('bshe,bthe->bhst', queries, key_rows, precision=HIGHEST) * HD ** (-0.5))
    maximum = lax.optimization_barrier(jnp.max(scores, -1, keepdims=True))
    exponent = jnp.exp(scores - maximum)
    weights_soft = exponent / lax.optimization_barrier(jnp.sum(exponent, -1, keepdims=True))
    return jnp.einsum('bhst,bthe->bshe', low(weights_soft), value_rows, precision=HIGHEST)

def mixer(block_kind, queries, key_rows, value_rows):
    reorder = (0, 2, 1, 3, 4) if block_kind == 1 else (0, 1, 2, 3, 4)
    moved_shape = tuple((queries.shape[dimension] for dimension in reorder))
    columns = queries.shape[-1]

    def arrange(tensor):
        return tensor.transpose(reorder).reshape(moved_shape[0], moved_shape[1], moved_shape[2] * moved_shape[3], columns // HD, HD)
    mixture = lax.map(jax.checkpoint(attend), (arrange(queries), arrange(key_rows), arrange(value_rows)))
    return mixture.reshape(moved_shape).transpose(reorder)

def block(block_kind, residual, gains, shifts, w_qkv, b_qv, w_out, b_out, w_up, b_up, w_down, b_down):
    normed = low(layer_norm(residual, gains[0], shifts[0]))
    projected = jnp.einsum('...d,dcj->...cj', normed, w_qkv, precision=HIGHEST)
    queries = low(low_back(projected[..., 0, :] + b_qv[0]))
    key_rows = low(low_back(projected[..., 1, :]))
    value_rows = low(low_back(projected[..., 2, :] + b_qv[1]))
    mixture = low(low_back(mixer(block_kind, queries, key_rows, value_rows)))
    middle = residual + low_back(jnp.einsum('...j,jd->...d', mixture, w_out, precision=HIGHEST)) + b_out
    normed_two = low(layer_norm(middle, gains[1], shifts[1]))
    hidden = low_back(jnp.einsum('...d,df->...f', normed_two, w_up, precision=HIGHEST) + b_up)
    active = low(jax.nn.gelu(hidden))
    return middle + low_back(jnp.einsum('...f,fd->...d', active, w_down, precision=HIGHEST)) + b_down

def forward(masked, tokens, mask_embed, norm_gains, norm_shifts, w_qkv, b_qv, w_out, b_out, w_up, b_up, w_down, b_down):
    residual = jnp.where(masked[..., None], mask_embed, tokens)
    for block_kind in range(2):
        residual = block(block_kind, residual, norm_gains[block_kind], norm_shifts[block_kind], w_qkv[block_kind], b_qv[block_kind], w_out[block_kind], b_out[block_kind], w_up[block_kind], b_up[block_kind], w_down[block_kind], b_down[block_kind])
    return residual

def reference(tokens, token_mask, mask_embed, norm_gains, norm_shifts, w_qkv, b_qv, w_out, b_out, w_up, b_up, w_down, b_down, cotangent):
    masked = token_mask == 1
    floats = tuple((operand.astype(jnp.float32) for operand in (tokens, mask_embed, norm_gains, norm_shifts, w_qkv, b_qv, w_out, b_out, w_up, b_up, w_down, b_down)))
    result, pullback = jax.vjp(partial(forward, masked), *floats)
    gradients = pullback(cotangent.astype(jnp.float32))
    return (result.astype(jnp.bfloat16), gradients[0].astype(jnp.bfloat16), gradients[1], gradients[2], gradients[3], gradients[4], gradients[5], gradients[6], gradients[7], gradients[8], gradients[9], gradients[10], gradients[11])
```

```python
from functools import partial

import jax
import jax.numpy as jnp
from jax import lax
from jax.sharding import PartitionSpec as P

HD = 64


EPS = 1e-05


def norm_forward(values, gain_vector, shift_vector):
    centre = values - jnp.mean(values, -1, keepdims=True)
    inverse = lax.rsqrt(jnp.mean(centre * centre, -1, keepdims=True) + EPS)
    normal = centre * inverse
    return (normal * gain_vector + shift_vector, normal, inverse)


def norm_backward(grad_out, normal, inverse, gain_vector):
    grad_normal = grad_out * gain_vector
    grad_in = inverse * (
        grad_normal
        - jnp.mean(grad_normal, -1, keepdims=True)
        - normal * jnp.mean(grad_normal * normal, -1, keepdims=True)
    )
    return (grad_in, jnp.sum(grad_out * normal, 0), jnp.sum(grad_out, 0))


def row_total(partial_sum):
    return lax.psum(partial_sum.astype(jnp.bfloat16), "head").astype(jnp.float32)


def input_total(partial_sum):
    return lax.psum(partial_sum.astype(jnp.bfloat16), "head").astype(jnp.float32)


def split_heads(tensor, batch_count, length):
    return tensor.reshape(batch_count, length, tensor.shape[-1] // HD, HD)


def attend(queries, key_rows, value_rows):
    scores = jnp.einsum(
        "bshe,bthe->bhst", queries, key_rows, preferred_element_type=jnp.float32
    ) * HD ** (-0.5)
    maximum = jnp.max(scores, -1, keepdims=True)
    exponent = jnp.exp(scores - maximum)
    denominator = jnp.sum(exponent, -1, keepdims=True)
    weights_soft = (exponent / denominator).astype(jnp.bfloat16)
    mixture = jnp.einsum(
        "bhst,bthe->bshe", weights_soft, value_rows, preferred_element_type=jnp.float32
    )
    return (mixture.astype(jnp.bfloat16), maximum + jnp.log(denominator))


def attend_back(queries, key_rows, value_rows, log_total, grad_mixture):
    scaling = HD ** (-0.5)
    scores = (
        jnp.einsum("bshe,bthe->bhst", queries, key_rows, preferred_element_type=jnp.float32)
        * scaling
    )
    weights_soft = jnp.exp(scores - log_total)
    grad_weights = jnp.einsum(
        "bshe,bthe->bhst", grad_mixture, value_rows, preferred_element_type=jnp.float32
    )
    grad_values = jnp.einsum(
        "bhst,bshe->bthe",
        weights_soft.astype(jnp.bfloat16),
        grad_mixture,
        preferred_element_type=jnp.float32,
    )
    grad_scores = (
        weights_soft * (grad_weights - jnp.sum(weights_soft * grad_weights, -1, keepdims=True))
    ).astype(jnp.bfloat16)
    grad_queries = (
        jnp.einsum("bhst,bthe->bshe", grad_scores, key_rows, preferred_element_type=jnp.float32)
        * scaling
    )
    grad_keys = (
        jnp.einsum("bhst,bshe->bthe", grad_scores, queries, preferred_element_type=jnp.float32)
        * scaling
    )
    return (grad_queries, grad_keys, grad_values)


def mixer_forward(block_kind, queries, key_rows, value_rows):
    clip_count, frame_count, tube_count, patch_count, columns = queries.shape
    if block_kind == 1:
        reorder = (0, 2, 1, 3, 4)
        pieces = [
            split_heads(
                tensor.transpose(reorder), clip_count * tube_count, frame_count * patch_count
            )
            for tensor in (queries, key_rows, value_rows)
        ]
        mixture, log_total = attend(pieces[0], pieces[1], pieces[2])
        mixture = mixture.reshape(
            clip_count, tube_count, frame_count, patch_count, columns
        ).transpose(reorder)
        return (mixture, (pieces, log_total))
    key_all, value_all = (
        lax.all_gather(key_rows, "tube", axis=2, tiled=True),
        lax.all_gather(value_rows, "tube", axis=2, tiled=True),
    )
    tube_all = key_all.shape[2]
    pieces = [
        split_heads(queries, clip_count * frame_count, tube_count * patch_count),
        split_heads(key_all, clip_count * frame_count, tube_all * patch_count),
        split_heads(value_all, clip_count * frame_count, tube_all * patch_count),
    ]
    mixture, log_total = attend(pieces[0], pieces[1], pieces[2])
    return (
        mixture.reshape(clip_count, frame_count, tube_count, patch_count, columns),
        (pieces, log_total),
    )


def mixer_backward(block_kind, retained, grad_mixture):
    pieces, log_total = retained
    clip_count, frame_count, tube_count, patch_count, columns = grad_mixture.shape
    if block_kind == 1:
        reorder = (0, 2, 1, 3, 4)
        moved = split_heads(
            grad_mixture.transpose(reorder), clip_count * tube_count, frame_count * patch_count
        )
        gradients = attend_back(pieces[0], pieces[1], pieces[2], log_total, moved)
        return [
            grad.astype(jnp.bfloat16)
            .reshape(clip_count, tube_count, frame_count, patch_count, columns)
            .transpose(reorder)
            for grad in gradients
        ]
    gradients = attend_back(
        pieces[0],
        pieces[1],
        pieces[2],
        log_total,
        split_heads(grad_mixture, clip_count * frame_count, tube_count * patch_count),
    )
    tube_all = pieces[1].shape[1] // patch_count
    grad_keys = gradients[1].reshape(clip_count, frame_count, tube_all, patch_count, columns)
    grad_values = gradients[2].reshape(clip_count, frame_count, tube_all, patch_count, columns)
    grad_keys, grad_values = (
        lax.psum_scatter(
            grad_keys.astype(jnp.bfloat16), "tube", scatter_dimension=2, tiled=True
        ).astype(jnp.float32),
        lax.psum_scatter(
            grad_values.astype(jnp.bfloat16), "tube", scatter_dimension=2, tiled=True
        ).astype(jnp.float32),
    )
    grad_queries = (
        gradients[0]
        .astype(jnp.bfloat16)
        .reshape(clip_count, frame_count, tube_count, patch_count, columns)
    )
    return [grad_queries, grad_keys.astype(jnp.bfloat16), grad_values.astype(jnp.bfloat16)]


def block_forward(block_kind, residual, layout, weights):
    gains, shifts, w_qkv, b_qv, w_out, b_out, w_up, b_up, w_down, b_down = weights
    columns = w_qkv.shape[-1]
    grid_shape = layout[:-1] + (columns,)
    normed_share, first_normal, first_inverse = norm_forward(residual, gains[0], shifts[0])
    normed = normed_share.astype(jnp.bfloat16)
    projected = jnp.einsum("rd,dcj->rcj", normed, w_qkv, preferred_element_type=jnp.float32)
    queries = (projected[:, 0] + b_qv[0]).astype(jnp.bfloat16).reshape(grid_shape)
    key_rows = projected[:, 1].astype(jnp.bfloat16).reshape(grid_shape)
    value_rows = (projected[:, 2] + b_qv[1]).astype(jnp.bfloat16).reshape(grid_shape)
    mixture, retained = mixer_forward(block_kind, queries, key_rows, value_rows)
    mixture = mixture.reshape(-1, columns)
    middle = (
        residual + row_total(jnp.dot(mixture, w_out, preferred_element_type=jnp.float32)) + b_out
    )
    second_share, second_normal, second_inverse = norm_forward(middle, gains[1], shifts[1])
    normed_two = second_share.astype(jnp.bfloat16)
    hidden = jnp.dot(normed_two, w_up, preferred_element_type=jnp.float32) + b_up
    active = jax.nn.gelu(hidden).astype(jnp.bfloat16)
    stored = (
        normed,
        first_normal,
        first_inverse,
        retained,
        mixture,
        normed_two,
        second_normal,
        second_inverse,
        hidden,
    )
    return (middle, active, stored)


def block_output(middle, active, w_down, b_down):
    return middle + row_total(jnp.dot(active, w_down, preferred_element_type=jnp.float32)) + b_down


def block_backward(block_kind, residual, layout, weights, grad_rows):
    gains, shifts, w_qkv, b_qv, w_out, b_out, w_up, b_up, w_down, b_down = weights
    middle, active, stored = block_forward(block_kind, residual, layout, weights)
    (
        normed,
        first_normal,
        first_inverse,
        retained,
        mixture,
        normed_two,
        second_normal,
        second_inverse,
        hidden,
    ) = stored
    columns = w_qkv.shape[-1]
    grad_low = grad_rows.astype(jnp.bfloat16)
    grad_wdown = jnp.dot(active.T, grad_low, preferred_element_type=jnp.float32)
    grad_bdown = jnp.sum(grad_rows, 0)
    grad_active = jnp.dot(grad_low, w_down.T, preferred_element_type=jnp.float32)
    gelu_pull = jax.vjp(jax.nn.gelu, hidden)[1]
    grad_hidden = gelu_pull(grad_active)[0].astype(jnp.bfloat16)
    grad_bup = jnp.sum(grad_hidden.astype(jnp.float32), 0)
    grad_wup = jnp.dot(normed_two.T, grad_hidden, preferred_element_type=jnp.float32)
    grad_normed_two = input_total(jnp.dot(grad_hidden, w_up.T, preferred_element_type=jnp.float32))
    grad_norm, grad_gain_two, grad_shift_two = norm_backward(
        grad_normed_two, second_normal, second_inverse, gains[1]
    )
    grad_middle = grad_rows + grad_norm
    grad_bout = jnp.sum(grad_middle, 0)
    grad_mid_low = grad_middle.astype(jnp.bfloat16)
    grad_wout = jnp.dot(mixture.T, grad_mid_low, preferred_element_type=jnp.float32)
    grad_mixture = jnp.dot(grad_mid_low, w_out.T, preferred_element_type=jnp.float32).astype(
        jnp.bfloat16
    )
    grad_parts = mixer_backward(
        block_kind, retained, grad_mixture.reshape(layout[:-1] + (columns,))
    )
    grad_flat = [grad.reshape(-1, columns) for grad in grad_parts]
    grad_project = jnp.stack(grad_flat, 1)
    grad_bqv = jnp.stack(
        [jnp.sum(grad_flat[0].astype(jnp.float32), 0), jnp.sum(grad_flat[2].astype(jnp.float32), 0)]
    )
    grad_wqkv = jnp.einsum("rd,rcj->dcj", normed, grad_project, preferred_element_type=jnp.float32)
    grad_normed = input_total(
        jnp.einsum("rcj,dcj->rd", grad_project, w_qkv, preferred_element_type=jnp.float32)
    )
    grad_input, grad_gain_one, grad_shift_one = norm_backward(
        grad_normed, first_normal, first_inverse, gains[0]
    )
    gradients = (
        jnp.stack([grad_gain_one, grad_gain_two]),
        jnp.stack([grad_shift_one, grad_shift_two]),
        grad_wqkv,
        grad_bqv,
        grad_wout,
        grad_bout,
        grad_wup,
        grad_bup,
        grad_wdown,
        grad_bdown,
    )
    return (grad_middle + grad_input, gradients)


def on_device_sums(
    tokens,
    token_mask,
    mask_embed,
    norm_gains,
    norm_shifts,
    w_qkv,
    b_qv,
    w_out,
    b_out,
    w_up,
    b_up,
    w_down,
    b_down,
    cotangent,
):
    layout = tokens.shape
    width = layout[-1]
    masked = (token_mask == 1).reshape(-1, 1)
    initial = jnp.where(masked, mask_embed[None, :], tokens.reshape(-1, width).astype(jnp.float32))
    upstream = cotangent.reshape(-1, width).astype(jnp.float32)

    def weights_of(block_kind):
        return (
            norm_gains[block_kind],
            norm_shifts[block_kind],
            w_qkv[block_kind],
            b_qv[block_kind],
            w_out[block_kind],
            b_out[block_kind],
            w_up[block_kind],
            b_up[block_kind],
            w_down[block_kind],
            b_down[block_kind],
        )

    middle, active, unused_first = block_forward(0, initial, layout, weights_of(0))
    second = block_output(middle, active, w_down[0], b_down[0])
    middle, active, unused_second = block_forward(1, second, layout, weights_of(1))
    output_rows = block_output(middle, active, w_down[1], b_down[1])
    grad_second, grads_later = block_backward(1, second, layout, weights_of(1), upstream)
    grad_initial, grads_earlier = block_backward(0, initial, layout, weights_of(0), grad_second)
    stacked = [
        jnp.stack([first_grad, later_grad])
        for first_grad, later_grad in zip(grads_earlier, grads_later)
    ]
    grad_embed = jnp.sum(jnp.where(masked, grad_initial, 0.0), 0)
    output_low = output_rows.astype(jnp.bfloat16)
    grad_low = jnp.where(masked, 0.0, grad_initial).astype(jnp.bfloat16)
    shares = (
        lax.psum_scatter(stacked[2], ("clip", "tube"), scatter_dimension=1, tiled=True),
        lax.psum_scatter(stacked[4], ("clip", "tube"), scatter_dimension=2, tiled=True),
        lax.psum_scatter(stacked[6], ("clip", "tube"), scatter_dimension=1, tiled=True),
        lax.psum_scatter(stacked[8], ("clip", "tube"), scatter_dimension=2, tiled=True),
    )
    whole = (
        lax.all_gather(shares[0].astype(jnp.bfloat16), ("clip", "tube"), axis=1, tiled=True).astype(
            jnp.float32
        ),
        lax.all_gather(shares[1].astype(jnp.bfloat16), ("clip", "tube"), axis=2, tiled=True).astype(
            jnp.float32
        ),
        lax.all_gather(shares[2].astype(jnp.bfloat16), ("clip", "tube"), axis=1, tiled=True).astype(
            jnp.float32
        ),
        lax.all_gather(shares[3].astype(jnp.bfloat16), ("clip", "tube"), axis=2, tiled=True).astype(
            jnp.float32
        ),
    )
    column_part = (
        grad_embed,
        stacked[0],
        stacked[1],
        stacked[5],
        stacked[9],
        stacked[3],
        stacked[7],
    )
    small = lax.psum(
        (
            column_part[0],
            column_part[1],
            column_part[2],
            column_part[3],
            column_part[4],
            column_part[5],
            column_part[6],
        ),
        ("clip", "tube"),
    )
    embed_grad, gain_grad, shift_grad, bout_grad, bdown_grad = (
        small[0],
        small[1],
        small[2],
        small[3],
        small[4],
    )
    bqv_grad, bup_grad = (small[5], small[6])
    return (
        output_low.reshape(layout),
        grad_low.reshape(layout),
        embed_grad,
        gain_grad,
        shift_grad,
        whole[0],
        bqv_grad,
        whole[1],
        bout_grad,
        whole[2],
        bup_grad,
        whole[3],
        bdown_grad,
    )


AXES = ("head", "tube", "clip")


def gather_shards(shard, parts):
    rows = shard.shape[0] // parts
    index = lax.axis_index("tube") * lax.axis_size("clip") + lax.axis_index("clip")
    piece = lax.dynamic_slice_in_dim(shard, index * rows, rows, 0)
    return lax.all_gather(piece, AXES, axis=0, tiled=True)


def shard_sum(partial_sum):
    share = lax.psum_scatter(
        partial_sum.astype(jnp.bfloat16), AXES, scatter_dimension=0, tiled=True
    )
    return lax.all_gather(share, ("tube", "clip"), axis=0, tiled=True)


def local_block_forward(residual, sequences, weights):
    gains, shifts, w_qkv, b_qv, w_out, b_out, w_up, b_up, w_down, b_down = weights
    shards, width, columns3 = w_qkv.shape
    columns = columns3 // 3
    rows = residual.shape[0]
    first, first_normal, first_inverse = norm_forward(residual, gains[0], shifts[0])
    normed = first.astype(jnp.bfloat16)
    projected = jnp.einsum("rd,hdc->hrc", normed, w_qkv, preferred_element_type=jnp.float32)
    projected = projected.reshape(shards, rows, 3, columns)
    queries = (projected[:, :, 0] + b_qv[0][:, None]).astype(jnp.bfloat16)
    key_rows = projected[:, :, 1].astype(jnp.bfloat16)
    value_rows = (projected[:, :, 2] + b_qv[1][:, None]).astype(jnp.bfloat16)
    pieces = [
        split_heads(tensor, shards * sequences, rows // sequences)
        for tensor in (queries, key_rows, value_rows)
    ]
    mixture, log_total = attend(*pieces)
    mixture = mixture.reshape(shards, rows, columns)
    middle = (
        residual
        + jnp.einsum("hrc,hcd->rd", mixture, w_out, preferred_element_type=jnp.float32)
        + b_out
    )
    second, second_normal, second_inverse = norm_forward(middle, gains[1], shifts[1])
    normed_two = second.astype(jnp.bfloat16)
    hidden = (
        jnp.einsum("rd,hdf->hrf", normed_two, w_up, preferred_element_type=jnp.float32)
        + b_up[:, None]
    )
    active = jax.nn.gelu(hidden).astype(jnp.bfloat16)
    result = (
        middle
        + jnp.einsum("hrf,hfd->rd", active, w_down, preferred_element_type=jnp.float32)
        + b_down
    )
    stored = (
        normed,
        first_normal,
        first_inverse,
        pieces,
        log_total,
        mixture,
        normed_two,
        second_normal,
        second_inverse,
        hidden,
        active,
    )
    return (result, stored)


def local_block_backward(weights, stored, grad_rows):
    gains, shifts, w_qkv, b_qv, w_out, b_out, w_up, b_up, w_down, b_down = weights
    (
        normed,
        first_normal,
        first_inverse,
        pieces,
        log_total,
        mixture,
        normed_two,
        second_normal,
        second_inverse,
        hidden,
        active,
    ) = stored
    shards, rows, columns = mixture.shape
    low = jnp.bfloat16
    grad_low = grad_rows.astype(low)
    dot = partial(jnp.einsum, preferred_element_type=jnp.float32)
    grad_wdown = dot("hrf,rd->hfd", active, grad_low)
    grad_bdown = jnp.sum(grad_rows, 0)
    grad_active = dot("rd,hfd->hrf", grad_low, w_down)
    gelu_pull = jax.vjp(jax.nn.gelu, hidden)[1]
    grad_hidden = gelu_pull(grad_active)[0].astype(low)
    grad_bup = jnp.sum(grad_hidden.astype(jnp.float32), 1)
    grad_wup = dot("rd,hrf->hdf", normed_two, grad_hidden)
    grad_normed_two = dot("hrf,hdf->rd", grad_hidden, w_up)
    grad_norm, grad_gain_two, grad_shift_two = norm_backward(
        grad_normed_two, second_normal, second_inverse, gains[1]
    )
    grad_middle = grad_rows + grad_norm
    grad_bout = jnp.sum(grad_middle, 0)
    grad_mid_low = grad_middle.astype(low)
    grad_wout = dot("hrc,rd->hcd", mixture, grad_mid_low)
    grad_mixture = dot("rd,hcd->hrc", grad_mid_low, w_out).astype(low)
    count, length = pieces[0].shape[:2]
    gradients = attend_back(*pieces, log_total, split_heads(grad_mixture, count, length))
    grad_flat = [grad.astype(low).reshape(shards, rows, columns) for grad in gradients]
    grad_bqv = jnp.stack(
        [jnp.sum(grad_flat[i].astype(jnp.float32), 1) for i in (0, 2)]
    )
    grad_project = jnp.concatenate(grad_flat, -1)
    grad_wqkv = dot("rd,hrc->hdc", normed, grad_project)
    grad_normed = dot("hrc,hdc->rd", grad_project, w_qkv)
    grad_input, grad_gain_one, grad_shift_one = norm_backward(
        grad_normed, first_normal, first_inverse, gains[0]
    )
    small = (
        jnp.stack([grad_gain_one, grad_gain_two]),
        jnp.stack([grad_shift_one, grad_shift_two]),
        grad_bqv,
        grad_bout,
        grad_bup,
        grad_bdown,
    )
    large = (grad_wqkv, grad_wout, grad_wup, grad_wdown)
    return (grad_middle + grad_input, small, large)


def on_device_local(
    tokens,
    token_mask,
    mask_embed,
    norm_gains,
    norm_shifts,
    w_qkv,
    b_qv,
    w_out,
    b_out,
    w_up,
    b_up,
    w_down,
    b_down,
    cotangent,
):
    low = jnp.bfloat16
    _, frames, tubes, patches, width = tokens.shape
    tube_size, head_size = lax.axis_size("tube"), lax.axis_size("head")
    head = lax.axis_index("head")
    parts = lax.axis_size("clip") * tube_size
    frame_share = frames // (tube_size * head_size)
    tube_share = tubes // head_size
    rows = frame_share * tube_size * tubes * patches

    def to_frames(array):
        mine = lax.dynamic_slice_in_dim(
            array[0], head * frame_share * tube_size, frame_share * tube_size, 0
        )
        return lax.all_to_all(mine, "tube", 0, 1, tiled=True)

    def frames_to_tubes(array):
        array = lax.all_to_all(array, ("tube", "head"), 1, 0, tiled=True)
        order = array.reshape(
            tube_size, head_size, frame_share, tube_share, patches, width
        ).transpose(3, 1, 0, 2, 4, 5)
        return order.reshape(rows, width)

    def tubes_to_frames(array):
        order = array.reshape(
            tube_share, head_size, tube_size, frame_share, patches, width
        ).transpose(2, 1, 3, 0, 4, 5)
        order = order.reshape(frames, tube_share, patches, width)
        return lax.all_to_all(order, ("tube", "head"), 0, 1, tiled=True).reshape(rows, width)

    columns = w_qkv.shape[-1]
    hidden_share = w_up.shape[-1]

    def weights_of(b):
        whole_bqv = lax.all_gather(b_qv[b], "head", axis=0)
        return (
            norm_gains[b],
            norm_shifts[b],
            gather_shards(w_qkv[b].reshape(width, 3 * columns), parts).reshape(
                head_size, width, 3 * columns
            ),
            whole_bqv.transpose(1, 0, 2),
            gather_shards(w_out[b], parts).reshape(head_size, columns, width),
            b_out[b],
            gather_shards(w_up[b], parts).reshape(head_size, width, hidden_share),
            lax.all_gather(b_up[b], "head", axis=0),
            gather_shards(w_down[b], parts).reshape(head_size, hidden_share, width),
            b_down[b],
        )

    masked = to_frames(token_mask[..., None]).reshape(-1, 1) == 1
    initial = jnp.where(
        masked,
        mask_embed[None, :],
        to_frames(tokens).reshape(rows, width).astype(jnp.float32),
    )
    sequences = frame_share
    weights = [weights_of(b) for b in range(2)]
    first, stored_first = local_block_forward(initial, frame_share, weights[0])
    second = frames_to_tubes(
        first.astype(low).reshape(frame_share, tube_size * tubes, patches, width)
    ).astype(jnp.float32)
    output, stored_second = local_block_forward(second, tube_share, weights[1])
    output = output.astype(low).reshape(tube_share, frames, patches, width).transpose(1, 0, 2, 3)
    output = lax.all_gather(output, "head", axis=1, tiled=True)[None]
    upstream = lax.dynamic_slice_in_dim(cotangent[0], head * tube_share, tube_share, 1)
    upstream = upstream.transpose(1, 0, 2, 3).reshape(rows, width).astype(jnp.float32)
    grad_second, small_second, large_second = local_block_backward(
        weights[1], stored_second, upstream
    )
    grad_first = tubes_to_frames(grad_second.astype(low)).astype(jnp.float32)
    grad_initial, small_first, large_first = local_block_backward(
        weights[0], stored_first, grad_first
    )
    grad_embed = jnp.sum(jnp.where(masked, grad_initial, 0.0), 0)
    grad_tokens = jnp.where(masked, 0.0, grad_initial).astype(low)
    grad_tokens = grad_tokens.reshape(frame_share, tube_size * tubes, patches, width)
    grad_tokens = lax.all_to_all(grad_tokens, "tube", 1, 0, tiled=True)
    grad_tokens = lax.all_gather(grad_tokens, "head", axis=0, tiled=True)[None]
    shapes = (w_qkv.shape[1:], w_out.shape[1:], w_up.shape[1:], w_down.shape[1:])
    whole = [
        jnp.stack(
            [
                shard_sum(part.reshape(-1, part.shape[-1])).reshape(shape)
                for part in (first_part, second_part)
            ]
        ).astype(jnp.float32)
        for first_part, second_part, shape in zip(large_first, large_second, shapes)
    ]
    small = [jnp.stack(pair) for pair in zip(small_first, small_second)]
    small = lax.psum((grad_embed, *small), AXES)
    embed_grad, gain_grad, shift_grad, bqv_grad, bout_grad, bup_grad, bdown_grad = small
    bqv_grad = lax.dynamic_index_in_dim(bqv_grad, head, 2, False)
    bup_grad = lax.dynamic_index_in_dim(bup_grad, head, 1, False)
    return (
        output,
        grad_tokens,
        embed_grad,
        gain_grad,
        shift_grad,
        whole[0],
        bqv_grad,
        whole[1],
        bout_grad,
        whole[2],
        bup_grad,
        whole[3],
        bdown_grad,
    )


def fits_local(tokens, clip_size, tube_size, head_size):
    clips, frames, tubes = tokens.shape[:3]
    return (
        clips == clip_size
        and frames % (tube_size * head_size) == 0
        and tubes % (tube_size * head_size) == 0
    )


def solution(mesh):
    sizes = [mesh.shape[name] for name in ("clip", "tube", "head")]

    def run(tokens, *others):
        on_device = on_device_local if fits_local(tokens, *sizes) else on_device_sums
        return on_mesh(on_device, mesh)(tokens, *others)

    return run


def on_mesh(on_device, mesh):
    return jax.shard_map(
        on_device,
        mesh=mesh,
        in_specs=(
            P("clip", None, "tube", None, None),
            P("clip", None, "tube", None),
            P(),
            P(),
            P(),
            P(None, None, None, "head"),
            P(None, None, "head"),
            P(None, "head", None),
            P(),
            P(None, None, "head"),
            P(None, "head"),
            P(None, "head", None),
            P(),
            P("clip", None, "tube", None, None),
        ),
        out_specs=(
            P("clip", None, "tube", None, None),
            P("clip", None, "tube", None, None),
            P(),
            P(),
            P(),
            P(None, None, None, "head"),
            P(None, None, "head"),
            P(None, "head", None),
            P(),
            P(None, None, "head"),
            P(None, "head"),
            P(None, "head", None),
            P(),
        ),
        check_vma=False,
    )
```

```python
import jax
import jax.numpy as jnp
from jax import lax
from jax.experimental import pallas as pl
from jax.experimental.pallas import tpu as pltpu
from jax.sharding import PartitionSpec as P

F32 = jnp.float32
LOW = jnp.bfloat16
MESH = pl.DeviceIdType.MESH

HD = 64


EPS = 1e-05


def norm_forward(values, gain_vector, shift_vector):
    centre = values - jnp.mean(values, -1, keepdims=True)
    inverse = lax.rsqrt(jnp.mean(centre * centre, -1, keepdims=True) + EPS)
    normal = centre * inverse
    return (normal * gain_vector + shift_vector, normal, inverse)


def norm_backward(grad_out, normal, inverse, gain_vector):
    grad_normal = grad_out * gain_vector
    grad_in = inverse * (
        grad_normal
        - jnp.mean(grad_normal, -1, keepdims=True)
        - normal * jnp.mean(grad_normal * normal, -1, keepdims=True)
    )
    return (grad_in, jnp.sum(grad_out * normal, 0), jnp.sum(grad_out, 0))


def row_total(partial_sum):
    return lax.psum(partial_sum.astype(jnp.bfloat16), "head").astype(jnp.float32)


def input_total(partial_sum):
    return lax.psum(partial_sum.astype(jnp.bfloat16), "head").astype(jnp.float32)


def split_heads(tensor, batch_count, length):
    return tensor.reshape(batch_count, length, tensor.shape[-1] // HD, HD)


def attend(queries, key_rows, value_rows):
    scores = jnp.einsum(
        "bshe,bthe->bhst", queries, key_rows, preferred_element_type=jnp.float32
    ) * HD ** (-0.5)
    maximum = jnp.max(scores, -1, keepdims=True)
    exponent = jnp.exp(scores - maximum)
    denominator = jnp.sum(exponent, -1, keepdims=True)
    weights_soft = (exponent / denominator).astype(jnp.bfloat16)
    mixture = jnp.einsum(
        "bhst,bthe->bshe", weights_soft, value_rows, preferred_element_type=jnp.float32
    )
    return (mixture.astype(jnp.bfloat16), maximum + jnp.log(denominator))


def attend_back(queries, key_rows, value_rows, log_total, grad_mixture):
    scaling = HD ** (-0.5)
    scores = (
        jnp.einsum("bshe,bthe->bhst", queries, key_rows, preferred_element_type=jnp.float32)
        * scaling
    )
    weights_soft = jnp.exp(scores - log_total)
    grad_weights = jnp.einsum(
        "bshe,bthe->bhst", grad_mixture, value_rows, preferred_element_type=jnp.float32
    )
    grad_values = jnp.einsum(
        "bhst,bshe->bthe",
        weights_soft.astype(jnp.bfloat16),
        grad_mixture,
        preferred_element_type=jnp.float32,
    )
    grad_scores = (
        weights_soft * (grad_weights - jnp.sum(weights_soft * grad_weights, -1, keepdims=True))
    ).astype(jnp.bfloat16)
    grad_queries = (
        jnp.einsum("bhst,bthe->bshe", grad_scores, key_rows, preferred_element_type=jnp.float32)
        * scaling
    )
    grad_keys = (
        jnp.einsum("bhst,bshe->bthe", grad_scores, queries, preferred_element_type=jnp.float32)
        * scaling
    )
    return (grad_queries, grad_keys, grad_values)


def mixer_forward(block_kind, queries, key_rows, value_rows):
    clip_count, frame_count, tube_count, patch_count, columns = queries.shape
    if block_kind == 1:
        reorder = (0, 2, 1, 3, 4)
        pieces = [
            split_heads(
                tensor.transpose(reorder), clip_count * tube_count, frame_count * patch_count
            )
            for tensor in (queries, key_rows, value_rows)
        ]
        mixture, log_total = attend(pieces[0], pieces[1], pieces[2])
        mixture = mixture.reshape(
            clip_count, tube_count, frame_count, patch_count, columns
        ).transpose(reorder)
        return (mixture, (pieces, log_total))
    key_all, value_all = (
        lax.all_gather(key_rows, "tube", axis=2, tiled=True),
        lax.all_gather(value_rows, "tube", axis=2, tiled=True),
    )
    tube_all = key_all.shape[2]
    pieces = [
        split_heads(queries, clip_count * frame_count, tube_count * patch_count),
        split_heads(key_all, clip_count * frame_count, tube_all * patch_count),
        split_heads(value_all, clip_count * frame_count, tube_all * patch_count),
    ]
    mixture, log_total = attend(pieces[0], pieces[1], pieces[2])
    return (
        mixture.reshape(clip_count, frame_count, tube_count, patch_count, columns),
        (pieces, log_total),
    )


def mixer_backward(block_kind, retained, grad_mixture):
    pieces, log_total = retained
    clip_count, frame_count, tube_count, patch_count, columns = grad_mixture.shape
    if block_kind == 1:
        reorder = (0, 2, 1, 3, 4)
        moved = split_heads(
            grad_mixture.transpose(reorder), clip_count * tube_count, frame_count * patch_count
        )
        gradients = attend_back(pieces[0], pieces[1], pieces[2], log_total, moved)
        return [
            grad.astype(jnp.bfloat16)
            .reshape(clip_count, tube_count, frame_count, patch_count, columns)
            .transpose(reorder)
            for grad in gradients
        ]
    gradients = attend_back(
        pieces[0],
        pieces[1],
        pieces[2],
        log_total,
        split_heads(grad_mixture, clip_count * frame_count, tube_count * patch_count),
    )
    tube_all = pieces[1].shape[1] // patch_count
    grad_keys = gradients[1].reshape(clip_count, frame_count, tube_all, patch_count, columns)
    grad_values = gradients[2].reshape(clip_count, frame_count, tube_all, patch_count, columns)
    grad_keys, grad_values = (
        lax.psum_scatter(
            grad_keys.astype(jnp.bfloat16), "tube", scatter_dimension=2, tiled=True
        ).astype(jnp.float32),
        lax.psum_scatter(
            grad_values.astype(jnp.bfloat16), "tube", scatter_dimension=2, tiled=True
        ).astype(jnp.float32),
    )
    grad_queries = (
        gradients[0]
        .astype(jnp.bfloat16)
        .reshape(clip_count, frame_count, tube_count, patch_count, columns)
    )
    return [grad_queries, grad_keys.astype(jnp.bfloat16), grad_values.astype(jnp.bfloat16)]


def block_forward(block_kind, residual, layout, weights):
    gains, shifts, w_qkv, b_qv, w_out, b_out, w_up, b_up, w_down, b_down = weights
    columns = w_qkv.shape[-1]
    grid_shape = layout[:-1] + (columns,)
    normed_share, first_normal, first_inverse = norm_forward(residual, gains[0], shifts[0])
    normed = normed_share.astype(jnp.bfloat16)
    projected = jnp.einsum("rd,dcj->rcj", normed, w_qkv, preferred_element_type=jnp.float32)
    queries = (projected[:, 0] + b_qv[0]).astype(jnp.bfloat16).reshape(grid_shape)
    key_rows = projected[:, 1].astype(jnp.bfloat16).reshape(grid_shape)
    value_rows = (projected[:, 2] + b_qv[1]).astype(jnp.bfloat16).reshape(grid_shape)
    mixture, retained = mixer_forward(block_kind, queries, key_rows, value_rows)
    mixture = mixture.reshape(-1, columns)
    middle = (
        residual + row_total(jnp.dot(mixture, w_out, preferred_element_type=jnp.float32)) + b_out
    )
    second_share, second_normal, second_inverse = norm_forward(middle, gains[1], shifts[1])
    normed_two = second_share.astype(jnp.bfloat16)
    hidden = jnp.dot(normed_two, w_up, preferred_element_type=jnp.float32) + b_up
    active = jax.nn.gelu(hidden).astype(jnp.bfloat16)
    stored = (
        normed,
        first_normal,
        first_inverse,
        retained,
        mixture,
        normed_two,
        second_normal,
        second_inverse,
        hidden,
    )
    return (middle, active, stored)


def block_output(middle, active, w_down, b_down):
    return middle + row_total(jnp.dot(active, w_down, preferred_element_type=jnp.float32)) + b_down


def block_backward(block_kind, residual, layout, weights, grad_rows):
    gains, shifts, w_qkv, b_qv, w_out, b_out, w_up, b_up, w_down, b_down = weights
    middle, active, stored = block_forward(block_kind, residual, layout, weights)
    (
        normed,
        first_normal,
        first_inverse,
        retained,
        mixture,
        normed_two,
        second_normal,
        second_inverse,
        hidden,
    ) = stored
    columns = w_qkv.shape[-1]
    grad_low = grad_rows.astype(jnp.bfloat16)
    grad_wdown = jnp.dot(active.T, grad_low, preferred_element_type=jnp.float32)
    grad_bdown = jnp.sum(grad_rows, 0)
    grad_active = jnp.dot(grad_low, w_down.T, preferred_element_type=jnp.float32)
    gelu_pull = jax.vjp(jax.nn.gelu, hidden)[1]
    grad_hidden = gelu_pull(grad_active)[0].astype(jnp.bfloat16)
    grad_bup = jnp.sum(grad_hidden.astype(jnp.float32), 0)
    grad_wup = jnp.dot(normed_two.T, grad_hidden, preferred_element_type=jnp.float32)
    grad_normed_two = input_total(jnp.dot(grad_hidden, w_up.T, preferred_element_type=jnp.float32))
    grad_norm, grad_gain_two, grad_shift_two = norm_backward(
        grad_normed_two, second_normal, second_inverse, gains[1]
    )
    grad_middle = grad_rows + grad_norm
    grad_bout = jnp.sum(grad_middle, 0)
    grad_mid_low = grad_middle.astype(jnp.bfloat16)
    grad_wout = jnp.dot(mixture.T, grad_mid_low, preferred_element_type=jnp.float32)
    grad_mixture = jnp.dot(grad_mid_low, w_out.T, preferred_element_type=jnp.float32).astype(
        jnp.bfloat16
    )
    grad_parts = mixer_backward(
        block_kind, retained, grad_mixture.reshape(layout[:-1] + (columns,))
    )
    grad_flat = [grad.reshape(-1, columns) for grad in grad_parts]
    grad_project = jnp.stack(grad_flat, 1)
    grad_bqv = jnp.stack(
        [jnp.sum(grad_flat[0].astype(jnp.float32), 0), jnp.sum(grad_flat[2].astype(jnp.float32), 0)]
    )
    grad_wqkv = jnp.einsum("rd,rcj->dcj", normed, grad_project, preferred_element_type=jnp.float32)
    grad_normed = input_total(
        jnp.einsum("rcj,dcj->rd", grad_project, w_qkv, preferred_element_type=jnp.float32)
    )
    grad_input, grad_gain_one, grad_shift_one = norm_backward(
        grad_normed, first_normal, first_inverse, gains[0]
    )
    gradients = (
        jnp.stack([grad_gain_one, grad_gain_two]),
        jnp.stack([grad_shift_one, grad_shift_two]),
        grad_wqkv,
        grad_bqv,
        grad_wout,
        grad_bout,
        grad_wup,
        grad_bup,
        grad_wdown,
        grad_bdown,
    )
    return (grad_middle + grad_input, gradients)


def on_device_sums(
    tokens,
    token_mask,
    mask_embed,
    norm_gains,
    norm_shifts,
    w_qkv,
    b_qv,
    w_out,
    b_out,
    w_up,
    b_up,
    w_down,
    b_down,
    cotangent,
):
    layout = tokens.shape
    width = layout[-1]
    masked = (token_mask == 1).reshape(-1, 1)
    initial = jnp.where(masked, mask_embed[None, :], tokens.reshape(-1, width).astype(jnp.float32))
    upstream = cotangent.reshape(-1, width).astype(jnp.float32)

    def weights_of(block_kind):
        return (
            norm_gains[block_kind],
            norm_shifts[block_kind],
            w_qkv[block_kind],
            b_qv[block_kind],
            w_out[block_kind],
            b_out[block_kind],
            w_up[block_kind],
            b_up[block_kind],
            w_down[block_kind],
            b_down[block_kind],
        )

    middle, active, unused_first = block_forward(0, initial, layout, weights_of(0))
    second = block_output(middle, active, w_down[0], b_down[0])
    middle, active, unused_second = block_forward(1, second, layout, weights_of(1))
    output_rows = block_output(middle, active, w_down[1], b_down[1])
    grad_second, grads_later = block_backward(1, second, layout, weights_of(1), upstream)
    grad_initial, grads_earlier = block_backward(0, initial, layout, weights_of(0), grad_second)
    stacked = [
        jnp.stack([first_grad, later_grad])
        for first_grad, later_grad in zip(grads_earlier, grads_later)
    ]
    grad_embed = jnp.sum(jnp.where(masked, grad_initial, 0.0), 0)
    output_low = output_rows.astype(jnp.bfloat16)
    grad_low = jnp.where(masked, 0.0, grad_initial).astype(jnp.bfloat16)
    shares = (
        lax.psum_scatter(stacked[2], ("clip", "tube"), scatter_dimension=1, tiled=True),
        lax.psum_scatter(stacked[4], ("clip", "tube"), scatter_dimension=2, tiled=True),
        lax.psum_scatter(stacked[6], ("clip", "tube"), scatter_dimension=1, tiled=True),
        lax.psum_scatter(stacked[8], ("clip", "tube"), scatter_dimension=2, tiled=True),
    )
    whole = (
        lax.all_gather(shares[0].astype(jnp.bfloat16), ("clip", "tube"), axis=1, tiled=True).astype(
            jnp.float32
        ),
        lax.all_gather(shares[1].astype(jnp.bfloat16), ("clip", "tube"), axis=2, tiled=True).astype(
            jnp.float32
        ),
        lax.all_gather(shares[2].astype(jnp.bfloat16), ("clip", "tube"), axis=1, tiled=True).astype(
            jnp.float32
        ),
        lax.all_gather(shares[3].astype(jnp.bfloat16), ("clip", "tube"), axis=2, tiled=True).astype(
            jnp.float32
        ),
    )
    column_part = (
        grad_embed,
        stacked[0],
        stacked[1],
        stacked[5],
        stacked[9],
        stacked[3],
        stacked[7],
    )
    small = lax.psum(
        (
            column_part[0],
            column_part[1],
            column_part[2],
            column_part[3],
            column_part[4],
            column_part[5],
            column_part[6],
        ),
        ("clip", "tube"),
    )
    embed_grad, gain_grad, shift_grad, bout_grad, bdown_grad = (
        small[0],
        small[1],
        small[2],
        small[3],
        small[4],
    )
    bqv_grad, bup_grad = (small[5], small[6])
    return (
        output_low.reshape(layout),
        grad_low.reshape(layout),
        embed_grad,
        gain_grad,
        shift_grad,
        whole[0],
        bqv_grad,
        whole[1],
        bout_grad,
        whole[2],
        bup_grad,
        whole[3],
        bdown_grad,
    )


GELU_A = 0.7978845608028654
GELU_B = 0.044715


def dot(left, right, dims):
    return lax.dot_general(left, right, (dims, ((), ())), preferred_element_type=F32)


NN, NT, TN = ((1,), (0,)), ((1,), (1,)), ((0,), (0,))


def standardize(values):
    centre = values - jnp.mean(values, -1, keepdims=True)
    inverse = lax.rsqrt(jnp.mean(centre * centre, -1, keepdims=True) + EPS)
    return centre * inverse, inverse


def head_masks(columns, scale):
    lane = lax.broadcasted_iota(jnp.int32, (1, columns), 1)
    return [
        jnp.where((lane >= j * HD) & (lane < (j + 1) * HD), scale, 0.0).astype(LOW)
        for j in range(columns // HD)
    ]


def gelu_pair(hidden):
    square = hidden * hidden
    tanh = jnp.tanh(GELU_A * hidden * (1.0 + GELU_B * square))
    half = 0.5 * (1.0 + tanh)
    slope = half + hidden * (0.5 * GELU_A) * (1.0 - tanh * tanh) * (1.0 + 3.0 * GELU_B * square)
    return hidden * half, slope


class Sizes:
    def __init__(self, rows, width, shards, columns, units, length):
        self.rows, self.width, self.shards = rows, width, shards
        self.columns, self.units, self.length = columns, units, length
        self.sequences = rows // length
        self.heads = columns // HD
        self.out_row = 3 * columns
        self.up_row = 4 * columns
        self.down_row = 4 * columns + width
        self.block_rows = 4 * columns + width + units


def norm_rows(sz, x_ref, gain, shift, n_ref, chunk=128):
    @pl.loop(0, sz.rows, step=chunk)
    def _(start):
        at = pl.ds(pl.multiple_of(start, chunk), chunk)
        normal, _ = standardize(x_ref[at, :].astype(F32))
        n_ref[at, :] = (normal * gain + shift).astype(LOW)


def forward_attention(sz, shard, w_ref, bqv, n_ref, q_ref, k_ref, v_ref, p_ref, o_ref, m_ref):
    cols, length = sz.columns, sz.length
    normed = n_ref[...]
    q_ref[shard] = (dot(normed, w_ref[shard, 0:cols, :], NT) + bqv[0:1, :]).astype(LOW)
    k_ref[shard] = dot(normed, w_ref[shard, cols : 2 * cols, :], NT).astype(LOW)
    v_ref[shard] = (dot(normed, w_ref[shard, 2 * cols : 3 * cols, :], NT) + bqv[1:2, :]).astype(LOW)
    scaled = head_masks(cols, HD**-0.5)
    masks = head_masks(cols, 1.0)
    for seq in range(sz.sequences):
        at = slice(seq * length, (seq + 1) * length)
        queries, keys, values = q_ref[shard, at, :], k_ref[shard, at, :], v_ref[shard, at, :]
        mixture = jnp.zeros((length, cols), F32)
        for head in range(sz.heads):
            scores = dot(queries * scaled[head], keys, NT)
            exponent = jnp.exp(scores - jnp.max(scores, -1, keepdims=True))
            weights = (exponent / jnp.sum(exponent, -1, keepdims=True)).astype(LOW)
            p_ref[shard, seq * sz.heads + head] = weights
            mixture += dot(weights, values * masks[head], NN)
        o_ref[shard, at, :] = mixture.astype(LOW)
    m_ref[...] += dot(o_ref[shard], w_ref[shard, sz.out_row : sz.out_row + cols, :], NN)


def forward_mlp(sz, shard, w_ref, b_up, n2_ref, a_ref, s_ref, y_ref):
    hidden = (
        dot(n2_ref[...], w_ref[shard, sz.up_row : sz.up_row + sz.width, :], NN) + b_up
    )
    active, slope = gelu_pair(hidden)
    a_ref[shard] = active.astype(LOW)
    s_ref[shard] = slope.astype(LOW)
    y_ref[...] += dot(a_ref[shard], w_ref[shard, sz.down_row : sz.down_row + sz.units, :], NN)


def forward_block(sz, x_ref, gains_ref, shifts_ref, w_ref, bqv_ref, bout_ref, bup_ref, bdown_ref,
                  n_ref, q_ref, k_ref, v_ref, p_ref, o_ref, m_ref, n2_ref, a_ref, s_ref, y_ref):
    norm_rows(sz, x_ref, gains_ref[0:1, :], shifts_ref[0:1, :], n_ref)
    m_ref[...] = x_ref[...].astype(F32) + bout_ref[...]

    @pl.loop(0, sz.shards)
    def _(shard):
        forward_attention(sz, shard, w_ref, bqv_ref[shard], n_ref, q_ref, k_ref, v_ref, p_ref, o_ref, m_ref)

    norm_rows(sz, m_ref, gains_ref[1:2, :], shifts_ref[1:2, :], n2_ref)
    y_ref[...] = m_ref[...] + bdown_ref[...]

    @pl.loop(0, sz.shards)
    def _(shard):
        forward_mlp(sz, shard, w_ref, bup_ref[shard], n2_ref, a_ref, s_ref, y_ref)


def backward_mlp(sz, shard, w_ref, gl_ref, n2_ref, a_ref, s_ref, du_ref, dn_ref, g_ref, gbup_ref):
    low = gl_ref[...]
    grad_active = dot(low, w_ref[shard, sz.down_row : sz.down_row + sz.units, :], NT)
    du_ref[...] = (grad_active * s_ref[shard].astype(F32)).astype(LOW)
    gbup_ref[shard] = jnp.sum(du_ref[...].astype(F32), 0, keepdims=True)
    g_ref[shard, sz.down_row : sz.down_row + sz.units, :] = dot(a_ref[shard], low, TN).astype(LOW)
    g_ref[shard, sz.up_row : sz.up_row + sz.width, :] = dot(n2_ref[...], du_ref[...], TN).astype(LOW)
    dn_ref[...] += dot(du_ref[...], w_ref[shard, sz.up_row : sz.up_row + sz.width, :], NT)


def norm_back_rows(sz, x_ref, gain, dn_ref, g_ref, out_ref, gain_ref, shift_ref, at_row, sum_ref, low_ref, chunk=128):
    gain_ref[at_row : at_row + 1, :] = jnp.zeros((1, sz.width), F32)
    shift_ref[at_row : at_row + 1, :] = jnp.zeros((1, sz.width), F32)
    if sum_ref is not None:
        sum_ref[...] = jnp.zeros_like(sum_ref)

    @pl.loop(0, sz.rows, step=chunk)
    def _(start):
        at = pl.ds(pl.multiple_of(start, chunk), chunk)
        normal, inverse = standardize(x_ref[at, :].astype(F32))
        dn = dn_ref[at, :]
        dy = dn * gain
        part = inverse * (
            dy - jnp.mean(dy, -1, keepdims=True) - normal * jnp.mean(dy * normal, -1, keepdims=True)
        )
        total = g_ref[at, :].astype(F32) + part
        out_ref[at, :] = total.astype(out_ref.dtype)
        if low_ref is not None:
            low_ref[at, :] = total.astype(LOW)
        gain_ref[at_row : at_row + 1, :] += jnp.sum(dn * normal, 0, keepdims=True)
        shift_ref[at_row : at_row + 1, :] += jnp.sum(dn, 0, keepdims=True)
        if sum_ref is not None:
            sum_ref[...] += jnp.sum(total, 0, keepdims=True)


def backward_attention(sz, shard, w_ref, dml_ref, n_ref, q_ref, k_ref, v_ref, p_ref, o_ref,
                       do_ref, dq_ref, dk_ref, dv_ref, dn_ref, g_ref, gbqv_ref):
    cols, length = sz.columns, sz.length
    low = dml_ref[...]
    w_out = w_ref[shard, sz.out_row : sz.out_row + cols, :]
    do_ref[...] = dot(low, w_out, NT).astype(LOW)
    g_ref[shard, sz.out_row : sz.out_row + cols, :] = dot(o_ref[shard], low, TN).astype(LOW)
    scaled = head_masks(cols, HD**-0.5)
    masks = head_masks(cols, 1.0)
    for seq in range(sz.sequences):
        at = slice(seq * length, (seq + 1) * length)
        queries, keys, values = q_ref[shard, at, :], k_ref[shard, at, :], v_ref[shard, at, :]
        grad_o = do_ref[at, :]
        dq = jnp.zeros((length, cols), F32)
        dk = jnp.zeros((length, cols), F32)
        dv = jnp.zeros((length, cols), F32)
        for head in range(sz.heads):
            weights = p_ref[shard, seq * sz.heads + head]
            grad_head = grad_o * masks[head]
            dp = dot(grad_head, values, NT)
            dv += dot(weights, grad_head, TN)
            wide = weights.astype(F32)
            ds = (wide * (dp - jnp.sum(wide * dp, -1, keepdims=True))).astype(LOW)
            dq += dot(ds, keys * scaled[head], NN)
            dk += dot(ds, queries * scaled[head], TN)
        dq_ref[at, :] = dq.astype(LOW)
        dk_ref[at, :] = dk.astype(LOW)
        dv_ref[at, :] = dv.astype(LOW)
    normed = n_ref[...]
    gbqv_ref[shard, 0:1, :] = jnp.sum(dq_ref[...].astype(F32), 0, keepdims=True)
    gbqv_ref[shard, 1:2, :] = jnp.sum(dv_ref[...].astype(F32), 0, keepdims=True)
    for i, part in enumerate((dq_ref, dk_ref, dv_ref)):
        g_ref[shard, i * cols : (i + 1) * cols, :] = dot(part[...], normed, TN).astype(LOW)
        dn_ref[...] += dot(part[...], w_ref[shard, i * cols : (i + 1) * cols, :], NN)


def backward_block(sz, up_ref, x_ref, gains_ref, w_ref, n_ref, q_ref, k_ref, v_ref, p_ref, o_ref, m_ref, n2_ref, a_ref, s_ref,
                   gl_ref, du_ref, dn_ref, dm_ref, do_ref, dq_ref, dk_ref, dv_ref,
                   dx_ref, g_ref, ggain_ref, gshift_ref, gbqv_ref, gbout_ref, gbup_ref, gbdown_ref):
    gl_ref[...] = up_ref[...].astype(LOW)
    gbdown_ref[...] = jnp.sum(up_ref[...].astype(F32), 0, keepdims=True)
    dn_ref[...] = jnp.zeros_like(dn_ref)

    @pl.loop(0, sz.shards)
    def _(shard):
        backward_mlp(sz, shard, w_ref, gl_ref, n2_ref, a_ref, s_ref, du_ref, dn_ref, g_ref, gbup_ref)

    norm_back_rows(sz, m_ref, gains_ref[1:2, :], dn_ref, up_ref, dm_ref, ggain_ref, gshift_ref, 1, gbout_ref, gl_ref)
    dn_ref[...] = jnp.zeros_like(dn_ref)

    @pl.loop(0, sz.shards)
    def _(shard):
        backward_attention(sz, shard, w_ref, gl_ref, n_ref, q_ref, k_ref, v_ref, p_ref, o_ref,
                           do_ref, dq_ref, dk_ref, dv_ref, dn_ref, g_ref, gbqv_ref)

    norm_back_rows(sz, x_ref, gains_ref[0:1, :], dn_ref, dm_ref, dx_ref, ggain_ref, gshift_ref, 0, None, None)


def saved_shapes(sz):
    s, r, c = sz.shards, sz.rows, sz.columns
    return [
        ((r, sz.width), LOW),
        ((s, r, c), LOW),
        ((s, r, c), LOW),
        ((s, r, c), LOW),
        ((s, sz.sequences * sz.heads, sz.length, sz.length), LOW),
        ((s, r, c), LOW),
        ((r, sz.width), F32),
        ((r, sz.width), LOW),
        ((s, r, sz.units), LOW),
        ((s, r, sz.units), LOW),
    ]


def work_shapes(sz):
    r, c = sz.rows, sz.columns
    return [
        ((r, sz.width), LOW),
        ((r, sz.units), LOW),
        ((r, sz.width), F32),
        ((r, sz.width), F32),
        ((r, c), LOW),
        ((r, c), LOW),
        ((r, c), LOW),
        ((r, c), LOW),
    ]


def grad_shapes(sz):
    return [
        ((sz.shards, sz.block_rows, sz.width), LOW),
        ((2, sz.width), F32),
        ((2, sz.width), F32),
        ((sz.shards, 2, sz.columns), F32),
        ((1, sz.width), F32),
        ((sz.shards, 1, sz.units), F32),
        ((1, sz.width), F32),
    ]


def structs(shapes):
    return [jax.ShapeDtypeStruct(s, d) for s, d in shapes]


def vmems(shapes):
    return [pltpu.VMEM(s, d) for s, d in shapes]


PARAMS = pltpu.CompilerParams(vmem_limit_bytes=62 * 2**20)


def run_forward(sz, x, weights):
    def kernel(*refs):
        forward_block(sz, *refs[:-1], refs[-1])
    out = pl.pallas_call(
        kernel, name="forward_first",
        out_shape=structs(saved_shapes(sz) + [((sz.rows, sz.width), F32)]),
        compiler_params=PARAMS,
    )(x, *weights)
    return out[-1], out[:-1]


def run_backward(sz, up, x, weights, saved):
    nw = len(work_shapes(sz))
    ng = len(grad_shapes(sz))
    def kernel(*refs):
        ins = refs[: 4 + 10]
        dx, grads = refs[14], refs[15 : 15 + ng]
        work = refs[15 + ng :]
        backward_block(sz, *ins, *work, dx, *grads)
    return pl.pallas_call(
        kernel, name="backward_first",
        out_shape=structs([((sz.rows, sz.width), F32)] + grad_shapes(sz)),
        scratch_shapes=vmems(work_shapes(sz)),
        compiler_params=PARAMS,
    )(up, x, weights[0], weights[2], *saved)


def run_both(sz, x, up, weights):
    ns, nw, ng = len(saved_shapes(sz)), len(work_shapes(sz)), len(grad_shapes(sz))
    def kernel(*refs):
        x_ref, up_ref = refs[:2]
        w = refs[2:9]
        y_ref, dx_ref = refs[9:11]
        grads = refs[11 : 11 + ng]
        acc, *rest = refs[11 + ng :]
        saved, work = rest[:ns], rest[ns:]
        forward_block(sz, x_ref, *w, *saved, acc)
        y_ref[...] = acc[...].astype(LOW)
        backward_block(sz, up_ref, x_ref, w[0], w[2], *saved, *work, dx_ref, *grads)
    return pl.pallas_call(
        kernel, name="both_second",
        out_shape=structs([((sz.rows, sz.width), LOW), ((sz.rows, sz.width), LOW)] + grad_shapes(sz)),
        scratch_shapes=vmems([((sz.rows, sz.width), F32)] + saved_shapes(sz) + work_shapes(sz)),
        compiler_params=PARAMS,
    )(x, up, *weights)


class Place:
    def __init__(self, heads, zs=None):
        self.clip, self.y, self.z = (lax.axis_index(n) for n in ("clip", "tube", "head"))
        self.heads = heads
        self.core, self.x = lax.rem(self.clip, 2), lax.div(self.clip, 2)
        c, x, y = self.core, self.x, self.y
        self.first = (c + 2 * (x + (1 - c) * (1 - 2 * x)), y + c * (1 - 2 * y), self.z)
        self.second = (c + 2 * (x + c * (1 - 2 * x)), y + (1 - c) * (1 - 2 * y), self.z)
        self.other = (1 - c + 2 * x, y, self.z)
        self.i = (1 - c) * x + c * y
        self.j = (1 - c) * y + c * x

    def head(self, step):
        return (self.clip, self.y, lax.rem(self.z + step + self.heads, self.heads))

    def peers(self):
        return [self.first, self.second, self.other] + [self.head(d) for d in range(1, self.heads)]


def greet(peers):
    barrier = pltpu.get_barrier_semaphore()
    for peer in peers:
        pl.semaphore_signal(barrier, inc=1, device_id=peer, device_id_type=MESH)
    pl.semaphore_wait(barrier, len(peers))


class Moves:
    def __init__(self, send_sem, recv_sem):
        self.send_sem, self.recv_sem, self.count, self.sent = send_sem, recv_sem, 0, []

    def phase(self, copies):
        made = []
        for src, dst, landing, target in copies:
            n = self.count
            self.count += 1
            made.append((src, dst, landing, target, n))
        return made

    def start(self, made):
        for src, dst, _, target, n in made:
            copy = pltpu.make_async_remote_copy(
                src, dst, self.send_sem.at[n], self.recv_sem.at[n], device_id=target, device_id_type=MESH
            )
            copy.start()
            self.sent.append(copy)

    def arrive(self, made):
        for src, _, landing, target, n in made:
            pltpu.make_async_remote_copy(
                src, landing, self.send_sem.at[n], self.recv_sem.at[n], device_id=target, device_id_type=MESH
            ).wait_recv()

    def finish(self):
        for copy in self.sent:
            copy.wait_send()
        self.sent = []


PIECES = 3


def gather_phases(place, moves, shard, full, base, offset, rows):
    q = rows // 8
    c, i, j, z, heads = place.core, place.i, place.j, place.z, place.heads

    def at(ref, head, start, size):
        return ref.at[head, pl.ds(pl.multiple_of(offset + start * q, q), size * q), :]

    def other(d):
        return lax.rem(z + d, heads)

    mine = 4 * c + 2 * j + i
    near = 4 * c + 2 * j + (1 - i)
    pair = 4 * c + 2 * j
    pair_far = 4 * c + 2 * (1 - j)
    src = shard.at[pl.ds(pl.multiple_of(base + offset + mine * q, q), q), :]
    steps = range(1, heads)
    return [
        moves.phase(
            [(src, at(full, z, mine, 1), at(full, lax.rem(z + heads - d, heads), mine, 1), place.head(d)) for d in steps]
        ),
        moves.phase(
            [(at(full, other(d), mine, 1), at(full, other(d), mine, 1), at(full, other(d), near, 1), place.first) for d in steps]
        ),
        moves.phase(
            [(at(full, other(d), pair, 2), at(full, other(d), pair, 2), at(full, other(d), pair_far, 2), place.second) for d in steps]
        ),
        moves.phase(
            [(at(full, other(d), 4 * c, 4), at(full, other(d), 4 * c, 4), at(full, other(d), 4 * (1 - c), 4), place.other) for d in steps]
        ),
    ]


def gather_kernel(heads, block_rows, blocks, shard, biases, tokens, marks, *refs):
    fulls, whole_bias, frames, frame_marks = refs[:blocks], *refs[blocks : blocks + 3]
    held, send_sem, recv_sem, local_sem, held_sem = refs[blocks + 3 :]
    place = Place(heads)
    moves = Moves(send_sem, recv_sem)
    rows = block_rows // PIECES
    y, z = place.y, place.z
    count, tubes = frames.shape[0], tokens.shape[1]
    greet(place.peers())
    owned = pl.ds((2 * z + y) * count, count)
    asked = pl.ds((2 * z + 1 - y) * count, count)
    here, there = pl.ds(y * tubes, tubes), pl.ds((1 - y) * tubes, tubes)
    across = (place.clip, 1 - y, z)
    exchange = moves.phase(
        [
            (src.at[asked], dst.at[:, here], dst.at[:, there], across)
            for src, dst in ((tokens, frames), (marks, frame_marks))
        ]
        + [
            (biases, whole_bias.at[z], whole_bias.at[lax.rem(z + heads - d, heads)], place.head(d))
            for d in range(1, heads)
        ]
    )
    moves.start(exchange)
    local = [
        pltpu.make_async_copy(tokens.at[owned], frames.at[:, here], local_sem.at[0]),
        pltpu.make_async_copy(marks.at[owned], frame_marks.at[:, here], local_sem.at[1]),
        pltpu.make_async_copy(biases, whole_bias.at[z], local_sem.at[2]),
    ]
    hold = [
        (
            pltpu.make_async_copy(shard.at[pl.ds(b * block_rows, block_rows), :], held.at[b], held_sem.at[b]),
            pltpu.make_async_copy(held.at[b], fulls[b].at[z], local_sem.at[3 + b]),
        )
        for b in range(blocks)
    ]
    for copy in local:
        copy.start()
    for fetch, _ in hold:
        fetch.start()
    work = [
        gather_phases(place, moves, shard, fulls[b], b * block_rows, i * rows, rows)
        for b in range(blocks)
        for i in range(PIECES)
    ]
    moves.start(work[0][0])
    for fetch, store in hold:
        fetch.wait()
        store.start()
    for n, phases in enumerate(work):
        moves.arrive(phases[0])
        if n + 1 < len(work):
            moves.start(work[n + 1][0])
        moves.start(phases[1])
        if n:
            moves.arrive(work[n - 1][2])
            moves.start(work[n - 1][3])
        moves.arrive(phases[1])
        moves.start(phases[2])
    moves.arrive(work[-1][2])
    moves.start(work[-1][3])
    for phases in work:
        moves.arrive(phases[3])
    moves.arrive(exchange)
    moves.finish()
    for copy in local:
        copy.wait()
    for _, store in hold:
        store.wait()


def gather_weights(heads, shard, blocks, biases, tokens, marks, frame_share):
    total, width = shard.shape
    block_rows = total // blocks
    count = blocks * PIECES * 4 * (heads - 1) + 2 + heads - 1
    hbm = pl.BlockSpec(memory_space=pl.ANY)
    whole = lambda array: jax.ShapeDtypeStruct(
        (frame_share, 2 * array.shape[1]) + array.shape[2:], array.dtype
    )
    out = pl.pallas_call(
        lambda *refs: gather_kernel(heads, block_rows, blocks, *refs),
        name="gather_weights",
        out_shape=[jax.ShapeDtypeStruct((heads, block_rows, width), LOW)] * blocks
        + [jax.ShapeDtypeStruct((heads,) + biases.shape, F32), whole(tokens), whole(marks)],
        in_specs=[hbm] * 4,
        out_specs=[hbm] * (blocks + 3),
        scratch_shapes=[
            pltpu.VMEM((blocks, block_rows, width), LOW),
            pltpu.SemaphoreType.DMA((count,)),
            pltpu.SemaphoreType.DMA((count,)),
            pltpu.SemaphoreType.DMA((3 + blocks,)),
            pltpu.SemaphoreType.DMA((blocks,)),
        ],
        compiler_params=pltpu.CompilerParams(
            collective_id=0, has_side_effects=True, vmem_limit_bytes=60 * 2**20
        ),
    )(shard, biases, tokens, marks)
    return out[:blocks], *out[blocks:]


class Reduction:
    def __init__(self, place, moves, grads, out, offset, out_row, rows, own, core_buf, first_buf, second_buf, head_buf, local_sem):
        q = rows // 8
        self.q, self.place, self.moves = q, place, moves
        self.grads, self.out, self.out_row = grads, out, out_row
        self.own, self.core_buf, self.first_buf, self.second_buf, self.head_buf = own, core_buf, first_buf, second_buf, head_buf
        c, i, j, z, heads = place.core, place.i, place.j, place.z, place.heads
        cut = lambda ref, start, size: ref.at[:, pl.ds(pl.multiple_of(start * q, q), size * q), :]
        half = lambda core: grads.at[:, pl.ds(pl.multiple_of(offset + core * 4 * q, q), 4 * q), :]
        row = lambda start, size: out.at[pl.ds(pl.multiple_of(out_row + start * q, q), size * q), :]
        self.load = pltpu.make_async_copy(half(c), own, local_sem)
        self.core = moves.phase([(half(1 - c), core_buf, core_buf, place.other)])
        self.first = moves.phase([(cut(own, 2 * (1 - i), 2), first_buf, first_buf, place.first)])
        self.second = moves.phase([(cut(own, 2 * i + 1 - j, 1), second_buf, second_buf, place.second)])
        mine = 2 * i + j
        at = pl.ds(pl.multiple_of(mine * q, q), q)
        self.mine = at
        self.heads = moves.phase(
            [(own.at[lax.rem(z + d, heads), at, :], head_buf.at[d - 1], head_buf.at[d - 1], place.head(d)) for d in range(1, heads)]
        )
        a = 4 * c
        self.share_second = moves.phase([(row(a + mine, 1), row(a + mine, 1), row(a + 2 * i + 1 - j, 1), place.second)])
        self.share_first = moves.phase([(row(a + 2 * i, 2), row(a + 2 * i, 2), row(a + 2 * (1 - i), 2), place.first)])
        self.share_core = moves.phase([(row(a, 4), row(a, 4), row(4 - a, 4), place.other)])
        self.final_row = row(a + mine, 1)

    def begin(self):
        self.load.start()
        self.moves.start(self.core)

    def add(self, buf, start, size):
        q = self.q
        shards = self.own.shape[0]
        at = pl.ds(pl.multiple_of(start * q, q), size * q)

        @pl.loop(0, shards)
        def _(s):
            self.own[s, at, :] = self.own[s, at, :] + buf[s]

    def step_first(self):
        self.load.wait()
        self.moves.arrive(self.core)
        self.add(self.core_buf, 0, 4)
        self.moves.start(self.first)

    def step_second(self):
        self.moves.arrive(self.first)
        self.add(self.first_buf, 2 * self.place.i, 2)
        self.moves.start(self.second)

    def step_heads(self):
        self.moves.arrive(self.second)
        self.add(self.second_buf, 2 * self.place.i + self.place.j, 1)
        self.moves.start(self.heads)

    def step_share(self, final_buf, sem):
        self.moves.arrive(self.heads)
        total = self.own[self.place.z, self.mine, :].astype(F32)
        for d in range(self.place.heads - 1):
            total += self.head_buf[d].astype(F32)
        final_buf[...] = total.astype(LOW)
        copy = pltpu.make_async_copy(final_buf, self.final_row, sem)
        copy.start()
        copy.wait()
        self.moves.start(self.share_second)

    def step_share_first(self):
        self.moves.arrive(self.share_second)
        self.moves.start(self.share_first)

    def step_share_core(self):
        self.moves.arrive(self.share_first)
        self.moves.start(self.share_core)

    def end(self):
        self.moves.arrive(self.share_core)


def reduce_kernel(heads, block_rows, blocks, *refs):
    grads, out = refs[:blocks], refs[blocks]
    own, core_buf, first_buf, second_buf, head_buf, final_buf, send_sem, recv_sem, local_sem, final_sem = refs[blocks + 1 :]
    place = Place(heads)
    moves = Moves(send_sem, recv_sem)
    rows = block_rows // PIECES
    greet(place.peers())
    work = []
    for n in range(blocks * PIECES):
        b, i = blocks - 1 - n // PIECES, PIECES - 1 - n % PIECES
        work.append(
            Reduction(
                place, moves, grads[b], out, i * rows, b * block_rows + i * rows, rows,
                own.at[n], core_buf.at[n], first_buf.at[n], second_buf.at[n], head_buf.at[n], local_sem.at[n],
            )
        )
    count = len(work)
    work[0].begin()
    for tick in range(count + 6):
        if tick + 1 < count:
            work[tick + 1].begin()
        if tick < count:
            work[tick].step_first()
        if 0 <= tick - 1 < count:
            work[tick - 1].step_second()
        if 0 <= tick - 2 < count:
            work[tick - 2].step_heads()
        if 0 <= tick - 3 < count:
            work[tick - 3].step_share(final_buf.at[tick - 3], final_sem.at[tick - 3])
        if 0 <= tick - 4 < count:
            work[tick - 4].step_share_first()
        if 0 <= tick - 5 < count:
            work[tick - 5].step_share_core()
        if 0 <= tick - 6 < count:
            work[tick - 6].end()
    moves.finish()


def reduce_grads(heads, grads):
    blocks = len(grads)
    _, block_rows, width = grads[0].shape
    rows = block_rows // PIECES
    n = blocks * PIECES
    q = rows // 8
    count = n * (6 + heads - 1)
    hbm = pl.BlockSpec(memory_space=pl.ANY)
    return pl.pallas_call(
        lambda *refs: reduce_kernel(heads, block_rows, blocks, *refs),
        name="reduce_grads",
        out_shape=jax.ShapeDtypeStruct((blocks * block_rows, width), LOW),
        in_specs=[hbm] * blocks,
        out_specs=hbm,
        scratch_shapes=[
            pltpu.VMEM((n, heads, 4 * q, width), LOW),
            pltpu.VMEM((n, heads, 4 * q, width), LOW),
            pltpu.VMEM((n, heads, 2 * q, width), LOW),
            pltpu.VMEM((n, heads, q, width), LOW),
            pltpu.VMEM((n, heads - 1, q, width), LOW),
            pltpu.VMEM((n, q, width), LOW),
            pltpu.SemaphoreType.DMA((count,)),
            pltpu.SemaphoreType.DMA((count,)),
            pltpu.SemaphoreType.DMA((n,)),
            pltpu.SemaphoreType.DMA((n,)),
        ],
        compiler_params=pltpu.CompilerParams(collective_id=1, has_side_effects=True, vmem_limit_bytes=60 * 2**20),
    )(*grads)


AXES = ("head", "tube", "clip")


def fits_local(arrays, clip_size, tube_size, head_size):
    clips, frames, tubes = arrays[0].shape[:3]
    width = arrays[0].shape[-1]
    columns, units = arrays[5].shape[3] // head_size, arrays[9].shape[2] // head_size
    devices = tube_size * head_size
    return (
        (clips, clip_size, tube_size) == (4, 4, 2)
        and frames % devices == 0
        and tubes % devices == 0
        and width == 4 * columns == units
        and width % 384 == 0
        and columns % HD == 0
    )


def on_device_local(
    tokens,
    token_mask,
    mask_embed,
    norm_gains,
    norm_shifts,
    w_qkv,
    b_qv,
    w_out,
    b_out,
    w_up,
    b_up,
    w_down,
    b_down,
    cotangent,
):
    _, frames, tubes, patches, width = tokens.shape
    tube_size, heads = lax.axis_size("tube"), lax.axis_size("head")
    head = lax.axis_index("head")
    blocks, columns, units = w_qkv.shape[0], w_qkv.shape[-1], w_up.shape[-1]
    frame_share = frames // (tube_size * heads)
    tube_share = tubes // heads
    rows = frame_share * tube_size * tubes * patches
    sz = Sizes(rows, width, heads, columns, units, rows // frame_share)
    pair = Sizes(rows, width, heads, columns, units, rows // tube_share)

    shard = jnp.concatenate(
        [w_qkv.transpose(0, 2, 3, 1).reshape(blocks, 3 * columns, width), w_out, w_up, w_down], 1
    ).reshape(blocks * sz.block_rows, width)
    marks = jnp.broadcast_to(token_mask[0][..., None], (frames, tubes, patches, 128)).astype(LOW)
    biases = jnp.concatenate([b_qv.reshape(-1), b_up.reshape(-1)]).reshape(-1, 128)
    full, whole_bias, x_frames, mark_frames = gather_weights(
        heads, shard, blocks, biases, tokens[0], marks, frame_share
    )
    whole_bias = whole_bias.reshape(heads, -1)
    cut = blocks * 2 * columns
    whole_bqv = whole_bias[:, :cut].reshape(heads, blocks, 2, columns)
    whole_bup = whole_bias[:, cut:].reshape(heads, blocks, 1, units)

    def weights_of(b):
        return (
            norm_gains[b],
            norm_shifts[b],
            full[b],
            whole_bqv[:, b],
            b_out[b][None],
            whole_bup[:, b],
            b_down[b][None],
        )

    def frames_to_tubes(array):
        array = array.reshape(frame_share, tube_size * tubes, patches, width)
        array = lax.all_to_all(array, ("tube", "head"), 1, 0, tiled=True)
        order = array.reshape(tube_size, heads, frame_share, tube_share, patches, width)
        return order.transpose(3, 1, 0, 2, 4, 5).reshape(rows, width)

    def tubes_to_frames(array):
        order = array.reshape(tube_share, heads, tube_size, frame_share, patches, width)
        order = order.transpose(2, 1, 3, 0, 4, 5).reshape(frames, tube_share, patches, width)
        return lax.all_to_all(order, ("tube", "head"), 0, 1, tiled=True).reshape(rows, width)

    masked = mark_frames[..., :1].reshape(rows, 1) > 0.5
    initial = jnp.where(masked, mask_embed[None, :], x_frames.reshape(rows, width).astype(F32))
    first, saved = run_forward(sz, initial, weights_of(0))
    second = frames_to_tubes(first.astype(LOW))
    upstream = lax.dynamic_slice_in_dim(cotangent[0], head * tube_share, tube_share, 1)
    upstream = upstream.transpose(1, 0, 2, 3).reshape(rows, width)
    output, grad_second, grads_second, *small_second = run_both(
        pair, second, upstream, weights_of(1)
    )
    output = output.reshape(tube_share, frames, patches, width).transpose(1, 0, 2, 3)
    output = lax.all_gather(output, "head", axis=1, tiled=True)[None]
    grad_first = tubes_to_frames(grad_second)
    grad_initial, grads_first, *small_first = run_backward(
        sz, grad_first, initial, weights_of(0), saved
    )
    grad_embed = jnp.sum(jnp.where(masked, grad_initial, 0.0), 0)
    grad_tokens = jnp.where(masked, 0.0, grad_initial).astype(LOW)
    grad_tokens = grad_tokens.reshape(frame_share, tube_size * tubes, patches, width)
    grad_tokens = lax.all_to_all(grad_tokens, "tube", 1, 0, tiled=True)
    grad_tokens = lax.all_gather(grad_tokens, "head", axis=0, tiled=True)[None]
    small = [jnp.stack(two) for two in zip(small_first, small_second)]
    small = lax.psum((grad_embed, *small), AXES)
    embed_grad, gain_grad, shift_grad, bqv_grad, bout_grad, bup_grad, bdown_grad = small
    bqv_grad = lax.dynamic_index_in_dim(bqv_grad, head, 1, False)
    bup_grad = lax.dynamic_index_in_dim(bup_grad, head, 1, False).reshape(blocks, units)
    whole = reduce_grads(heads, [grads_first, grads_second]).astype(F32)
    whole = whole.reshape(blocks, sz.block_rows, width)
    qkv_grad = whole[:, : sz.out_row].reshape(blocks, 3, columns, width).transpose(0, 3, 1, 2)
    return (
        output,
        grad_tokens,
        embed_grad,
        gain_grad,
        shift_grad,
        qkv_grad,
        bqv_grad,
        whole[:, sz.out_row : sz.up_row],
        bout_grad[:, 0],
        whole[:, sz.up_row : sz.down_row],
        bup_grad,
        whole[:, sz.down_row :],
        bdown_grad[:, 0],
    )


def solution(mesh):
    sizes = [mesh.shape[name] for name in ("clip", "tube", "head")]

    def run(*arrays):
        on_device = on_device_local if fits_local(arrays, *sizes) else on_device_sums
        return on_mesh(on_device, mesh)(*arrays)

    return run


def on_mesh(on_device, mesh):
    return jax.shard_map(
        on_device,
        mesh=mesh,
        in_specs=(
            P("clip", None, "tube", None, None),
            P("clip", None, "tube", None),
            P(),
            P(),
            P(),
            P(None, None, None, "head"),
            P(None, None, "head"),
            P(None, "head", None),
            P(),
            P(None, None, "head"),
            P(None, "head"),
            P(None, "head", None),
            P(),
            P("clip", None, "tube", None, None),
        ),
        out_specs=(
            P("clip", None, "tube", None, None),
            P("clip", None, "tube", None, None),
            P(),
            P(),
            P(),
            P(None, None, None, "head"),
            P(None, None, "head"),
            P(None, "head", None),
            P(),
            P(None, None, "head"),
            P(None, "head"),
            P(None, "head", None),
            P(),
        ),
        check_vma=False,
    )
```

```python
import jax
import jax.numpy as jnp
from jax import lax
from jax.experimental import pallas as pl
from jax.experimental.pallas import tpu as pltpu
from jax.sharding import PartitionSpec as P

F32 = jnp.float32
LOW = jnp.bfloat16
MESH = pl.DeviceIdType.MESH

HD = 64


EPS = 1e-05


def norm_forward(values, gain_vector, shift_vector):
    centre = values - jnp.mean(values, -1, keepdims=True)
    inverse = lax.rsqrt(jnp.mean(centre * centre, -1, keepdims=True) + EPS)
    normal = centre * inverse
    return (normal * gain_vector + shift_vector, normal, inverse)


def norm_backward(grad_out, normal, inverse, gain_vector):
    grad_normal = grad_out * gain_vector
    grad_in = inverse * (
        grad_normal
        - jnp.mean(grad_normal, -1, keepdims=True)
        - normal * jnp.mean(grad_normal * normal, -1, keepdims=True)
    )
    return (grad_in, jnp.sum(grad_out * normal, 0), jnp.sum(grad_out, 0))


def row_total(partial_sum):
    return lax.psum(partial_sum.astype(jnp.bfloat16), "head").astype(jnp.float32)


def input_total(partial_sum):
    return lax.psum(partial_sum.astype(jnp.bfloat16), "head").astype(jnp.float32)


def split_heads(tensor, batch_count, length):
    return tensor.reshape(batch_count, length, tensor.shape[-1] // HD, HD)


def attend(queries, key_rows, value_rows):
    scores = jnp.einsum(
        "bshe,bthe->bhst", queries, key_rows, preferred_element_type=jnp.float32
    ) * HD ** (-0.5)
    maximum = jnp.max(scores, -1, keepdims=True)
    exponent = jnp.exp(scores - maximum)
    denominator = jnp.sum(exponent, -1, keepdims=True)
    weights_soft = (exponent / denominator).astype(jnp.bfloat16)
    mixture = jnp.einsum(
        "bhst,bthe->bshe", weights_soft, value_rows, preferred_element_type=jnp.float32
    )
    return (mixture.astype(jnp.bfloat16), maximum + jnp.log(denominator))


def attend_back(queries, key_rows, value_rows, log_total, grad_mixture):
    scaling = HD ** (-0.5)
    scores = (
        jnp.einsum("bshe,bthe->bhst", queries, key_rows, preferred_element_type=jnp.float32)
        * scaling
    )
    weights_soft = jnp.exp(scores - log_total)
    grad_weights = jnp.einsum(
        "bshe,bthe->bhst", grad_mixture, value_rows, preferred_element_type=jnp.float32
    )
    grad_values = jnp.einsum(
        "bhst,bshe->bthe",
        weights_soft.astype(jnp.bfloat16),
        grad_mixture,
        preferred_element_type=jnp.float32,
    )
    grad_scores = (
        weights_soft * (grad_weights - jnp.sum(weights_soft * grad_weights, -1, keepdims=True))
    ).astype(jnp.bfloat16)
    grad_queries = (
        jnp.einsum("bhst,bthe->bshe", grad_scores, key_rows, preferred_element_type=jnp.float32)
        * scaling
    )
    grad_keys = (
        jnp.einsum("bhst,bshe->bthe", grad_scores, queries, preferred_element_type=jnp.float32)
        * scaling
    )
    return (grad_queries, grad_keys, grad_values)


def mixer_forward(block_kind, queries, key_rows, value_rows):
    clip_count, frame_count, tube_count, patch_count, columns = queries.shape
    if block_kind == 1:
        reorder = (0, 2, 1, 3, 4)
        pieces = [
            split_heads(
                tensor.transpose(reorder), clip_count * tube_count, frame_count * patch_count
            )
            for tensor in (queries, key_rows, value_rows)
        ]
        mixture, log_total = attend(pieces[0], pieces[1], pieces[2])
        mixture = mixture.reshape(
            clip_count, tube_count, frame_count, patch_count, columns
        ).transpose(reorder)
        return (mixture, (pieces, log_total))
    key_all, value_all = (
        lax.all_gather(key_rows, "tube", axis=2, tiled=True),
        lax.all_gather(value_rows, "tube", axis=2, tiled=True),
    )
    tube_all = key_all.shape[2]
    pieces = [
        split_heads(queries, clip_count * frame_count, tube_count * patch_count),
        split_heads(key_all, clip_count * frame_count, tube_all * patch_count),
        split_heads(value_all, clip_count * frame_count, tube_all * patch_count),
    ]
    mixture, log_total = attend(pieces[0], pieces[1], pieces[2])
    return (
        mixture.reshape(clip_count, frame_count, tube_count, patch_count, columns),
        (pieces, log_total),
    )


def mixer_backward(block_kind, retained, grad_mixture):
    pieces, log_total = retained
    clip_count, frame_count, tube_count, patch_count, columns = grad_mixture.shape
    if block_kind == 1:
        reorder = (0, 2, 1, 3, 4)
        moved = split_heads(
            grad_mixture.transpose(reorder), clip_count * tube_count, frame_count * patch_count
        )
        gradients = attend_back(pieces[0], pieces[1], pieces[2], log_total, moved)
        return [
            grad.astype(jnp.bfloat16)
            .reshape(clip_count, tube_count, frame_count, patch_count, columns)
            .transpose(reorder)
            for grad in gradients
        ]
    gradients = attend_back(
        pieces[0],
        pieces[1],
        pieces[2],
        log_total,
        split_heads(grad_mixture, clip_count * frame_count, tube_count * patch_count),
    )
    tube_all = pieces[1].shape[1] // patch_count
    grad_keys = gradients[1].reshape(clip_count, frame_count, tube_all, patch_count, columns)
    grad_values = gradients[2].reshape(clip_count, frame_count, tube_all, patch_count, columns)
    grad_keys, grad_values = (
        lax.psum_scatter(
            grad_keys.astype(jnp.bfloat16), "tube", scatter_dimension=2, tiled=True
        ).astype(jnp.float32),
        lax.psum_scatter(
            grad_values.astype(jnp.bfloat16), "tube", scatter_dimension=2, tiled=True
        ).astype(jnp.float32),
    )
    grad_queries = (
        gradients[0]
        .astype(jnp.bfloat16)
        .reshape(clip_count, frame_count, tube_count, patch_count, columns)
    )
    return [grad_queries, grad_keys.astype(jnp.bfloat16), grad_values.astype(jnp.bfloat16)]


def block_forward(block_kind, residual, layout, weights):
    gains, shifts, w_qkv, b_qv, w_out, b_out, w_up, b_up, w_down, b_down = weights
    columns = w_qkv.shape[-1]
    grid_shape = layout[:-1] + (columns,)
    normed_share, first_normal, first_inverse = norm_forward(residual, gains[0], shifts[0])
    normed = normed_share.astype(jnp.bfloat16)
    projected = jnp.einsum("rd,dcj->rcj", normed, w_qkv, preferred_element_type=jnp.float32)
    queries = (projected[:, 0] + b_qv[0]).astype(jnp.bfloat16).reshape(grid_shape)
    key_rows = projected[:, 1].astype(jnp.bfloat16).reshape(grid_shape)
    value_rows = (projected[:, 2] + b_qv[1]).astype(jnp.bfloat16).reshape(grid_shape)
    mixture, retained = mixer_forward(block_kind, queries, key_rows, value_rows)
    mixture = mixture.reshape(-1, columns)
    middle = (
        residual + row_total(jnp.dot(mixture, w_out, preferred_element_type=jnp.float32)) + b_out
    )
    second_share, second_normal, second_inverse = norm_forward(middle, gains[1], shifts[1])
    normed_two = second_share.astype(jnp.bfloat16)
    hidden = jnp.dot(normed_two, w_up, preferred_element_type=jnp.float32) + b_up
    active = jax.nn.gelu(hidden).astype(jnp.bfloat16)
    stored = (
        normed,
        first_normal,
        first_inverse,
        retained,
        mixture,
        normed_two,
        second_normal,
        second_inverse,
        hidden,
    )
    return (middle, active, stored)


def block_output(middle, active, w_down, b_down):
    return middle + row_total(jnp.dot(active, w_down, preferred_element_type=jnp.float32)) + b_down


def block_backward(block_kind, residual, layout, weights, grad_rows):
    gains, shifts, w_qkv, b_qv, w_out, b_out, w_up, b_up, w_down, b_down = weights
    middle, active, stored = block_forward(block_kind, residual, layout, weights)
    (
        normed,
        first_normal,
        first_inverse,
        retained,
        mixture,
        normed_two,
        second_normal,
        second_inverse,
        hidden,
    ) = stored
    columns = w_qkv.shape[-1]
    grad_low = grad_rows.astype(jnp.bfloat16)
    grad_wdown = jnp.dot(active.T, grad_low, preferred_element_type=jnp.float32)
    grad_bdown = jnp.sum(grad_rows, 0)
    grad_active = jnp.dot(grad_low, w_down.T, preferred_element_type=jnp.float32)
    gelu_pull = jax.vjp(jax.nn.gelu, hidden)[1]
    grad_hidden = gelu_pull(grad_active)[0].astype(jnp.bfloat16)
    grad_bup = jnp.sum(grad_hidden.astype(jnp.float32), 0)
    grad_wup = jnp.dot(normed_two.T, grad_hidden, preferred_element_type=jnp.float32)
    grad_normed_two = input_total(jnp.dot(grad_hidden, w_up.T, preferred_element_type=jnp.float32))
    grad_norm, grad_gain_two, grad_shift_two = norm_backward(
        grad_normed_two, second_normal, second_inverse, gains[1]
    )
    grad_middle = grad_rows + grad_norm
    grad_bout = jnp.sum(grad_middle, 0)
    grad_mid_low = grad_middle.astype(jnp.bfloat16)
    grad_wout = jnp.dot(mixture.T, grad_mid_low, preferred_element_type=jnp.float32)
    grad_mixture = jnp.dot(grad_mid_low, w_out.T, preferred_element_type=jnp.float32).astype(
        jnp.bfloat16
    )
    grad_parts = mixer_backward(
        block_kind, retained, grad_mixture.reshape(layout[:-1] + (columns,))
    )
    grad_flat = [grad.reshape(-1, columns) for grad in grad_parts]
    grad_project = jnp.stack(grad_flat, 1)
    grad_bqv = jnp.stack(
        [jnp.sum(grad_flat[0].astype(jnp.float32), 0), jnp.sum(grad_flat[2].astype(jnp.float32), 0)]
    )
    grad_wqkv = jnp.einsum("rd,rcj->dcj", normed, grad_project, preferred_element_type=jnp.float32)
    grad_normed = input_total(
        jnp.einsum("rcj,dcj->rd", grad_project, w_qkv, preferred_element_type=jnp.float32)
    )
    grad_input, grad_gain_one, grad_shift_one = norm_backward(
        grad_normed, first_normal, first_inverse, gains[0]
    )
    gradients = (
        jnp.stack([grad_gain_one, grad_gain_two]),
        jnp.stack([grad_shift_one, grad_shift_two]),
        grad_wqkv,
        grad_bqv,
        grad_wout,
        grad_bout,
        grad_wup,
        grad_bup,
        grad_wdown,
        grad_bdown,
    )
    return (grad_middle + grad_input, gradients)


def on_device_sums(
    tokens,
    token_mask,
    mask_embed,
    norm_gains,
    norm_shifts,
    w_qkv,
    b_qv,
    w_out,
    b_out,
    w_up,
    b_up,
    w_down,
    b_down,
    cotangent,
):
    layout = tokens.shape
    width = layout[-1]
    masked = (token_mask == 1).reshape(-1, 1)
    initial = jnp.where(masked, mask_embed[None, :], tokens.reshape(-1, width).astype(jnp.float32))
    upstream = cotangent.reshape(-1, width).astype(jnp.float32)

    def weights_of(block_kind):
        return (
            norm_gains[block_kind],
            norm_shifts[block_kind],
            w_qkv[block_kind],
            b_qv[block_kind],
            w_out[block_kind],
            b_out[block_kind],
            w_up[block_kind],
            b_up[block_kind],
            w_down[block_kind],
            b_down[block_kind],
        )

    middle, active, unused_first = block_forward(0, initial, layout, weights_of(0))
    second = block_output(middle, active, w_down[0], b_down[0])
    middle, active, unused_second = block_forward(1, second, layout, weights_of(1))
    output_rows = block_output(middle, active, w_down[1], b_down[1])
    grad_second, grads_later = block_backward(1, second, layout, weights_of(1), upstream)
    grad_initial, grads_earlier = block_backward(0, initial, layout, weights_of(0), grad_second)
    stacked = [
        jnp.stack([first_grad, later_grad])
        for first_grad, later_grad in zip(grads_earlier, grads_later)
    ]
    grad_embed = jnp.sum(jnp.where(masked, grad_initial, 0.0), 0)
    output_low = output_rows.astype(jnp.bfloat16)
    grad_low = jnp.where(masked, 0.0, grad_initial).astype(jnp.bfloat16)
    shares = (
        lax.psum_scatter(stacked[2], ("clip", "tube"), scatter_dimension=1, tiled=True),
        lax.psum_scatter(stacked[4], ("clip", "tube"), scatter_dimension=2, tiled=True),
        lax.psum_scatter(stacked[6], ("clip", "tube"), scatter_dimension=1, tiled=True),
        lax.psum_scatter(stacked[8], ("clip", "tube"), scatter_dimension=2, tiled=True),
    )
    whole = (
        lax.all_gather(shares[0].astype(jnp.bfloat16), ("clip", "tube"), axis=1, tiled=True).astype(
            jnp.float32
        ),
        lax.all_gather(shares[1].astype(jnp.bfloat16), ("clip", "tube"), axis=2, tiled=True).astype(
            jnp.float32
        ),
        lax.all_gather(shares[2].astype(jnp.bfloat16), ("clip", "tube"), axis=1, tiled=True).astype(
            jnp.float32
        ),
        lax.all_gather(shares[3].astype(jnp.bfloat16), ("clip", "tube"), axis=2, tiled=True).astype(
            jnp.float32
        ),
    )
    column_part = (
        grad_embed,
        stacked[0],
        stacked[1],
        stacked[5],
        stacked[9],
        stacked[3],
        stacked[7],
    )
    small = lax.psum(
        (
            column_part[0],
            column_part[1],
            column_part[2],
            column_part[3],
            column_part[4],
            column_part[5],
            column_part[6],
        ),
        ("clip", "tube"),
    )
    embed_grad, gain_grad, shift_grad, bout_grad, bdown_grad = (
        small[0],
        small[1],
        small[2],
        small[3],
        small[4],
    )
    bqv_grad, bup_grad = (small[5], small[6])
    return (
        output_low.reshape(layout),
        grad_low.reshape(layout),
        embed_grad,
        gain_grad,
        shift_grad,
        whole[0],
        bqv_grad,
        whole[1],
        bout_grad,
        whole[2],
        bup_grad,
        whole[3],
        bdown_grad,
    )


GELU_A = 0.7978845608028654
GELU_B = 0.044715


def dot(left, right, dims):
    return lax.dot_general(left, right, (dims, ((), ())), preferred_element_type=F32)


NN, NT, TN = ((1,), (0,)), ((1,), (1,)), ((0,), (0,))


def standardize(values):
    centre = values - jnp.mean(values, -1, keepdims=True)
    inverse = lax.rsqrt(jnp.mean(centre * centre, -1, keepdims=True) + EPS)
    return centre * inverse, inverse


def head_masks(columns, scale):
    lane = lax.broadcasted_iota(jnp.int32, (1, columns), 1)
    return [
        jnp.where((lane >= j * HD) & (lane < (j + 1) * HD), scale, 0.0).astype(LOW)
        for j in range(columns // HD)
    ]


def gelu_pair(hidden):
    square = hidden * hidden
    tanh = jnp.tanh(GELU_A * hidden * (1.0 + GELU_B * square))
    half = 0.5 * (1.0 + tanh)
    slope = half + hidden * (0.5 * GELU_A) * (1.0 - tanh * tanh) * (1.0 + 3.0 * GELU_B * square)
    return hidden * half, slope


class Sizes:
    def __init__(self, rows, width, shards, columns, units, length):
        self.rows, self.width, self.shards = rows, width, shards
        self.columns, self.units, self.length = columns, units, length
        self.sequences = rows // length
        self.heads = columns // HD
        self.out_row = 3 * columns
        self.up_row = 4 * columns
        self.down_row = 4 * columns + width
        self.block_rows = 4 * columns + width + units


def norm_rows(sz, x_ref, gain, shift, n_ref, chunk=128):
    @pl.loop(0, sz.rows, step=chunk)
    def _(start):
        at = pl.ds(pl.multiple_of(start, chunk), chunk)
        normal, _ = standardize(x_ref[at, :].astype(F32))
        n_ref[at, :] = (normal * gain + shift).astype(LOW)


def forward_attention(sz, shard, w_ref, b_query, b_value, n_ref, t_ref, p_ref, m_ref):
    cols, length = sz.columns, sz.length
    normed = n_ref[...]
    q_ref, k_ref, v_ref, o_ref = (t_ref.at[shard, i] for i in range(4))
    q_ref[...] = (dot(normed, w_ref[shard, 0:cols, :], NT) + b_query).astype(LOW)
    k_ref[...] = dot(normed, w_ref[shard, cols : 2 * cols, :], NT).astype(LOW)
    v_ref[...] = (dot(normed, w_ref[shard, 2 * cols : 3 * cols, :], NT) + b_value).astype(LOW)
    scaled = head_masks(cols, HD**-0.5)
    masks = head_masks(cols, 1.0)
    for seq in range(sz.sequences):
        at = slice(seq * length, (seq + 1) * length)
        queries, keys, values = q_ref[at, :], k_ref[at, :], v_ref[at, :]
        mixture = jnp.zeros((length, cols), F32)
        for head in range(sz.heads):
            scores = dot(queries * scaled[head], keys, NT)
            exponent = jnp.exp(scores - jnp.max(scores, -1, keepdims=True))
            weights = (exponent / jnp.sum(exponent, -1, keepdims=True)).astype(LOW)
            p_ref[shard, seq * sz.heads + head] = weights
            mixture += dot(weights, values * masks[head], NN)
        o_ref[at, :] = mixture.astype(LOW)
    m_ref[...] += dot(o_ref[...], w_ref[shard, sz.out_row : sz.out_row + cols, :], NN)


def forward_up(sz, shard, w_ref, b_up, n2_ref, as_ref):
    hidden = dot(n2_ref[...], w_ref[shard, sz.up_row : sz.up_row + sz.width, :], NN) + b_up
    active, slope = gelu_pair(hidden)
    as_ref[shard, 0] = active.astype(LOW)
    as_ref[shard, 1] = slope.astype(LOW)


def forward_down(sz, shard, w_ref, as_ref, y_ref):
    y_ref[...] += dot(as_ref[shard, 0], w_ref[shard, sz.down_row : sz.down_row + sz.units, :], NN)


def backward_mlp(sz, shard, w_ref, gl_ref, n2_ref, as_ref, du_ref, dn_ref, g_ref, gbup_ref):
    low = gl_ref[...]
    grad_active = dot(low, w_ref[shard, sz.down_row : sz.down_row + sz.units, :], NT)
    du_ref[...] = (grad_active * as_ref[shard, 1].astype(F32)).astype(LOW)
    gbup_ref[shard] = jnp.sum(du_ref[...].astype(F32), 0, keepdims=True)
    g_ref[shard, sz.down_row : sz.down_row + sz.units, :] = dot(as_ref[shard, 0], low, TN).astype(LOW)
    g_ref[shard, sz.up_row : sz.up_row + sz.width, :] = dot(n2_ref[...], du_ref[...], TN).astype(LOW)
    dn_ref[...] += dot(du_ref[...], w_ref[shard, sz.up_row : sz.up_row + sz.width, :], NT)


def norm_back_rows(sz, x_ref, gain, dn_ref, g_ref, out_ref, gain_ref, shift_ref, at_row, sum_ref, low_ref, chunk=128):
    gain_ref[at_row : at_row + 1, :] = jnp.zeros((1, sz.width), F32)
    shift_ref[at_row : at_row + 1, :] = jnp.zeros((1, sz.width), F32)
    if sum_ref is not None:
        sum_ref[...] = jnp.zeros_like(sum_ref)

    @pl.loop(0, sz.rows, step=chunk)
    def _(start):
        at = pl.ds(pl.multiple_of(start, chunk), chunk)
        normal, inverse = standardize(x_ref[at, :].astype(F32))
        dn = dn_ref[at, :]
        dy = dn * gain
        part = inverse * (
            dy - jnp.mean(dy, -1, keepdims=True) - normal * jnp.mean(dy * normal, -1, keepdims=True)
        )
        total = g_ref[at, :].astype(F32) + part
        out_ref[at, :] = total.astype(out_ref.dtype)
        if low_ref is not None:
            low_ref[at, :] = total.astype(LOW)
        gain_ref[at_row : at_row + 1, :] += jnp.sum(dn * normal, 0, keepdims=True)
        shift_ref[at_row : at_row + 1, :] += jnp.sum(dn, 0, keepdims=True)
        if sum_ref is not None:
            sum_ref[...] += jnp.sum(total, 0, keepdims=True)


def backward_attention(sz, shard, w_ref, dml_ref, n_ref, t_ref, p_ref,
                       do_ref, dq_ref, dk_ref, dv_ref, dn_ref, g_ref, gbqv_ref):
    cols, length = sz.columns, sz.length
    low = dml_ref[...]
    q_ref, k_ref, v_ref, o_ref = (t_ref.at[shard, i] for i in range(4))
    w_out = w_ref[shard, sz.out_row : sz.out_row + cols, :]
    do_ref[...] = dot(low, w_out, NT).astype(LOW)
    g_ref[shard, sz.out_row : sz.out_row + cols, :] = dot(o_ref[...], low, TN).astype(LOW)
    scaled = head_masks(cols, HD**-0.5)
    masks = head_masks(cols, 1.0)
    for seq in range(sz.sequences):
        at = slice(seq * length, (seq + 1) * length)
        queries, keys, values = q_ref[at, :], k_ref[at, :], v_ref[at, :]
        grad_o = do_ref[at, :]
        dq = jnp.zeros((length, cols), F32)
        dk = jnp.zeros((length, cols), F32)
        dv = jnp.zeros((length, cols), F32)
        for head in range(sz.heads):
            weights = p_ref[shard, seq * sz.heads + head]
            grad_head = grad_o * masks[head]
            dp = dot(grad_head, values, NT)
            dv += dot(weights, grad_head, TN)
            wide = weights.astype(F32)
            ds = (wide * (dp - jnp.sum(wide * dp, -1, keepdims=True))).astype(LOW)
            dq += dot(ds, keys * scaled[head], NN)
            dk += dot(ds, queries * scaled[head], TN)
        dq_ref[at, :] = dq.astype(LOW)
        dk_ref[at, :] = dk.astype(LOW)
        dv_ref[at, :] = dv.astype(LOW)
    normed = n_ref[...]
    gbqv_ref[shard, 0:1, :] = jnp.sum(dq_ref[...].astype(F32), 0, keepdims=True)
    gbqv_ref[shard, 1:2, :] = jnp.sum(dv_ref[...].astype(F32), 0, keepdims=True)
    for i, part in enumerate((dq_ref, dk_ref, dv_ref)):
        g_ref[shard, i * cols : (i + 1) * cols, :] = dot(part[...], normed, TN).astype(LOW)
        dn_ref[...] += dot(part[...], w_ref[shard, i * cols : (i + 1) * cols, :], NN)


def backward_block(sz, up_ref, x_ref, gains_ref, w_ref, n_ref, t_ref, p_ref, m_ref, n2_ref, as_ref,
                   gl_ref, du_ref, dn_ref, dm_ref, do_ref, dq_ref, dk_ref, dv_ref,
                   dx_ref, g_ref, ggain_ref, gshift_ref, gbqv_ref, gbout_ref, gbup_ref, gbdown_ref):
    gl_ref[...] = up_ref[...].astype(LOW)
    gbdown_ref[...] = jnp.sum(up_ref[...].astype(F32), 0, keepdims=True)
    dn_ref[...] = jnp.zeros_like(dn_ref)

    @pl.loop(0, sz.shards)
    def _(shard):
        backward_mlp(sz, shard, w_ref, gl_ref, n2_ref, as_ref, du_ref, dn_ref, g_ref, gbup_ref)

    norm_back_rows(sz, m_ref, gains_ref[1:2, :], dn_ref, up_ref, dm_ref, ggain_ref, gshift_ref, 1, gbout_ref, gl_ref)
    dn_ref[...] = jnp.zeros_like(dn_ref)

    @pl.loop(0, sz.shards)
    def _(shard):
        backward_attention(sz, shard, w_ref, gl_ref, n_ref, t_ref, p_ref,
                           do_ref, dq_ref, dk_ref, dv_ref, dn_ref, g_ref, gbqv_ref)

    norm_back_rows(sz, x_ref, gains_ref[0:1, :], dn_ref, dm_ref, dx_ref, ggain_ref, gshift_ref, 0, None, None)


def saved_shapes(sz):
    s, r, c = sz.shards, sz.rows, sz.columns
    return [
        ((r, sz.width), LOW),
        ((s, 4, r, c), LOW),
        ((s, sz.sequences * sz.heads, sz.length, sz.length), LOW),
        ((r, sz.width), F32),
        ((r, sz.width), LOW),
        ((s, 2, r, sz.units), LOW),
    ]


def work_shapes(sz):
    r, c = sz.rows, sz.columns
    return [
        ((r, sz.width), LOW),
        ((r, sz.units), LOW),
        ((r, sz.width), F32),
        ((r, sz.width), F32),
        ((r, c), LOW),
        ((r, c), LOW),
        ((r, c), LOW),
        ((r, c), LOW),
    ]


def grad_shapes(sz):
    return [
        ((sz.shards, sz.block_rows, sz.width), LOW),
        ((2, sz.width), F32),
        ((2, sz.width), F32),
        ((sz.shards, 2, sz.columns), F32),
        ((1, sz.width), F32),
        ((sz.shards, 1, sz.units), F32),
        ((1, sz.width), F32),
    ]


def structs(shapes):
    return [jax.ShapeDtypeStruct(s, d) for s, d in shapes]


def vmems(shapes):
    return [pltpu.VMEM(s, d) for s, d in shapes]


PARAMS = pltpu.CompilerParams(vmem_limit_bytes=62 * 2**20)


def run_backward(sz, up, x, gains, full, saved, name):
    count = len(grad_shapes(sz))
    inputs = 4 + len(saved)

    def kernel(*refs):
        backward_block(sz, *refs[:inputs], *refs[inputs + 1 + count :], *refs[inputs : inputs + 1 + count])

    return pl.pallas_call(
        kernel,
        name=name,
        out_shape=structs([((sz.rows, sz.width), F32)] + grad_shapes(sz)),
        scratch_shapes=vmems(work_shapes(sz)),
        compiler_params=PARAMS,
    )(up, x, gains, full, *saved)


class Place:
    def __init__(self, heads, zs=None):
        self.clip, self.y, self.z = (lax.axis_index(n) for n in ("clip", "tube", "head"))
        self.heads = heads
        self.core, self.x = lax.rem(self.clip, 2), lax.div(self.clip, 2)
        c, x, y = self.core, self.x, self.y
        self.first = (c + 2 * (x + (1 - c) * (1 - 2 * x)), y + c * (1 - 2 * y), self.z)
        self.second = (c + 2 * (x + c * (1 - 2 * x)), y + (1 - c) * (1 - 2 * y), self.z)
        self.other = (1 - c + 2 * x, y, self.z)
        self.i = (1 - c) * x + c * y
        self.j = (1 - c) * y + c * x

    def head(self, step):
        return (self.clip, self.y, lax.rem(self.z + step + self.heads, self.heads))

    def across(self, step):
        return (self.clip, 1 - self.y, lax.rem(self.z + step + self.heads, self.heads))

    def peers(self):
        return [self.first, self.second, self.other] + [self.head(d) for d in range(1, self.heads)]

    def clip_peers(self):
        return [self.head(d) for d in range(1, self.heads)] + [self.across(d) for d in range(self.heads)]

    def all_peers(self):
        return [
            (self.first[0] * (1 - self.core) + self.second[0] * self.core, self.y, self.z),
            self.other,
        ] + self.clip_peers()


def greet(peers):
    barrier = pltpu.get_barrier_semaphore()
    for peer in peers:
        pl.semaphore_signal(barrier, inc=1, device_id=peer, device_id_type=MESH)
    pl.semaphore_wait(barrier, len(peers))


class Moves:
    def __init__(self, send_sem, recv_sem):
        self.send_sem, self.recv_sem, self.count, self.sent = send_sem, recv_sem, 0, []

    def phase(self, copies):
        made = []
        for src, dst, landing, target in copies:
            n = self.count
            self.count += 1
            made.append((src, dst, landing, target, n))
        return made

    def start(self, made):
        for src, dst, _, target, n in made:
            copy = pltpu.make_async_remote_copy(
                src, dst, self.send_sem.at[n], self.recv_sem.at[n], device_id=target, device_id_type=MESH
            )
            copy.start()
            self.sent.append(copy)

    def arrive(self, made):
        for src, _, landing, target, n in made:
            pltpu.make_async_remote_copy(
                src, landing, self.send_sem.at[n], self.recv_sem.at[n], device_id=target, device_id_type=MESH
            ).wait_recv()

    def finish(self):
        for copy in self.sent:
            copy.wait_send()
        self.sent = []


PIECES = 3


def gather_phases(place, moves, shard, full, base, offset, rows):
    q = rows // 8
    c, i, j, z, heads = place.core, place.i, place.j, place.z, place.heads

    def at(ref, head, start, size):
        return ref.at[head, pl.ds(pl.multiple_of(offset + start * q, q), size * q), :]

    def other(d):
        return lax.rem(z + d, heads)

    mine = 4 * c + 2 * j + i
    near = 4 * c + 2 * j + (1 - i)
    pair = 4 * c + 2 * j
    pair_far = 4 * c + 2 * (1 - j)
    src = shard.at[pl.ds(pl.multiple_of(base + offset + mine * q, q), q), :]
    steps = range(1, heads)
    return [
        moves.phase(
            [(src, at(full, z, mine, 1), at(full, lax.rem(z + heads - d, heads), mine, 1), place.head(d)) for d in steps]
        ),
        moves.phase(
            [(at(full, other(d), mine, 1), at(full, other(d), mine, 1), at(full, other(d), near, 1), place.first) for d in steps]
        ),
        moves.phase(
            [(at(full, other(d), pair, 2), at(full, other(d), pair, 2), at(full, other(d), pair_far, 2), place.second) for d in steps]
        ),
        moves.phase(
            [(at(full, other(d), 4 * c, 4), at(full, other(d), 4 * c, 4), at(full, other(d), 4 * (1 - c), 4), place.other) for d in steps]
        ),
    ]


class Saves:
    def __init__(self, sem):
        self.sem, self.count = sem, 0

    def start(self, src, dst):
        copy = pltpu.make_async_copy(src, dst, self.sem.at[self.count])
        self.count += 1
        copy.start()
        return copy


def forward_kernel(sz, blocks, frame_share, tube_share, *refs):
    (shard, tokens, marks, b_qv, b_up, embed, gains, shifts, b_out, b_down), refs = refs[:10], refs[10:]
    fulls, refs = refs[:blocks], refs[blocks:]
    saved, refs = [refs[7 * b : 7 * b + 7] for b in range(blocks)], refs[7 * blocks :]
    (result, frame_marks), refs = refs[:2], refs[2:]
    w = refs[:blocks]
    (
        frames, bqv, bup, x, n, t, p, m, n2, act, y, y_low, second, send_sem, recv_sem, local_sem, save_sem,
    ) = refs[blocks:]
    heads, block_rows, length = sz.shards, sz.block_rows, sz.length
    place = Place(heads)
    moves = Moves(send_sem, recv_sem)
    local, saves = Saves(local_sem), Saves(save_sem)
    rows = block_rows // PIECES
    yy, z = place.y, place.z
    tubes = tokens.shape[1]
    greet(place.all_peers())

    owned = pl.ds((2 * z + yy) * frame_share, frame_share)
    asked = pl.ds((2 * z + 1 - yy) * frame_share, frame_share)
    here, there = pl.ds(yy * tubes, tubes), pl.ds((1 - yy) * tubes, tubes)
    exchange = moves.phase(
        [
            (src.at[asked], dst.at[:, here], dst.at[:, there], place.across(0))
            for src, dst in ((tokens, frames), (marks, frame_marks))
        ]
        + [
            (src, dst.at[z], dst.at[lax.rem(z + heads - d, heads)], place.head(d))
            for src, dst in ((b_qv, bqv), (b_up, bup))
            for d in range(1, heads)
        ]
    )
    spread = moves.phase(
        [
            (
                y_low.at[:, pl.ds((heads * ty + tz) * tube_share, tube_share)],
                second.at[pl.ds((2 * z + yy) * frame_share, frame_share)],
                second.at[pl.ds((2 * fz + ty) * frame_share, frame_share)],
                target,
            )
            for ty, tz, fz, target in [
                (yy, lax.rem(z + d, heads), lax.rem(z + heads - d, heads), place.head(d)) for d in range(1, heads)
            ]
            + [
                (1 - yy, lax.rem(z + d, heads), lax.rem(z + heads - d, heads), place.across(d)) for d in range(heads)
            ]
        ]
    )
    work = [
        gather_phases(place, moves, shard, w[b], b * block_rows, i * rows, rows)
        for b in range(blocks)
        for i in range(PIECES)
    ]
    moves.start(exchange)
    moves.start(work[0][0])
    owns = [
        local.start(tokens.at[owned], frames.at[:, here]),
        local.start(marks.at[owned], frame_marks.at[:, here]),
        local.start(b_qv, bqv.at[z]),
        local.start(b_up, bup.at[z]),
    ] + [local.start(shard.at[pl.ds(b * block_rows, block_rows), :], w[b].at[z]) for b in range(blocks)]

    def save(b, index, src, part=None):
        dst = saved[b][index]
        return saves.start(src, dst if part is None else dst.at[part])

    def begin_block(b):
        norm_rows(sz, x, gains[b, 0:1, :], shifts[b, 0:1, :], n)
        m[...] = x[...] + b_out[b]
        return [save(b, 0, x), save(b, 1, n)]

    def attention(b, low, high):
        @pl.loop(low, high)
        def _(s):
            forward_attention(sz, s, w[b], bqv[s, 2 * b : 2 * b + 1, :], bqv[s, 2 * b + 1 : 2 * b + 2, :], n, t, p, m)

        at = pl.ds(low, high - low)
        return [save(b, 2, t.at[at], at), save(b, 3, p.at[at], at)]

    def middle(b):
        norm_rows(sz, m, gains[b, 1:2, :], shifts[b, 1:2, :], n2)
        y[...] = m[...] + b_down[b]
        return [save(b, 4, m), save(b, 5, n2)]

    def up(b, low, high):
        @pl.loop(low, high)
        def _(s):
            forward_up(sz, s, w[b], bup[s, b : b + 1, :], n2, act)

        at = pl.ds(low, high - low)
        return [save(b, 6, act.at[at], at)]

    def down(b):
        @pl.loop(0, heads)
        def _(s):
            forward_down(sz, s, w[b], act, y)

    def keep(piece):
        b, i = piece // PIECES, piece % PIECES
        at = pl.ds(i * rows, rows)
        return [saves.start(w[b].at[:, at], fulls[b].at[:, at])]

    def arrived(piece):
        moves.arrive(work[piece][3])
        return keep(piece)

    def settle(copies):
        for copy in copies:
            copy.wait()

    half = heads // 2
    kept = []
    early = []
    for tick in range(6):
        moves.arrive(work[tick][0])
        if tick + 1 < 6:
            moves.start(work[tick + 1][0])
        moves.start(work[tick][1])
        if tick:
            moves.arrive(work[tick - 1][2])
            moves.start(work[tick - 1][3])
        if tick == 0:
            settle(owns)
            moves.arrive(exchange)
            tok = frames[...].astype(F32).reshape(sz.rows, sz.width)
            mark = frame_marks[...].astype(F32).reshape(sz.rows, 128)[:, 0:1]
            x[...] = jnp.where(mark > 0.5, embed[...], tok)
            early += begin_block(0)
        if tick == 2:
            kept += arrived(0)
            early += attention(0, 0, half)
        if tick == 3:
            kept += arrived(1)
            early += middle(0)
            early += up(0, 0, half)
        if tick == 4:
            kept += arrived(2)
            down(0)
            y_low[...] = y[...].astype(LOW).reshape(y_low.shape)
            moves.start(spread)
            mine = local.start(
                y_low.at[:, pl.ds((heads * yy + z) * tube_share, tube_share)],
                second.at[pl.ds((2 * z + yy) * frame_share, frame_share)],
            )
        if tick == 5:
            kept += arrived(3)
            kept += attention(1, 0, half)
        moves.arrive(work[tick][1])
        moves.start(work[tick][2])
        if tick == 2:
            early += attention(0, half, heads)
        if tick == 3:
            early += up(0, half, heads)
        if tick == 4:
            moves.arrive(spread)
            mine.wait()
            settle(early)
            for j in range(tube_share):
                x[j * length : (j + 1) * length, :] = second[:, j].astype(F32).reshape(length, sz.width)
            kept += begin_block(1)
        if tick == 5:
            kept += attention(1, half, heads)
    kept += middle(1)
    kept += arrived(4)
    kept += up(1, 0, heads)
    moves.arrive(work[5][2])
    moves.start(work[5][3])
    kept += arrived(5)
    down(1)
    moves.finish()
    y_low[...] = y[...].astype(LOW).reshape(y_low.shape)
    kept.append(saves.start(y_low, result))
    settle(kept)


def run_forward(sz, blocks, frame_share, tube_share, shard, tokens, marks, b_qv, b_up, embed, gains, shifts, b_out, b_down):
    heads, width, rows = sz.shards, sz.width, sz.rows
    tubes, patches = 2 * tokens.shape[1], tokens.shape[2]
    frames = tokens.shape[0]
    saved = [((rows, width), F32)] + saved_shapes(sz)
    whole_frames = (frame_share, tubes, patches)
    count = blocks * PIECES * 4 * (heads - 1) + 2 + 2 * (heads - 1) + 2 * heads - 1
    hbm, vmem = pl.BlockSpec(memory_space=pl.ANY), pl.BlockSpec(memory_space=pltpu.VMEM)
    full = ((heads, sz.block_rows, width), LOW)
    out = pl.pallas_call(
        lambda *refs: forward_kernel(sz, blocks, frame_share, tube_share, *refs),
        name="forward_both",
        out_shape=structs([full] * blocks + saved * blocks + [(whole_frames + (width,), LOW), (whole_frames + (128,), LOW)]),
        in_specs=[hbm] * 5 + [vmem] * 5,
        out_specs=[hbm] * (blocks + 7 * blocks + 1) + [vmem],
        scratch_shapes=vmems(
            [full] * blocks
            + [
                (whole_frames + (width,), LOW),
                ((heads,) + b_qv.shape, F32),
                ((heads,) + b_up.shape, F32),
            ]
            + saved
            + [
                ((rows, width), F32),
                (whole_frames + (width,), LOW),
                ((frames, tube_share, patches, width), LOW),
            ]
        )
        + [
            pltpu.SemaphoreType.DMA((count,)),
            pltpu.SemaphoreType.DMA((count,)),
            pltpu.SemaphoreType.DMA((8,)),
            pltpu.SemaphoreType.DMA((32,)),
        ],
        compiler_params=pltpu.CompilerParams(
            collective_id=0, has_side_effects=True, vmem_limit_bytes=62 * 2**20
        ),
    )(shard, tokens, marks, b_qv, b_up, embed, gains, shifts, b_out, b_down)
    fulls, out = out[:blocks], out[blocks:]
    saved = [out[7 * b : 7 * b + 7] for b in range(blocks)]
    return fulls, saved, out[-2], out[-1]


class Reduction:
    def __init__(self, place, moves, grads, out, offset, out_row, rows, own, core_buf, first_buf, second_buf, head_buf, local_sem):
        q = rows // 8
        self.q, self.place, self.moves = q, place, moves
        self.grads, self.out, self.out_row = grads, out, out_row
        self.own, self.core_buf, self.first_buf, self.second_buf, self.head_buf = own, core_buf, first_buf, second_buf, head_buf
        c, i, j, z, heads = place.core, place.i, place.j, place.z, place.heads
        cut = lambda ref, start, size: ref.at[:, pl.ds(pl.multiple_of(start * q, q), size * q), :]
        half = lambda core: grads.at[:, pl.ds(pl.multiple_of(offset + core * 4 * q, q), 4 * q), :]
        row = lambda start, size: out.at[pl.ds(pl.multiple_of(out_row + start * q, q), size * q), :]
        self.load = pltpu.make_async_copy(half(c), own, local_sem)
        self.core = moves.phase([(half(1 - c), core_buf, core_buf, place.other)])
        self.first = moves.phase([(cut(own, 2 * (1 - i), 2), first_buf, first_buf, place.first)])
        self.second = moves.phase([(cut(own, 2 * i + 1 - j, 1), second_buf, second_buf, place.second)])
        mine = 2 * i + j
        at = pl.ds(pl.multiple_of(mine * q, q), q)
        self.mine = at
        self.heads = moves.phase(
            [(own.at[lax.rem(z + d, heads), at, :], head_buf.at[d - 1], head_buf.at[d - 1], place.head(d)) for d in range(1, heads)]
        )
        a = 4 * c
        self.share_second = moves.phase([(row(a + mine, 1), row(a + mine, 1), row(a + 2 * i + 1 - j, 1), place.second)])
        self.share_first = moves.phase([(row(a + 2 * i, 2), row(a + 2 * i, 2), row(a + 2 * (1 - i), 2), place.first)])
        self.share_core = moves.phase([(row(a, 4), row(a, 4), row(4 - a, 4), place.other)])
        self.final_row = row(a + mine, 1)

    def begin(self):
        self.load.start()
        self.moves.start(self.core)

    def add(self, buf, start, size):
        q = self.q
        shards = self.own.shape[0]
        at = pl.ds(pl.multiple_of(start * q, q), size * q)

        @pl.loop(0, shards)
        def _(s):
            self.own[s, at, :] = self.own[s, at, :] + buf[s]

    def step_first(self):
        self.load.wait()
        self.moves.arrive(self.core)
        self.add(self.core_buf, 0, 4)
        self.moves.start(self.first)

    def step_second(self):
        self.moves.arrive(self.first)
        self.add(self.first_buf, 2 * self.place.i, 2)
        self.moves.start(self.second)

    def step_heads(self):
        self.moves.arrive(self.second)
        self.add(self.second_buf, 2 * self.place.i + self.place.j, 1)
        self.moves.start(self.heads)

    def step_share(self, final_buf, sem):
        self.moves.arrive(self.heads)
        total = self.own[self.place.z, self.mine, :].astype(F32)
        for d in range(self.place.heads - 1):
            total += self.head_buf[d].astype(F32)
        final_buf[...] = total.astype(LOW)
        copy = pltpu.make_async_copy(final_buf, self.final_row, sem)
        copy.start()
        copy.wait()
        self.moves.start(self.share_second)

    def step_share_first(self):
        self.moves.arrive(self.share_second)
        self.moves.start(self.share_first)

    def step_share_core(self):
        self.moves.arrive(self.share_first)
        self.moves.start(self.share_core)

    def end(self):
        self.moves.arrive(self.share_core)


def reduce_kernel(heads, block_rows, blocks, *refs):
    grads, out = refs[:blocks], refs[blocks]
    own, core_buf, first_buf, second_buf, head_buf, final_buf, send_sem, recv_sem, local_sem, final_sem = refs[blocks + 1 :]
    place = Place(heads)
    moves = Moves(send_sem, recv_sem)
    rows = block_rows // PIECES
    greet(place.peers())
    work = []
    for n in range(blocks * PIECES):
        b, i = blocks - 1 - n // PIECES, PIECES - 1 - n % PIECES
        work.append(
            Reduction(
                place, moves, grads[b], out, i * rows, b * block_rows + i * rows, rows,
                own.at[n], core_buf.at[n], first_buf.at[n], second_buf.at[n], head_buf.at[n], local_sem.at[n],
            )
        )
    count = len(work)
    work[0].begin()
    for tick in range(count + 6):
        if tick + 1 < count:
            work[tick + 1].begin()
        if tick < count:
            work[tick].step_first()
        if 0 <= tick - 1 < count:
            work[tick - 1].step_second()
        if 0 <= tick - 2 < count:
            work[tick - 2].step_heads()
        if 0 <= tick - 3 < count:
            work[tick - 3].step_share(final_buf.at[tick - 3], final_sem.at[tick - 3])
        if 0 <= tick - 4 < count:
            work[tick - 4].step_share_first()
        if 0 <= tick - 5 < count:
            work[tick - 5].step_share_core()
        if 0 <= tick - 6 < count:
            work[tick - 6].end()
    moves.finish()


def reduce_grads(heads, grads):
    blocks = len(grads)
    _, block_rows, width = grads[0].shape
    rows = block_rows // PIECES
    n = blocks * PIECES
    q = rows // 8
    count = n * (6 + heads - 1)
    hbm = pl.BlockSpec(memory_space=pl.ANY)
    return pl.pallas_call(
        lambda *refs: reduce_kernel(heads, block_rows, blocks, *refs),
        name="reduce_grads",
        out_shape=jax.ShapeDtypeStruct((blocks * block_rows, width), LOW),
        in_specs=[hbm] * blocks,
        out_specs=hbm,
        scratch_shapes=[
            pltpu.VMEM((n, heads, 4 * q, width), LOW),
            pltpu.VMEM((n, heads, 4 * q, width), LOW),
            pltpu.VMEM((n, heads, 2 * q, width), LOW),
            pltpu.VMEM((n, heads, q, width), LOW),
            pltpu.VMEM((n, heads - 1, q, width), LOW),
            pltpu.VMEM((n, q, width), LOW),
            pltpu.SemaphoreType.DMA((count,)),
            pltpu.SemaphoreType.DMA((count,)),
            pltpu.SemaphoreType.DMA((n,)),
            pltpu.SemaphoreType.DMA((n,)),
        ],
        compiler_params=pltpu.CompilerParams(collective_id=1, has_side_effects=True, vmem_limit_bytes=60 * 2**20),
    )(*grads)


AXES = ("head", "tube", "clip")


def fits_local(arrays, clip_size, tube_size, head_size):
    clips, frames, tubes = arrays[0].shape[:3]
    width = arrays[0].shape[-1]
    columns, units = arrays[5].shape[3] // head_size, arrays[9].shape[2] // head_size
    devices = tube_size * head_size
    return (
        (clips, clip_size, tube_size) == (4, 4, 2)
        and frames % devices == 0
        and frames == tubes
        and head_size % 2 == 0
        and width == 4 * columns == units
        and width % 384 == 0
        and columns % HD == 0
    )


def on_device_local(
    tokens,
    token_mask,
    mask_embed,
    norm_gains,
    norm_shifts,
    w_qkv,
    b_qv,
    w_out,
    b_out,
    w_up,
    b_up,
    w_down,
    b_down,
    cotangent,
):
    _, frames, tubes, patches, width = tokens.shape
    tube_size, heads = lax.axis_size("tube"), lax.axis_size("head")
    head = lax.axis_index("head")
    blocks, columns, units = w_qkv.shape[0], w_qkv.shape[-1], w_up.shape[-1]
    frame_share = frames // (tube_size * heads)
    tube_share = tubes // heads
    rows = frame_share * tube_size * tubes * patches
    sz = Sizes(rows, width, heads, columns, units, rows // frame_share)

    shard = jnp.concatenate(
        [w_qkv.transpose(0, 2, 3, 1).reshape(blocks, 3 * columns, width), w_out, w_up, w_down], 1
    ).reshape(blocks * sz.block_rows, width)
    marks = jnp.broadcast_to(token_mask[0][..., None], (frames, tubes, patches, 128)).astype(LOW)
    full, saved, output, mark_frames = run_forward(
        sz,
        blocks,
        frame_share,
        tube_share,
        shard,
        tokens[0],
        marks,
        b_qv.reshape(2 * blocks, columns),
        b_up,
        mask_embed[None],
        norm_gains,
        norm_shifts,
        b_out[:, None],
        b_down[:, None],
    )
    output = output.reshape(tube_share, frames, patches, width).transpose(1, 0, 2, 3)
    output = lax.all_gather(output, "head", axis=1, tiled=True)[None]

    def tubes_to_frames(array):
        order = array.reshape(tube_share, heads, tube_size, frame_share, patches, width)
        order = order.transpose(2, 1, 3, 0, 4, 5).reshape(frames, tube_share, patches, width)
        return lax.all_to_all(order, ("tube", "head"), 0, 1, tiled=True).reshape(rows, width)

    masked = mark_frames[..., :1].reshape(rows, 1) > 0.5
    upstream = lax.dynamic_slice_in_dim(cotangent[0], head * tube_share, tube_share, 1)
    upstream = upstream.transpose(1, 0, 2, 3).reshape(rows, width)
    grad_second, grads_second, *small_second = run_backward(
        sz, upstream, saved[1][0], norm_gains[1], full[1], saved[1][1:], "backward_second"
    )
    grad_first = tubes_to_frames(grad_second.astype(LOW))
    grad_initial, grads_first, *small_first = run_backward(
        sz, grad_first, saved[0][0], norm_gains[0], full[0], saved[0][1:], "backward_first"
    )
    grad_embed = jnp.sum(jnp.where(masked, grad_initial, 0.0), 0)
    grad_tokens = jnp.where(masked, 0.0, grad_initial).astype(LOW)
    grad_tokens = grad_tokens.reshape(frame_share, tube_size * tubes, patches, width)
    grad_tokens = lax.all_to_all(grad_tokens, "tube", 1, 0, tiled=True)
    grad_tokens = lax.all_gather(grad_tokens, "head", axis=0, tiled=True)[None]
    small = [jnp.stack(two) for two in zip(small_first, small_second)]
    small = lax.psum((grad_embed, *small), AXES)
    embed_grad, gain_grad, shift_grad, bqv_grad, bout_grad, bup_grad, bdown_grad = small
    bqv_grad = lax.dynamic_index_in_dim(bqv_grad, head, 1, False)
    bup_grad = lax.dynamic_index_in_dim(bup_grad, head, 1, False).reshape(blocks, units)
    whole = reduce_grads(heads, [grads_first, grads_second]).astype(F32)
    whole = whole.reshape(blocks, sz.block_rows, width)
    qkv_grad = whole[:, : sz.out_row].reshape(blocks, 3, columns, width).transpose(0, 3, 1, 2)
    return (
        output,
        grad_tokens,
        embed_grad,
        gain_grad,
        shift_grad,
        qkv_grad,
        bqv_grad,
        whole[:, sz.out_row : sz.up_row],
        bout_grad[:, 0],
        whole[:, sz.up_row : sz.down_row],
        bup_grad,
        whole[:, sz.down_row :],
        bdown_grad[:, 0],
    )


def solution(mesh):
    sizes = [mesh.shape[name] for name in ("clip", "tube", "head")]

    def run(*arrays):
        on_device = on_device_local if fits_local(arrays, *sizes) else on_device_sums
        return on_mesh(on_device, mesh)(*arrays)

    return run


def on_mesh(on_device, mesh):
    return jax.shard_map(
        on_device,
        mesh=mesh,
        in_specs=(
            P("clip", None, "tube", None, None),
            P("clip", None, "tube", None),
            P(),
            P(),
            P(),
            P(None, None, None, "head"),
            P(None, None, "head"),
            P(None, "head", None),
            P(),
            P(None, None, "head"),
            P(None, "head"),
            P(None, "head", None),
            P(),
            P("clip", None, "tube", None, None),
        ),
        out_specs=(
            P("clip", None, "tube", None, None),
            P("clip", None, "tube", None, None),
            P(),
            P(),
            P(),
            P(None, None, None, "head"),
            P(None, None, "head"),
            P(None, "head", None),
            P(),
            P(None, None, "head"),
            P(None, "head"),
            P(None, "head", None),
            P(),
        ),
        check_vma=False,
    )
```

```python
import jax
import jax.numpy as jnp
from jax import lax
from jax.experimental import pallas as pl
from jax.experimental.pallas import tpu as pltpu
from jax.sharding import PartitionSpec as P

F32 = jnp.float32
LOW = jnp.bfloat16
MESH = pl.DeviceIdType.MESH

HD = 64


EPS = 1e-05


def norm_forward(values, gain_vector, shift_vector):
    centre = values - jnp.mean(values, -1, keepdims=True)
    inverse = lax.rsqrt(jnp.mean(centre * centre, -1, keepdims=True) + EPS)
    normal = centre * inverse
    return (normal * gain_vector + shift_vector, normal, inverse)


def norm_backward(grad_out, normal, inverse, gain_vector):
    grad_normal = grad_out * gain_vector
    grad_in = inverse * (
        grad_normal
        - jnp.mean(grad_normal, -1, keepdims=True)
        - normal * jnp.mean(grad_normal * normal, -1, keepdims=True)
    )
    return (grad_in, jnp.sum(grad_out * normal, 0), jnp.sum(grad_out, 0))


def row_total(partial_sum):
    return lax.psum(partial_sum.astype(jnp.bfloat16), "head").astype(jnp.float32)


def input_total(partial_sum):
    return lax.psum(partial_sum.astype(jnp.bfloat16), "head").astype(jnp.float32)


def split_heads(tensor, batch_count, length):
    return tensor.reshape(batch_count, length, tensor.shape[-1] // HD, HD)


def attend(queries, key_rows, value_rows):
    scores = jnp.einsum(
        "bshe,bthe->bhst", queries, key_rows, preferred_element_type=jnp.float32
    ) * HD ** (-0.5)
    maximum = jnp.max(scores, -1, keepdims=True)
    exponent = jnp.exp(scores - maximum)
    denominator = jnp.sum(exponent, -1, keepdims=True)
    weights_soft = (exponent / denominator).astype(jnp.bfloat16)
    mixture = jnp.einsum(
        "bhst,bthe->bshe", weights_soft, value_rows, preferred_element_type=jnp.float32
    )
    return (mixture.astype(jnp.bfloat16), maximum + jnp.log(denominator))


def attend_back(queries, key_rows, value_rows, log_total, grad_mixture):
    scaling = HD ** (-0.5)
    scores = (
        jnp.einsum("bshe,bthe->bhst", queries, key_rows, preferred_element_type=jnp.float32)
        * scaling
    )
    weights_soft = jnp.exp(scores - log_total)
    grad_weights = jnp.einsum(
        "bshe,bthe->bhst", grad_mixture, value_rows, preferred_element_type=jnp.float32
    )
    grad_values = jnp.einsum(
        "bhst,bshe->bthe",
        weights_soft.astype(jnp.bfloat16),
        grad_mixture,
        preferred_element_type=jnp.float32,
    )
    grad_scores = (
        weights_soft * (grad_weights - jnp.sum(weights_soft * grad_weights, -1, keepdims=True))
    ).astype(jnp.bfloat16)
    grad_queries = (
        jnp.einsum("bhst,bthe->bshe", grad_scores, key_rows, preferred_element_type=jnp.float32)
        * scaling
    )
    grad_keys = (
        jnp.einsum("bhst,bshe->bthe", grad_scores, queries, preferred_element_type=jnp.float32)
        * scaling
    )
    return (grad_queries, grad_keys, grad_values)


def mixer_forward(block_kind, queries, key_rows, value_rows):
    clip_count, frame_count, tube_count, patch_count, columns = queries.shape
    if block_kind == 1:
        reorder = (0, 2, 1, 3, 4)
        pieces = [
            split_heads(
                tensor.transpose(reorder), clip_count * tube_count, frame_count * patch_count
            )
            for tensor in (queries, key_rows, value_rows)
        ]
        mixture, log_total = attend(pieces[0], pieces[1], pieces[2])
        mixture = mixture.reshape(
            clip_count, tube_count, frame_count, patch_count, columns
        ).transpose(reorder)
        return (mixture, (pieces, log_total))
    key_all, value_all = (
        lax.all_gather(key_rows, "tube", axis=2, tiled=True),
        lax.all_gather(value_rows, "tube", axis=2, tiled=True),
    )
    tube_all = key_all.shape[2]
    pieces = [
        split_heads(queries, clip_count * frame_count, tube_count * patch_count),
        split_heads(key_all, clip_count * frame_count, tube_all * patch_count),
        split_heads(value_all, clip_count * frame_count, tube_all * patch_count),
    ]
    mixture, log_total = attend(pieces[0], pieces[1], pieces[2])
    return (
        mixture.reshape(clip_count, frame_count, tube_count, patch_count, columns),
        (pieces, log_total),
    )


def mixer_backward(block_kind, retained, grad_mixture):
    pieces, log_total = retained
    clip_count, frame_count, tube_count, patch_count, columns = grad_mixture.shape
    if block_kind == 1:
        reorder = (0, 2, 1, 3, 4)
        moved = split_heads(
            grad_mixture.transpose(reorder), clip_count * tube_count, frame_count * patch_count
        )
        gradients = attend_back(pieces[0], pieces[1], pieces[2], log_total, moved)
        return [
            grad.astype(jnp.bfloat16)
            .reshape(clip_count, tube_count, frame_count, patch_count, columns)
            .transpose(reorder)
            for grad in gradients
        ]
    gradients = attend_back(
        pieces[0],
        pieces[1],
        pieces[2],
        log_total,
        split_heads(grad_mixture, clip_count * frame_count, tube_count * patch_count),
    )
    tube_all = pieces[1].shape[1] // patch_count
    grad_keys = gradients[1].reshape(clip_count, frame_count, tube_all, patch_count, columns)
    grad_values = gradients[2].reshape(clip_count, frame_count, tube_all, patch_count, columns)
    grad_keys, grad_values = (
        lax.psum_scatter(
            grad_keys.astype(jnp.bfloat16), "tube", scatter_dimension=2, tiled=True
        ).astype(jnp.float32),
        lax.psum_scatter(
            grad_values.astype(jnp.bfloat16), "tube", scatter_dimension=2, tiled=True
        ).astype(jnp.float32),
    )
    grad_queries = (
        gradients[0]
        .astype(jnp.bfloat16)
        .reshape(clip_count, frame_count, tube_count, patch_count, columns)
    )
    return [grad_queries, grad_keys.astype(jnp.bfloat16), grad_values.astype(jnp.bfloat16)]


def block_forward(block_kind, residual, layout, weights):
    gains, shifts, w_qkv, b_qv, w_out, b_out, w_up, b_up, w_down, b_down = weights
    columns = w_qkv.shape[-1]
    grid_shape = layout[:-1] + (columns,)
    normed_share, first_normal, first_inverse = norm_forward(residual, gains[0], shifts[0])
    normed = normed_share.astype(jnp.bfloat16)
    projected = jnp.einsum("rd,dcj->rcj", normed, w_qkv, preferred_element_type=jnp.float32)
    queries = (projected[:, 0] + b_qv[0]).astype(jnp.bfloat16).reshape(grid_shape)
    key_rows = projected[:, 1].astype(jnp.bfloat16).reshape(grid_shape)
    value_rows = (projected[:, 2] + b_qv[1]).astype(jnp.bfloat16).reshape(grid_shape)
    mixture, retained = mixer_forward(block_kind, queries, key_rows, value_rows)
    mixture = mixture.reshape(-1, columns)
    middle = (
        residual + row_total(jnp.dot(mixture, w_out, preferred_element_type=jnp.float32)) + b_out
    )
    second_share, second_normal, second_inverse = norm_forward(middle, gains[1], shifts[1])
    normed_two = second_share.astype(jnp.bfloat16)
    hidden = jnp.dot(normed_two, w_up, preferred_element_type=jnp.float32) + b_up
    active = jax.nn.gelu(hidden).astype(jnp.bfloat16)
    stored = (
        normed,
        first_normal,
        first_inverse,
        retained,
        mixture,
        normed_two,
        second_normal,
        second_inverse,
        hidden,
    )
    return (middle, active, stored)


def block_output(middle, active, w_down, b_down):
    return middle + row_total(jnp.dot(active, w_down, preferred_element_type=jnp.float32)) + b_down


def block_backward(block_kind, residual, layout, weights, grad_rows):
    gains, shifts, w_qkv, b_qv, w_out, b_out, w_up, b_up, w_down, b_down = weights
    middle, active, stored = block_forward(block_kind, residual, layout, weights)
    (
        normed,
        first_normal,
        first_inverse,
        retained,
        mixture,
        normed_two,
        second_normal,
        second_inverse,
        hidden,
    ) = stored
    columns = w_qkv.shape[-1]
    grad_low = grad_rows.astype(jnp.bfloat16)
    grad_wdown = jnp.dot(active.T, grad_low, preferred_element_type=jnp.float32)
    grad_bdown = jnp.sum(grad_rows, 0)
    grad_active = jnp.dot(grad_low, w_down.T, preferred_element_type=jnp.float32)
    gelu_pull = jax.vjp(jax.nn.gelu, hidden)[1]
    grad_hidden = gelu_pull(grad_active)[0].astype(jnp.bfloat16)
    grad_bup = jnp.sum(grad_hidden.astype(jnp.float32), 0)
    grad_wup = jnp.dot(normed_two.T, grad_hidden, preferred_element_type=jnp.float32)
    grad_normed_two = input_total(jnp.dot(grad_hidden, w_up.T, preferred_element_type=jnp.float32))
    grad_norm, grad_gain_two, grad_shift_two = norm_backward(
        grad_normed_two, second_normal, second_inverse, gains[1]
    )
    grad_middle = grad_rows + grad_norm
    grad_bout = jnp.sum(grad_middle, 0)
    grad_mid_low = grad_middle.astype(jnp.bfloat16)
    grad_wout = jnp.dot(mixture.T, grad_mid_low, preferred_element_type=jnp.float32)
    grad_mixture = jnp.dot(grad_mid_low, w_out.T, preferred_element_type=jnp.float32).astype(
        jnp.bfloat16
    )
    grad_parts = mixer_backward(
        block_kind, retained, grad_mixture.reshape(layout[:-1] + (columns,))
    )
    grad_flat = [grad.reshape(-1, columns) for grad in grad_parts]
    grad_project = jnp.stack(grad_flat, 1)
    grad_bqv = jnp.stack(
        [jnp.sum(grad_flat[0].astype(jnp.float32), 0), jnp.sum(grad_flat[2].astype(jnp.float32), 0)]
    )
    grad_wqkv = jnp.einsum("rd,rcj->dcj", normed, grad_project, preferred_element_type=jnp.float32)
    grad_normed = input_total(
        jnp.einsum("rcj,dcj->rd", grad_project, w_qkv, preferred_element_type=jnp.float32)
    )
    grad_input, grad_gain_one, grad_shift_one = norm_backward(
        grad_normed, first_normal, first_inverse, gains[0]
    )
    gradients = (
        jnp.stack([grad_gain_one, grad_gain_two]),
        jnp.stack([grad_shift_one, grad_shift_two]),
        grad_wqkv,
        grad_bqv,
        grad_wout,
        grad_bout,
        grad_wup,
        grad_bup,
        grad_wdown,
        grad_bdown,
    )
    return (grad_middle + grad_input, gradients)


def on_device_sums(
    tokens,
    token_mask,
    mask_embed,
    norm_gains,
    norm_shifts,
    w_qkv,
    b_qv,
    w_out,
    b_out,
    w_up,
    b_up,
    w_down,
    b_down,
    cotangent,
):
    layout = tokens.shape
    width = layout[-1]
    masked = (token_mask == 1).reshape(-1, 1)
    initial = jnp.where(masked, mask_embed[None, :], tokens.reshape(-1, width).astype(jnp.float32))
    upstream = cotangent.reshape(-1, width).astype(jnp.float32)

    def weights_of(block_kind):
        return (
            norm_gains[block_kind],
            norm_shifts[block_kind],
            w_qkv[block_kind],
            b_qv[block_kind],
            w_out[block_kind],
            b_out[block_kind],
            w_up[block_kind],
            b_up[block_kind],
            w_down[block_kind],
            b_down[block_kind],
        )

    middle, active, unused_first = block_forward(0, initial, layout, weights_of(0))
    second = block_output(middle, active, w_down[0], b_down[0])
    middle, active, unused_second = block_forward(1, second, layout, weights_of(1))
    output_rows = block_output(middle, active, w_down[1], b_down[1])
    grad_second, grads_later = block_backward(1, second, layout, weights_of(1), upstream)
    grad_initial, grads_earlier = block_backward(0, initial, layout, weights_of(0), grad_second)
    stacked = [
        jnp.stack([first_grad, later_grad])
        for first_grad, later_grad in zip(grads_earlier, grads_later)
    ]
    grad_embed = jnp.sum(jnp.where(masked, grad_initial, 0.0), 0)
    output_low = output_rows.astype(jnp.bfloat16)
    grad_low = jnp.where(masked, 0.0, grad_initial).astype(jnp.bfloat16)
    shares = (
        lax.psum_scatter(stacked[2], ("clip", "tube"), scatter_dimension=1, tiled=True),
        lax.psum_scatter(stacked[4], ("clip", "tube"), scatter_dimension=2, tiled=True),
        lax.psum_scatter(stacked[6], ("clip", "tube"), scatter_dimension=1, tiled=True),
        lax.psum_scatter(stacked[8], ("clip", "tube"), scatter_dimension=2, tiled=True),
    )
    whole = (
        lax.all_gather(shares[0].astype(jnp.bfloat16), ("clip", "tube"), axis=1, tiled=True).astype(
            jnp.float32
        ),
        lax.all_gather(shares[1].astype(jnp.bfloat16), ("clip", "tube"), axis=2, tiled=True).astype(
            jnp.float32
        ),
        lax.all_gather(shares[2].astype(jnp.bfloat16), ("clip", "tube"), axis=1, tiled=True).astype(
            jnp.float32
        ),
        lax.all_gather(shares[3].astype(jnp.bfloat16), ("clip", "tube"), axis=2, tiled=True).astype(
            jnp.float32
        ),
    )
    column_part = (
        grad_embed,
        stacked[0],
        stacked[1],
        stacked[5],
        stacked[9],
        stacked[3],
        stacked[7],
    )
    small = lax.psum(
        (
            column_part[0],
            column_part[1],
            column_part[2],
            column_part[3],
            column_part[4],
            column_part[5],
            column_part[6],
        ),
        ("clip", "tube"),
    )
    embed_grad, gain_grad, shift_grad, bout_grad, bdown_grad = (
        small[0],
        small[1],
        small[2],
        small[3],
        small[4],
    )
    bqv_grad, bup_grad = (small[5], small[6])
    return (
        output_low.reshape(layout),
        grad_low.reshape(layout),
        embed_grad,
        gain_grad,
        shift_grad,
        whole[0],
        bqv_grad,
        whole[1],
        bout_grad,
        whole[2],
        bup_grad,
        whole[3],
        bdown_grad,
    )


GELU_A = 0.7978845608028654
GELU_B = 0.044715


def dot(left, right, dims):
    return lax.dot_general(left, right, (dims, ((), ())), preferred_element_type=F32)


NN, NT, TN = ((1,), (0,)), ((1,), (1,)), ((0,), (0,))


def standardize(values):
    centre = values - jnp.mean(values, -1, keepdims=True)
    inverse = lax.rsqrt(jnp.mean(centre * centre, -1, keepdims=True) + EPS)
    return centre * inverse, inverse


def head_masks(columns, scale):
    lane = lax.broadcasted_iota(jnp.int32, (1, columns), 1)
    return [
        jnp.where((lane >= j * HD) & (lane < (j + 1) * HD), scale, 0.0).astype(LOW)
        for j in range(columns // HD)
    ]


def gelu_pair(hidden):
    square = hidden * hidden
    tanh = jnp.tanh(GELU_A * hidden * (1.0 + GELU_B * square))
    half = 0.5 * (1.0 + tanh)
    slope = half + hidden * (0.5 * GELU_A) * (1.0 - tanh * tanh) * (1.0 + 3.0 * GELU_B * square)
    return hidden * half, slope


class Sizes:
    def __init__(self, rows, width, shards, columns, units, length):
        self.rows, self.width, self.shards = rows, width, shards
        self.columns, self.units, self.length = columns, units, length
        self.sequences = rows // length
        self.heads = columns // HD
        self.out_row = 3 * columns
        self.up_row = 4 * columns
        self.down_row = 4 * columns + width
        self.block_rows = 4 * columns + width + units


def norm_rows(sz, x_ref, gain, shift, n_ref, chunk=128):
    @pl.loop(0, sz.rows, step=chunk)
    def _(start):
        at = pl.ds(pl.multiple_of(start, chunk), chunk)
        normal, _ = standardize(x_ref[at, :].astype(F32))
        n_ref[at, :] = (normal * gain + shift).astype(LOW)


def forward_attention(sz, shard, w_ref, b_query, b_value, n_ref, t_ref, p_ref, m_ref):
    cols, length = sz.columns, sz.length
    normed = n_ref[...]
    q_ref, k_ref, v_ref, o_ref = (t_ref.at[shard, i] for i in range(4))
    q_ref[...] = (dot(normed, w_ref[shard, 0:cols, :], NT) + b_query).astype(LOW)
    k_ref[...] = dot(normed, w_ref[shard, cols : 2 * cols, :], NT).astype(LOW)
    v_ref[...] = (dot(normed, w_ref[shard, 2 * cols : 3 * cols, :], NT) + b_value).astype(LOW)
    scaled = head_masks(cols, HD**-0.5)
    masks = head_masks(cols, 1.0)
    for seq in range(sz.sequences):
        at = slice(seq * length, (seq + 1) * length)
        queries, keys, values = q_ref[at, :], k_ref[at, :], v_ref[at, :]
        mixture = jnp.zeros((length, cols), F32)
        for head in range(sz.heads):
            scores = dot(queries * scaled[head], keys, NT)
            exponent = jnp.exp(scores - jnp.max(scores, -1, keepdims=True))
            weights = (exponent / jnp.sum(exponent, -1, keepdims=True)).astype(LOW)
            p_ref[shard, seq * sz.heads + head] = weights
            mixture += dot(weights, values * masks[head], NN)
        o_ref[at, :] = mixture.astype(LOW)
    m_ref[...] += dot(o_ref[...], w_ref[shard, sz.out_row : sz.out_row + cols, :], NN)


def forward_up(sz, shard, w_ref, b_up, n2_ref, as_ref):
    hidden = dot(n2_ref[...], w_ref[shard, sz.up_row : sz.up_row + sz.width, :], NN) + b_up
    active, slope = gelu_pair(hidden)
    as_ref[shard, 0] = active.astype(LOW)
    as_ref[shard, 1] = slope.astype(LOW)


def forward_down(sz, shard, w_ref, as_ref, y_ref):
    y_ref[...] += dot(as_ref[shard, 0], w_ref[shard, sz.down_row : sz.down_row + sz.units, :], NN)


def backward_mlp(sz, w_ref, as_ref, low_ref, n2_ref, du_ref, dn_ref, down_ref, up_ref, sum_row):
    low = low_ref[...]
    grad_active = dot(low, w_ref[sz.width : sz.width + sz.units, :], NT)
    du_ref[...] = (grad_active * as_ref[1].astype(F32)).astype(LOW)
    sum_row[...] = jnp.sum(du_ref[...].astype(F32), 0, keepdims=True)
    down_ref[...] = dot(as_ref[0], low, TN).astype(LOW)
    up_ref[...] = dot(n2_ref[...], du_ref[...], TN).astype(LOW)
    dn_ref[...] += dot(du_ref[...], w_ref[0 : sz.width, :], NT)


def norm_back_rows(sz, x_ref, gain, dn_ref, g_ref, out_ref, gain_row, shift_row, sum_row, low_ref, chunk=128):
    for row in (gain_row, shift_row, sum_row):
        if row is not None:
            row[...] = jnp.zeros_like(row)

    @pl.loop(0, sz.rows, step=chunk)
    def _(start):
        at = pl.ds(pl.multiple_of(start, chunk), chunk)
        normal, inverse = standardize(x_ref[at, :])
        dn = dn_ref[at, :]
        dy = dn * gain
        part = inverse * (
            dy - jnp.mean(dy, -1, keepdims=True) - normal * jnp.mean(dy * normal, -1, keepdims=True)
        )
        total = g_ref[at, :].astype(F32) + part
        out_ref[at, :] = total
        if low_ref is not None:
            low_ref[at, :] = total.astype(LOW)
        gain_row[...] += jnp.sum(dn * normal, 0, keepdims=True)
        shift_row[...] += jnp.sum(dn, 0, keepdims=True)
        if sum_row is not None:
            sum_row[...] += jnp.sum(total, 0, keepdims=True)


def backward_attention(sz, w_ref, t_ref, p_ref, dml_ref, n_ref, do_ref, dq_ref, dk_ref, dv_ref, dn_ref, g_ref, query_row, value_row):
    cols, length = sz.columns, sz.length
    low = dml_ref[...]
    q_ref, k_ref, v_ref, o_ref = (t_ref.at[i] for i in range(4))
    w_out = w_ref[sz.out_row : sz.out_row + cols, :]
    do_ref[...] = dot(low, w_out, NT).astype(LOW)
    g_ref[sz.out_row : sz.out_row + cols, :] = dot(o_ref[...], low, TN).astype(LOW)
    scaled = head_masks(cols, HD**-0.5)
    masks = head_masks(cols, 1.0)
    for seq in range(sz.sequences):
        at = slice(seq * length, (seq + 1) * length)
        queries, keys, values = q_ref[at, :], k_ref[at, :], v_ref[at, :]
        grad_o = do_ref[at, :]
        dq = jnp.zeros((length, cols), F32)
        dk = jnp.zeros((length, cols), F32)
        dv = jnp.zeros((length, cols), F32)
        for head in range(sz.heads):
            weights = p_ref[seq * sz.heads + head]
            grad_head = grad_o * masks[head]
            dp = dot(grad_head, values, NT)
            dv += dot(weights, grad_head, TN)
            wide = weights.astype(F32)
            ds = (wide * (dp - jnp.sum(wide * dp, -1, keepdims=True))).astype(LOW)
            dq += dot(ds, keys * scaled[head], NN)
            dk += dot(ds, queries * scaled[head], TN)
        dq_ref[at, :] = dq.astype(LOW)
        dk_ref[at, :] = dk.astype(LOW)
        dv_ref[at, :] = dv.astype(LOW)
    normed = n_ref[...]
    query_row[...] = jnp.sum(dq_ref[...].astype(F32), 0, keepdims=True)
    value_row[...] = jnp.sum(dv_ref[...].astype(F32), 0, keepdims=True)
    for i, part in enumerate((dq_ref, dk_ref, dv_ref)):
        g_ref[i * cols : (i + 1) * cols, :] = dot(part[...], normed, TN).astype(LOW)
        dn_ref[...] += dot(part[...], w_ref[i * cols : (i + 1) * cols, :], NN)


def saved_shapes(sz):
    s, r, c = sz.shards, sz.rows, sz.columns
    return [
        ((r, sz.width), LOW),
        ((s, 4, r, c), LOW),
        ((s, sz.sequences * sz.heads, sz.length, sz.length), LOW),
        ((r, sz.width), F32),
        ((r, sz.width), LOW),
        ((s, 2, r, sz.units), LOW),
    ]


def structs(shapes):
    return [jax.ShapeDtypeStruct(s, d) for s, d in shapes]


def vmems(shapes):
    return [pltpu.VMEM(s, d) for s, d in shapes]


class Place:
    def __init__(self, heads, zs=None):
        self.clip, self.y, self.z = (lax.axis_index(n) for n in ("clip", "tube", "head"))
        self.heads = heads
        self.core, self.x = lax.rem(self.clip, 2), lax.div(self.clip, 2)
        c, x, y = self.core, self.x, self.y
        self.first = (c + 2 * (x + (1 - c) * (1 - 2 * x)), y + c * (1 - 2 * y), self.z)
        self.second = (c + 2 * (x + c * (1 - 2 * x)), y + (1 - c) * (1 - 2 * y), self.z)
        self.other = (1 - c + 2 * x, y, self.z)
        self.i = (1 - c) * x + c * y
        self.j = (1 - c) * y + c * x

    def head(self, step):
        return (self.clip, self.y, lax.rem(self.z + step + self.heads, self.heads))

    def across(self, step):
        return (self.clip, 1 - self.y, lax.rem(self.z + step + self.heads, self.heads))

    def peers(self):
        return [self.first, self.second, self.other] + [self.head(d) for d in range(1, self.heads)]

    def clip_peers(self):
        return [self.head(d) for d in range(1, self.heads)] + [self.across(d) for d in range(self.heads)]

    def all_peers(self):
        return [
            (self.first[0] * (1 - self.core) + self.second[0] * self.core, self.y, self.z),
            self.other,
        ] + self.clip_peers()


def greet(peers):
    barrier = pltpu.get_barrier_semaphore()
    for peer in peers:
        pl.semaphore_signal(barrier, inc=1, device_id=peer, device_id_type=MESH)
    pl.semaphore_wait(barrier, len(peers))


class Moves:
    def __init__(self, send_sem, recv_sem):
        self.send_sem, self.recv_sem, self.count, self.sent = send_sem, recv_sem, 0, {}

    def phase(self, copies):
        made = []
        for src, dst, landing, target in copies:
            n = self.count
            self.count += 1
            made.append((src, dst, landing, target, n))
        return made

    def start(self, made):
        for src, dst, _, target, n in made:
            copy = pltpu.make_async_remote_copy(
                src, dst, self.send_sem.at[n], self.recv_sem.at[n], device_id=target, device_id_type=MESH
            )
            copy.start()
            self.sent[n] = copy

    def arrive(self, made):
        for src, _, landing, target, n in made:
            pltpu.make_async_remote_copy(
                src, landing, self.send_sem.at[n], self.recv_sem.at[n], device_id=target, device_id_type=MESH
            ).wait_recv()

    def left(self, made):
        for *_, n in made:
            if n in self.sent:
                self.sent.pop(n).wait_send()

    def finish(self):
        for copy in self.sent.values():
            copy.wait_send()
        self.sent = {}


PIECES = 3


def gather_phases(place, moves, shard, full, base, offset, rows):
    q = rows // 8
    c, i, j, z, heads = place.core, place.i, place.j, place.z, place.heads

    def at(ref, head, start, size):
        return ref.at[head, pl.ds(pl.multiple_of(offset + start * q, q), size * q), :]

    def other(d):
        return lax.rem(z + d, heads)

    mine = 4 * c + 2 * j + i
    near = 4 * c + 2 * j + (1 - i)
    pair = 4 * c + 2 * j
    pair_far = 4 * c + 2 * (1 - j)
    src = shard.at[pl.ds(pl.multiple_of(base + offset + mine * q, q), q), :]
    steps = range(1, heads)
    return [
        moves.phase(
            [(src, at(full, z, mine, 1), at(full, lax.rem(z + heads - d, heads), mine, 1), place.head(d)) for d in steps]
        ),
        moves.phase(
            [(at(full, other(d), mine, 1), at(full, other(d), mine, 1), at(full, other(d), near, 1), place.first) for d in steps]
        ),
        moves.phase(
            [(at(full, other(d), pair, 2), at(full, other(d), pair, 2), at(full, other(d), pair_far, 2), place.second) for d in steps]
        ),
        moves.phase(
            [(at(full, other(d), 4 * c, 4), at(full, other(d), 4 * c, 4), at(full, other(d), 4 * (1 - c), 4), place.other) for d in steps]
        ),
    ]


class Saves:
    def __init__(self, sem):
        self.sem, self.count = sem, 0

    def start(self, src, dst):
        copy = pltpu.make_async_copy(src, dst, self.sem.at[self.count])
        self.count += 1
        copy.start()
        return copy


def forward_kernel(sz, blocks, frame_share, tube_share, *refs):
    (shard, tokens, marks, b_qv, b_up, embed, gains, shifts, b_out, b_down), refs = refs[:10], refs[10:]
    fulls, refs = refs[:blocks], refs[blocks:]
    saved, refs = [refs[7 * b : 7 * b + 7] for b in range(blocks)], refs[7 * blocks :]
    (result, frame_marks), refs = refs[:2], refs[2:]
    w = refs[:blocks]
    (
        frames, bqv, bup, x, n, t, p, m, n2, act, y, y_low, second, send_sem, recv_sem, local_sem, save_sem,
    ) = refs[blocks:]
    heads, block_rows, length = sz.shards, sz.block_rows, sz.length
    place = Place(heads)
    moves = Moves(send_sem, recv_sem)
    local, saves = Saves(local_sem), Saves(save_sem)
    rows = block_rows // PIECES
    yy, z = place.y, place.z
    tubes = tokens.shape[1]
    greet(place.all_peers())

    owned = pl.ds((2 * z + yy) * frame_share, frame_share)
    asked = pl.ds((2 * z + 1 - yy) * frame_share, frame_share)
    here, there = pl.ds(yy * tubes, tubes), pl.ds((1 - yy) * tubes, tubes)
    exchange = moves.phase(
        [
            (src.at[asked], dst.at[:, here], dst.at[:, there], place.across(0))
            for src, dst in ((tokens, frames), (marks, frame_marks))
        ]
        + [
            (src, dst.at[z], dst.at[lax.rem(z + heads - d, heads)], place.head(d))
            for src, dst in ((b_qv, bqv), (b_up, bup))
            for d in range(1, heads)
        ]
    )
    spread = moves.phase(
        [
            (
                y_low.at[:, pl.ds((heads * ty + tz) * tube_share, tube_share)],
                second.at[pl.ds((2 * z + yy) * frame_share, frame_share)],
                second.at[pl.ds((2 * fz + ty) * frame_share, frame_share)],
                target,
            )
            for ty, tz, fz, target in [
                (yy, lax.rem(z + d, heads), lax.rem(z + heads - d, heads), place.head(d)) for d in range(1, heads)
            ]
            + [
                (1 - yy, lax.rem(z + d, heads), lax.rem(z + heads - d, heads), place.across(d)) for d in range(heads)
            ]
        ]
    )
    work = [
        gather_phases(place, moves, shard, w[b], b * block_rows, i * rows, rows)
        for b in range(blocks)
        for i in range(PIECES)
    ]
    moves.start(exchange)
    moves.start(work[0][0])
    owns = [
        local.start(tokens.at[owned], frames.at[:, here]),
        local.start(marks.at[owned], frame_marks.at[:, here]),
        local.start(b_qv, bqv.at[z]),
        local.start(b_up, bup.at[z]),
    ] + [local.start(shard.at[pl.ds(b * block_rows, block_rows), :], w[b].at[z]) for b in range(blocks)]

    def save(b, index, src, part=None):
        dst = saved[b][index]
        return saves.start(src, dst if part is None else dst.at[part])

    def begin_block(b):
        norm_rows(sz, x, gains[b, 0:1, :], shifts[b, 0:1, :], n)
        m[...] = x[...] + b_out[b]
        return [save(b, 0, x), save(b, 1, n)]

    def attention(b, low, high):
        @pl.loop(low, high)
        def _(s):
            forward_attention(sz, s, w[b], bqv[s, 2 * b : 2 * b + 1, :], bqv[s, 2 * b + 1 : 2 * b + 2, :], n, t, p, m)

        at = pl.ds(low, high - low)
        return [save(b, 2, t.at[at], at), save(b, 3, p.at[at], at)]

    def middle(b):
        norm_rows(sz, m, gains[b, 1:2, :], shifts[b, 1:2, :], n2)
        y[...] = m[...] + b_down[b]
        return [save(b, 4, m), save(b, 5, n2)]

    def up(b, low, high):
        @pl.loop(low, high)
        def _(s):
            forward_up(sz, s, w[b], bup[s, b : b + 1, :], n2, act)

        at = pl.ds(low, high - low)
        return [save(b, 6, act.at[at], at)]

    def down(b):
        @pl.loop(0, heads)
        def _(s):
            forward_down(sz, s, w[b], act, y)

    def keep(piece):
        b, i = piece // PIECES, piece % PIECES
        at = pl.ds(i * rows, rows)
        return [saves.start(w[b].at[:, at], fulls[b].at[:, at])]

    def arrived(piece):
        moves.arrive(work[piece][3])
        return keep(piece)

    def settle(copies):
        for copy in copies:
            copy.wait()

    half = heads // 2
    kept = []
    early = []
    for tick in range(6):
        moves.arrive(work[tick][0])
        if tick + 1 < 6:
            moves.start(work[tick + 1][0])
        moves.start(work[tick][1])
        if tick:
            moves.arrive(work[tick - 1][2])
            moves.start(work[tick - 1][3])
        if tick == 0:
            settle(owns)
            moves.arrive(exchange)
            tok = frames[...].astype(F32).reshape(sz.rows, sz.width)
            mark = frame_marks[...].astype(F32).reshape(sz.rows, 128)[:, 0:1]
            x[...] = jnp.where(mark > 0.5, embed[...], tok)
            early += begin_block(0)
        if tick == 2:
            kept += arrived(0)
            early += attention(0, 0, half)
        if tick == 3:
            kept += arrived(1)
            early += middle(0)
            early += up(0, 0, half)
        if tick == 4:
            kept += arrived(2)
            down(0)
            y_low[...] = y[...].astype(LOW).reshape(y_low.shape)
            moves.start(spread)
            mine = local.start(
                y_low.at[:, pl.ds((heads * yy + z) * tube_share, tube_share)],
                second.at[pl.ds((2 * z + yy) * frame_share, frame_share)],
            )
        if tick == 5:
            kept += arrived(3)
            kept += attention(1, 0, half)
        moves.arrive(work[tick][1])
        moves.start(work[tick][2])
        if tick == 2:
            early += attention(0, half, heads)
        if tick == 3:
            early += up(0, half, heads)
        if tick == 4:
            moves.arrive(spread)
            mine.wait()
            settle(early)
            for j in range(tube_share):
                x[j * length : (j + 1) * length, :] = second[:, j].astype(F32).reshape(length, sz.width)
            kept += begin_block(1)
        if tick == 5:
            kept += attention(1, half, heads)
    kept += middle(1)
    kept += arrived(4)
    kept += up(1, 0, heads)
    moves.arrive(work[5][2])
    moves.start(work[5][3])
    kept += arrived(5)
    down(1)
    moves.finish()
    y_low[...] = y[...].astype(LOW).reshape(y_low.shape)
    kept.append(saves.start(y_low, result))
    settle(kept)


def run_forward(sz, blocks, frame_share, tube_share, shard, tokens, marks, b_qv, b_up, embed, gains, shifts, b_out, b_down):
    heads, width, rows = sz.shards, sz.width, sz.rows
    tubes, patches = 2 * tokens.shape[1], tokens.shape[2]
    frames = tokens.shape[0]
    saved = [((rows, width), F32)] + saved_shapes(sz)
    whole_frames = (frame_share, tubes, patches)
    count = blocks * PIECES * 4 * (heads - 1) + 2 + 2 * (heads - 1) + 2 * heads - 1
    hbm, vmem = pl.BlockSpec(memory_space=pl.ANY), pl.BlockSpec(memory_space=pltpu.VMEM)
    full = ((heads, sz.block_rows, width), LOW)
    out = pl.pallas_call(
        lambda *refs: forward_kernel(sz, blocks, frame_share, tube_share, *refs),
        name="forward_both",
        out_shape=structs([full] * blocks + saved * blocks + [(whole_frames + (width,), LOW), (whole_frames + (128,), LOW)]),
        in_specs=[hbm] * 5 + [vmem] * 5,
        out_specs=[hbm] * (blocks + 7 * blocks + 1) + [vmem],
        scratch_shapes=vmems(
            [full] * blocks
            + [
                (whole_frames + (width,), LOW),
                ((heads,) + b_qv.shape, F32),
                ((heads,) + b_up.shape, F32),
            ]
            + saved
            + [
                ((rows, width), F32),
                (whole_frames + (width,), LOW),
                ((frames, tube_share, patches, width), LOW),
            ]
        )
        + [
            pltpu.SemaphoreType.DMA((count,)),
            pltpu.SemaphoreType.DMA((count,)),
            pltpu.SemaphoreType.DMA((8,)),
            pltpu.SemaphoreType.DMA((32,)),
        ],
        compiler_params=pltpu.CompilerParams(
            collective_id=0, has_side_effects=True, vmem_limit_bytes=62 * 2**20
        ),
    )(shard, tokens, marks, b_qv, b_up, embed, gains, shifts, b_out, b_down)
    fulls, out = out[:blocks], out[blocks:]
    saved = [out[7 * b : 7 * b + 7] for b in range(blocks)]
    return fulls, saved, out[-2], out[-1]


class Line:
    def __init__(self, place, send_sem, recv_sem, region):
        self.place, self.send_sem, self.recv_sem, self.region = place, send_sem, recv_sem, region
        self.steps = place.heads - 1

    def moves(self, step):
        z, last = self.place.z, self.place.heads - 1
        return [
            ((z >= step) & (z < last), z - step, 1, z > step, z - 1 - step, 2 * step),
            ((z <= last - step) & (z > 0), z + step, -1, z < last - step, z + 1 + step, 2 * step + 1),
        ]

    def copy(self, block, way, n):
        return pltpu.make_async_remote_copy(
            self.region(block),
            self.region(block),
            self.send_sem.at[n],
            self.recv_sem.at[n],
            device_id=self.place.head(way),
            device_id_type=MESH,
        )

    def start(self, step):
        for sends, block, way, _, _, n in self.moves(step):
            pl.when(sends)(lambda block=block, way=way, n=n: self.copy(block, way, n).start())

    def arrive(self, step):
        for _, _, way, gets, block, n in self.moves(step):
            pl.when(gets)(lambda block=block, way=way, n=n: self.copy(block, way, n).wait_recv())

    def finish(self):
        for step in range(self.steps):
            for sends, block, way, _, _, n in self.moves(step):
                pl.when(sends)(lambda block=block, way=way, n=n: self.copy(block, way, n).wait_send())


class Reduction:
    def __init__(self, place, moves, grads, out, out_row, rows, bufs, final_buf, final_sem):
        q = rows // 8
        self.q, self.place, self.moves, self.grads = q, place, moves, grads
        self.core_buf, self.first_buf, self.second_buf, self.head_buf = bufs
        self.final_buf, self.final_sem = final_buf, final_sem
        c, i, j, z, heads = place.core, place.i, place.j, place.z, place.heads
        cut = lambda start, size: pl.ds(pl.multiple_of(start * q, q), size * q)
        row = lambda start, size: out.at[pl.ds(pl.multiple_of(out_row + start * q, q), size * q), :]
        self.kept, self.given = cut(4 * c, 4), cut(4 * (1 - c), 4)
        self.part, self.subpart = cut(2 * i, 2), cut(j, 1)
        shards = range(heads)
        self.core = moves.phase(
            [(grads.at[s % 2, self.given, :], self.core_buf.at[s], self.core_buf.at[s], place.other) for s in shards]
        )
        self.first = moves.phase(
            [
                (self.core_buf.at[s, cut(2 * (1 - i), 2), :], self.first_buf.at[s], self.first_buf.at[s], place.first)
                for s in shards
            ]
        )
        self.second = moves.phase(
            [(self.first_buf.at[:, cut(1 - j, 1), :], self.second_buf, self.second_buf, place.second)]
        )
        self.heads = moves.phase(
            [
                (self.second_buf.at[lax.rem(z + d, heads)], self.head_buf.at[d - 1], self.head_buf.at[d - 1], place.head(d))
                for d in range(1, heads)
            ]
        )
        a, mine = 4 * c, 2 * i + j
        self.share_second = moves.phase([(row(a + mine, 1), row(a + mine, 1), row(a + 2 * i + 1 - j, 1), place.second)])
        self.share_first = moves.phase([(row(a + 2 * i, 2), row(a + 2 * i, 2), row(a + 2 * (1 - i), 2), place.first)])
        self.share_core = moves.phase([(row(a, 4), row(a, 4), row(4 - a, 4), place.other)])
        self.final_row = row(a + mine, 1)

    def give(self, s):
        self.moves.start([self.core[s]])

    def step_first(self, s):
        self.moves.arrive([self.core[s]])
        self.core_buf[s] = self.core_buf[s] + self.grads[s % 2, self.kept, :]
        self.moves.start([self.first[s]])

    def step_second(self, free_sem=None):
        self.moves.arrive(self.first)

        @pl.loop(0, self.place.heads)
        def _(s):
            self.first_buf[s] = self.first_buf[s] + self.core_buf[s, self.part, :]

        self.moves.start(self.second)
        if free_sem is not None:
            self.moves.left(self.first)
            pl.semaphore_signal(free_sem, inc=1, device_id=self.place.other, device_id_type=MESH)

    def step_heads(self):
        self.moves.arrive(self.second)

        @pl.loop(0, self.place.heads)
        def _(s):
            self.second_buf[s] = self.second_buf[s] + self.first_buf[s, self.subpart, :]

        self.moves.start(self.heads)

    def step_share(self):
        self.moves.arrive(self.heads)
        total = self.second_buf[self.place.z].astype(F32)
        for d in range(self.place.heads - 1):
            total += self.head_buf[d].astype(F32)
        self.final_buf[...] = total.astype(LOW)
        copy = pltpu.make_async_copy(self.final_buf, self.final_row, self.final_sem)
        copy.start()
        copy.wait()
        self.moves.start(self.share_second)

    def step_share_first(self):
        self.moves.arrive(self.share_second)
        self.moves.start(self.share_first)

    def step_share_core(self):
        self.moves.arrive(self.share_first)
        self.moves.start(self.share_core)

    def end(self):
        self.moves.arrive(self.share_core)


SMALL_ROWS = 48
GAIN_ROW, SHIFT_ROW, BOUT_ROW, BDOWN_ROW, BUP_ROW, BQV_ROW = 1, 5, 9, 11, 16, 24
DOWN, UP, ATTN = 0, 1, 2


def backward_kernel(sz, blocks, frame_share, tube_share, *refs):
    fulls, refs = refs[:blocks], refs[blocks:]
    saved, refs = [refs[7 * b : 7 * b + 7] for b in range(blocks)], refs[7 * blocks :]
    (cotangent, result, marks, gains), refs = refs[:4], refs[4:]
    (out_result, out_tokens, out_grads, out_small), refs = refs[:4], refs[4:]
    (
        wm, act, wa, t, p, m, n2, n, x, low, dn, dm, du, do, dq, dk, dv, cot, dx_low, back, res,
        grads, core_buf, first_buf, second_buf, head_buf, final_buf, small, small_in, small_heads, small_last,
        send_sem, recv_sem, line_sem, load_sem, copy_sem, final_sem, free_sem,
    ) = refs
    heads, width, length = sz.shards, sz.width, sz.length
    place = Place(heads)
    moves = Moves(send_sem, recv_sem)
    loads = Saves(copy_sem)
    yy, z = place.y, place.z
    tubes = cotangent.shape[1]

    def step_loads(b, kind, s):
        slot = s % 2
        if kind == "mlp":
            pairs = [(fulls[b].at[s, pl.ds(sz.up_row, 2 * width), :], wm.at[slot]), (saved[b][6].at[s], act.at[slot])]
            base = 0
        else:
            pairs = [
                (fulls[b].at[s, pl.ds(0, sz.up_row), :], wa.at[slot]),
                (saved[b][2].at[s], t.at[slot]),
                (saved[b][3].at[s], p.at[slot]),
            ]
            base = 4
        return [
            pltpu.make_async_copy(src, dst, load_sem.at[base + slot * len(pairs) + i]) for i, (src, dst) in enumerate(pairs)
        ]

    steps = [(b, kind, s) for b in (1, 0) for kind in ("mlp", "attn") for s in range(heads)]

    def fetch(i):
        if i < len(steps):
            for copy in step_loads(*steps[i]):
                copy.start()

    def ready(i):
        for copy in step_loads(*steps[i]):
            copy.wait()
        fetch(i + 1)

    first_loads = [
        loads.start(cotangent.at[:, pl.ds(z * tube_share, tube_share)], cot),
        loads.start(result, res),
    ]
    fetch(0)
    norm_loads = [loads.start(saved[1][4], m), loads.start(saved[1][5], n2)]
    later_loads = [loads.start(saved[1][1], n), loads.start(saved[1][0], x)]
    small[...] = jnp.zeros_like(small)
    greet(place.all_peers())

    red = {}
    for b in (1, 0):
        for k in (DOWN, UP, ATTN):
            base = b * sz.block_rows + (sz.down_row, sz.up_row, 0)[k]
            red[b, k] = Reduction(
                place,
                moves,
                grads.at[k],
                out_grads,
                base,
                width,
                (core_buf.at[k], first_buf.at[b, k], second_buf.at[b, k], head_buf.at[b, k]),
                final_buf.at[b, k],
                final_sem.at[b * 3 + k],
            )
    tube_region = lambda block: out_result.at[:, pl.ds(block * tube_share, tube_share)]
    line = Line(place, line_sem.at[0], line_sem.at[1], tube_region)
    spread = moves.phase(
        [
            (
                dx_low.at[pl.ds((2 * tz + ty) * frame_share, frame_share)],
                back.at[:, pl.ds((heads * yy + z) * tube_share, tube_share)],
                back.at[:, pl.ds((heads * ty + fz) * tube_share, tube_share)],
                target,
            )
            for ty, tz, fz, target in [
                (yy, lax.rem(z + d, heads), lax.rem(z + heads - d, heads), place.head(d)) for d in range(1, heads)
            ]
            + [
                (1 - yy, lax.rem(z + d, heads), lax.rem(z + heads - d, heads), place.across(d)) for d in range(heads)
            ]
        ]
    )

    for copy in first_loads:
        copy.wait()
    own_result = [
        loads.start(res.at[j], out_result.at[:, z * tube_share + j]) for j in range(tube_share)
    ]
    frames = cot.shape[0]
    for j in range(tube_share):
        low[j * length : (j + 1) * length, :] = cot[:, j].reshape(length, width)
    for copy in own_result:
        copy.wait()
    line.start(0)

    def row(r, columns=None):
        return small.at[r : r + 1, :] if columns is None else small.at[r : r + 1, 0:columns]

    def mlp(b, pumps):
        row(BDOWN_ROW + b)[...] = jnp.sum(low[...].astype(F32), 0, keepdims=True)
        dn[...] = jnp.zeros_like(dn)
        for copy in norm_loads:
            copy.wait()
        for s in range(heads):
            ready((1 - b) * 2 * heads + s)
            for k in (DOWN, UP):
                if s >= 2:
                    moves.left([red[b, k].core[s - 2]])
                elif b == 0:
                    moves.left([red[1, k].core[s + heads - 2]])
            backward_mlp(
                sz, wm.at[s % 2], act.at[s % 2], low, n2, du, dn, grads.at[DOWN, s % 2], grads.at[UP, s % 2],
                row(BUP_ROW + b * heads + s),
            )
            for k in (DOWN, UP):
                if s == 0 and b == 0:
                    pl.semaphore_wait(free_sem.at[k], 1)
                red[b, k].give(s)
            if s:
                for k in (DOWN, UP):
                    red[b, k].step_first(s - 1)
            pumps[s]()
        norm_back_rows(
            sz, m, gains[b, 1:2, :], dn, low, dm, row(GAIN_ROW + 2 * b + 1), row(SHIFT_ROW + 2 * b + 1), row(BOUT_ROW + b), low
        )
        for k in (DOWN, UP):
            red[b, k].step_first(heads - 1)

    def attention(b, pumps):
        dn[...] = jnp.zeros_like(dn)
        for copy in later_loads:
            copy.wait()
        for s in range(heads):
            ready((1 - b) * 2 * heads + heads + s)
            if s >= 2:
                moves.left([red[b, ATTN].core[s - 2]])
            elif b == 0:
                moves.left([red[1, ATTN].core[s + heads - 2]])
            r = BQV_ROW + 2 * (b * heads + s)
            backward_attention(
                sz, wa.at[s % 2], t.at[s % 2], p.at[s % 2], low, n, do, dq, dk, dv, dn, grads.at[ATTN, s % 2],
                row(r, sz.columns), row(r + 1, sz.columns),
            )
            if s == 0 and b == 0:
                pl.semaphore_wait(free_sem.at[ATTN], 1)
            red[b, ATTN].give(s)
            if s:
                red[b, ATTN].step_first(s - 1)
            pumps[s]()
        norm_back_rows(
            sz, x, gains[b, 0:1, :], dn, dm, dm, row(GAIN_ROW + 2 * b), row(SHIFT_ROW + 2 * b), None, None
        )

    def nothing():
        pass

    def pass_on(step):
        line.arrive(step)
        if step + 1 < line.steps:
            line.start(step + 1)

    def do_all(*actions):
        def run():
            for action in actions:
                action()

        return run

    one = {k: red[1, k] for k in (DOWN, UP, ATTN)}
    nought = {k: red[0, k] for k in (DOWN, UP, ATTN)}

    mlp(1, [nothing] * heads)
    norm_loads = [loads.start(saved[0][4], m), loads.start(saved[0][5], n2)]
    attention(1, [nothing, lambda: pass_on(0), nothing, nothing])
    later_loads = [loads.start(saved[0][1], n), loads.start(saved[0][0], x)]
    for j in range(tube_share):
        dx_low[:, j] = dm[j * length : (j + 1) * length, :].astype(LOW).reshape(frames, length // frames, width)
    moves.start(spread)
    mine = loads.start(
        dx_low.at[pl.ds((2 * z + yy) * frame_share, frame_share)],
        back.at[:, pl.ds((heads * yy + z) * tube_share, tube_share)],
    )
    one[ATTN].step_first(heads - 1)
    one[DOWN].step_second(free_sem.at[DOWN])
    one[UP].step_second(free_sem.at[UP])
    moves.arrive(spread)
    mine.wait()
    low[...] = back[...].reshape(sz.rows, width)
    mlp(
        0,
        [
            lambda: one[DOWN].step_heads(),
            do_all(lambda: one[ATTN].step_second(free_sem.at[ATTN]), lambda: pass_on(1)),
            lambda: one[UP].step_heads(),
            lambda: one[DOWN].step_share(),
        ],
    )
    attention(
        0,
        [
            do_all(lambda: one[ATTN].step_heads(), lambda: one[DOWN].step_share_first()),
            do_all(lambda: one[UP].step_share(), lambda: one[DOWN].step_share_core()),
            do_all(lambda: pass_on(2), lambda: one[UP].step_share_first()),
            do_all(lambda: one[ATTN].step_share(), lambda: one[UP].step_share_core()),
        ],
    )
    mark = marks[...].astype(F32).reshape(sz.rows, 128)[:, 0:1] > 0.5
    grad = dm[...]
    row(0)[...] = jnp.sum(jnp.where(mark, grad, 0.0), 0, keepdims=True)
    back[...] = jnp.where(mark, 0.0, grad).astype(LOW).reshape(back.shape)
    here, there = pl.ds(yy * tubes, tubes), pl.ds((1 - yy) * tubes, tubes)
    own_frames = lambda block: out_tokens.at[pl.ds((2 * block + yy) * frame_share, frame_share)]
    far_frames = lambda block: out_tokens.at[pl.ds((2 * block + 1 - yy) * frame_share, frame_share)]
    cross = moves.phase([(back.at[:, there], own_frames(z), far_frames(z), place.across(0))])
    own_line = Line(place, line_sem.at[2], line_sem.at[3], own_frames)
    far_line = Line(place, line_sem.at[4], line_sem.at[5], far_frames)
    half = SMALL_ROWS // 2
    part = pl.ds(pl.multiple_of(place.core * half, half), half)
    small_steps = [
        moves.phase([(small, small_in.at[i], small_in.at[i], target)])
        for i, target in enumerate((place.other, place.first, place.second))
    ]
    small_z = moves.phase(
        [(small.at[part], small_heads.at[d - 1], small_heads.at[d - 1], place.head(d)) for d in range(1, heads)]
    )
    far_part = pl.ds(pl.multiple_of((1 - place.core) * half, half), half)
    small_end = moves.phase([(small_last.at[part], small_last.at[part], small_last.at[far_part], place.other)])

    def add_small(i):
        moves.arrive(small_steps[i])
        moves.left(small_steps[i])
        small[...] += small_in[i]
        moves.start(small_steps[i + 1] if i + 1 < len(small_steps) else small_z)

    moves.start(cross)
    own_copy = loads.start(back.at[:, here], own_frames(z))
    moves.start(small_steps[0])
    nought[ATTN].step_first(heads - 1)
    own_copy.wait()
    own_line.start(0)
    nought[DOWN].step_second()
    add_small(0)
    nought[UP].step_second()
    moves.arrive(cross)
    far_line.start(0)
    add_small(1)
    nought[DOWN].step_heads()
    nought[ATTN].step_second()
    add_small(2)
    one[ATTN].step_share_first()
    own_line.arrive(0)
    own_line.start(1)
    nought[UP].step_heads()
    one[UP].end()
    one[DOWN].end()
    nought[DOWN].step_share()
    far_line.arrive(0)
    far_line.start(1)
    nought[ATTN].step_heads()
    one[ATTN].step_share_core()
    nought[UP].step_share()
    nought[DOWN].step_share_first()
    own_line.arrive(1)
    own_line.start(2)
    moves.arrive(small_z)
    total = small[part, :]
    for d in range(heads - 1):
        total += small_heads[d]
    small_last[part, :] = total
    moves.start(small_end)
    nought[DOWN].step_share_core()
    nought[UP].step_share_first()
    nought[ATTN].step_share()
    far_line.arrive(1)
    far_line.start(2)
    nought[UP].step_share_core()
    nought[ATTN].step_share_first()
    moves.arrive(small_end)
    out_small[...] = small_last[...]
    nought[ATTN].step_share_core()
    own_line.arrive(2)
    far_line.arrive(2)
    one[ATTN].end()
    for k in (DOWN, UP, ATTN):
        nought[k].end()
    for each in (line, own_line, far_line):
        each.finish()
    moves.finish()


def run_backward(sz, blocks, frame_share, tube_share, fulls, saved, cotangent, result, marks, gains):
    heads, width, rows, cols = sz.shards, sz.width, sz.rows, sz.columns
    frames, tubes, patches = cotangent.shape[:3]
    hbm, vmem = pl.BlockSpec(memory_space=pl.ANY), pl.BlockSpec(memory_space=pltpu.VMEM)
    q = width // 8
    local = (frame_share, 2 * tubes, patches, width)
    mixed = (frames, tube_share, patches, width)
    kinds = 3 * blocks
    count = kinds * (2 * heads + 4 + heads - 1) + 2 * heads - 1 + 1 + 4 + heads - 1
    flat = [array for per in saved for array in per]
    return pl.pallas_call(
        lambda *refs: backward_kernel(sz, blocks, frame_share, tube_share, *refs),
        name="backward_both",
        out_shape=structs(
            [
                (cotangent.shape, LOW),
                (cotangent.shape, LOW),
                ((blocks * sz.block_rows, width), LOW),
                ((SMALL_ROWS, width), F32),
            ]
        ),
        in_specs=[hbm] * (blocks + len(flat) + 2) + [vmem] * 2,
        out_specs=[hbm] * 3 + [vmem],
        scratch_shapes=vmems(
            [
                ((2, 2 * width, width), LOW),
                ((2, 2, rows, sz.units), LOW),
                ((2, sz.up_row, width), LOW),
                ((2, 4, rows, cols), LOW),
                ((2, sz.sequences * sz.heads, sz.length, sz.length), LOW),
                ((rows, width), F32),
                ((rows, width), LOW),
                ((rows, width), LOW),
                ((rows, width), F32),
                ((rows, width), LOW),
                ((rows, width), F32),
                ((rows, width), F32),
                ((rows, sz.units), LOW),
                ((rows, cols), LOW),
                ((rows, cols), LOW),
                ((rows, cols), LOW),
                ((rows, cols), LOW),
                (mixed, LOW),
                (mixed, LOW),
                (local, LOW),
                (result.shape, LOW),
                ((3, 2, width, width), LOW),
                ((3, heads, 4 * q, width), LOW),
                ((blocks, 3, heads, 2 * q, width), LOW),
                ((blocks, 3, heads, q, width), LOW),
                ((blocks, 3, heads - 1, q, width), LOW),
                ((blocks, 3, q, width), LOW),
                ((SMALL_ROWS, width), F32),
                ((3, SMALL_ROWS, width), F32),
                ((heads - 1, SMALL_ROWS // 2, width), F32),
                ((SMALL_ROWS, width), F32),
            ]
        )
        + [
            pltpu.SemaphoreType.DMA((count,)),
            pltpu.SemaphoreType.DMA((count,)),
            pltpu.SemaphoreType.DMA((6, 2 * (heads - 1))),
            pltpu.SemaphoreType.DMA((10,)),
            pltpu.SemaphoreType.DMA((24,)),
            pltpu.SemaphoreType.DMA((kinds,)),
            pltpu.SemaphoreType.REGULAR((3,)),
        ],
        compiler_params=pltpu.CompilerParams(
            collective_id=1, has_side_effects=True, vmem_limit_bytes=63 * 2**20
        ),
    )(*fulls, *flat, cotangent, result, marks, gains)


def fits_local(arrays, clip_size, tube_size, head_size):
    clips, frames, tubes = arrays[0].shape[:3]
    width = arrays[0].shape[-1]
    columns, units = arrays[5].shape[3] // head_size, arrays[9].shape[2] // head_size
    devices = tube_size * head_size
    return (
        (clips, clip_size, tube_size) == (4, 4, 2)
        and frames % devices == 0
        and frames == tubes
        and head_size % 2 == 0
        and width == 4 * columns == units
        and width % 384 == 0
        and columns % HD == 0
    )


def on_device_local(
    tokens,
    token_mask,
    mask_embed,
    norm_gains,
    norm_shifts,
    w_qkv,
    b_qv,
    w_out,
    b_out,
    w_up,
    b_up,
    w_down,
    b_down,
    cotangent,
):
    _, frames, tubes, patches, width = tokens.shape
    tube_size, heads = lax.axis_size("tube"), lax.axis_size("head")
    head = lax.axis_index("head")
    blocks, columns, units = w_qkv.shape[0], w_qkv.shape[-1], w_up.shape[-1]
    frame_share = frames // (tube_size * heads)
    tube_share = tubes // heads
    rows = frame_share * tube_size * tubes * patches
    sz = Sizes(rows, width, heads, columns, units, rows // frame_share)

    shard = jnp.concatenate(
        [w_qkv.transpose(0, 2, 3, 1).reshape(blocks, 3 * columns, width), w_out, w_up, w_down], 1
    ).reshape(blocks * sz.block_rows, width)
    marks = jnp.broadcast_to(token_mask[0][..., None], (frames, tubes, patches, 128)).astype(LOW)
    full, saved, output, mark_frames = run_forward(
        sz,
        blocks,
        frame_share,
        tube_share,
        shard,
        tokens[0],
        marks,
        b_qv.reshape(2 * blocks, columns),
        b_up,
        mask_embed[None],
        norm_gains,
        norm_shifts,
        b_out[:, None],
        b_down[:, None],
    )
    output, grad_tokens, whole, small = run_backward(
        sz, blocks, frame_share, tube_share, full, saved, cotangent[0], output, mark_frames, norm_gains
    )
    rows_of = lambda start, size: small[start : start + size]
    bup_grad = rows_of(BUP_ROW, blocks * heads).reshape(blocks, heads, units)
    bqv_grad = rows_of(BQV_ROW, 2 * blocks * heads)[:, :columns].reshape(blocks, heads, 2, columns)
    of_head = lambda array: lax.dynamic_index_in_dim(array, head, 1, False)
    whole = whole.astype(F32)
    whole = whole.reshape(blocks, sz.block_rows, width)
    qkv_grad = whole[:, : sz.out_row].reshape(blocks, 3, columns, width).transpose(0, 3, 1, 2)
    return (
        output[None],
        grad_tokens[None],
        small[0],
        rows_of(GAIN_ROW, 2 * blocks).reshape(blocks, 2, width),
        rows_of(SHIFT_ROW, 2 * blocks).reshape(blocks, 2, width),
        qkv_grad,
        of_head(bqv_grad),
        whole[:, sz.out_row : sz.up_row],
        rows_of(BOUT_ROW, blocks),
        whole[:, sz.up_row : sz.down_row],
        of_head(bup_grad),
        whole[:, sz.down_row :],
        rows_of(BDOWN_ROW, blocks),
    )


def solution(mesh):
    sizes = [mesh.shape[name] for name in ("clip", "tube", "head")]

    def run(*arrays):
        on_device = on_device_local if fits_local(arrays, *sizes) else on_device_sums
        return on_mesh(on_device, mesh)(*arrays)

    return run


def on_mesh(on_device, mesh):
    return jax.shard_map(
        on_device,
        mesh=mesh,
        in_specs=(
            P("clip", None, "tube", None, None),
            P("clip", None, "tube", None),
            P(),
            P(),
            P(),
            P(None, None, None, "head"),
            P(None, None, "head"),
            P(None, "head", None),
            P(),
            P(None, None, "head"),
            P(None, "head"),
            P(None, "head", None),
            P(),
            P("clip", None, "tube", None, None),
        ),
        out_specs=(
            P("clip", None, "tube", None, None),
            P("clip", None, "tube", None, None),
            P(),
            P(),
            P(),
            P(None, None, None, "head"),
            P(None, None, "head"),
            P(None, "head", None),
            P(),
            P(None, None, "head"),
            P(None, "head"),
            P(None, "head", None),
            P(),
        ),
        check_vma=False,
    )
```

```python
import functools

import jax
import jax.numpy as jnp
from jax import lax
from jax.experimental import pallas as pl
from jax.experimental.pallas import tpu as pltpu
from jax.sharding import PartitionSpec as P

F32 = jnp.float32
LOW = jnp.bfloat16
MESH = pl.DeviceIdType.MESH

HD = 64


EPS = 1e-05


def norm_forward(values, gain_vector, shift_vector):
    centre = values - jnp.mean(values, -1, keepdims=True)
    inverse = lax.rsqrt(jnp.mean(centre * centre, -1, keepdims=True) + EPS)
    normal = centre * inverse
    return (normal * gain_vector + shift_vector, normal, inverse)


def norm_backward(grad_out, normal, inverse, gain_vector):
    grad_normal = grad_out * gain_vector
    grad_in = inverse * (
        grad_normal
        - jnp.mean(grad_normal, -1, keepdims=True)
        - normal * jnp.mean(grad_normal * normal, -1, keepdims=True)
    )
    return (grad_in, jnp.sum(grad_out * normal, 0), jnp.sum(grad_out, 0))


def row_total(partial_sum):
    return lax.psum(partial_sum.astype(jnp.bfloat16), "head").astype(jnp.float32)


def input_total(partial_sum):
    return lax.psum(partial_sum.astype(jnp.bfloat16), "head").astype(jnp.float32)


def split_heads(tensor, batch_count, length):
    return tensor.reshape(batch_count, length, tensor.shape[-1] // HD, HD)


def attend(queries, key_rows, value_rows):
    scores = jnp.einsum(
        "bshe,bthe->bhst", queries, key_rows, preferred_element_type=jnp.float32
    ) * HD ** (-0.5)
    maximum = jnp.max(scores, -1, keepdims=True)
    exponent = jnp.exp(scores - maximum)
    denominator = jnp.sum(exponent, -1, keepdims=True)
    weights_soft = (exponent / denominator).astype(jnp.bfloat16)
    mixture = jnp.einsum(
        "bhst,bthe->bshe", weights_soft, value_rows, preferred_element_type=jnp.float32
    )
    return (mixture.astype(jnp.bfloat16), maximum + jnp.log(denominator))


def attend_back(queries, key_rows, value_rows, log_total, grad_mixture):
    scaling = HD ** (-0.5)
    scores = (
        jnp.einsum("bshe,bthe->bhst", queries, key_rows, preferred_element_type=jnp.float32)
        * scaling
    )
    weights_soft = jnp.exp(scores - log_total)
    grad_weights = jnp.einsum(
        "bshe,bthe->bhst", grad_mixture, value_rows, preferred_element_type=jnp.float32
    )
    grad_values = jnp.einsum(
        "bhst,bshe->bthe",
        weights_soft.astype(jnp.bfloat16),
        grad_mixture,
        preferred_element_type=jnp.float32,
    )
    grad_scores = (
        weights_soft * (grad_weights - jnp.sum(weights_soft * grad_weights, -1, keepdims=True))
    ).astype(jnp.bfloat16)
    grad_queries = (
        jnp.einsum("bhst,bthe->bshe", grad_scores, key_rows, preferred_element_type=jnp.float32)
        * scaling
    )
    grad_keys = (
        jnp.einsum("bhst,bshe->bthe", grad_scores, queries, preferred_element_type=jnp.float32)
        * scaling
    )
    return (grad_queries, grad_keys, grad_values)


def mixer_forward(block_kind, queries, key_rows, value_rows):
    clip_count, frame_count, tube_count, patch_count, columns = queries.shape
    if block_kind == 1:
        reorder = (0, 2, 1, 3, 4)
        pieces = [
            split_heads(
                tensor.transpose(reorder), clip_count * tube_count, frame_count * patch_count
            )
            for tensor in (queries, key_rows, value_rows)
        ]
        mixture, log_total = attend(pieces[0], pieces[1], pieces[2])
        mixture = mixture.reshape(
            clip_count, tube_count, frame_count, patch_count, columns
        ).transpose(reorder)
        return (mixture, (pieces, log_total))
    key_all, value_all = (
        lax.all_gather(key_rows, "tube", axis=2, tiled=True),
        lax.all_gather(value_rows, "tube", axis=2, tiled=True),
    )
    tube_all = key_all.shape[2]
    pieces = [
        split_heads(queries, clip_count * frame_count, tube_count * patch_count),
        split_heads(key_all, clip_count * frame_count, tube_all * patch_count),
        split_heads(value_all, clip_count * frame_count, tube_all * patch_count),
    ]
    mixture, log_total = attend(pieces[0], pieces[1], pieces[2])
    return (
        mixture.reshape(clip_count, frame_count, tube_count, patch_count, columns),
        (pieces, log_total),
    )


def mixer_backward(block_kind, retained, grad_mixture):
    pieces, log_total = retained
    clip_count, frame_count, tube_count, patch_count, columns = grad_mixture.shape
    if block_kind == 1:
        reorder = (0, 2, 1, 3, 4)
        moved = split_heads(
            grad_mixture.transpose(reorder), clip_count * tube_count, frame_count * patch_count
        )
        gradients = attend_back(pieces[0], pieces[1], pieces[2], log_total, moved)
        return [
            grad.astype(jnp.bfloat16)
            .reshape(clip_count, tube_count, frame_count, patch_count, columns)
            .transpose(reorder)
            for grad in gradients
        ]
    gradients = attend_back(
        pieces[0],
        pieces[1],
        pieces[2],
        log_total,
        split_heads(grad_mixture, clip_count * frame_count, tube_count * patch_count),
    )
    tube_all = pieces[1].shape[1] // patch_count
    grad_keys = gradients[1].reshape(clip_count, frame_count, tube_all, patch_count, columns)
    grad_values = gradients[2].reshape(clip_count, frame_count, tube_all, patch_count, columns)
    grad_keys, grad_values = (
        lax.psum_scatter(
            grad_keys.astype(jnp.bfloat16), "tube", scatter_dimension=2, tiled=True
        ).astype(jnp.float32),
        lax.psum_scatter(
            grad_values.astype(jnp.bfloat16), "tube", scatter_dimension=2, tiled=True
        ).astype(jnp.float32),
    )
    grad_queries = (
        gradients[0]
        .astype(jnp.bfloat16)
        .reshape(clip_count, frame_count, tube_count, patch_count, columns)
    )
    return [grad_queries, grad_keys.astype(jnp.bfloat16), grad_values.astype(jnp.bfloat16)]


def block_forward(block_kind, residual, layout, weights):
    gains, shifts, w_qkv, b_qv, w_out, b_out, w_up, b_up, w_down, b_down = weights
    columns = w_qkv.shape[-1]
    grid_shape = layout[:-1] + (columns,)
    normed_share, first_normal, first_inverse = norm_forward(residual, gains[0], shifts[0])
    normed = normed_share.astype(jnp.bfloat16)
    projected = jnp.einsum("rd,dcj->rcj", normed, w_qkv, preferred_element_type=jnp.float32)
    queries = (projected[:, 0] + b_qv[0]).astype(jnp.bfloat16).reshape(grid_shape)
    key_rows = projected[:, 1].astype(jnp.bfloat16).reshape(grid_shape)
    value_rows = (projected[:, 2] + b_qv[1]).astype(jnp.bfloat16).reshape(grid_shape)
    mixture, retained = mixer_forward(block_kind, queries, key_rows, value_rows)
    mixture = mixture.reshape(-1, columns)
    middle = (
        residual + row_total(jnp.dot(mixture, w_out, preferred_element_type=jnp.float32)) + b_out
    )
    second_share, second_normal, second_inverse = norm_forward(middle, gains[1], shifts[1])
    normed_two = second_share.astype(jnp.bfloat16)
    hidden = jnp.dot(normed_two, w_up, preferred_element_type=jnp.float32) + b_up
    active = jax.nn.gelu(hidden).astype(jnp.bfloat16)
    stored = (
        normed,
        first_normal,
        first_inverse,
        retained,
        mixture,
        normed_two,
        second_normal,
        second_inverse,
        hidden,
    )
    return (middle, active, stored)


def block_output(middle, active, w_down, b_down):
    return middle + row_total(jnp.dot(active, w_down, preferred_element_type=jnp.float32)) + b_down


def block_backward(block_kind, residual, layout, weights, grad_rows):
    gains, shifts, w_qkv, b_qv, w_out, b_out, w_up, b_up, w_down, b_down = weights
    middle, active, stored = block_forward(block_kind, residual, layout, weights)
    (
        normed,
        first_normal,
        first_inverse,
        retained,
        mixture,
        normed_two,
        second_normal,
        second_inverse,
        hidden,
    ) = stored
    columns = w_qkv.shape[-1]
    grad_low = grad_rows.astype(jnp.bfloat16)
    grad_wdown = jnp.dot(active.T, grad_low, preferred_element_type=jnp.float32)
    grad_bdown = jnp.sum(grad_rows, 0)
    grad_active = jnp.dot(grad_low, w_down.T, preferred_element_type=jnp.float32)
    gelu_pull = jax.vjp(jax.nn.gelu, hidden)[1]
    grad_hidden = gelu_pull(grad_active)[0].astype(jnp.bfloat16)
    grad_bup = jnp.sum(grad_hidden.astype(jnp.float32), 0)
    grad_wup = jnp.dot(normed_two.T, grad_hidden, preferred_element_type=jnp.float32)
    grad_normed_two = input_total(jnp.dot(grad_hidden, w_up.T, preferred_element_type=jnp.float32))
    grad_norm, grad_gain_two, grad_shift_two = norm_backward(
        grad_normed_two, second_normal, second_inverse, gains[1]
    )
    grad_middle = grad_rows + grad_norm
    grad_bout = jnp.sum(grad_middle, 0)
    grad_mid_low = grad_middle.astype(jnp.bfloat16)
    grad_wout = jnp.dot(mixture.T, grad_mid_low, preferred_element_type=jnp.float32)
    grad_mixture = jnp.dot(grad_mid_low, w_out.T, preferred_element_type=jnp.float32).astype(
        jnp.bfloat16
    )
    grad_parts = mixer_backward(
        block_kind, retained, grad_mixture.reshape(layout[:-1] + (columns,))
    )
    grad_flat = [grad.reshape(-1, columns) for grad in grad_parts]
    grad_project = jnp.stack(grad_flat, 1)
    grad_bqv = jnp.stack(
        [jnp.sum(grad_flat[0].astype(jnp.float32), 0), jnp.sum(grad_flat[2].astype(jnp.float32), 0)]
    )
    grad_wqkv = jnp.einsum("rd,rcj->dcj", normed, grad_project, preferred_element_type=jnp.float32)
    grad_normed = input_total(
        jnp.einsum("rcj,dcj->rd", grad_project, w_qkv, preferred_element_type=jnp.float32)
    )
    grad_input, grad_gain_one, grad_shift_one = norm_backward(
        grad_normed, first_normal, first_inverse, gains[0]
    )
    gradients = (
        jnp.stack([grad_gain_one, grad_gain_two]),
        jnp.stack([grad_shift_one, grad_shift_two]),
        grad_wqkv,
        grad_bqv,
        grad_wout,
        grad_bout,
        grad_wup,
        grad_bup,
        grad_wdown,
        grad_bdown,
    )
    return (grad_middle + grad_input, gradients)


def on_device_sums(
    tokens,
    token_mask,
    mask_embed,
    norm_gains,
    norm_shifts,
    w_qkv,
    b_qv,
    w_out,
    b_out,
    w_up,
    b_up,
    w_down,
    b_down,
    cotangent,
):
    layout = tokens.shape
    width = layout[-1]
    masked = (token_mask == 1).reshape(-1, 1)
    initial = jnp.where(masked, mask_embed[None, :], tokens.reshape(-1, width).astype(jnp.float32))
    upstream = cotangent.reshape(-1, width).astype(jnp.float32)

    def weights_of(block_kind):
        return (
            norm_gains[block_kind],
            norm_shifts[block_kind],
            w_qkv[block_kind],
            b_qv[block_kind],
            w_out[block_kind],
            b_out[block_kind],
            w_up[block_kind],
            b_up[block_kind],
            w_down[block_kind],
            b_down[block_kind],
        )

    middle, active, unused_first = block_forward(0, initial, layout, weights_of(0))
    second = block_output(middle, active, w_down[0], b_down[0])
    middle, active, unused_second = block_forward(1, second, layout, weights_of(1))
    output_rows = block_output(middle, active, w_down[1], b_down[1])
    grad_second, grads_later = block_backward(1, second, layout, weights_of(1), upstream)
    grad_initial, grads_earlier = block_backward(0, initial, layout, weights_of(0), grad_second)
    stacked = [
        jnp.stack([first_grad, later_grad])
        for first_grad, later_grad in zip(grads_earlier, grads_later)
    ]
    grad_embed = jnp.sum(jnp.where(masked, grad_initial, 0.0), 0)
    output_low = output_rows.astype(jnp.bfloat16)
    grad_low = jnp.where(masked, 0.0, grad_initial).astype(jnp.bfloat16)
    shares = (
        lax.psum_scatter(stacked[2], ("clip", "tube"), scatter_dimension=1, tiled=True),
        lax.psum_scatter(stacked[4], ("clip", "tube"), scatter_dimension=2, tiled=True),
        lax.psum_scatter(stacked[6], ("clip", "tube"), scatter_dimension=1, tiled=True),
        lax.psum_scatter(stacked[8], ("clip", "tube"), scatter_dimension=2, tiled=True),
    )
    whole = (
        lax.all_gather(shares[0].astype(jnp.bfloat16), ("clip", "tube"), axis=1, tiled=True).astype(
            jnp.float32
        ),
        lax.all_gather(shares[1].astype(jnp.bfloat16), ("clip", "tube"), axis=2, tiled=True).astype(
            jnp.float32
        ),
        lax.all_gather(shares[2].astype(jnp.bfloat16), ("clip", "tube"), axis=1, tiled=True).astype(
            jnp.float32
        ),
        lax.all_gather(shares[3].astype(jnp.bfloat16), ("clip", "tube"), axis=2, tiled=True).astype(
            jnp.float32
        ),
    )
    column_part = (
        grad_embed,
        stacked[0],
        stacked[1],
        stacked[5],
        stacked[9],
        stacked[3],
        stacked[7],
    )
    small = lax.psum(
        (
            column_part[0],
            column_part[1],
            column_part[2],
            column_part[3],
            column_part[4],
            column_part[5],
            column_part[6],
        ),
        ("clip", "tube"),
    )
    embed_grad, gain_grad, shift_grad, bout_grad, bdown_grad = (
        small[0],
        small[1],
        small[2],
        small[3],
        small[4],
    )
    bqv_grad, bup_grad = (small[5], small[6])
    return (
        output_low.reshape(layout),
        grad_low.reshape(layout),
        embed_grad,
        gain_grad,
        shift_grad,
        whole[0],
        bqv_grad,
        whole[1],
        bout_grad,
        whole[2],
        bup_grad,
        whole[3],
        bdown_grad,
    )


DOWN, UP, ATTN = range(3)
SEND, PASS, FIRST_INPUT, SECOND_INPUT, SPREAD, RESULT, ATTEND, MIDDLE, EXPAND, CONTRACT = range(10)
FORWARD_ORDER = (
    (SEND, 0), (PASS, 0, 0), (SEND, 1), (FIRST_INPUT,), (PASS, 0, 1), (PASS, 1, 0), (SEND, 2), (PASS, 1, 1),
    (PASS, 0, 2), (PASS, 0, 3), (PASS, 1, 2), (PASS, 2, 0), (SEND, 3), (PASS, 1, 3), (ATTEND, 0, 0), (ATTEND, 0, 1),
    (ATTEND, 0, 2), (PASS, 2, 1), (ATTEND, 0, 3), (MIDDLE, 0), (PASS, 3, 0), (SEND, 4), (PASS, 2, 2), (PASS, 3, 1),
    (PASS, 2, 3), (EXPAND, 0, 0), (PASS, 4, 0), (SEND, 5), (EXPAND, 0, 1), (EXPAND, 0, 2), (EXPAND, 0, 3),
    (PASS, 3, 2), (PASS, 4, 1), (PASS, 5, 0), (SEND, 6), (PASS, 3, 3), (CONTRACT, 0, 0), (CONTRACT, 0, 1),
    (CONTRACT, 0, 2), (CONTRACT, 0, 3), (SPREAD,), (PASS, 5, 1), (PASS, 4, 2), (PASS, 4, 3), (PASS, 6, 0),
    (SECOND_INPUT,), (ATTEND, 1, 0), (PASS, 6, 1), (PASS, 5, 2), (ATTEND, 1, 1), (ATTEND, 1, 2), (PASS, 5, 3),
    (ATTEND, 1, 3), (MIDDLE, 1), (EXPAND, 1, 0), (PASS, 6, 2), (EXPAND, 1, 1), (EXPAND, 1, 2), (EXPAND, 1, 3),
    (PASS, 6, 3), (CONTRACT, 1, 0), (CONTRACT, 1, 1), (CONTRACT, 1, 2), (CONTRACT, 1, 3), (RESULT,),
)
MLP_BACK, MLP_NORM, ATTN_BACK, ATTN_NORM, UPSTREAM, RESULT_LINE, OWN_LINE, FAR_START, FAR_LINE, SMALL = range(10)
ADD_CORE, ADD_FIRST, ADD_SECOND, ADD_HEADS, SHARE_FIRST, SHARE_CORE, ARRIVED = range(10, 17)
BACKWARD_ORDER = (
    (MLP_BACK, 1, 0), (MLP_BACK, 1, 1), (ADD_CORE, 1, DOWN, 0), (ADD_CORE, 1, UP, 0), (MLP_BACK, 1, 2),
    (ADD_CORE, 1, UP, 1), (ADD_CORE, 1, DOWN, 1), (MLP_BACK, 1, 3), (ADD_CORE, 1, DOWN, 2), (ADD_CORE, 1, UP, 2),
    (MLP_NORM, 1), (RESULT_LINE, 0), (ATTN_BACK, 1, 0), (ATTN_BACK, 1, 1), (ADD_CORE, 1, DOWN, 3),
    (ADD_CORE, 1, ATTN, 0), (ATTN_BACK, 1, 2), (ADD_CORE, 1, ATTN, 1), (ATTN_BACK, 1, 3), (ADD_CORE, 1, UP, 3),
    (ATTN_NORM, 1), (RESULT_LINE, 1), (ADD_FIRST, 1, UP), (ADD_FIRST, 1, DOWN), (ADD_CORE, 1, ATTN, 3),
    (ADD_SECOND, 1, UP), (ADD_CORE, 1, ATTN, 2), (UPSTREAM,), (MLP_BACK, 0, 0), (MLP_BACK, 0, 1),
    (ADD_CORE, 0, DOWN, 0), (ADD_CORE, 0, UP, 0), (MLP_BACK, 0, 2), (ADD_SECOND, 1, DOWN), (ADD_CORE, 0, DOWN, 1),
    (ADD_FIRST, 1, ATTN), (ADD_CORE, 0, UP, 1), (MLP_BACK, 0, 3), (MLP_NORM, 0), (ATTN_BACK, 0, 0), (ATTN_BACK, 0, 1),
    (ADD_CORE, 0, ATTN, 0), (ADD_SECOND, 1, ATTN), (ATTN_BACK, 0, 2), (ADD_CORE, 0, ATTN, 1), (ATTN_BACK, 0, 3),
    (ATTN_NORM, 0), (ADD_CORE, 0, DOWN, 2), (FAR_START,), (ADD_CORE, 0, DOWN, 3), (ADD_CORE, 0, UP, 3),
    (ADD_HEADS, 1, ATTN), (ADD_CORE, 0, ATTN, 3), (OWN_LINE, 0), (FAR_LINE, 0), (ADD_CORE, 0, UP, 2),
    (ADD_FIRST, 0, DOWN), (SHARE_FIRST, 1, ATTN), (ADD_SECOND, 0, DOWN), (ADD_FIRST, 0, UP), (ADD_CORE, 0, ATTN, 2),
    (SHARE_CORE, 1, ATTN), (FAR_LINE, 1), (ADD_HEADS, 1, DOWN), (SMALL, 0), (ADD_HEADS, 1, UP), (ADD_FIRST, 0, ATTN),
    (ADD_SECOND, 0, UP), (ADD_HEADS, 0, DOWN), (FAR_LINE, 2), (SHARE_FIRST, 1, UP), (SMALL, 1), (ADD_SECOND, 0, ATTN),
    (SHARE_FIRST, 1, DOWN), (SMALL, 2), (SHARE_FIRST, 0, DOWN), (ADD_HEADS, 0, UP), (SHARE_FIRST, 0, UP),
    (SHARE_CORE, 0, DOWN), (SHARE_CORE, 1, DOWN), (OWN_LINE, 1), (ADD_HEADS, 0, ATTN), (RESULT_LINE, 2),
    (SHARE_CORE, 1, UP), (SHARE_FIRST, 0, ATTN), (SHARE_CORE, 0, UP), (ARRIVED, 0, DOWN), (ARRIVED, 1, ATTN),
    (SMALL, 3), (SHARE_CORE, 0, ATTN), (ARRIVED, 0, UP), (ARRIVED, 0, ATTN), (ARRIVED, 1, UP), (ARRIVED, 1, DOWN),
    (SMALL, 4), (OWN_LINE, 2),
)

GELU_A = 0.7978845608028654
GELU_B = 0.044715


def dot(left, right, dims):
    return lax.dot_general(left, right, (dims, ((), ())), preferred_element_type=F32)


NN, NT, TN = ((1,), (0,)), ((1,), (1,)), ((0,), (0,))


def standardize(values):
    centre = values - jnp.mean(values, -1, keepdims=True)
    inverse = lax.rsqrt(jnp.mean(centre * centre, -1, keepdims=True) + EPS)
    return centre * inverse, inverse


def head_masks(columns, scale):
    lane = lax.broadcasted_iota(jnp.int32, (1, columns), 1)
    return [
        jnp.where((lane >= j * HD) & (lane < (j + 1) * HD), scale, 0.0).astype(LOW)
        for j in range(columns // HD)
    ]


def gelu_pair(hidden):
    square = hidden * hidden
    tanh = jnp.tanh(GELU_A * hidden * (1.0 + GELU_B * square))
    half = 0.5 * (1.0 + tanh)
    slope = half + hidden * (0.5 * GELU_A) * (1.0 - tanh * tanh) * (1.0 + 3.0 * GELU_B * square)
    return hidden * half, slope


class Sizes:
    def __init__(self, rows, width, shards, columns, units, length):
        self.rows, self.width, self.shards = rows, width, shards
        self.columns, self.units, self.length = columns, units, length
        self.sequences = rows // length
        self.heads = columns // HD
        self.out_row = 3 * columns
        self.up_row = 4 * columns
        self.down_row = 4 * columns + width
        self.block_rows = 4 * columns + width + units


def norm_rows(sz, x_ref, gain, shift, n_ref, chunk=128):
    @pl.loop(0, sz.rows, step=chunk)
    def _(start):
        at = pl.ds(pl.multiple_of(start, chunk), chunk)
        normal, _ = standardize(x_ref[at, :].astype(F32))
        n_ref[at, :] = (normal * gain + shift).astype(LOW)


def forward_attention(sz, shard, w_ref, b_query, b_value, n_ref, t_ref, p_ref, m_ref):
    cols, length = sz.columns, sz.length
    normed = n_ref[...]
    q_ref, k_ref, v_ref, o_ref = (t_ref.at[shard, i] for i in range(4))
    q_ref[...] = (dot(normed, w_ref[shard, 0:cols, :], NT) + b_query).astype(LOW)
    k_ref[...] = dot(normed, w_ref[shard, cols : 2 * cols, :], NT).astype(LOW)
    v_ref[...] = (dot(normed, w_ref[shard, 2 * cols : 3 * cols, :], NT) + b_value).astype(LOW)
    scaled = head_masks(cols, HD**-0.5)
    masks = head_masks(cols, 1.0)
    for seq in range(sz.sequences):
        at = slice(seq * length, (seq + 1) * length)
        queries, keys, values = q_ref[at, :], k_ref[at, :], v_ref[at, :]
        mixture = jnp.zeros((length, cols), F32)
        for head in range(sz.heads):
            scores = dot(queries * scaled[head], keys, NT)
            exponent = jnp.exp(scores - jnp.max(scores, -1, keepdims=True))
            weights = (exponent / jnp.sum(exponent, -1, keepdims=True)).astype(LOW)
            p_ref[shard, seq * sz.heads + head] = weights
            mixture += dot(weights, values * masks[head], NN)
        o_ref[at, :] = mixture.astype(LOW)
    m_ref[...] += dot(o_ref[...], w_ref[shard, sz.out_row : sz.out_row + cols, :], NN)


def forward_up(sz, shard, w_ref, b_up, n2_ref, as_ref):
    hidden = dot(n2_ref[...], w_ref[shard, sz.up_row : sz.up_row + sz.width, :], NN) + b_up
    active, slope = gelu_pair(hidden)
    as_ref[shard, 0] = active.astype(LOW)
    as_ref[shard, 1] = slope.astype(LOW)


def forward_down(sz, shard, w_ref, as_ref, y_ref):
    y_ref[...] += dot(as_ref[shard, 0], w_ref[shard, sz.down_row : sz.down_row + sz.units, :], NN)


def backward_mlp(sz, w_ref, as_ref, low_ref, n2_ref, du_ref, dn_ref, down_ref, up_ref, sum_row):
    low = low_ref[...]
    grad_active = dot(low, w_ref[sz.width : sz.width + sz.units, :], NT)
    du_ref[...] = (grad_active * as_ref[1].astype(F32)).astype(LOW)
    sum_row[...] = jnp.sum(du_ref[...].astype(F32), 0, keepdims=True)
    down_ref[...] = dot(as_ref[0], low, TN).astype(LOW)
    up_ref[...] = dot(n2_ref[...], du_ref[...], TN).astype(LOW)
    dn_ref[...] += dot(du_ref[...], w_ref[0 : sz.width, :], NT)


def norm_back_rows(sz, x_ref, gain, dn_ref, g_ref, out_ref, gain_row, shift_row, sum_row, low_ref, chunk=128):
    for row in (gain_row, shift_row, sum_row):
        if row is not None:
            row[...] = jnp.zeros_like(row)

    @pl.loop(0, sz.rows, step=chunk)
    def _(start):
        at = pl.ds(pl.multiple_of(start, chunk), chunk)
        normal, inverse = standardize(x_ref[at, :])
        dn = dn_ref[at, :]
        dy = dn * gain
        part = inverse * (
            dy - jnp.mean(dy, -1, keepdims=True) - normal * jnp.mean(dy * normal, -1, keepdims=True)
        )
        total = g_ref[at, :].astype(F32) + part
        out_ref[at, :] = total
        if low_ref is not None:
            low_ref[at, :] = total.astype(LOW)
        gain_row[...] += jnp.sum(dn * normal, 0, keepdims=True)
        shift_row[...] += jnp.sum(dn, 0, keepdims=True)
        if sum_row is not None:
            sum_row[...] += jnp.sum(total, 0, keepdims=True)


def backward_attention(sz, w_ref, t_ref, p_ref, dml_ref, n_ref, do_ref, dq_ref, dk_ref, dv_ref, dn_ref, g_ref, query_row, value_row):
    cols, length = sz.columns, sz.length
    low = dml_ref[...]
    q_ref, k_ref, v_ref, o_ref = (t_ref.at[i] for i in range(4))
    w_out = w_ref[sz.out_row : sz.out_row + cols, :]
    do_ref[...] = dot(low, w_out, NT).astype(LOW)
    g_ref[sz.out_row : sz.out_row + cols, :] = dot(o_ref[...], low, TN).astype(LOW)
    scaled = head_masks(cols, HD**-0.5)
    masks = head_masks(cols, 1.0)
    for seq in range(sz.sequences):
        at = slice(seq * length, (seq + 1) * length)
        queries, keys, values = q_ref[at, :], k_ref[at, :], v_ref[at, :]
        grad_o = do_ref[at, :]
        dq = jnp.zeros((length, cols), F32)
        dk = jnp.zeros((length, cols), F32)
        dv = jnp.zeros((length, cols), F32)
        for head in range(sz.heads):
            weights = p_ref[seq * sz.heads + head]
            grad_head = grad_o * masks[head]
            dp = dot(grad_head, values, NT)
            dv += dot(weights, grad_head, TN)
            wide = weights.astype(F32)
            ds = (wide * (dp - jnp.sum(wide * dp, -1, keepdims=True))).astype(LOW)
            dq += dot(ds, keys * scaled[head], NN)
            dk += dot(ds, queries * scaled[head], TN)
        dq_ref[at, :] = dq.astype(LOW)
        dk_ref[at, :] = dk.astype(LOW)
        dv_ref[at, :] = dv.astype(LOW)
    normed = n_ref[...]
    query_row[...] = jnp.sum(dq_ref[...].astype(F32), 0, keepdims=True)
    value_row[...] = jnp.sum(dv_ref[...].astype(F32), 0, keepdims=True)
    for i, part in enumerate((dq_ref, dk_ref, dv_ref)):
        g_ref[i * cols : (i + 1) * cols, :] = dot(part[...], normed, TN).astype(LOW)
        dn_ref[...] += dot(part[...], w_ref[i * cols : (i + 1) * cols, :], NN)


def saved_shapes(sz):
    s, r, c = sz.shards, sz.rows, sz.columns
    return [
        ((r, sz.width), LOW),
        ((s, 4, r, c), LOW),
        ((s, sz.sequences * sz.heads, sz.length, sz.length), LOW),
        ((r, sz.width), F32),
        ((r, sz.width), LOW),
        ((s, 2, r, sz.units), LOW),
    ]


def structs(shapes):
    return [jax.ShapeDtypeStruct(s, d) for s, d in shapes]


def vmems(shapes):
    return [pltpu.VMEM(s, d) for s, d in shapes]


class Place:
    def __init__(self, heads, zs=None):
        self.clip, self.y, self.z = (lax.axis_index(n) for n in ("clip", "tube", "head"))
        self.heads = heads
        self.core, self.x = lax.rem(self.clip, 2), lax.div(self.clip, 2)
        c, x, y = self.core, self.x, self.y
        self.first = (c + 2 * (x + (1 - c) * (1 - 2 * x)), y + c * (1 - 2 * y), self.z)
        self.second = (c + 2 * (x + c * (1 - 2 * x)), y + (1 - c) * (1 - 2 * y), self.z)
        self.other = (1 - c + 2 * x, y, self.z)
        self.i = (1 - c) * x + c * y
        self.j = (1 - c) * y + c * x
        self.along_x = (c + 2 * (1 - x), y, self.z)

    def head(self, step):
        return (self.clip, self.y, lax.rem(self.z + step + self.heads, self.heads))

    def across(self, step):
        return (self.clip, 1 - self.y, lax.rem(self.z + step + self.heads, self.heads))

    def clip_peers(self):
        return [self.head(d) for d in range(1, self.heads)] + [self.across(d) for d in range(self.heads)]

    def all_peers(self):
        return [self.along_x, self.other] + self.clip_peers()


def greet(peers):
    barrier = pltpu.get_barrier_semaphore()
    for peer in peers:
        pl.semaphore_signal(barrier, inc=1, device_id=peer, device_id_type=MESH)
    pl.semaphore_wait(barrier, len(peers))


class Moves:
    def __init__(self, send_sem, recv_sem):
        self.send_sem, self.recv_sem, self.count, self.sent = send_sem, recv_sem, 0, {}

    def phase(self, copies):
        made = []
        for src, dst, landing, target in copies:
            n = self.count
            self.count += 1
            made.append((src, dst, landing, target, n))
        return made

    def start(self, made):
        for src, dst, _, target, n in made:
            copy = pltpu.make_async_remote_copy(
                src, dst, self.send_sem.at[n], self.recv_sem.at[n], device_id=target, device_id_type=MESH
            )
            copy.start()
            self.sent[n] = copy

    def arrive(self, made):
        for src, _, landing, target, n in made:
            pltpu.make_async_remote_copy(
                src, landing, self.send_sem.at[n], self.recv_sem.at[n], device_id=target, device_id_type=MESH
            ).wait_recv()

    def left(self, made):
        for *_, n in made:
            if n in self.sent:
                self.sent.pop(n).wait_send()

    def finish(self):
        for copy in self.sent.values():
            copy.wait_send()
        self.sent = {}


def piece_list(sz, blocks):
    out = []
    for b in range(blocks):
        for kind, start in ((ATTN, 0), (UP, sz.up_row), (DOWN, sz.down_row)):
            parts = 2 if (b, kind) == (0, ATTN) else 1
            size = sz.width // parts
            out += [(b, kind, start + i * size, size) for i in range(parts)]
    return out


def gather_phases(place, moves, full, offset, rows):
    q = rows // 8
    c, i, j, z, heads = place.core, place.i, place.j, place.z, place.heads

    def at(ref, head, start, size):
        return ref.at[head, pl.ds(pl.multiple_of(offset + start * q, q), size * q), :]

    def other(d):
        return lax.rem(z + d, heads)

    mine = 4 * c + 2 * j + i
    near = 4 * c + 2 * j + (1 - i)
    pair = 4 * c + 2 * j
    pair_far = 4 * c + 2 * (1 - j)
    steps = range(1, heads)
    return [
        moves.phase(
            [(at(full, z, mine, 1), at(full, z, mine, 1), at(full, lax.rem(z + heads - d, heads), mine, 1), place.head(d)) for d in steps]
        ),
        moves.phase(
            [(at(full, other(d), mine, 1), at(full, other(d), mine, 1), at(full, other(d), near, 1), place.first) for d in steps]
        ),
        moves.phase(
            [(at(full, other(d), pair, 2), at(full, other(d), pair, 2), at(full, other(d), pair_far, 2), place.second) for d in steps]
        ),
        moves.phase(
            [(at(full, other(d), 4 * c, 4), at(full, other(d), 4 * c, 4), at(full, other(d), 4 * (1 - c), 4), place.other) for d in steps]
        ),
    ]


class Saves:
    def __init__(self, sem):
        self.sem, self.count = sem, 0

    def start(self, src, dst):
        copy = pltpu.make_async_copy(src, dst, self.sem.at[self.count])
        self.count += 1
        copy.start()
        return copy


def forward_kernel(sz, blocks, frame_share, tube_share, *refs):
    (w_qkv, w_out, w_up, w_down, tokens, marks, b_qv, b_up, embed, gains, shifts, b_out, b_down), refs = refs[:13], refs[13:]
    fulls, refs = refs[:blocks], refs[blocks:]
    saved, refs = [refs[7 * b : 7 * b + 7] for b in range(blocks)], refs[7 * blocks :]
    (result, frame_marks), refs = refs[:2], refs[2:]
    w = refs[:blocks]
    (
        frames, bqv, bup, x, n, t, p, m, n2, act, y, y_low, second, send_sem, recv_sem, local_sem, save_sem,
    ) = refs[blocks:]
    heads, block_rows, length = sz.shards, sz.block_rows, sz.length
    place = Place(heads)
    moves = Moves(send_sem, recv_sem)
    local, saves = Saves(local_sem), Saves(save_sem)

    def settle(copies):
        for copy in copies:
            copy.wait()

    yy, z = place.y, place.z
    tubes = tokens.shape[1]
    greet(place.all_peers())

    owned = pl.ds((2 * z + yy) * frame_share, frame_share)
    asked = pl.ds((2 * z + 1 - yy) * frame_share, frame_share)
    here, there = pl.ds(yy * tubes, tubes), pl.ds((1 - yy) * tubes, tubes)
    exchange = moves.phase(
        [
            (src.at[asked], dst.at[:, here], dst.at[:, there], place.across(0))
            for src, dst in ((tokens, frames), (marks, frame_marks))
        ]
        + [
            (src, dst.at[z], dst.at[lax.rem(z + heads - d, heads)], place.head(d))
            for src, dst in ((b_qv, bqv), (b_up, bup))
            for d in range(1, heads)
        ]
    )
    spread = moves.phase(
        [
            (
                y_low.at[:, pl.ds((heads * ty + tz) * tube_share, tube_share)],
                second.at[pl.ds((2 * z + yy) * frame_share, frame_share)],
                second.at[pl.ds((2 * fz + ty) * frame_share, frame_share)],
                target,
            )
            for ty, tz, fz, target in [
                (yy, lax.rem(z + d, heads), lax.rem(z + heads - d, heads), place.head(d)) for d in range(1, heads)
            ]
            + [
                (1 - yy, lax.rem(z + d, heads), lax.rem(z + heads - d, heads), place.across(d)) for d in range(heads)
            ]
        ]
    )
    pieces = piece_list(sz, blocks)
    work = [gather_phases(place, moves, w[b], start, size) for b, _, start, size in pieces]
    moves.start(exchange)
    own_parts = {}
    for b in range(blocks):
        mine = w[b].at[z]
        own_parts[b, ATTN] = [
            local.start(w_qkv.at[b], mine.at[pl.ds(0, sz.out_row)]),
            local.start(w_out.at[b], mine.at[pl.ds(sz.out_row, sz.columns)]),
        ]
        own_parts[b, UP] = [local.start(w_up.at[b], mine.at[pl.ds(sz.up_row, sz.width)])]
        own_parts[b, DOWN] = [local.start(w_down.at[b], mine.at[pl.ds(sz.down_row, sz.units)])]

    def begin_piece(piece):
        b, kind, _, _ = pieces[piece]
        settle(own_parts.pop((b, kind), ()))
        moves.start(work[piece][0])
    owns = [
        local.start(tokens.at[owned], frames.at[:, here]),
        local.start(marks.at[owned], frame_marks.at[:, here]),
        local.start(b_qv, bqv.at[z]),
        local.start(b_up, bup.at[z]),
    ]

    def save(b, index, src, part=None):
        dst = saved[b][index]
        return saves.start(src, dst if part is None else dst.at[part])

    def begin_block(b):
        norm_rows(sz, x, gains[b, 0:1, :], shifts[b, 0:1, :], n)
        m[...] = x[...] + b_out[b : b + 1, :]
        return [save(b, 0, x), save(b, 1, n)]

    def attention(b, s):
        forward_attention(sz, s, w[b], bqv[s, b, 0:1, :], bqv[s, b, 1:2, :], n, t, p, m)
        return [save(b, 2, t.at[s], s), save(b, 3, p.at[s], s)]

    def middle(b):
        norm_rows(sz, m, gains[b, 1:2, :], shifts[b, 1:2, :], n2)
        y[...] = m[...] + b_down[b : b + 1, :]
        return [save(b, 4, m), save(b, 5, n2)]

    def up(b, s):
        forward_up(sz, s, w[b], bup[s, b : b + 1, :], n2, act)
        return [save(b, 6, act.at[s], s)]

    def down(b, s):
        forward_down(sz, s, w[b], act, y)

    def keep(piece):
        b, _, start, size = pieces[piece]
        at = pl.ds(start, size)
        return [saves.start(w[b].at[:, at], fulls[b].at[:, at])]

    kept, early = [], []
    wide = [None] * blocks

    def first_input():
        settle(owns)
        moves.arrive(exchange)
        tok = frames[...].astype(F32).reshape(sz.rows, sz.width)
        mark = frame_marks[...].astype(F32).reshape(sz.rows, 128)[:, 0:1]
        x[...] = jnp.where(mark > 0.5, embed[...].reshape(1, sz.width), tok)
        early.extend(begin_block(0))

    def second_input():
        moves.arrive(spread)
        wide[1].wait()
        settle(early)
        for j in range(tube_share):
            x[j * length : (j + 1) * length, :] = second[:, j].astype(F32).reshape(length, sz.width)
        kept.extend(begin_block(1))

    def spread_first():
        y_low[...] = y[...].astype(LOW).reshape(y_low.shape)
        moves.start(spread)
        wide[1] = local.start(
            y_low.at[:, pl.ds((heads * yy + z) * tube_share, tube_share)],
            second.at[pl.ds((2 * z + yy) * frame_share, frame_share)],
        )

    def finish_second():
        for j in range(tube_share):
            at = slice(j * length, (j + 1) * length)
            second[:, j] = y[at, :].astype(LOW).reshape(second.shape[0], second.shape[2], sz.width)
        kept.append(saves.start(second, result))

    def advance(piece, phase):
        moves.arrive(work[piece][phase])
        if phase < 3:
            moves.start(work[piece][phase + 1])
        else:
            kept.extend(keep(piece))

    steps = {(FIRST_INPUT,): first_input, (SPREAD,): spread_first, (SECOND_INPUT,): second_input, (RESULT,): finish_second}
    for piece in range(len(work)):
        steps[SEND, piece] = functools.partial(begin_piece, piece)
        for phase in range(4):
            steps[PASS, piece, phase] = functools.partial(advance, piece, phase)
    for b in range(blocks):
        held = kept if b else early
        run = lambda f, *args, held=held: held.extend(f(*args) or ())
        steps[MIDDLE, b] = functools.partial(run, middle, b)
        for s in range(heads):
            steps[ATTEND, b, s] = functools.partial(run, attention, b, s)
            steps[EXPAND, b, s] = functools.partial(run, up, b, s)
            steps[CONTRACT, b, s] = functools.partial(run, down, b, s)
    for step in FORWARD_ORDER:
        steps[step]()
    moves.finish()
    settle(kept)


def run_forward(sz, blocks, frame_share, tube_share, weights, tokens, marks, b_qv, b_up, embed, gains, shifts, b_out, b_down):
    heads, width, rows = sz.shards, sz.width, sz.rows
    tubes, patches = 2 * tokens.shape[1], tokens.shape[2]
    frames = tokens.shape[0]
    saved = [((rows, width), F32)] + saved_shapes(sz)
    whole_frames = (frame_share, tubes, patches)
    count = len(piece_list(sz, blocks)) * 4 * (heads - 1) + 2 + 2 * (heads - 1) + 2 * heads - 1
    hbm, vmem = pl.BlockSpec(memory_space=pl.ANY), pl.BlockSpec(memory_space=pltpu.VMEM)
    full = ((heads, sz.block_rows, width), LOW)
    mixed = (frames, tube_share, patches, width)
    out = pl.pallas_call(
        lambda *refs: forward_kernel(sz, blocks, frame_share, tube_share, *refs),
        name="forward_both",
        out_shape=structs([full] * blocks + saved * blocks + [(mixed, LOW), (whole_frames + (128,), LOW)]),
        in_specs=[hbm] * 8 + [vmem] * 5,
        out_specs=[hbm] * (blocks + 7 * blocks + 1) + [vmem],
        scratch_shapes=vmems(
            [full] * blocks
            + [
                (whole_frames + (width,), LOW),
                ((heads,) + b_qv.shape, F32),
                ((heads,) + b_up.shape, F32),
            ]
            + saved
            + [
                ((rows, width), F32),
                (whole_frames + (width,), LOW),
                (mixed, LOW),
            ]
        )
        + [
            pltpu.SemaphoreType.DMA((count,)),
            pltpu.SemaphoreType.DMA((count,)),
            pltpu.SemaphoreType.DMA((16,)),
            pltpu.SemaphoreType.DMA((64,)),
        ],
        compiler_params=pltpu.CompilerParams(
            collective_id=0, has_side_effects=True, vmem_limit_bytes=62 * 2**20
        ),
    )(*weights, tokens, marks, b_qv, b_up, embed, gains, shifts, b_out, b_down)
    fulls, out = out[:blocks], out[blocks:]
    saved = [out[7 * b : 7 * b + 7] for b in range(blocks)]
    return fulls, saved, out[-2], out[-1]


class Line:
    def __init__(self, place, send_sem, recv_sem, region, own=None):
        self.place, self.send_sem, self.recv_sem, self.region = place, send_sem, recv_sem, region
        self.own = own
        self.steps = place.heads - 1

    def moves(self, step):
        z, last = self.place.z, self.place.heads - 1
        return [
            ((z >= step) & (z < last), z - step, 1, z > step, z - 1 - step, 2 * step),
            ((z <= last - step) & (z > 0), z + step, -1, z < last - step, z + 1 + step, 2 * step + 1),
        ]

    def copy(self, block, way, n):
        return pltpu.make_async_remote_copy(
            self.own if n < 2 and self.own is not None else self.region(block),
            self.region(block),
            self.send_sem.at[n],
            self.recv_sem.at[n],
            device_id=self.place.head(way),
            device_id_type=MESH,
        )

    def start(self, step):
        for sends, block, way, _, _, n in self.moves(step):
            pl.when(sends)(lambda block=block, way=way, n=n: self.copy(block, way, n).start())

    def arrive(self, step):
        for _, _, way, gets, block, n in self.moves(step):
            pl.when(gets)(lambda block=block, way=way, n=n: self.copy(block, way, n).wait_recv())

    def finish(self):
        for step in range(self.steps):
            for sends, block, way, _, _, n in self.moves(step):
                pl.when(sends)(lambda block=block, way=way, n=n: self.copy(block, way, n).wait_send())


class Reduction:
    def __init__(self, place, moves, grads, out, out_row, rows, bufs, final_buf, final_sem):
        q = rows // 8
        self.q, self.place, self.moves, self.grads = q, place, moves, grads
        self.core_buf, self.first_buf, self.second_buf, self.head_buf = bufs
        self.final_buf, self.final_sem = final_buf, final_sem
        c, i, j, z, heads = place.core, place.i, place.j, place.z, place.heads
        cut = lambda start, size: pl.ds(pl.multiple_of(start * q, q), size * q)
        row = lambda start, size: out.at[pl.ds(pl.multiple_of(out_row + start * q, q), size * q), :]
        self.kept, self.given = cut(4 * c, 4), cut(4 * (1 - c), 4)
        self.part, self.subpart = cut(2 * i, 2), cut(j, 1)
        shards = range(heads)
        self.core = moves.phase(
            [(grads.at[s % 2, self.given, :], self.core_buf.at[s], self.core_buf.at[s], place.other) for s in shards]
        )
        self.first = moves.phase(
            [(self.core_buf.at[s, cut(2 * (1 - i), 2), :], self.first_buf.at[s], self.first_buf.at[s], place.first) for s in shards]
        )
        self.second = moves.phase(
            [(self.first_buf.at[s, cut(1 - j, 1), :], self.second_buf.at[s], self.second_buf.at[s], place.second) for s in shards]
        )
        self.heads = moves.phase(
            [
                (self.second_buf.at[lax.rem(z + d, heads)], self.head_buf.at[d - 1], self.head_buf.at[d - 1], place.head(d))
                for d in range(1, heads)
            ]
        )
        a, mine = 4 * c, 2 * i + j
        self.share_second = moves.phase([(final_buf, row(a + mine, 1), row(a + 2 * i + 1 - j, 1), place.second)])
        self.share_first = moves.phase([(row(a + 2 * i, 2), row(a + 2 * i, 2), row(a + 2 * (1 - i), 2), place.first)])
        self.share_core = moves.phase([(row(a, 4), row(a, 4), row(4 - a, 4), place.other)])
        self.keep = pltpu.make_async_copy(final_buf, row(a + mine, 1), final_sem)

    def give(self, s):
        self.moves.start([self.core[s]])

    def step_first(self, s):
        self.moves.arrive([self.core[s]])
        self.core_buf[s] = self.core_buf[s] + self.grads[s % 2, self.kept, :]
        self.moves.start([self.first[s]])

    def step_second(self, free_sem=None):
        for s in range(self.place.heads):
            self.moves.arrive([self.first[s]])
            self.first_buf[s] = self.first_buf[s] + self.core_buf[s, self.part, :]
            self.moves.start([self.second[s]])
        if free_sem is not None:
            self.moves.left(self.first)
            pl.semaphore_signal(free_sem, inc=1, device_id=self.place.other, device_id_type=MESH)

    def step_heads(self):
        for s in range(self.place.heads):
            self.moves.arrive([self.second[s]])
            self.second_buf[s] = self.second_buf[s] + self.first_buf[s, self.subpart, :]
        self.moves.start(self.heads)

    def step_share(self):
        self.moves.arrive(self.heads)
        total = self.second_buf[self.place.z].astype(F32)
        for d in range(self.place.heads - 1):
            total += self.head_buf[d].astype(F32)
        self.final_buf[...] = total.astype(LOW)
        self.keep.start()
        self.moves.start(self.share_second)

    def step_share_first(self):
        self.keep.wait()
        self.moves.arrive(self.share_second)
        self.moves.start(self.share_first)

    def step_share_core(self):
        self.moves.arrive(self.share_first)
        self.moves.start(self.share_core)

    def end(self):
        self.moves.arrive(self.share_core)


SMALL_ROWS = 48
GAIN_ROW, SHIFT_ROW, BOUT_ROW, BDOWN_ROW, BUP_ROW, BQV_ROW = 1, 5, 9, 11, 16, 24


def backward_kernel(sz, blocks, frame_share, tube_share, *refs):
    fulls, refs = refs[:blocks], refs[blocks:]
    saved, refs = [refs[7 * b : 7 * b + 7] for b in range(blocks)], refs[7 * blocks :]
    (cotangent, result, marks, gains), refs = refs[:4], refs[4:]
    (out_result, out_tokens, out_grads, out_small), refs = refs[:4], refs[4:]
    (
        wm, act, wa, t, p, m, n2, n, x, low, dn, dm, du, do, dq, dk, dv, cot, dx_low, back,
        grads, core_buf, first_buf, second_buf, head_buf, final_buf, small, small_in, small_heads, small_last,
        send_sem, recv_sem, line_sem, load_sem, copy_sem, final_sem, free_sem,
    ) = refs
    heads, width, length = sz.shards, sz.width, sz.length
    place = Place(heads)
    moves = Moves(send_sem, recv_sem)
    loads = Saves(copy_sem)
    yy, z = place.y, place.z
    tubes = cotangent.shape[1]

    def step_loads(b, kind, s):
        slot = s % 2
        if kind == MLP_BACK:
            pairs = [(fulls[b].at[s, pl.ds(sz.up_row, 2 * width), :], wm.at[slot]), (saved[b][6].at[s], act.at[slot])]
            base = 0
        else:
            pairs = [
                (fulls[b].at[s, pl.ds(0, sz.up_row), :], wa.at[slot]),
                (saved[b][2].at[s], t.at[slot]),
                (saved[b][3].at[s], p.at[slot]),
            ]
            base = 4
        return [
            pltpu.make_async_copy(src, dst, load_sem.at[base + slot * len(pairs) + i]) for i, (src, dst) in enumerate(pairs)
        ]

    steps = [(b, kind, s) for b in (1, 0) for kind in (MLP_BACK, ATTN_BACK) for s in range(heads)]

    def fetch(i):
        if i < len(steps):
            for copy in step_loads(*steps[i]):
                copy.start()

    def ready(i):
        for copy in step_loads(*steps[i]):
            copy.wait()
        fetch(i + 1)

    first_load = loads.start(cotangent.at[:, pl.ds(z * tube_share, tube_share)], cot)
    fetch(0)
    norm_loads = {1: [loads.start(saved[1][4], m), loads.start(saved[1][5], n2)]}
    later_loads = {1: [loads.start(saved[1][1], n), loads.start(saved[1][0], x)]}
    small[...] = jnp.zeros_like(small)
    greet(place.all_peers())

    red = {}
    for b in (1, 0):
        for k in (DOWN, UP, ATTN):
            base = b * sz.block_rows + (sz.down_row, sz.up_row, 0)[k]
            red[b, k] = Reduction(
                place,
                moves,
                grads.at[k],
                out_grads,
                base,
                width,
                (core_buf.at[k], first_buf.at[b, k], second_buf.at[b, k], head_buf.at[b, k]),
                final_buf.at[b, k],
                final_sem.at[b * 3 + k],
            )
    tube_region = lambda block: out_result.at[:, pl.ds(block * tube_share, tube_share)]
    line = Line(place, line_sem.at[0], line_sem.at[1], tube_region, result)
    spread = moves.phase(
        [
            (
                dx_low.at[pl.ds((2 * tz + ty) * frame_share, frame_share)],
                back.at[:, pl.ds((heads * yy + z) * tube_share, tube_share)],
                back.at[:, pl.ds((heads * ty + fz) * tube_share, tube_share)],
                target,
            )
            for ty, tz, fz, target in [
                (yy, lax.rem(z + d, heads), lax.rem(z + heads - d, heads), place.head(d)) for d in range(1, heads)
            ]
            + [
                (1 - yy, lax.rem(z + d, heads), lax.rem(z + heads - d, heads), place.across(d)) for d in range(heads)
            ]
        ]
    )

    line.start(0)
    first_load.wait()
    frames = cot.shape[0]
    for j in range(tube_share):
        low[j * length : (j + 1) * length, :] = cot[:, j].reshape(length, width)
    own_result = loads.start(result, tube_region(z))

    def row(r, columns=None):
        return small.at[r : r + 1, :] if columns is None else small.at[r : r + 1, 0:columns]

    def mlp(b, s):
        if s == 0:
            row(BDOWN_ROW + b)[...] = jnp.sum(low[...].astype(F32), 0, keepdims=True)
            dn[...] = jnp.zeros_like(dn)
            for copy in norm_loads[b]:
                copy.wait()
        ready((1 - b) * 2 * heads + s)
        for k in (DOWN, UP):
            if s >= 2:
                moves.left([red[b, k].core[s - 2]])
            elif b == 0:
                moves.left([red[1, k].core[s + heads - 2]])
        backward_mlp(
            sz, wm.at[s % 2], act.at[s % 2], low, n2, du, dn, grads.at[DOWN, s % 2], grads.at[UP, s % 2],
            row(BUP_ROW + b * heads + s),
        )
        for k in (DOWN, UP):
            if s == 0 and b == 0:
                pl.semaphore_wait(free_sem.at[k], 1)
            red[b, k].give(s)

    def mlp_norm(b):
        norm_back_rows(
            sz, m, gains[b, 1:2, :], dn, low, dm, row(GAIN_ROW + 2 * b + 1), row(SHIFT_ROW + 2 * b + 1), row(BOUT_ROW + b), low
        )
        if b:
            norm_loads[0] = [loads.start(saved[0][4], m), loads.start(saved[0][5], n2)]

    def attention(b, s):
        if s == 0:
            dn[...] = jnp.zeros_like(dn)
            for copy in later_loads[b]:
                copy.wait()
        ready((1 - b) * 2 * heads + heads + s)
        if s >= 2:
            moves.left([red[b, ATTN].core[s - 2]])
        elif b == 0:
            moves.left([red[1, ATTN].core[s + heads - 2]])
        r = BQV_ROW + 2 * (b * heads + s)
        backward_attention(
            sz, wa.at[s % 2], t.at[s % 2], p.at[s % 2], low, n, do, dq, dk, dv, dn, grads.at[ATTN, s % 2],
            row(r, sz.columns), row(r + 1, sz.columns),
        )
        if s == 0 and b == 0:
            pl.semaphore_wait(free_sem.at[ATTN], 1)
        red[b, ATTN].give(s)

    own_spread = []

    def attention_norm(b):
        norm_back_rows(
            sz, x, gains[b, 0:1, :], dn, dm, dm, row(GAIN_ROW + 2 * b), row(SHIFT_ROW + 2 * b), None, None
        )
        if b:
            later_loads[0] = [loads.start(saved[0][1], n), loads.start(saved[0][0], x)]
            for j in range(tube_share):
                dx_low[:, j] = dm[j * length : (j + 1) * length, :].astype(LOW).reshape(frames, length // frames, width)
            moves.start(spread)
            own_spread.append(
                loads.start(
                    dx_low.at[pl.ds((2 * z + yy) * frame_share, frame_share)],
                    back.at[:, pl.ds((heads * yy + z) * tube_share, tube_share)],
                )
            )
            return
        mark = marks[...].astype(F32).reshape(sz.rows, 128)[:, 0:1] > 0.5
        grad = dm[...]
        row(0)[...] = jnp.sum(jnp.where(mark, grad, 0.0), 0, keepdims=True)
        back[...] = jnp.where(mark, 0.0, grad).astype(LOW).reshape(back.shape)
        moves.start(cross)
        own_copy = loads.start(back.at[:, here], own_frames(z))
        moves.start(small_steps[0])
        own_copy.wait()
        own_line.start(0)

    def second_upstream():
        moves.arrive(spread)
        for copy in own_spread:
            copy.wait()
        low[...] = back[...].reshape(sz.rows, width)

    here, there = pl.ds(yy * tubes, tubes), pl.ds((1 - yy) * tubes, tubes)
    own_frames = lambda block: out_tokens.at[pl.ds((2 * block + yy) * frame_share, frame_share)]
    far_frames = lambda block: out_tokens.at[pl.ds((2 * block + 1 - yy) * frame_share, frame_share)]
    cross = moves.phase([(back.at[:, there], own_frames(z), far_frames(z), place.across(0))])
    own_line = Line(place, line_sem.at[2], line_sem.at[3], own_frames)
    far_line = Line(place, line_sem.at[4], line_sem.at[5], far_frames)

    def start_far():
        moves.arrive(cross)
        far_line.start(0)

    half = SMALL_ROWS // 2
    part = pl.ds(pl.multiple_of(place.core * half, half), half)
    far_part = pl.ds(pl.multiple_of((1 - place.core) * half, half), half)
    small_steps = [
        moves.phase([(small, small_in.at[i], small_in.at[i], target)])
        for i, target in enumerate((place.other, place.first, place.second))
    ]
    small_z = moves.phase(
        [(small.at[part], small_heads.at[d - 1], small_heads.at[d - 1], place.head(d)) for d in range(1, heads)]
    )
    small_end = moves.phase([(small_last.at[part], small_last.at[part], small_last.at[far_part], place.other)])

    def add_small(i):
        moves.arrive(small_steps[i])
        moves.left(small_steps[i])
        small[...] += small_in[i]
        moves.start(small_steps[i + 1] if i + 1 < len(small_steps) else small_z)

    def add_small_heads():
        moves.arrive(small_z)
        total = small[part, :]
        for d in range(heads - 1):
            total += small_heads[d]
        small_last[part, :] = total
        moves.start(small_end)

    def end_small():
        moves.arrive(small_end)
        out_small[...] = small_last[...]

    def pass_on(way, step):
        way.arrive(step)
        if step + 1 < way.steps:
            way.start(step + 1)

    todo = {(UPSTREAM,): second_upstream, (FAR_START,): start_far, (SMALL, 3): add_small_heads, (SMALL, 4): end_small}
    for i in range(3):
        todo[SMALL, i] = functools.partial(add_small, i)
    for name, way in ((RESULT_LINE, line), (OWN_LINE, own_line), (FAR_LINE, far_line)):
        for step in range(way.steps):
            todo[name, step] = functools.partial(pass_on, way, step)
    for b in range(blocks):
        todo[MLP_NORM, b] = functools.partial(mlp_norm, b)
        todo[ATTN_NORM, b] = functools.partial(attention_norm, b)
        for s in range(heads):
            todo[MLP_BACK, b, s] = functools.partial(mlp, b, s)
            todo[ATTN_BACK, b, s] = functools.partial(attention, b, s)
        for k in (DOWN, UP, ATTN):
            each = red[b, k]
            for s in range(heads):
                todo[ADD_CORE, b, k, s] = functools.partial(each.step_first, s)
            todo[ADD_FIRST, b, k] = functools.partial(each.step_second, free_sem.at[k] if b else None)
            todo[ADD_SECOND, b, k] = each.step_heads
            todo[ADD_HEADS, b, k] = each.step_share
            todo[SHARE_FIRST, b, k] = each.step_share_first
            todo[SHARE_CORE, b, k] = each.step_share_core
            todo[ARRIVED, b, k] = each.end
    for step in BACKWARD_ORDER:
        todo[step]()
    own_result.wait()
    for each in (line, own_line, far_line):
        each.finish()
    moves.finish()


def run_backward(sz, blocks, frame_share, tube_share, fulls, saved, cotangent, result, marks, gains):
    heads, width, rows, cols = sz.shards, sz.width, sz.rows, sz.columns
    frames, tubes, patches = cotangent.shape[:3]
    hbm, vmem = pl.BlockSpec(memory_space=pl.ANY), pl.BlockSpec(memory_space=pltpu.VMEM)
    q = width // 8
    local = (frame_share, 2 * tubes, patches, width)
    mixed = (frames, tube_share, patches, width)
    kinds = 3 * blocks
    count = kinds * (3 * heads + 3 + heads - 1) + 2 * heads - 1 + 1 + 4 + heads - 1
    flat = [array for per in saved for array in per]
    return pl.pallas_call(
        lambda *refs: backward_kernel(sz, blocks, frame_share, tube_share, *refs),
        name="backward_both",
        out_shape=structs(
            [
                (cotangent.shape, LOW),
                (cotangent.shape, LOW),
                ((blocks * sz.block_rows, width), LOW),
                ((SMALL_ROWS, width), F32),
            ]
        ),
        in_specs=[hbm] * (blocks + len(flat) + 2) + [vmem] * 2,
        out_specs=[hbm] * 3 + [vmem],
        scratch_shapes=vmems(
            [
                ((2, 2 * width, width), LOW),
                ((2, 2, rows, sz.units), LOW),
                ((2, sz.up_row, width), LOW),
                ((2, 4, rows, cols), LOW),
                ((2, sz.sequences * sz.heads, sz.length, sz.length), LOW),
                ((rows, width), F32),
                ((rows, width), LOW),
                ((rows, width), LOW),
                ((rows, width), F32),
                ((rows, width), LOW),
                ((rows, width), F32),
                ((rows, width), F32),
                ((rows, sz.units), LOW),
                ((rows, cols), LOW),
                ((rows, cols), LOW),
                ((rows, cols), LOW),
                ((rows, cols), LOW),
                (mixed, LOW),
                (mixed, LOW),
                (local, LOW),
                ((3, 2, width, width), LOW),
                ((3, heads, 4 * q, width), LOW),
                ((blocks, 3, heads, 2 * q, width), LOW),
                ((blocks, 3, heads, q, width), LOW),
                ((blocks, 3, heads - 1, q, width), LOW),
                ((blocks, 3, q, width), LOW),
                ((SMALL_ROWS, width), F32),
                ((3, SMALL_ROWS, width), F32),
                ((heads - 1, SMALL_ROWS // 2, width), F32),
                ((SMALL_ROWS, width), F32),
            ]
        )
        + [
            pltpu.SemaphoreType.DMA((count,)),
            pltpu.SemaphoreType.DMA((count,)),
            pltpu.SemaphoreType.DMA((6, 2 * (heads - 1))),
            pltpu.SemaphoreType.DMA((10,)),
            pltpu.SemaphoreType.DMA((24,)),
            pltpu.SemaphoreType.DMA((kinds,)),
            pltpu.SemaphoreType.REGULAR((3,)),
        ],
        compiler_params=pltpu.CompilerParams(
            collective_id=1, has_side_effects=True, vmem_limit_bytes=63 * 2**20
        ),
    )(*fulls, *flat, cotangent, result, marks, gains)


def fits_local(arrays, clip_size, tube_size, head_size):
    clips, frames, tubes = arrays[0].shape[:3]
    width = arrays[0].shape[-1]
    columns, units = arrays[5].shape[3] // head_size, arrays[9].shape[2] // head_size
    devices = tube_size * head_size
    return (
        (clips, clip_size, tube_size) == (4, 4, 2)
        and frames % devices == 0
        and frames == tubes
        and head_size % 2 == 0
        and width == 4 * columns == units
        and width % 384 == 0
        and columns % HD == 0
    )


def on_device_local(
    tokens,
    token_mask,
    mask_embed,
    norm_gains,
    norm_shifts,
    w_qkv,
    b_qv,
    w_out,
    b_out,
    w_up,
    b_up,
    w_down,
    b_down,
    cotangent,
):
    _, frames, tubes, patches, width = tokens.shape
    tube_size, heads = lax.axis_size("tube"), lax.axis_size("head")
    head = lax.axis_index("head")
    blocks, columns, units = w_qkv.shape[0], w_qkv.shape[-1], w_up.shape[-1]
    frame_share = frames // (tube_size * heads)
    tube_share = tubes // heads
    rows = frame_share * tube_size * tubes * patches
    sz = Sizes(rows, width, heads, columns, units, rows // frame_share)

    marks = jnp.broadcast_to(token_mask[0][..., None], (frames, tubes, patches, 128)).astype(LOW)
    full, saved, output, mark_frames = run_forward(
        sz,
        blocks,
        frame_share,
        tube_share,
        (w_qkv.transpose(0, 2, 3, 1).reshape(blocks, 3 * columns, width), w_out, w_up, w_down),
        tokens[0],
        marks,
        b_qv,
        b_up,
        mask_embed,
        norm_gains,
        norm_shifts,
        b_out,
        b_down,
    )
    output, grad_tokens, whole, small = run_backward(
        sz, blocks, frame_share, tube_share, full, saved, cotangent[0], output, mark_frames, norm_gains
    )
    rows_of = lambda start, size: small[start : start + size]
    bup_grad = rows_of(BUP_ROW, blocks * heads).reshape(blocks, heads, units)
    bqv_grad = rows_of(BQV_ROW, 2 * blocks * heads)[:, :columns].reshape(blocks, heads, 2, columns)
    of_head = lambda array: lax.dynamic_index_in_dim(array, head, 1, False)
    whole = whole.astype(F32)
    whole = whole.reshape(blocks, sz.block_rows, width)
    qkv_grad = whole[:, : sz.out_row].reshape(blocks, 3, columns, width).transpose(0, 3, 1, 2)
    return (
        output[None],
        grad_tokens[None],
        small[0],
        rows_of(GAIN_ROW, 2 * blocks).reshape(blocks, 2, width),
        rows_of(SHIFT_ROW, 2 * blocks).reshape(blocks, 2, width),
        qkv_grad,
        of_head(bqv_grad),
        whole[:, sz.out_row : sz.up_row],
        rows_of(BOUT_ROW, blocks),
        whole[:, sz.up_row : sz.down_row],
        of_head(bup_grad),
        whole[:, sz.down_row :],
        rows_of(BDOWN_ROW, blocks),
    )


def solution(mesh):
    sizes = [mesh.shape[name] for name in ("clip", "tube", "head")]

    def run(*arrays):
        on_device = on_device_local if fits_local(arrays, *sizes) else on_device_sums
        return on_mesh(on_device, mesh)(*arrays)

    return run


def on_mesh(on_device, mesh):
    return jax.shard_map(
        on_device,
        mesh=mesh,
        in_specs=(
            P("clip", None, "tube", None, None),
            P("clip", None, "tube", None),
            P(),
            P(),
            P(),
            P(None, None, None, "head"),
            P(None, None, "head"),
            P(None, "head", None),
            P(),
            P(None, None, "head"),
            P(None, "head"),
            P(None, "head", None),
            P(),
            P("clip", None, "tube", None, None),
        ),
        out_specs=(
            P("clip", None, "tube", None, None),
            P("clip", None, "tube", None, None),
            P(),
            P(),
            P(),
            P(None, None, None, "head"),
            P(None, None, "head"),
            P(None, "head", None),
            P(),
            P(None, None, "head"),
            P(None, "head"),
            P(None, "head", None),
            P(),
        ),
        check_vma=False,
    )
```

```python
import functools

import jax
import jax.numpy as jnp
from jax import lax
from jax.experimental import pallas as pl
from jax.experimental.pallas import tpu as pltpu
from jax.sharding import PartitionSpec as P

F32 = jnp.float32
LOW = jnp.bfloat16
MESH = pl.DeviceIdType.MESH

HD = 64


EPS = 1e-05


def norm_forward(values, gain_vector, shift_vector):
    centre = values - jnp.mean(values, -1, keepdims=True)
    inverse = lax.rsqrt(jnp.mean(centre * centre, -1, keepdims=True) + EPS)
    normal = centre * inverse
    return (normal * gain_vector + shift_vector, normal, inverse)


def norm_backward(grad_out, normal, inverse, gain_vector):
    grad_normal = grad_out * gain_vector
    grad_in = inverse * (
        grad_normal
        - jnp.mean(grad_normal, -1, keepdims=True)
        - normal * jnp.mean(grad_normal * normal, -1, keepdims=True)
    )
    return (grad_in, jnp.sum(grad_out * normal, 0), jnp.sum(grad_out, 0))


def row_total(partial_sum):
    return lax.psum(partial_sum.astype(jnp.bfloat16), "head").astype(jnp.float32)


def input_total(partial_sum):
    return lax.psum(partial_sum.astype(jnp.bfloat16), "head").astype(jnp.float32)


def split_heads(tensor, batch_count, length):
    return tensor.reshape(batch_count, length, tensor.shape[-1] // HD, HD)


def attend(queries, key_rows, value_rows):
    scores = jnp.einsum(
        "bshe,bthe->bhst", queries, key_rows, preferred_element_type=jnp.float32
    ) * HD ** (-0.5)
    maximum = jnp.max(scores, -1, keepdims=True)
    exponent = jnp.exp(scores - maximum)
    denominator = jnp.sum(exponent, -1, keepdims=True)
    weights_soft = (exponent / denominator).astype(jnp.bfloat16)
    mixture = jnp.einsum(
        "bhst,bthe->bshe", weights_soft, value_rows, preferred_element_type=jnp.float32
    )
    return (mixture.astype(jnp.bfloat16), maximum + jnp.log(denominator))


def attend_back(queries, key_rows, value_rows, log_total, grad_mixture):
    scaling = HD ** (-0.5)
    scores = (
        jnp.einsum("bshe,bthe->bhst", queries, key_rows, preferred_element_type=jnp.float32)
        * scaling
    )
    weights_soft = jnp.exp(scores - log_total)
    grad_weights = jnp.einsum(
        "bshe,bthe->bhst", grad_mixture, value_rows, preferred_element_type=jnp.float32
    )
    grad_values = jnp.einsum(
        "bhst,bshe->bthe",
        weights_soft.astype(jnp.bfloat16),
        grad_mixture,
        preferred_element_type=jnp.float32,
    )
    grad_scores = (
        weights_soft * (grad_weights - jnp.sum(weights_soft * grad_weights, -1, keepdims=True))
    ).astype(jnp.bfloat16)
    grad_queries = (
        jnp.einsum("bhst,bthe->bshe", grad_scores, key_rows, preferred_element_type=jnp.float32)
        * scaling
    )
    grad_keys = (
        jnp.einsum("bhst,bshe->bthe", grad_scores, queries, preferred_element_type=jnp.float32)
        * scaling
    )
    return (grad_queries, grad_keys, grad_values)


def mixer_forward(block_kind, queries, key_rows, value_rows):
    clip_count, frame_count, tube_count, patch_count, columns = queries.shape
    if block_kind == 1:
        reorder = (0, 2, 1, 3, 4)
        pieces = [
            split_heads(
                tensor.transpose(reorder), clip_count * tube_count, frame_count * patch_count
            )
            for tensor in (queries, key_rows, value_rows)
        ]
        mixture, log_total = attend(pieces[0], pieces[1], pieces[2])
        mixture = mixture.reshape(
            clip_count, tube_count, frame_count, patch_count, columns
        ).transpose(reorder)
        return (mixture, (pieces, log_total))
    key_all, value_all = (
        lax.all_gather(key_rows, "tube", axis=2, tiled=True),
        lax.all_gather(value_rows, "tube", axis=2, tiled=True),
    )
    tube_all = key_all.shape[2]
    pieces = [
        split_heads(queries, clip_count * frame_count, tube_count * patch_count),
        split_heads(key_all, clip_count * frame_count, tube_all * patch_count),
        split_heads(value_all, clip_count * frame_count, tube_all * patch_count),
    ]
    mixture, log_total = attend(pieces[0], pieces[1], pieces[2])
    return (
        mixture.reshape(clip_count, frame_count, tube_count, patch_count, columns),
        (pieces, log_total),
    )


def mixer_backward(block_kind, retained, grad_mixture):
    pieces, log_total = retained
    clip_count, frame_count, tube_count, patch_count, columns = grad_mixture.shape
    if block_kind == 1:
        reorder = (0, 2, 1, 3, 4)
        moved = split_heads(
            grad_mixture.transpose(reorder), clip_count * tube_count, frame_count * patch_count
        )
        gradients = attend_back(pieces[0], pieces[1], pieces[2], log_total, moved)
        return [
            grad.astype(jnp.bfloat16)
            .reshape(clip_count, tube_count, frame_count, patch_count, columns)
            .transpose(reorder)
            for grad in gradients
        ]
    gradients = attend_back(
        pieces[0],
        pieces[1],
        pieces[2],
        log_total,
        split_heads(grad_mixture, clip_count * frame_count, tube_count * patch_count),
    )
    tube_all = pieces[1].shape[1] // patch_count
    grad_keys = gradients[1].reshape(clip_count, frame_count, tube_all, patch_count, columns)
    grad_values = gradients[2].reshape(clip_count, frame_count, tube_all, patch_count, columns)
    grad_keys, grad_values = (
        lax.psum_scatter(
            grad_keys.astype(jnp.bfloat16), "tube", scatter_dimension=2, tiled=True
        ).astype(jnp.float32),
        lax.psum_scatter(
            grad_values.astype(jnp.bfloat16), "tube", scatter_dimension=2, tiled=True
        ).astype(jnp.float32),
    )
    grad_queries = (
        gradients[0]
        .astype(jnp.bfloat16)
        .reshape(clip_count, frame_count, tube_count, patch_count, columns)
    )
    return [grad_queries, grad_keys.astype(jnp.bfloat16), grad_values.astype(jnp.bfloat16)]


def block_forward(block_kind, residual, layout, weights):
    gains, shifts, w_qkv, b_qv, w_out, b_out, w_up, b_up, w_down, b_down = weights
    columns = w_qkv.shape[-1]
    grid_shape = layout[:-1] + (columns,)
    normed_share, first_normal, first_inverse = norm_forward(residual, gains[0], shifts[0])
    normed = normed_share.astype(jnp.bfloat16)
    projected = jnp.einsum("rd,dcj->rcj", normed, w_qkv, preferred_element_type=jnp.float32)
    queries = (projected[:, 0] + b_qv[0]).astype(jnp.bfloat16).reshape(grid_shape)
    key_rows = projected[:, 1].astype(jnp.bfloat16).reshape(grid_shape)
    value_rows = (projected[:, 2] + b_qv[1]).astype(jnp.bfloat16).reshape(grid_shape)
    mixture, retained = mixer_forward(block_kind, queries, key_rows, value_rows)
    mixture = mixture.reshape(-1, columns)
    middle = (
        residual + row_total(jnp.dot(mixture, w_out, preferred_element_type=jnp.float32)) + b_out
    )
    second_share, second_normal, second_inverse = norm_forward(middle, gains[1], shifts[1])
    normed_two = second_share.astype(jnp.bfloat16)
    hidden = jnp.dot(normed_two, w_up, preferred_element_type=jnp.float32) + b_up
    active = jax.nn.gelu(hidden).astype(jnp.bfloat16)
    stored = (
        normed,
        first_normal,
        first_inverse,
        retained,
        mixture,
        normed_two,
        second_normal,
        second_inverse,
        hidden,
    )
    return (middle, active, stored)


def block_output(middle, active, w_down, b_down):
    return middle + row_total(jnp.dot(active, w_down, preferred_element_type=jnp.float32)) + b_down


def block_backward(block_kind, residual, layout, weights, grad_rows):
    gains, shifts, w_qkv, b_qv, w_out, b_out, w_up, b_up, w_down, b_down = weights
    middle, active, stored = block_forward(block_kind, residual, layout, weights)
    (
        normed,
        first_normal,
        first_inverse,
        retained,
        mixture,
        normed_two,
        second_normal,
        second_inverse,
        hidden,
    ) = stored
    columns = w_qkv.shape[-1]
    grad_low = grad_rows.astype(jnp.bfloat16)
    grad_wdown = jnp.dot(active.T, grad_low, preferred_element_type=jnp.float32)
    grad_bdown = jnp.sum(grad_rows, 0)
    grad_active = jnp.dot(grad_low, w_down.T, preferred_element_type=jnp.float32)
    gelu_pull = jax.vjp(jax.nn.gelu, hidden)[1]
    grad_hidden = gelu_pull(grad_active)[0].astype(jnp.bfloat16)
    grad_bup = jnp.sum(grad_hidden.astype(jnp.float32), 0)
    grad_wup = jnp.dot(normed_two.T, grad_hidden, preferred_element_type=jnp.float32)
    grad_normed_two = input_total(jnp.dot(grad_hidden, w_up.T, preferred_element_type=jnp.float32))
    grad_norm, grad_gain_two, grad_shift_two = norm_backward(
        grad_normed_two, second_normal, second_inverse, gains[1]
    )
    grad_middle = grad_rows + grad_norm
    grad_bout = jnp.sum(grad_middle, 0)
    grad_mid_low = grad_middle.astype(jnp.bfloat16)
    grad_wout = jnp.dot(mixture.T, grad_mid_low, preferred_element_type=jnp.float32)
    grad_mixture = jnp.dot(grad_mid_low, w_out.T, preferred_element_type=jnp.float32).astype(
        jnp.bfloat16
    )
    grad_parts = mixer_backward(
        block_kind, retained, grad_mixture.reshape(layout[:-1] + (columns,))
    )
    grad_flat = [grad.reshape(-1, columns) for grad in grad_parts]
    grad_project = jnp.stack(grad_flat, 1)
    grad_bqv = jnp.stack(
        [jnp.sum(grad_flat[0].astype(jnp.float32), 0), jnp.sum(grad_flat[2].astype(jnp.float32), 0)]
    )
    grad_wqkv = jnp.einsum("rd,rcj->dcj", normed, grad_project, preferred_element_type=jnp.float32)
    grad_normed = input_total(
        jnp.einsum("rcj,dcj->rd", grad_project, w_qkv, preferred_element_type=jnp.float32)
    )
    grad_input, grad_gain_one, grad_shift_one = norm_backward(
        grad_normed, first_normal, first_inverse, gains[0]
    )
    gradients = (
        jnp.stack([grad_gain_one, grad_gain_two]),
        jnp.stack([grad_shift_one, grad_shift_two]),
        grad_wqkv,
        grad_bqv,
        grad_wout,
        grad_bout,
        grad_wup,
        grad_bup,
        grad_wdown,
        grad_bdown,
    )
    return (grad_middle + grad_input, gradients)


def on_device_sums(
    tokens,
    token_mask,
    mask_embed,
    norm_gains,
    norm_shifts,
    w_qkv,
    b_qv,
    w_out,
    b_out,
    w_up,
    b_up,
    w_down,
    b_down,
    cotangent,
):
    layout = tokens.shape
    width = layout[-1]
    masked = (token_mask == 1).reshape(-1, 1)
    initial = jnp.where(masked, mask_embed[None, :], tokens.reshape(-1, width).astype(jnp.float32))
    upstream = cotangent.reshape(-1, width).astype(jnp.float32)

    def weights_of(block_kind):
        return (
            norm_gains[block_kind],
            norm_shifts[block_kind],
            w_qkv[block_kind],
            b_qv[block_kind],
            w_out[block_kind],
            b_out[block_kind],
            w_up[block_kind],
            b_up[block_kind],
            w_down[block_kind],
            b_down[block_kind],
        )

    middle, active, unused_first = block_forward(0, initial, layout, weights_of(0))
    second = block_output(middle, active, w_down[0], b_down[0])
    middle, active, unused_second = block_forward(1, second, layout, weights_of(1))
    output_rows = block_output(middle, active, w_down[1], b_down[1])
    grad_second, grads_later = block_backward(1, second, layout, weights_of(1), upstream)
    grad_initial, grads_earlier = block_backward(0, initial, layout, weights_of(0), grad_second)
    stacked = [
        jnp.stack([first_grad, later_grad])
        for first_grad, later_grad in zip(grads_earlier, grads_later)
    ]
    grad_embed = jnp.sum(jnp.where(masked, grad_initial, 0.0), 0)
    output_low = output_rows.astype(jnp.bfloat16)
    grad_low = jnp.where(masked, 0.0, grad_initial).astype(jnp.bfloat16)
    shares = (
        lax.psum_scatter(stacked[2], ("clip", "tube"), scatter_dimension=1, tiled=True),
        lax.psum_scatter(stacked[4], ("clip", "tube"), scatter_dimension=2, tiled=True),
        lax.psum_scatter(stacked[6], ("clip", "tube"), scatter_dimension=1, tiled=True),
        lax.psum_scatter(stacked[8], ("clip", "tube"), scatter_dimension=2, tiled=True),
    )
    whole = (
        lax.all_gather(shares[0].astype(jnp.bfloat16), ("clip", "tube"), axis=1, tiled=True).astype(
            jnp.float32
        ),
        lax.all_gather(shares[1].astype(jnp.bfloat16), ("clip", "tube"), axis=2, tiled=True).astype(
            jnp.float32
        ),
        lax.all_gather(shares[2].astype(jnp.bfloat16), ("clip", "tube"), axis=1, tiled=True).astype(
            jnp.float32
        ),
        lax.all_gather(shares[3].astype(jnp.bfloat16), ("clip", "tube"), axis=2, tiled=True).astype(
            jnp.float32
        ),
    )
    column_part = (
        grad_embed,
        stacked[0],
        stacked[1],
        stacked[5],
        stacked[9],
        stacked[3],
        stacked[7],
    )
    small = lax.psum(
        (
            column_part[0],
            column_part[1],
            column_part[2],
            column_part[3],
            column_part[4],
            column_part[5],
            column_part[6],
        ),
        ("clip", "tube"),
    )
    embed_grad, gain_grad, shift_grad, bout_grad, bdown_grad = (
        small[0],
        small[1],
        small[2],
        small[3],
        small[4],
    )
    bqv_grad, bup_grad = (small[5], small[6])
    return (
        output_low.reshape(layout),
        grad_low.reshape(layout),
        embed_grad,
        gain_grad,
        shift_grad,
        whole[0],
        bqv_grad,
        whole[1],
        bout_grad,
        whole[2],
        bup_grad,
        whole[3],
        bdown_grad,
    )


DOWN, UP, ATTN = range(3)
SEND, PASS, FIRST_INPUT, SECOND_INPUT, SPREAD, ATTEND, MIDDLE, EXPAND, CONTRACT = range(9)
FORWARD_ORDER = (
    (SEND, 0), (PASS, 0, 0), (SEND, 1), (FIRST_INPUT,), (PASS, 0, 1), (PASS, 1, 0), (SEND, 2), (PASS, 1, 1),
    (PASS, 0, 2), (PASS, 0, 3), (PASS, 1, 2), (PASS, 2, 0), (SEND, 3), (PASS, 1, 3), (ATTEND, 0, 0), (ATTEND, 0, 1),
    (ATTEND, 0, 2), (PASS, 2, 1), (ATTEND, 0, 3), (MIDDLE, 0), (PASS, 3, 0), (SEND, 4), (PASS, 2, 2), (PASS, 3, 1),
    (PASS, 2, 3), (EXPAND, 0, 0), (PASS, 4, 0), (SEND, 5), (EXPAND, 0, 1), (EXPAND, 0, 2), (EXPAND, 0, 3),
    (PASS, 3, 2), (PASS, 4, 1), (PASS, 5, 0), (SEND, 6), (PASS, 3, 3), (CONTRACT, 0, 0), (CONTRACT, 0, 1),
    (CONTRACT, 0, 2), (CONTRACT, 0, 3), (SPREAD,), (PASS, 5, 1), (PASS, 4, 2), (PASS, 4, 3), (PASS, 6, 0),
    (SECOND_INPUT,), (ATTEND, 1, 0), (PASS, 6, 1), (PASS, 5, 2), (ATTEND, 1, 1), (ATTEND, 1, 2), (PASS, 5, 3),
    (ATTEND, 1, 3), (MIDDLE, 1), (EXPAND, 1, 0), (PASS, 6, 2), (EXPAND, 1, 1), (EXPAND, 1, 2), (EXPAND, 1, 3),
    (PASS, 6, 3),
)
MLP_BACK, MLP_NORM, ATTN_BACK, ATTN_NORM, UPSTREAM, RESULT_LINE, OWN_LINE, FAR_START, FAR_LINE, SMALL = range(10)
ADD_CORE, ADD_FIRST, ADD_SECOND, PASS_HEADS, ADD_HEADS, SHARE_FIRST, SHARE_CORE, ARRIVED, MLP_START, SEND_RESULT = range(10, 20)
BACKWARD_ORDER = (
    (MLP_START,), (MLP_BACK, 1, 0), (ADD_CORE, 1, DOWN, 0), (MLP_BACK, 1, 1), (ADD_CORE, 1, UP, 0), (MLP_BACK, 1, 2),
    (ADD_CORE, 1, UP, 1), (ADD_CORE, 1, DOWN, 1), (MLP_BACK, 1, 3), (SEND_RESULT,), (ADD_CORE, 1, DOWN, 2),
    (ADD_CORE, 1, UP, 2), (MLP_NORM, 1), (ADD_CORE, 1, DOWN, 3), (ATTN_BACK, 1, 0), (ADD_CORE, 1, UP, 3),
    (ATTN_BACK, 1, 1), (ADD_CORE, 1, ATTN, 0), (ATTN_BACK, 1, 2), (ADD_FIRST, 1, UP), (ADD_CORE, 1, ATTN, 1),
    (ATTN_BACK, 1, 3), (ATTN_NORM, 1), (ADD_CORE, 1, ATTN, 3), (ADD_SECOND, 1, UP), (ADD_CORE, 1, ATTN, 2),
    (RESULT_LINE, 0), (ADD_FIRST, 1, DOWN), (UPSTREAM,), (ADD_FIRST, 1, ATTN), (MLP_BACK, 0, 0), (MLP_BACK, 0, 1),
    (ADD_SECOND, 1, DOWN), (ADD_CORE, 0, DOWN, 0), (ADD_CORE, 0, UP, 0), (MLP_BACK, 0, 2), (ADD_CORE, 0, UP, 1),
    (PASS_HEADS, 1, UP, 1), (ADD_CORE, 0, DOWN, 1), (MLP_BACK, 0, 3), (ADD_CORE, 0, UP, 2), (MLP_NORM, 0),
    (PASS_HEADS, 1, DOWN, 1), (ADD_SECOND, 1, ATTN), (RESULT_LINE, 1), (ATTN_BACK, 0, 0), (ADD_CORE, 0, UP, 3),
    (ADD_CORE, 0, DOWN, 2), (ATTN_BACK, 0, 1), (ADD_CORE, 0, ATTN, 0), (ATTN_BACK, 0, 2), (ADD_CORE, 0, DOWN, 3),
    (ADD_CORE, 0, ATTN, 1), (PASS_HEADS, 1, ATTN, 1), (PASS_HEADS, 1, DOWN, 2), (ATTN_BACK, 0, 3), (ATTN_NORM, 0),
    (PASS_HEADS, 1, ATTN, 2), (ADD_FIRST, 0, UP), (ADD_FIRST, 0, DOWN), (ADD_CORE, 0, ATTN, 2),
    (ADD_CORE, 0, ATTN, 3), (FAR_START,), (OWN_LINE, 0), (PASS_HEADS, 1, UP, 2), (SMALL, 0), (ADD_SECOND, 0, UP),
    (RESULT_LINE, 2), (FAR_LINE, 0), (ADD_SECOND, 0, DOWN), (ADD_FIRST, 0, ATTN), (PASS_HEADS, 0, UP, 1),
    (ADD_HEADS, 1, UP), (ADD_HEADS, 1, ATTN), (ADD_SECOND, 0, ATTN), (OWN_LINE, 1), (SMALL, 1), (SHARE_FIRST, 1, UP),
    (SHARE_FIRST, 1, ATTN), (ADD_HEADS, 1, DOWN), (PASS_HEADS, 0, DOWN, 1), (PASS_HEADS, 0, UP, 2),
    (PASS_HEADS, 0, ATTN, 1), (PASS_HEADS, 0, DOWN, 2), (SHARE_FIRST, 1, DOWN), (ADD_HEADS, 0, UP), (SMALL, 2),
    (ADD_HEADS, 0, DOWN), (SHARE_FIRST, 0, UP), (PASS_HEADS, 0, ATTN, 2), (FAR_LINE, 1), (SHARE_CORE, 1, DOWN),
    (SHARE_FIRST, 0, DOWN), (SHARE_CORE, 1, UP), (ADD_HEADS, 0, ATTN), (ARRIVED, 1, DOWN), (SHARE_CORE, 1, ATTN),
    (SHARE_CORE, 0, UP), (SHARE_CORE, 0, DOWN), (SHARE_FIRST, 0, ATTN), (OWN_LINE, 2), (ARRIVED, 1, ATTN),
    (ARRIVED, 0, DOWN), (ARRIVED, 0, UP), (FAR_LINE, 2), (SMALL, 3), (ARRIVED, 1, UP), (SHARE_CORE, 0, ATTN),
    (SMALL, 4), (ARRIVED, 0, ATTN),
)

GELU_A = 0.7978845608028654
GELU_B = 0.044715


def dot(left, right, dims):
    return lax.dot_general(left, right, (dims, ((), ())), preferred_element_type=F32)


NN, NT, TN = ((1,), (0,)), ((1,), (1,)), ((0,), (0,))


def standardize(values):
    centre = values - jnp.mean(values, -1, keepdims=True)
    inverse = lax.rsqrt(jnp.mean(centre * centre, -1, keepdims=True) + EPS)
    return centre * inverse, inverse


def head_masks(columns, scale):
    lane = lax.broadcasted_iota(jnp.int32, (1, columns), 1)
    return [
        jnp.where((lane >= j * HD) & (lane < (j + 1) * HD), scale, 0.0).astype(LOW)
        for j in range(columns // HD)
    ]


def gelu_pair(hidden):
    square = hidden * hidden
    tanh = jnp.tanh(GELU_A * hidden * (1.0 + GELU_B * square))
    half = 0.5 * (1.0 + tanh)
    slope = half + hidden * (0.5 * GELU_A) * (1.0 - tanh * tanh) * (1.0 + 3.0 * GELU_B * square)
    return hidden * half, slope


class Sizes:
    def __init__(self, rows, width, shards, columns, units, length):
        self.rows, self.width, self.shards = rows, width, shards
        self.columns, self.units, self.length = columns, units, length
        self.sequences = rows // length
        self.heads = columns // HD
        self.out_row = 3 * columns
        self.up_row = 4 * columns
        self.down_row = 4 * columns + width
        self.block_rows = 4 * columns + width + units


def norm_rows(sz, x_ref, gain, shift, n_ref, chunk=128):
    @pl.loop(0, sz.rows, step=chunk)
    def _(start):
        at = pl.ds(pl.multiple_of(start, chunk), chunk)
        normal, _ = standardize(x_ref[at, :].astype(F32))
        n_ref[at, :] = (normal * gain + shift).astype(LOW)


def forward_attention(sz, shard, w_ref, b_query, b_value, n_ref, t_ref, p_ref, m_ref):
    cols, length = sz.columns, sz.length
    normed = n_ref[...]
    q_ref, k_ref, v_ref, o_ref = (t_ref.at[shard, i] for i in range(4))
    q_ref[...] = (dot(normed, w_ref[shard, 0:cols, :], NT) + b_query).astype(LOW)
    k_ref[...] = dot(normed, w_ref[shard, cols : 2 * cols, :], NT).astype(LOW)
    v_ref[...] = (dot(normed, w_ref[shard, 2 * cols : 3 * cols, :], NT) + b_value).astype(LOW)
    scaled = head_masks(cols, HD**-0.5)
    masks = head_masks(cols, 1.0)
    for seq in range(sz.sequences):
        at = slice(seq * length, (seq + 1) * length)
        queries, keys, values = q_ref[at, :], k_ref[at, :], v_ref[at, :]
        mixture = jnp.zeros((length, cols), F32)
        for head in range(sz.heads):
            scores = dot(queries * scaled[head], keys, NT)
            exponent = jnp.exp(scores - jnp.max(scores, -1, keepdims=True))
            weights = (exponent / jnp.sum(exponent, -1, keepdims=True)).astype(LOW)
            p_ref[shard, seq * sz.heads + head] = weights
            mixture += dot(weights, values * masks[head], NN)
        o_ref[at, :] = mixture.astype(LOW)
    m_ref[...] += dot(o_ref[...], w_ref[shard, sz.out_row : sz.out_row + cols, :], NN)


def forward_up(sz, shard, w_ref, b_up, n2_ref, as_ref):
    hidden = dot(n2_ref[...], w_ref[shard, sz.up_row : sz.up_row + sz.width, :], NN) + b_up
    active, slope = gelu_pair(hidden)
    as_ref[shard, 0] = active.astype(LOW)
    as_ref[shard, 1] = slope.astype(LOW)


def forward_down(sz, shard, w_ref, as_ref, y_ref):
    y_ref[...] += dot(as_ref[shard, 0], w_ref[shard, sz.down_row : sz.down_row + sz.units, :], NN)


def backward_mlp(sz, w_ref, as_ref, low_ref, n2_ref, du_ref, dn_ref, down_ref, up_ref, sum_row):
    low = low_ref[...]
    grad_active = dot(low, w_ref[sz.width : sz.width + sz.units, :], NT)
    du_ref[...] = (grad_active * as_ref[1].astype(F32)).astype(LOW)
    sum_row[...] = jnp.sum(du_ref[...].astype(F32), 0, keepdims=True)
    if down_ref is not None:
        down_ref[...] = dot(as_ref[0], low, TN).astype(LOW)
    up_ref[...] = dot(n2_ref[...], du_ref[...], TN).astype(LOW)
    dn_ref[...] += dot(du_ref[...], w_ref[0 : sz.width, :], NT)


def norm_back_rows(sz, x_ref, gain, dn_ref, g_ref, out_ref, gain_row, shift_row, sum_row, low_ref, chunk=128):
    for row in (gain_row, shift_row, sum_row):
        if row is not None:
            row[...] = jnp.zeros_like(row)

    @pl.loop(0, sz.rows, step=chunk)
    def _(start):
        at = pl.ds(pl.multiple_of(start, chunk), chunk)
        normal, inverse = standardize(x_ref[at, :])
        dn = dn_ref[at, :]
        dy = dn * gain
        part = inverse * (
            dy - jnp.mean(dy, -1, keepdims=True) - normal * jnp.mean(dy * normal, -1, keepdims=True)
        )
        total = g_ref[at, :].astype(F32) + part
        out_ref[at, :] = total
        if low_ref is not None:
            low_ref[at, :] = total.astype(LOW)
        gain_row[...] += jnp.sum(dn * normal, 0, keepdims=True)
        shift_row[...] += jnp.sum(dn, 0, keepdims=True)
        if sum_row is not None:
            sum_row[...] += jnp.sum(total, 0, keepdims=True)


def backward_attention(sz, w_ref, t_ref, p_ref, dml_ref, n_ref, do_ref, dq_ref, dk_ref, dv_ref, dn_ref, g_ref, query_row, value_row):
    cols, length = sz.columns, sz.length
    low = dml_ref[...]
    q_ref, k_ref, v_ref, o_ref = (t_ref.at[i] for i in range(4))
    w_out = w_ref[sz.out_row : sz.out_row + cols, :]
    do_ref[...] = dot(low, w_out, NT).astype(LOW)
    g_ref[sz.out_row : sz.out_row + cols, :] = dot(o_ref[...], low, TN).astype(LOW)
    scaled = head_masks(cols, HD**-0.5)
    masks = head_masks(cols, 1.0)
    for seq in range(sz.sequences):
        at = slice(seq * length, (seq + 1) * length)
        queries, keys, values = q_ref[at, :], k_ref[at, :], v_ref[at, :]
        grad_o = do_ref[at, :]
        dq = jnp.zeros((length, cols), F32)
        dk = jnp.zeros((length, cols), F32)
        dv = jnp.zeros((length, cols), F32)
        for head in range(sz.heads):
            weights = p_ref[seq * sz.heads + head]
            grad_head = grad_o * masks[head]
            dp = dot(grad_head, values, NT)
            dv += dot(weights, grad_head, TN)
            wide = weights.astype(F32)
            ds = (wide * (dp - jnp.sum(wide * dp, -1, keepdims=True))).astype(LOW)
            dq += dot(ds, keys * scaled[head], NN)
            dk += dot(ds, queries * scaled[head], TN)
        dq_ref[at, :] = dq.astype(LOW)
        dk_ref[at, :] = dk.astype(LOW)
        dv_ref[at, :] = dv.astype(LOW)
    normed = n_ref[...]
    query_row[...] = jnp.sum(dq_ref[...].astype(F32), 0, keepdims=True)
    value_row[...] = jnp.sum(dv_ref[...].astype(F32), 0, keepdims=True)
    for i, part in enumerate((dq_ref, dk_ref, dv_ref)):
        g_ref[i * cols : (i + 1) * cols, :] = dot(part[...], normed, TN).astype(LOW)
        dn_ref[...] += dot(part[...], w_ref[i * cols : (i + 1) * cols, :], NN)


def saved_shapes(sz):
    s, r, c = sz.shards, sz.rows, sz.columns
    return [
        ((r, sz.width), LOW),
        ((s, 4, r, c), LOW),
        ((s, sz.sequences * sz.heads, sz.length, sz.length), LOW),
        ((r, sz.width), F32),
        ((r, sz.width), LOW),
        ((s, 2, r, sz.units), LOW),
    ]


def structs(shapes):
    return [jax.ShapeDtypeStruct(s, d) for s, d in shapes]


def vmems(shapes):
    return [pltpu.VMEM(s, d) for s, d in shapes]


class Place:
    def __init__(self, heads, zs=None):
        self.clip, self.y, self.z = (lax.axis_index(n) for n in ("clip", "tube", "head"))
        self.heads = heads
        self.core, self.x = lax.rem(self.clip, 2), lax.div(self.clip, 2)
        c, x, y = self.core, self.x, self.y
        self.first = (c + 2 * (x + (1 - c) * (1 - 2 * x)), y + c * (1 - 2 * y), self.z)
        self.second = (c + 2 * (x + c * (1 - 2 * x)), y + (1 - c) * (1 - 2 * y), self.z)
        self.other = (1 - c + 2 * x, y, self.z)
        self.i = (1 - c) * x + c * y
        self.j = (1 - c) * y + c * x
        self.along_x = (c + 2 * (1 - x), y, self.z)

    def head(self, step):
        return (self.clip, self.y, lax.rem(self.z + step + self.heads, self.heads))

    def across(self, step):
        return (self.clip, 1 - self.y, lax.rem(self.z + step + self.heads, self.heads))

    def clip_peers(self):
        return [self.head(d) for d in range(1, self.heads)] + [self.across(d) for d in range(self.heads)]

    def all_peers(self):
        return [self.along_x, self.other] + self.clip_peers()


def greet(peers):
    barrier = pltpu.get_barrier_semaphore()
    for peer in peers:
        pl.semaphore_signal(barrier, inc=1, device_id=peer, device_id_type=MESH)
    pl.semaphore_wait(barrier, len(peers))


class Moves:
    def __init__(self, send_sem, recv_sem):
        self.send_sem, self.recv_sem, self.count, self.sent = send_sem, recv_sem, 0, {}

    def reserve(self):
        self.count += 1
        return self.count - 1

    def one(self, n, src, dst, target):
        return pltpu.make_async_remote_copy(
            src, dst, self.send_sem.at[n], self.recv_sem.at[n], device_id=target, device_id_type=MESH
        )

    def phase(self, copies):
        made = []
        for src, dst, landing, target in copies:
            n = self.count
            self.count += 1
            made.append((src, dst, landing, target, n))
        return made

    def start(self, made):
        for src, dst, _, target, n in made:
            copy = pltpu.make_async_remote_copy(
                src, dst, self.send_sem.at[n], self.recv_sem.at[n], device_id=target, device_id_type=MESH
            )
            copy.start()
            self.sent[n] = copy

    def arrive(self, made):
        for src, _, landing, target, n in made:
            pltpu.make_async_remote_copy(
                src, landing, self.send_sem.at[n], self.recv_sem.at[n], device_id=target, device_id_type=MESH
            ).wait_recv()

    def left(self, made):
        for *_, n in made:
            if n in self.sent:
                self.sent.pop(n).wait_send()

    def finish(self):
        for copy in self.sent.values():
            copy.wait_send()
        self.sent = {}


def piece_list(sz, blocks):
    out = []
    for b in range(blocks):
        for kind, start in ((ATTN, 0), (UP, sz.up_row), (DOWN, sz.down_row)):
            parts = 2 if (b, kind) == (0, ATTN) else 1
            size = sz.width // parts
            out += [(b, kind, start + i * size, size) for i in range(parts)]
    return out


def gather_phases(place, moves, full, offset, rows):
    q = rows // 8
    c, i, j, z, heads = place.core, place.i, place.j, place.z, place.heads

    def at(ref, head, start, size):
        return ref.at[head, pl.ds(pl.multiple_of(offset + start * q, q), size * q), :]

    def other(d):
        return lax.rem(z + d, heads)

    mine = 4 * c + 2 * j + i
    near = 4 * c + 2 * j + (1 - i)
    pair = 4 * c + 2 * j
    pair_far = 4 * c + 2 * (1 - j)
    steps = range(1, heads)
    return [
        moves.phase(
            [(at(full, z, mine, 1), at(full, z, mine, 1), at(full, lax.rem(z + heads - d, heads), mine, 1), place.head(d)) for d in steps]
        ),
        moves.phase(
            [(at(full, other(d), mine, 1), at(full, other(d), mine, 1), at(full, other(d), near, 1), place.first) for d in steps]
        ),
        moves.phase(
            [(at(full, other(d), pair, 2), at(full, other(d), pair, 2), at(full, other(d), pair_far, 2), place.second) for d in steps]
        ),
        moves.phase(
            [(at(full, other(d), 4 * c, 4), at(full, other(d), 4 * c, 4), at(full, other(d), 4 * (1 - c), 4), place.other) for d in steps]
        ),
    ]


class Saves:
    def __init__(self, sem):
        self.sem, self.count = sem, 0

    def start(self, src, dst):
        copy = pltpu.make_async_copy(src, dst, self.sem.at[self.count])
        self.count += 1
        copy.start()
        return copy


def forward_kernel(sz, blocks, frame_share, tube_share, *refs):
    (w_qkv, w_out, w_up, w_down, tokens, marks, b_qv, b_up, embed, gains, shifts, b_out, b_down), refs = refs[:13], refs[13:]
    fulls, refs = refs[:blocks], refs[blocks:]
    saved, refs = [refs[7 * b : 7 * b + 7] for b in range(blocks)], refs[7 * blocks :]
    (frame_marks,), refs = refs[:1], refs[1:]
    w = refs[:blocks]
    (
        frames, bqv, bup, x, n, t, p, m, n2, act, y, y_low, second, send_sem, recv_sem, local_sem, save_sem,
    ) = refs[blocks:]
    heads, block_rows, length = sz.shards, sz.block_rows, sz.length
    place = Place(heads)
    moves = Moves(send_sem, recv_sem)
    local, saves = Saves(local_sem), Saves(save_sem)

    def settle(copies):
        for copy in copies:
            copy.wait()

    yy, z = place.y, place.z
    tubes = tokens.shape[1]
    greet(place.all_peers())

    owned = pl.ds((2 * z + yy) * frame_share, frame_share)
    asked = pl.ds((2 * z + 1 - yy) * frame_share, frame_share)
    here, there = pl.ds(yy * tubes, tubes), pl.ds((1 - yy) * tubes, tubes)
    exchange = moves.phase(
        [
            (src.at[asked], dst.at[:, here], dst.at[:, there], place.across(0))
            for src, dst in ((tokens, frames), (marks, frame_marks))
        ]
        + [
            (src, dst.at[z], dst.at[lax.rem(z + heads - d, heads)], place.head(d))
            for src, dst in ((b_qv, bqv), (b_up, bup))
            for d in range(1, heads)
        ]
    )
    spread = moves.phase(
        [
            (
                y_low.at[:, pl.ds((heads * ty + tz) * tube_share, tube_share)],
                second.at[pl.ds((2 * z + yy) * frame_share, frame_share)],
                second.at[pl.ds((2 * fz + ty) * frame_share, frame_share)],
                target,
            )
            for ty, tz, fz, target in [
                (yy, lax.rem(z + d, heads), lax.rem(z + heads - d, heads), place.head(d)) for d in range(1, heads)
            ]
            + [
                (1 - yy, lax.rem(z + d, heads), lax.rem(z + heads - d, heads), place.across(d)) for d in range(heads)
            ]
        ]
    )
    pieces = piece_list(sz, blocks)
    work = [gather_phases(place, moves, w[b], start, size) for b, _, start, size in pieces]
    moves.start(exchange)
    own_parts = {}
    for b in range(blocks):
        mine = w[b].at[z]
        own_parts[b, ATTN] = [
            local.start(w_qkv.at[b], mine.at[pl.ds(0, sz.out_row)]),
            local.start(w_out.at[b], mine.at[pl.ds(sz.out_row, sz.columns)]),
        ]
        own_parts[b, UP] = [local.start(w_up.at[b], mine.at[pl.ds(sz.up_row, sz.width)])]
        own_parts[b, DOWN] = [local.start(w_down.at[b], mine.at[pl.ds(sz.down_row, sz.units)])]

    def begin_piece(piece):
        b, kind, _, _ = pieces[piece]
        settle(own_parts.pop((b, kind), ()))
        moves.start(work[piece][0])
    owns = [
        local.start(tokens.at[owned], frames.at[:, here]),
        local.start(marks.at[owned], frame_marks.at[:, here]),
        local.start(b_qv, bqv.at[z]),
        local.start(b_up, bup.at[z]),
    ]

    def save(b, index, src, part=None):
        dst = saved[b][index]
        return saves.start(src, dst if part is None else dst.at[part])

    def begin_block(b):
        norm_rows(sz, x, gains[b, 0:1, :], shifts[b, 0:1, :], n)
        m[...] = x[...] + b_out[b : b + 1, :]
        return [save(b, 0, x), save(b, 1, n)]

    def attention(b, s):
        forward_attention(sz, s, w[b], bqv[s, b, 0:1, :], bqv[s, b, 1:2, :], n, t, p, m)
        return [save(b, 2, t.at[s], s), save(b, 3, p.at[s], s)]

    def middle(b):
        norm_rows(sz, m, gains[b, 1:2, :], shifts[b, 1:2, :], n2)
        y[...] = m[...] + b_down[b : b + 1, :]
        return [save(b, 4, m), save(b, 5, n2)]

    def up(b, s):
        forward_up(sz, s, w[b], bup[s, b : b + 1, :], n2, act)
        return [save(b, 6, act.at[s], s)]

    def down(b, s):
        forward_down(sz, s, w[b], act, y)

    def keep(piece):
        b, _, start, size = pieces[piece]
        at = pl.ds(start, size)
        return [saves.start(w[b].at[:, at], fulls[b].at[:, at])]

    kept, early = [], []
    wide = [None] * blocks

    def first_input():
        settle(owns)
        moves.arrive(exchange)
        tok = frames[...].astype(F32).reshape(sz.rows, sz.width)
        mark = frame_marks[...].astype(F32).reshape(sz.rows, 128)[:, 0:1]
        x[...] = jnp.where(mark > 0.5, embed[...].reshape(1, sz.width), tok)
        early.extend(begin_block(0))

    def second_input():
        moves.arrive(spread)
        wide[1].wait()
        settle(early)
        for j in range(tube_share):
            x[j * length : (j + 1) * length, :] = second[:, j].astype(F32).reshape(length, sz.width)
        kept.extend(begin_block(1))

    def spread_first():
        y_low[...] = y[...].astype(LOW).reshape(y_low.shape)
        moves.start(spread)
        wide[1] = local.start(
            y_low.at[:, pl.ds((heads * yy + z) * tube_share, tube_share)],
            second.at[pl.ds((2 * z + yy) * frame_share, frame_share)],
        )

    def advance(piece, phase):
        moves.arrive(work[piece][phase])
        if phase < 3:
            moves.start(work[piece][phase + 1])
        else:
            kept.extend(keep(piece))

    steps = {(FIRST_INPUT,): first_input, (SPREAD,): spread_first, (SECOND_INPUT,): second_input}
    for piece in range(len(work)):
        steps[SEND, piece] = functools.partial(begin_piece, piece)
        for phase in range(4):
            steps[PASS, piece, phase] = functools.partial(advance, piece, phase)
    for b in range(blocks):
        held = kept if b else early
        run = lambda f, *args, held=held: held.extend(f(*args) or ())
        steps[MIDDLE, b] = functools.partial(run, middle, b)
        for s in range(heads):
            steps[ATTEND, b, s] = functools.partial(run, attention, b, s)
            steps[EXPAND, b, s] = functools.partial(run, up, b, s)
            steps[CONTRACT, b, s] = functools.partial(run, down, b, s)
    for step in FORWARD_ORDER:
        steps[step]()
    moves.finish()
    settle(kept)


def run_forward(sz, blocks, frame_share, tube_share, weights, tokens, marks, b_qv, b_up, embed, gains, shifts, b_out, b_down):
    heads, width, rows = sz.shards, sz.width, sz.rows
    tubes, patches = 2 * tokens.shape[1], tokens.shape[2]
    frames = tokens.shape[0]
    saved = [((rows, width), F32)] + saved_shapes(sz)
    whole_frames = (frame_share, tubes, patches)
    count = len(piece_list(sz, blocks)) * 4 * (heads - 1) + 2 + 2 * (heads - 1) + 2 * heads - 1
    hbm, vmem = pl.BlockSpec(memory_space=pl.ANY), pl.BlockSpec(memory_space=pltpu.VMEM)
    full = ((heads, sz.block_rows, width), LOW)
    mixed = (frames, tube_share, patches, width)
    out = pl.pallas_call(
        lambda *refs: forward_kernel(sz, blocks, frame_share, tube_share, *refs),
        name="forward_both",
        out_shape=structs([full] * blocks + saved * blocks + [(whole_frames + (128,), LOW)]),
        in_specs=[hbm] * 8 + [vmem] * 5,
        out_specs=[hbm] * (blocks + 7 * blocks) + [vmem],
        scratch_shapes=vmems(
            [full] * blocks
            + [
                (whole_frames + (width,), LOW),
                ((heads,) + b_qv.shape, F32),
                ((heads,) + b_up.shape, F32),
            ]
            + saved
            + [
                ((rows, width), F32),
                (whole_frames + (width,), LOW),
                (mixed, LOW),
            ]
        )
        + [
            pltpu.SemaphoreType.DMA((count,)),
            pltpu.SemaphoreType.DMA((count,)),
            pltpu.SemaphoreType.DMA((16,)),
            pltpu.SemaphoreType.DMA((64,)),
        ],
        compiler_params=pltpu.CompilerParams(
            collective_id=0, has_side_effects=True, vmem_limit_bytes=62 * 2**20
        ),
    )(*weights, tokens, marks, b_qv, b_up, embed, gains, shifts, b_out, b_down)
    fulls, out = out[:blocks], out[blocks:]
    saved = [out[7 * b : 7 * b + 7] for b in range(blocks)]
    return fulls, saved, out[-1]


class Line:
    def __init__(self, place, send_sem, recv_sem, region, own=None):
        self.place, self.send_sem, self.recv_sem, self.region = place, send_sem, recv_sem, region
        self.own = own
        self.steps = place.heads - 1

    def moves(self, step):
        z, last = self.place.z, self.place.heads - 1
        return [
            ((z >= step) & (z < last), z - step, 1, z > step, z - 1 - step, 2 * step),
            ((z <= last - step) & (z > 0), z + step, -1, z < last - step, z + 1 + step, 2 * step + 1),
        ]

    def copy(self, block, way, n):
        return pltpu.make_async_remote_copy(
            self.own if n < 2 and self.own is not None else self.region(block),
            self.region(block),
            self.send_sem.at[n],
            self.recv_sem.at[n],
            device_id=self.place.head(way),
            device_id_type=MESH,
        )

    def start(self, step):
        for sends, block, way, _, _, n in self.moves(step):
            pl.when(sends)(lambda block=block, way=way, n=n: self.copy(block, way, n).start())

    def arrive(self, step):
        for _, _, way, gets, block, n in self.moves(step):
            pl.when(gets)(lambda block=block, way=way, n=n: self.copy(block, way, n).wait_recv())

    def finish(self):
        for step in range(self.steps):
            for sends, block, way, _, _, n in self.moves(step):
                pl.when(sends)(lambda block=block, way=way, n=n: self.copy(block, way, n).wait_send())


class Reduction:
    def __init__(self, place, moves, grads, out, out_row, rows, bufs, final_buf, final_sem):
        q = rows // 8
        self.q, self.place, self.moves, self.grads = q, place, moves, grads
        self.core_buf, self.first_buf, self.second_buf, self.head_buf = bufs
        self.final_buf, self.final_sem = final_buf, final_sem
        c, i, j, z, heads = place.core, place.i, place.j, place.z, place.heads
        cut = lambda start, size: pl.ds(pl.multiple_of(start * q, q), size * q)
        row = lambda start, size: out.at[pl.ds(pl.multiple_of(out_row + start * q, q), size * q), :]
        self.kept, self.given = cut(4 * c, 4), cut(4 * (1 - c), 4)
        self.part, self.subpart = cut(2 * i, 2), cut(j, 1)
        shards = range(heads)
        self.core = moves.phase(
            [(grads.at[s % 2, self.given, :], self.core_buf.at[s], self.core_buf.at[s], place.other) for s in shards]
        )
        self.first = moves.phase(
            [(self.core_buf.at[s, cut(2 * (1 - i), 2), :], self.first_buf.at[s], self.first_buf.at[s], place.first) for s in shards]
        )
        self.second = moves.phase(
            [(self.first_buf.at[s, cut(1 - j, 1), :], self.second_buf.at[s], self.second_buf.at[s], place.second) for s in shards]
        )
        self.to_right = moves.reserve()
        self.to_left = moves.reserve()
        a, mine = 4 * c, 2 * i + j
        self.share_second = moves.phase([(final_buf, row(a + mine, 1), row(a + 2 * i + 1 - j, 1), place.second)])
        self.share_first = moves.phase([(row(a + 2 * i, 2), row(a + 2 * i, 2), row(a + 2 * (1 - i), 2), place.first)])
        self.share_core = moves.phase([(row(a, 4), row(a, 4), row(4 - a, 4), place.other)])
        self.keep = pltpu.make_async_copy(final_buf, row(a + mine, 1), final_sem)

    def give(self, s):
        self.moves.start([self.core[s]])

    def step_first(self, s):
        self.moves.arrive([self.core[s]])
        self.core_buf[s] = self.core_buf[s] + self.grads[s % 2, self.kept, :]
        self.moves.start([self.first[s]])

    def step_second(self, free_sem=None):
        for s in range(self.place.heads):
            self.moves.arrive([self.first[s]])
            self.first_buf[s] = self.first_buf[s] + self.core_buf[s, self.part, :]
            self.moves.start([self.second[s]])
        if free_sem is not None:
            self.moves.left(self.first)
            pl.semaphore_signal(free_sem, inc=1, device_id=self.place.other, device_id_type=MESH)

    def step_heads(self):
        for s in range(self.place.heads):
            self.moves.arrive([self.second[s]])
            self.second_buf[s] = self.second_buf[s] + self.first_buf[s, self.subpart, :]
        last = self.place.heads - 1
        pl.when(self.place.z == 0)(functools.partial(self.send_right, 0))
        pl.when(self.place.z == last)(functools.partial(self.send_left, last))

    def right_copy(self, z):
        return self.moves.one(
            self.to_right, self.second_buf.at[z + 1 :], self.head_buf.at[z + 2 :], self.place.head(1)
        )

    def left_copy(self, z):
        return self.moves.one(self.to_left, self.second_buf.at[:z], self.head_buf.at[:z], self.place.head(-1))

    def send_right(self, z):
        self.right_copy(z).start()

    def send_left(self, z):
        self.left_copy(z).start()

    def from_left(self, z):
        self.right_copy(z - 1).wait_recv()
        for s in range(z + 1, self.place.heads):
            self.second_buf[s] = self.second_buf[s] + self.head_buf[s + 1]
        if z < self.place.heads - 1:
            self.send_right(z)

    def from_right(self, z):
        self.left_copy(z + 1).wait_recv()
        for s in range(z):
            self.second_buf[s] = self.second_buf[s] + self.head_buf[s]
        if z > 0:
            self.send_left(z)

    def step_pass(self, hop):
        heads = self.place.heads
        pl.when(self.place.z == hop)(functools.partial(self.from_left, hop))
        pl.when(self.place.z == heads - 1 - hop)(functools.partial(self.from_right, heads - 1 - hop))

    def step_share(self):
        z, last = self.place.z, self.place.heads - 1
        self.step_pass(last)

        @pl.when(z == 0)
        def _():
            self.final_buf[...] = self.second_buf[0] + self.head_buf[0]

        @pl.when(z == last)
        def _():
            self.final_buf[...] = self.second_buf[last] + self.head_buf[last + 1]

        @pl.when((z > 0) & (z < last))
        def _():
            total = self.second_buf[z].astype(F32) + self.head_buf[z].astype(F32)
            self.final_buf[...] = (total + self.head_buf[z + 1].astype(F32)).astype(LOW)

        self.keep.start()
        self.moves.start(self.share_second)

    def finish(self):
        last = self.place.heads - 1
        for z in range(last + 1):
            if z < last:
                pl.when(self.place.z == z)(lambda z=z: self.right_copy(z).wait_send())
            if z > 0:
                pl.when(self.place.z == z)(lambda z=z: self.left_copy(z).wait_send())

    def step_share_first(self):
        self.keep.wait()
        self.moves.arrive(self.share_second)
        self.moves.start(self.share_first)

    def step_share_core(self):
        self.moves.arrive(self.share_first)
        self.moves.start(self.share_core)

    def end(self):
        self.moves.arrive(self.share_core)


SMALL_ROWS = 48
GAIN_ROW, SHIFT_ROW, BOUT_ROW, BDOWN_ROW, BUP_ROW, BQV_ROW = 1, 5, 9, 11, 16, 24


def backward_kernel(sz, blocks, frame_share, tube_share, *refs):
    fulls, refs = refs[:blocks], refs[blocks:]
    saved, refs = [refs[7 * b : 7 * b + 7] for b in range(blocks)], refs[7 * blocks :]
    (cotangent, marks, gains, b_down), refs = refs[:4], refs[4:]
    (out_result, out_tokens, out_grads, out_small), refs = refs[:4], refs[4:]
    (
        wm, act, wa, t, p, m, n2, n, x, low, dn, dm, du, do, dq, dk, dv, cot, dx_low, back, result,
        grads, core_buf, first_buf, second_buf, head_buf, final_buf, small, small_in, small_heads, small_last,
        send_sem, recv_sem, line_sem, load_sem, copy_sem, final_sem, free_sem,
    ) = refs
    heads, width, length = sz.shards, sz.width, sz.length
    place = Place(heads)
    moves = Moves(send_sem, recv_sem)
    loads = Saves(copy_sem)
    yy, z = place.y, place.z
    tubes = cotangent.shape[1]

    def step_loads(b, kind, s):
        slot = s % 2
        if kind == MLP_BACK:
            pairs = [(fulls[b].at[s, pl.ds(sz.up_row, 2 * width), :], wm.at[slot]), (saved[b][6].at[s], act.at[slot])]
            base = 0
        else:
            pairs = [
                (fulls[b].at[s, pl.ds(0, sz.up_row), :], wa.at[slot]),
                (saved[b][2].at[s], t.at[slot]),
                (saved[b][3].at[s], p.at[slot]),
            ]
            base = 4
        return [
            pltpu.make_async_copy(src, dst, load_sem.at[base + slot * len(pairs) + i]) for i, (src, dst) in enumerate(pairs)
        ]

    steps = [(b, kind, s) for b in (1, 0) for kind in (MLP_BACK, ATTN_BACK) for s in range(heads)]

    def fetch(i):
        if i < len(steps):
            for copy in step_loads(*steps[i]):
                copy.start()

    def ready(i):
        for copy in step_loads(*steps[i]):
            copy.wait()
        fetch(i + 1)

    first_load = loads.start(cotangent.at[:, pl.ds(z * tube_share, tube_share)], cot)
    fetch(0)
    norm_loads = {1: [loads.start(saved[1][4], m), loads.start(saved[1][5], n2)]}
    later_loads = {1: [loads.start(saved[1][1], n), loads.start(saved[1][0], x)]}
    small[...] = jnp.zeros_like(small)
    greet(place.all_peers())

    red = {}
    for b in (1, 0):
        for k in (DOWN, UP, ATTN):
            base = b * sz.block_rows + (sz.down_row, sz.up_row, 0)[k]
            red[b, k] = Reduction(
                place,
                moves,
                grads.at[k],
                out_grads,
                base,
                width,
                (core_buf.at[k], first_buf.at[b, k], second_buf.at[b, k], head_buf.at[b, k]),
                final_buf.at[b, k],
                final_sem.at[b * 3 + k],
            )
    tube_region = lambda block: out_result.at[:, pl.ds(block * tube_share, tube_share)]
    line = Line(place, line_sem.at[0], line_sem.at[1], tube_region, result)
    spread = moves.phase(
        [
            (
                dx_low.at[pl.ds((2 * tz + ty) * frame_share, frame_share)],
                back.at[:, pl.ds((heads * yy + z) * tube_share, tube_share)],
                back.at[:, pl.ds((heads * ty + fz) * tube_share, tube_share)],
                target,
            )
            for ty, tz, fz, target in [
                (yy, lax.rem(z + d, heads), lax.rem(z + heads - d, heads), place.head(d)) for d in range(1, heads)
            ]
            + [
                (1 - yy, lax.rem(z + d, heads), lax.rem(z + heads - d, heads), place.across(d)) for d in range(heads)
            ]
        ]
    )

    first_load.wait()
    frames = cot.shape[0]
    for j in range(tube_share):
        low[j * length : (j + 1) * length, :] = cot[:, j].reshape(length, width)
    own_result = []

    def send_result():
        for j in range(tube_share):
            at = slice(j * length, (j + 1) * length)
            result[:, j] = dm[at, :].astype(LOW).reshape(frames, length // frames, width)
        line.start(0)
        own_result.append(loads.start(result, tube_region(z)))

    def mlp_start():
        begin_mlp(1)
        grads[DOWN, 0] = dot(act[0, 0], low[...], TN).astype(LOW)
        red[1, DOWN].give(0)

    def row(r, columns=None):
        return small.at[r : r + 1, :] if columns is None else small.at[r : r + 1, 0:columns]

    def begin_mlp(b):
        row(BDOWN_ROW + b)[...] = jnp.sum(low[...].astype(F32), 0, keepdims=True)
        dn[...] = jnp.zeros_like(dn)
        for copy in norm_loads[b]:
            copy.wait()
        if b:
            dm[...] = m[...] + b_down[b : b + 1, :]
        ready((1 - b) * 2 * heads)

    def mlp(b, s):
        if s:
            ready((1 - b) * 2 * heads + s)
        elif b == 0:
            begin_mlp(b)
        for k in (DOWN, UP):
            if s >= 2:
                moves.left([red[b, k].core[s - 2]])
            elif b == 0:
                moves.left([red[1, k].core[s + heads - 2]])
        first = (b, s) == (1, 0)
        slot = s % 2
        backward_mlp(
            sz, wm.at[slot], act.at[slot], low, n2, du, dn, None if first else grads.at[DOWN, slot], grads.at[UP, slot],
            row(BUP_ROW + b * heads + s),
        )
        for k in (UP,) if first else (DOWN, UP):
            if s == 0 and b == 0:
                pl.semaphore_wait(free_sem.at[k], 1)
            red[b, k].give(s)
        if b:
            dm[...] += dot(act[slot, 0], wm[slot, width : width + sz.units, :], NN)

    def mlp_norm(b):
        norm_back_rows(
            sz, m, gains[b, 1:2, :], dn, low, dm, row(GAIN_ROW + 2 * b + 1), row(SHIFT_ROW + 2 * b + 1), row(BOUT_ROW + b), low
        )
        if b:
            norm_loads[0] = [loads.start(saved[0][4], m), loads.start(saved[0][5], n2)]

    def attention(b, s):
        if s == 0:
            dn[...] = jnp.zeros_like(dn)
            for copy in later_loads[b]:
                copy.wait()
        ready((1 - b) * 2 * heads + heads + s)
        if s >= 2:
            moves.left([red[b, ATTN].core[s - 2]])
        elif b == 0:
            moves.left([red[1, ATTN].core[s + heads - 2]])
        r = BQV_ROW + 2 * (b * heads + s)
        backward_attention(
            sz, wa.at[s % 2], t.at[s % 2], p.at[s % 2], low, n, do, dq, dk, dv, dn, grads.at[ATTN, s % 2],
            row(r, sz.columns), row(r + 1, sz.columns),
        )
        if s == 0 and b == 0:
            pl.semaphore_wait(free_sem.at[ATTN], 1)
        red[b, ATTN].give(s)

    own_spread = []

    def attention_norm(b):
        norm_back_rows(
            sz, x, gains[b, 0:1, :], dn, dm, dm, row(GAIN_ROW + 2 * b), row(SHIFT_ROW + 2 * b), None, None
        )
        if b:
            later_loads[0] = [loads.start(saved[0][1], n), loads.start(saved[0][0], x)]
            for j in range(tube_share):
                dx_low[:, j] = dm[j * length : (j + 1) * length, :].astype(LOW).reshape(frames, length // frames, width)
            moves.start(spread)
            own_spread.append(
                loads.start(
                    dx_low.at[pl.ds((2 * z + yy) * frame_share, frame_share)],
                    back.at[:, pl.ds((heads * yy + z) * tube_share, tube_share)],
                )
            )
            return
        mark = marks[...].astype(F32).reshape(sz.rows, 128)[:, 0:1] > 0.5
        grad = dm[...]
        row(0)[...] = jnp.sum(jnp.where(mark, grad, 0.0), 0, keepdims=True)
        back[...] = jnp.where(mark, 0.0, grad).astype(LOW).reshape(back.shape)
        moves.start(cross)
        own_copy = loads.start(back.at[:, here], own_frames(z))
        moves.start(small_steps[0])
        own_copy.wait()
        own_line.start(0)

    def second_upstream():
        moves.arrive(spread)
        for copy in own_spread:
            copy.wait()
        low[...] = back[...].reshape(sz.rows, width)

    here, there = pl.ds(yy * tubes, tubes), pl.ds((1 - yy) * tubes, tubes)
    own_frames = lambda block: out_tokens.at[pl.ds((2 * block + yy) * frame_share, frame_share)]
    far_frames = lambda block: out_tokens.at[pl.ds((2 * block + 1 - yy) * frame_share, frame_share)]
    cross = moves.phase([(back.at[:, there], own_frames(z), far_frames(z), place.across(0))])
    own_line = Line(place, line_sem.at[2], line_sem.at[3], own_frames)
    far_line = Line(place, line_sem.at[4], line_sem.at[5], far_frames)

    def start_far():
        moves.arrive(cross)
        far_line.start(0)

    half = SMALL_ROWS // 2
    part = pl.ds(pl.multiple_of(place.core * half, half), half)
    far_part = pl.ds(pl.multiple_of((1 - place.core) * half, half), half)
    small_steps = [
        moves.phase([(small, small_in.at[i], small_in.at[i], target)])
        for i, target in enumerate((place.other, place.first, place.second))
    ]
    small_z = moves.phase(
        [(small.at[part], small_heads.at[d - 1], small_heads.at[d - 1], place.head(d)) for d in range(1, heads)]
    )
    small_end = moves.phase([(small_last.at[part], small_last.at[part], small_last.at[far_part], place.other)])

    def add_small(i):
        moves.arrive(small_steps[i])
        moves.left(small_steps[i])
        small[...] += small_in[i]
        moves.start(small_steps[i + 1] if i + 1 < len(small_steps) else small_z)

    def add_small_heads():
        moves.arrive(small_z)
        total = small[part, :]
        for d in range(heads - 1):
            total += small_heads[d]
        small_last[part, :] = total
        moves.start(small_end)

    def end_small():
        moves.arrive(small_end)
        out_small[...] = small_last[...]

    def pass_on(way, step):
        way.arrive(step)
        if step + 1 < way.steps:
            way.start(step + 1)

    todo = {(UPSTREAM,): second_upstream, (MLP_START,): mlp_start, (SEND_RESULT,): send_result, (FAR_START,): start_far, (SMALL, 3): add_small_heads, (SMALL, 4): end_small}
    for i in range(3):
        todo[SMALL, i] = functools.partial(add_small, i)
    for name, way in ((RESULT_LINE, line), (OWN_LINE, own_line), (FAR_LINE, far_line)):
        for step in range(way.steps):
            todo[name, step] = functools.partial(pass_on, way, step)
    for b in range(blocks):
        todo[MLP_NORM, b] = functools.partial(mlp_norm, b)
        todo[ATTN_NORM, b] = functools.partial(attention_norm, b)
        for s in range(heads):
            todo[MLP_BACK, b, s] = functools.partial(mlp, b, s)
            todo[ATTN_BACK, b, s] = functools.partial(attention, b, s)
        for k in (DOWN, UP, ATTN):
            each = red[b, k]
            for s in range(heads):
                todo[ADD_CORE, b, k, s] = functools.partial(each.step_first, s)
            todo[ADD_FIRST, b, k] = functools.partial(each.step_second, free_sem.at[k] if b else None)
            todo[ADD_SECOND, b, k] = each.step_heads
            for hop in range(1, heads - 1):
                todo[PASS_HEADS, b, k, hop] = functools.partial(each.step_pass, hop)
            todo[ADD_HEADS, b, k] = each.step_share
            todo[SHARE_FIRST, b, k] = each.step_share_first
            todo[SHARE_CORE, b, k] = each.step_share_core
            todo[ARRIVED, b, k] = each.end
    for step in BACKWARD_ORDER:
        todo[step]()
    for copy in own_result:
        copy.wait()
    for each in (line, own_line, far_line, *red.values()):
        each.finish()
    moves.finish()


def run_backward(sz, blocks, frame_share, tube_share, fulls, saved, cotangent, marks, gains, b_down):
    heads, width, rows, cols = sz.shards, sz.width, sz.rows, sz.columns
    frames, tubes, patches = cotangent.shape[:3]
    hbm, vmem = pl.BlockSpec(memory_space=pl.ANY), pl.BlockSpec(memory_space=pltpu.VMEM)
    q = width // 8
    local = (frame_share, 2 * tubes, patches, width)
    mixed = (frames, tube_share, patches, width)
    kinds = 3 * blocks
    count = kinds * (3 * heads + 3 + 2) + 2 * heads - 1 + 1 + 4 + heads - 1
    flat = [array for per in saved for array in per]
    return pl.pallas_call(
        lambda *refs: backward_kernel(sz, blocks, frame_share, tube_share, *refs),
        name="backward_both",
        out_shape=structs(
            [
                (cotangent.shape, LOW),
                (cotangent.shape, LOW),
                ((blocks * sz.block_rows, width), LOW),
                ((SMALL_ROWS, width), F32),
            ]
        ),
        in_specs=[hbm] * (blocks + len(flat) + 1) + [vmem] * 3,
        out_specs=[hbm] * 3 + [vmem],
        scratch_shapes=vmems(
            [
                ((2, 2 * width, width), LOW),
                ((2, 2, rows, sz.units), LOW),
                ((2, sz.up_row, width), LOW),
                ((2, 4, rows, cols), LOW),
                ((2, sz.sequences * sz.heads, sz.length, sz.length), LOW),
                ((rows, width), F32),
                ((rows, width), LOW),
                ((rows, width), LOW),
                ((rows, width), F32),
                ((rows, width), LOW),
                ((rows, width), F32),
                ((rows, width), F32),
                ((rows, sz.units), LOW),
                ((rows, cols), LOW),
                ((rows, cols), LOW),
                ((rows, cols), LOW),
                ((rows, cols), LOW),
                (mixed, LOW),
                (mixed, LOW),
                (local, LOW),
                (mixed, LOW),
                ((3, 2, width, width), LOW),
                ((3, heads, 4 * q, width), LOW),
                ((blocks, 3, heads, 2 * q, width), LOW),
                ((blocks, 3, heads, q, width), LOW),
                ((blocks, 3, heads + 1, q, width), LOW),
                ((blocks, 3, q, width), LOW),
                ((SMALL_ROWS, width), F32),
                ((3, SMALL_ROWS, width), F32),
                ((heads - 1, SMALL_ROWS // 2, width), F32),
                ((SMALL_ROWS, width), F32),
            ]
        )
        + [
            pltpu.SemaphoreType.DMA((count,)),
            pltpu.SemaphoreType.DMA((count,)),
            pltpu.SemaphoreType.DMA((6, 2 * (heads - 1))),
            pltpu.SemaphoreType.DMA((10,)),
            pltpu.SemaphoreType.DMA((24,)),
            pltpu.SemaphoreType.DMA((kinds,)),
            pltpu.SemaphoreType.REGULAR((3,)),
        ],
        compiler_params=pltpu.CompilerParams(
            collective_id=1, has_side_effects=True, vmem_limit_bytes=63 * 2**20
        ),
    )(*fulls, *flat, cotangent, marks, gains, b_down)


def finish(sz, blocks, output, tokens, whole, small):
    heads, width, cols, units = sz.shards, sz.width, sz.columns, sz.units
    parts = 4

    def kernel(o_in, t_in, a_in, c_in, u_in, d_in, small, o_out, t_out, embed, gain, shift, a, bqv, c, bout, u, bup, d, bdown):
        for src, dst in ((o_in, o_out), (t_in, t_out)):
            dst[...] = src[...]
        for src, dst in ((a_in, a), (c_in, c), (u_in, u), (d_in, d)):
            dst[...] = src[...].astype(F32)

        @pl.when((pl.program_id(0) == 0) & (pl.program_id(1) == 0))
        def _():
            head = lax.axis_index("head")
            embed[...] = small[0:1, :]
            for b in range(blocks):
                for norm in range(2):
                    gain[b, norm : norm + 1, :] = small[GAIN_ROW + 2 * b + norm : GAIN_ROW + 2 * b + norm + 1, :]
                    shift[b, norm : norm + 1, :] = small[SHIFT_ROW + 2 * b + norm : SHIFT_ROW + 2 * b + norm + 1, :]
                bout[b : b + 1, :] = small[BOUT_ROW + b : BOUT_ROW + b + 1, :]
                bdown[b : b + 1, :] = small[BDOWN_ROW + b : BDOWN_ROW + b + 1, :]
                bup[b : b + 1, :] = small[pl.ds(BUP_ROW + b * heads + head, 1), :]
                for i in range(2):
                    bqv[b, i : i + 1, :] = small[pl.ds(BQV_ROW + 2 * (b * heads + head) + i, 1), 0:cols]

    def rows(size, first):
        return pl.BlockSpec((1, size // parts, width), lambda b, i: (b, first * parts // size + i, 0))

    def kept(*shape):
        return pl.BlockSpec(shape, lambda b, i: (0,) * len(shape))

    share = output.shape[0] // (blocks * parts)
    cut = pl.BlockSpec((share,) + output.shape[1:], lambda b, i: (b * parts + i, 0, 0, 0))
    pair, triple = (blocks, width), (blocks, 2, width)
    sizes = (3 * cols, cols, width, units)
    shapes = [(output.shape, LOW), (output.shape, LOW)] + [
        (s, F32)
        for s in (
            (1, width),
            triple,
            triple,
            (blocks, sizes[0], width),
            (blocks, 2, cols),
            (blocks, sizes[1], width),
            pair,
            (blocks, sizes[2], width),
            pair,
            (blocks, sizes[3], width),
            pair,
        )
    ]
    out = [rows(size, 0) for size in sizes]
    return pl.pallas_call(
        kernel,
        name="finish",
        grid=(blocks, parts),
        out_shape=structs(shapes),
        in_specs=[
            cut,
            cut,
            rows(sizes[0], 0),
            rows(sizes[1], sz.out_row),
            rows(sizes[2], sz.up_row),
            rows(sizes[3], sz.down_row),
            kept(SMALL_ROWS, width),
        ],
        out_specs=[
            cut,
            cut,
            kept(1, width),
            kept(*triple),
            kept(*triple),
            out[0],
            kept(blocks, 2, cols),
            out[1],
            kept(*pair),
            out[2],
            kept(*pair),
            out[3],
            kept(*pair),
        ],
        compiler_params=pltpu.CompilerParams(vmem_limit_bytes=62 * 2**20),
    )(output, tokens, whole, whole, whole, whole, small)


def fits_local(arrays, clip_size, tube_size, head_size):
    clips, frames, tubes = arrays[0].shape[:3]
    width = arrays[0].shape[-1]
    columns, units = arrays[5].shape[3] // head_size, arrays[9].shape[2] // head_size
    devices = tube_size * head_size
    return (
        (clips, clip_size, tube_size) == (4, 4, 2)
        and frames % devices == 0
        and frames == tubes
        and head_size % 2 == 0
        and width == 4 * columns == units
        and width % 384 == 0
        and columns % HD == 0
    )


def on_device_local(
    tokens,
    token_mask,
    mask_embed,
    norm_gains,
    norm_shifts,
    w_qkv,
    b_qv,
    w_out,
    b_out,
    w_up,
    b_up,
    w_down,
    b_down,
    cotangent,
):
    _, frames, tubes, patches, width = tokens.shape
    tube_size, heads = lax.axis_size("tube"), lax.axis_size("head")
    head = lax.axis_index("head")
    blocks, columns, units = w_qkv.shape[0], w_qkv.shape[-1], w_up.shape[-1]
    frame_share = frames // (tube_size * heads)
    tube_share = tubes // heads
    rows = frame_share * tube_size * tubes * patches
    sz = Sizes(rows, width, heads, columns, units, rows // frame_share)

    marks = jnp.broadcast_to(token_mask[0][..., None], (frames, tubes, patches, 128)).astype(LOW)
    full, saved, mark_frames = run_forward(
        sz,
        blocks,
        frame_share,
        tube_share,
        (w_qkv.transpose(0, 2, 3, 1).reshape(blocks, 3 * columns, width), w_out, w_up, w_down),
        tokens[0],
        marks,
        b_qv,
        b_up,
        mask_embed,
        norm_gains,
        norm_shifts,
        b_out,
        b_down,
    )
    output, grad_tokens, whole, small = run_backward(
        sz, blocks, frame_share, tube_share, full, saved, cotangent[0], mark_frames, norm_gains, b_down
    )
    out = finish(sz, blocks, output, grad_tokens, whole.reshape(blocks, sz.block_rows, width), small)
    output, grad_tokens, embed, gains, shifts, qkv_grad, bqv, out_grad, bout, up_grad, bup, down_grad, bdown = out
    qkv_grad = qkv_grad.reshape(blocks, 3, columns, width).transpose(0, 3, 1, 2)
    return (
        output[None],
        grad_tokens[None],
        embed.reshape(width),
        gains,
        shifts,
        qkv_grad,
        bqv,
        out_grad,
        bout,
        up_grad,
        bup,
        down_grad,
        bdown,
    )


def solution(mesh):
    sizes = [mesh.shape[name] for name in ("clip", "tube", "head")]

    def run(*arrays):
        on_device = on_device_local if fits_local(arrays, *sizes) else on_device_sums
        return on_mesh(on_device, mesh)(*arrays)

    return run


def on_mesh(on_device, mesh):
    return jax.shard_map(
        on_device,
        mesh=mesh,
        in_specs=(
            P("clip", None, "tube", None, None),
            P("clip", None, "tube", None),
            P(),
            P(),
            P(),
            P(None, None, None, "head"),
            P(None, None, "head"),
            P(None, "head", None),
            P(),
            P(None, None, "head"),
            P(None, "head"),
            P(None, "head", None),
            P(),
            P("clip", None, "tube", None, None),
        ),
        out_specs=(
            P("clip", None, "tube", None, None),
            P("clip", None, "tube", None, None),
            P(),
            P(),
            P(),
            P(None, None, None, "head"),
            P(None, None, "head"),
            P(None, "head", None),
            P(),
            P(None, None, "head"),
            P(None, "head"),
            P(None, "head", None),
            P(),
        ),
        check_vma=False,
    )
```

```python
import functools

import jax
import jax.numpy as jnp
from jax import lax
from jax.experimental import pallas as pl
from jax.experimental.pallas import tpu as pltpu
from jax.sharding import PartitionSpec as P

F32 = jnp.float32
LOW = jnp.bfloat16
MESH = pl.DeviceIdType.MESH

HD = 64


EPS = 1e-05


def norm_forward(values, gain_vector, shift_vector):
    centre = values - jnp.mean(values, -1, keepdims=True)
    inverse = lax.rsqrt(jnp.mean(centre * centre, -1, keepdims=True) + EPS)
    normal = centre * inverse
    return (normal * gain_vector + shift_vector, normal, inverse)


def norm_backward(grad_out, normal, inverse, gain_vector):
    grad_normal = grad_out * gain_vector
    grad_in = inverse * (
        grad_normal
        - jnp.mean(grad_normal, -1, keepdims=True)
        - normal * jnp.mean(grad_normal * normal, -1, keepdims=True)
    )
    return (grad_in, jnp.sum(grad_out * normal, 0), jnp.sum(grad_out, 0))


def row_total(partial_sum):
    return lax.psum(partial_sum.astype(jnp.bfloat16), "head").astype(jnp.float32)


def input_total(partial_sum):
    return lax.psum(partial_sum.astype(jnp.bfloat16), "head").astype(jnp.float32)


def split_heads(tensor, batch_count, length):
    return tensor.reshape(batch_count, length, tensor.shape[-1] // HD, HD)


def attend(queries, key_rows, value_rows):
    scores = jnp.einsum(
        "bshe,bthe->bhst", queries, key_rows, preferred_element_type=jnp.float32
    ) * HD ** (-0.5)
    maximum = jnp.max(scores, -1, keepdims=True)
    exponent = jnp.exp(scores - maximum)
    denominator = jnp.sum(exponent, -1, keepdims=True)
    weights_soft = (exponent / denominator).astype(jnp.bfloat16)
    mixture = jnp.einsum(
        "bhst,bthe->bshe", weights_soft, value_rows, preferred_element_type=jnp.float32
    )
    return (mixture.astype(jnp.bfloat16), maximum + jnp.log(denominator))


def attend_back(queries, key_rows, value_rows, log_total, grad_mixture):
    scaling = HD ** (-0.5)
    scores = (
        jnp.einsum("bshe,bthe->bhst", queries, key_rows, preferred_element_type=jnp.float32)
        * scaling
    )
    weights_soft = jnp.exp(scores - log_total)
    grad_weights = jnp.einsum(
        "bshe,bthe->bhst", grad_mixture, value_rows, preferred_element_type=jnp.float32
    )
    grad_values = jnp.einsum(
        "bhst,bshe->bthe",
        weights_soft.astype(jnp.bfloat16),
        grad_mixture,
        preferred_element_type=jnp.float32,
    )
    grad_scores = (
        weights_soft * (grad_weights - jnp.sum(weights_soft * grad_weights, -1, keepdims=True))
    ).astype(jnp.bfloat16)
    grad_queries = (
        jnp.einsum("bhst,bthe->bshe", grad_scores, key_rows, preferred_element_type=jnp.float32)
        * scaling
    )
    grad_keys = (
        jnp.einsum("bhst,bshe->bthe", grad_scores, queries, preferred_element_type=jnp.float32)
        * scaling
    )
    return (grad_queries, grad_keys, grad_values)


def mixer_forward(block_kind, queries, key_rows, value_rows):
    clip_count, frame_count, tube_count, patch_count, columns = queries.shape
    if block_kind == 1:
        reorder = (0, 2, 1, 3, 4)
        pieces = [
            split_heads(
                tensor.transpose(reorder), clip_count * tube_count, frame_count * patch_count
            )
            for tensor in (queries, key_rows, value_rows)
        ]
        mixture, log_total = attend(pieces[0], pieces[1], pieces[2])
        mixture = mixture.reshape(
            clip_count, tube_count, frame_count, patch_count, columns
        ).transpose(reorder)
        return (mixture, (pieces, log_total))
    key_all, value_all = (
        lax.all_gather(key_rows, "tube", axis=2, tiled=True),
        lax.all_gather(value_rows, "tube", axis=2, tiled=True),
    )
    tube_all = key_all.shape[2]
    pieces = [
        split_heads(queries, clip_count * frame_count, tube_count * patch_count),
        split_heads(key_all, clip_count * frame_count, tube_all * patch_count),
        split_heads(value_all, clip_count * frame_count, tube_all * patch_count),
    ]
    mixture, log_total = attend(pieces[0], pieces[1], pieces[2])
    return (
        mixture.reshape(clip_count, frame_count, tube_count, patch_count, columns),
        (pieces, log_total),
    )


def mixer_backward(block_kind, retained, grad_mixture):
    pieces, log_total = retained
    clip_count, frame_count, tube_count, patch_count, columns = grad_mixture.shape
    if block_kind == 1:
        reorder = (0, 2, 1, 3, 4)
        moved = split_heads(
            grad_mixture.transpose(reorder), clip_count * tube_count, frame_count * patch_count
        )
        gradients = attend_back(pieces[0], pieces[1], pieces[2], log_total, moved)
        return [
            grad.astype(jnp.bfloat16)
            .reshape(clip_count, tube_count, frame_count, patch_count, columns)
            .transpose(reorder)
            for grad in gradients
        ]
    gradients = attend_back(
        pieces[0],
        pieces[1],
        pieces[2],
        log_total,
        split_heads(grad_mixture, clip_count * frame_count, tube_count * patch_count),
    )
    tube_all = pieces[1].shape[1] // patch_count
    grad_keys = gradients[1].reshape(clip_count, frame_count, tube_all, patch_count, columns)
    grad_values = gradients[2].reshape(clip_count, frame_count, tube_all, patch_count, columns)
    grad_keys, grad_values = (
        lax.psum_scatter(
            grad_keys.astype(jnp.bfloat16), "tube", scatter_dimension=2, tiled=True
        ).astype(jnp.float32),
        lax.psum_scatter(
            grad_values.astype(jnp.bfloat16), "tube", scatter_dimension=2, tiled=True
        ).astype(jnp.float32),
    )
    grad_queries = (
        gradients[0]
        .astype(jnp.bfloat16)
        .reshape(clip_count, frame_count, tube_count, patch_count, columns)
    )
    return [grad_queries, grad_keys.astype(jnp.bfloat16), grad_values.astype(jnp.bfloat16)]


def block_forward(block_kind, residual, layout, weights):
    gains, shifts, w_qkv, b_qv, w_out, b_out, w_up, b_up, w_down, b_down = weights
    columns = w_qkv.shape[-1]
    grid_shape = layout[:-1] + (columns,)
    normed_share, first_normal, first_inverse = norm_forward(residual, gains[0], shifts[0])
    normed = normed_share.astype(jnp.bfloat16)
    projected = jnp.einsum("rd,dcj->rcj", normed, w_qkv, preferred_element_type=jnp.float32)
    queries = (projected[:, 0] + b_qv[0]).astype(jnp.bfloat16).reshape(grid_shape)
    key_rows = projected[:, 1].astype(jnp.bfloat16).reshape(grid_shape)
    value_rows = (projected[:, 2] + b_qv[1]).astype(jnp.bfloat16).reshape(grid_shape)
    mixture, retained = mixer_forward(block_kind, queries, key_rows, value_rows)
    mixture = mixture.reshape(-1, columns)
    middle = (
        residual + row_total(jnp.dot(mixture, w_out, preferred_element_type=jnp.float32)) + b_out
    )
    second_share, second_normal, second_inverse = norm_forward(middle, gains[1], shifts[1])
    normed_two = second_share.astype(jnp.bfloat16)
    hidden = jnp.dot(normed_two, w_up, preferred_element_type=jnp.float32) + b_up
    active = jax.nn.gelu(hidden).astype(jnp.bfloat16)
    stored = (
        normed,
        first_normal,
        first_inverse,
        retained,
        mixture,
        normed_two,
        second_normal,
        second_inverse,
        hidden,
    )
    return (middle, active, stored)


def block_output(middle, active, w_down, b_down):
    return middle + row_total(jnp.dot(active, w_down, preferred_element_type=jnp.float32)) + b_down


def block_backward(block_kind, residual, layout, weights, grad_rows):
    gains, shifts, w_qkv, b_qv, w_out, b_out, w_up, b_up, w_down, b_down = weights
    middle, active, stored = block_forward(block_kind, residual, layout, weights)
    (
        normed,
        first_normal,
        first_inverse,
        retained,
        mixture,
        normed_two,
        second_normal,
        second_inverse,
        hidden,
    ) = stored
    columns = w_qkv.shape[-1]
    grad_low = grad_rows.astype(jnp.bfloat16)
    grad_wdown = jnp.dot(active.T, grad_low, preferred_element_type=jnp.float32)
    grad_bdown = jnp.sum(grad_rows, 0)
    grad_active = jnp.dot(grad_low, w_down.T, preferred_element_type=jnp.float32)
    gelu_pull = jax.vjp(jax.nn.gelu, hidden)[1]
    grad_hidden = gelu_pull(grad_active)[0].astype(jnp.bfloat16)
    grad_bup = jnp.sum(grad_hidden.astype(jnp.float32), 0)
    grad_wup = jnp.dot(normed_two.T, grad_hidden, preferred_element_type=jnp.float32)
    grad_normed_two = input_total(jnp.dot(grad_hidden, w_up.T, preferred_element_type=jnp.float32))
    grad_norm, grad_gain_two, grad_shift_two = norm_backward(
        grad_normed_two, second_normal, second_inverse, gains[1]
    )
    grad_middle = grad_rows + grad_norm
    grad_bout = jnp.sum(grad_middle, 0)
    grad_mid_low = grad_middle.astype(jnp.bfloat16)
    grad_wout = jnp.dot(mixture.T, grad_mid_low, preferred_element_type=jnp.float32)
    grad_mixture = jnp.dot(grad_mid_low, w_out.T, preferred_element_type=jnp.float32).astype(
        jnp.bfloat16
    )
    grad_parts = mixer_backward(
        block_kind, retained, grad_mixture.reshape(layout[:-1] + (columns,))
    )
    grad_flat = [grad.reshape(-1, columns) for grad in grad_parts]
    grad_project = jnp.stack(grad_flat, 1)
    grad_bqv = jnp.stack(
        [jnp.sum(grad_flat[0].astype(jnp.float32), 0), jnp.sum(grad_flat[2].astype(jnp.float32), 0)]
    )
    grad_wqkv = jnp.einsum("rd,rcj->dcj", normed, grad_project, preferred_element_type=jnp.float32)
    grad_normed = input_total(
        jnp.einsum("rcj,dcj->rd", grad_project, w_qkv, preferred_element_type=jnp.float32)
    )
    grad_input, grad_gain_one, grad_shift_one = norm_backward(
        grad_normed, first_normal, first_inverse, gains[0]
    )
    gradients = (
        jnp.stack([grad_gain_one, grad_gain_two]),
        jnp.stack([grad_shift_one, grad_shift_two]),
        grad_wqkv,
        grad_bqv,
        grad_wout,
        grad_bout,
        grad_wup,
        grad_bup,
        grad_wdown,
        grad_bdown,
    )
    return (grad_middle + grad_input, gradients)


def on_device_sums(
    tokens,
    token_mask,
    mask_embed,
    norm_gains,
    norm_shifts,
    w_qkv,
    b_qv,
    w_out,
    b_out,
    w_up,
    b_up,
    w_down,
    b_down,
    cotangent,
):
    layout = tokens.shape
    width = layout[-1]
    masked = (token_mask == 1).reshape(-1, 1)
    initial = jnp.where(masked, mask_embed[None, :], tokens.reshape(-1, width).astype(jnp.float32))
    upstream = cotangent.reshape(-1, width).astype(jnp.float32)

    def weights_of(block_kind):
        return (
            norm_gains[block_kind],
            norm_shifts[block_kind],
            w_qkv[block_kind],
            b_qv[block_kind],
            w_out[block_kind],
            b_out[block_kind],
            w_up[block_kind],
            b_up[block_kind],
            w_down[block_kind],
            b_down[block_kind],
        )

    middle, active, unused_first = block_forward(0, initial, layout, weights_of(0))
    second = block_output(middle, active, w_down[0], b_down[0])
    middle, active, unused_second = block_forward(1, second, layout, weights_of(1))
    output_rows = block_output(middle, active, w_down[1], b_down[1])
    grad_second, grads_later = block_backward(1, second, layout, weights_of(1), upstream)
    grad_initial, grads_earlier = block_backward(0, initial, layout, weights_of(0), grad_second)
    stacked = [
        jnp.stack([first_grad, later_grad])
        for first_grad, later_grad in zip(grads_earlier, grads_later)
    ]
    grad_embed = jnp.sum(jnp.where(masked, grad_initial, 0.0), 0)
    output_low = output_rows.astype(jnp.bfloat16)
    grad_low = jnp.where(masked, 0.0, grad_initial).astype(jnp.bfloat16)
    shares = (
        lax.psum_scatter(stacked[2], ("clip", "tube"), scatter_dimension=1, tiled=True),
        lax.psum_scatter(stacked[4], ("clip", "tube"), scatter_dimension=2, tiled=True),
        lax.psum_scatter(stacked[6], ("clip", "tube"), scatter_dimension=1, tiled=True),
        lax.psum_scatter(stacked[8], ("clip", "tube"), scatter_dimension=2, tiled=True),
    )
    whole = (
        lax.all_gather(shares[0].astype(jnp.bfloat16), ("clip", "tube"), axis=1, tiled=True).astype(
            jnp.float32
        ),
        lax.all_gather(shares[1].astype(jnp.bfloat16), ("clip", "tube"), axis=2, tiled=True).astype(
            jnp.float32
        ),
        lax.all_gather(shares[2].astype(jnp.bfloat16), ("clip", "tube"), axis=1, tiled=True).astype(
            jnp.float32
        ),
        lax.all_gather(shares[3].astype(jnp.bfloat16), ("clip", "tube"), axis=2, tiled=True).astype(
            jnp.float32
        ),
    )
    column_part = (
        grad_embed,
        stacked[0],
        stacked[1],
        stacked[5],
        stacked[9],
        stacked[3],
        stacked[7],
    )
    small = lax.psum(
        (
            column_part[0],
            column_part[1],
            column_part[2],
            column_part[3],
            column_part[4],
            column_part[5],
            column_part[6],
        ),
        ("clip", "tube"),
    )
    embed_grad, gain_grad, shift_grad, bout_grad, bdown_grad = (
        small[0],
        small[1],
        small[2],
        small[3],
        small[4],
    )
    bqv_grad, bup_grad = (small[5], small[6])
    return (
        output_low.reshape(layout),
        grad_low.reshape(layout),
        embed_grad,
        gain_grad,
        shift_grad,
        whole[0],
        bqv_grad,
        whole[1],
        bout_grad,
        whole[2],
        bup_grad,
        whole[3],
        bdown_grad,
    )


DOWN, UP, ATTN = range(3)
SEND, PASS, FIRST_INPUT, SECOND_INPUT, SPREAD, ATTEND, MIDDLE, EXPAND, CONTRACT = range(9)
FORWARD_ORDER = (
    (SEND, 0), (PASS, 0, 0), (SEND, 1), (FIRST_INPUT,), (PASS, 0, 1), (PASS, 1, 0), (SEND, 2), (PASS, 1, 1),
    (PASS, 0, 2), (PASS, 0, 3), (PASS, 1, 2), (PASS, 2, 0), (SEND, 3), (PASS, 1, 3), (ATTEND, 0, 0), (ATTEND, 0, 1),
    (ATTEND, 0, 2), (PASS, 2, 1), (ATTEND, 0, 3), (MIDDLE, 0), (PASS, 3, 0), (SEND, 4), (PASS, 2, 2), (PASS, 3, 1),
    (PASS, 2, 3), (EXPAND, 0, 0), (PASS, 4, 0), (SEND, 5), (EXPAND, 0, 1), (EXPAND, 0, 2), (EXPAND, 0, 3),
    (PASS, 3, 2), (PASS, 4, 1), (PASS, 5, 0), (SEND, 6), (PASS, 3, 3), (CONTRACT, 0, 0), (CONTRACT, 0, 1),
    (CONTRACT, 0, 2), (CONTRACT, 0, 3), (SPREAD,), (PASS, 5, 1), (PASS, 4, 2), (PASS, 4, 3), (PASS, 6, 0),
    (SECOND_INPUT,), (ATTEND, 1, 0), (PASS, 6, 1), (PASS, 5, 2), (ATTEND, 1, 1), (ATTEND, 1, 2), (PASS, 5, 3),
    (ATTEND, 1, 3), (MIDDLE, 1), (EXPAND, 1, 0), (PASS, 6, 2), (EXPAND, 1, 1), (EXPAND, 1, 2), (EXPAND, 1, 3),
    (PASS, 6, 3),
)
MLP_BACK, MLP_NORM, ATTN_BACK, ATTN_NORM, UPSTREAM, RESULT_LINE, OWN_LINE, FAR_START, FAR_LINE, SMALL = range(10)
ADD_CORE, ADD_FIRST, ADD_SECOND, PASS_HEADS, ADD_HEADS, SHARE_FIRST, SHARE_CORE, ARRIVED, MLP_START, SEND_RESULT = range(10, 20)
BACKWARD_ORDER = (
    (MLP_START,), (MLP_BACK, 1, 0), (ADD_CORE, 1, DOWN, 0), (MLP_BACK, 1, 1), (ADD_CORE, 1, UP, 0), (MLP_BACK, 1, 2),
    (ADD_CORE, 1, UP, 1), (ADD_CORE, 1, DOWN, 1), (MLP_BACK, 1, 3), (SEND_RESULT,), (ADD_CORE, 1, DOWN, 2),
    (ADD_CORE, 1, UP, 2), (MLP_NORM, 1), (ADD_CORE, 1, DOWN, 3), (ATTN_BACK, 1, 0), (ADD_CORE, 1, UP, 3),
    (ATTN_BACK, 1, 1), (ADD_CORE, 1, ATTN, 0), (ATTN_BACK, 1, 2), (ADD_FIRST, 1, UP), (ADD_CORE, 1, ATTN, 1),
    (ATTN_BACK, 1, 3), (ATTN_NORM, 1), (ADD_CORE, 1, ATTN, 3), (ADD_SECOND, 1, UP), (ADD_CORE, 1, ATTN, 2),
    (RESULT_LINE, 0), (ADD_FIRST, 1, DOWN), (UPSTREAM,), (ADD_FIRST, 1, ATTN), (MLP_BACK, 0, 0), (MLP_BACK, 0, 1),
    (ADD_SECOND, 1, DOWN), (ADD_CORE, 0, DOWN, 0), (ADD_CORE, 0, UP, 0), (MLP_BACK, 0, 2), (ADD_CORE, 0, UP, 1),
    (PASS_HEADS, 1, UP, 1), (ADD_CORE, 0, DOWN, 1), (MLP_BACK, 0, 3), (ADD_CORE, 0, UP, 2), (MLP_NORM, 0),
    (PASS_HEADS, 1, DOWN, 1), (ADD_SECOND, 1, ATTN), (RESULT_LINE, 1), (ATTN_BACK, 0, 0), (ADD_CORE, 0, UP, 3),
    (ADD_CORE, 0, DOWN, 2), (ATTN_BACK, 0, 1), (ADD_CORE, 0, ATTN, 0), (ATTN_BACK, 0, 2), (ADD_CORE, 0, DOWN, 3),
    (ADD_CORE, 0, ATTN, 1), (PASS_HEADS, 1, ATTN, 1), (PASS_HEADS, 1, DOWN, 2), (ATTN_BACK, 0, 3), (ATTN_NORM, 0),
    (PASS_HEADS, 1, ATTN, 2), (ADD_FIRST, 0, UP), (ADD_FIRST, 0, DOWN), (ADD_CORE, 0, ATTN, 2),
    (ADD_CORE, 0, ATTN, 3), (FAR_START,), (OWN_LINE, 0), (PASS_HEADS, 1, UP, 2), (SMALL, 0), (ADD_SECOND, 0, UP),
    (RESULT_LINE, 2), (FAR_LINE, 0), (ADD_SECOND, 0, DOWN), (ADD_FIRST, 0, ATTN), (PASS_HEADS, 0, UP, 1),
    (ADD_HEADS, 1, UP), (ADD_HEADS, 1, ATTN), (ADD_SECOND, 0, ATTN), (OWN_LINE, 1), (SMALL, 1), (SHARE_FIRST, 1, UP),
    (SHARE_FIRST, 1, ATTN), (ADD_HEADS, 1, DOWN), (PASS_HEADS, 0, DOWN, 1), (PASS_HEADS, 0, UP, 2),
    (PASS_HEADS, 0, ATTN, 1), (PASS_HEADS, 0, DOWN, 2), (SHARE_FIRST, 1, DOWN), (ADD_HEADS, 0, UP), (SMALL, 2),
    (ADD_HEADS, 0, DOWN), (SHARE_FIRST, 0, UP), (PASS_HEADS, 0, ATTN, 2), (FAR_LINE, 1), (SHARE_CORE, 1, DOWN),
    (SHARE_FIRST, 0, DOWN), (SHARE_CORE, 1, UP), (ADD_HEADS, 0, ATTN), (ARRIVED, 1, DOWN), (SHARE_CORE, 1, ATTN),
    (SHARE_CORE, 0, UP), (SHARE_CORE, 0, DOWN), (SHARE_FIRST, 0, ATTN), (OWN_LINE, 2), (ARRIVED, 1, ATTN),
    (ARRIVED, 0, DOWN), (ARRIVED, 0, UP), (FAR_LINE, 2), (SMALL, 3), (ARRIVED, 1, UP), (SHARE_CORE, 0, ATTN),
    (SMALL, 4), (ARRIVED, 0, ATTN),
)

GELU_A = 0.7978845608028654
GELU_B = 0.044715


def dot(left, right, dims):
    return lax.dot_general(left, right, (dims, ((), ())), preferred_element_type=F32)


NN, NT, TN = ((1,), (0,)), ((1,), (1,)), ((0,), (0,))


def standardize(values):
    centre = values - jnp.mean(values, -1, keepdims=True)
    inverse = lax.rsqrt(jnp.mean(centre * centre, -1, keepdims=True) + EPS)
    return centre * inverse, inverse


def head_masks(columns, scale):
    lane = lax.broadcasted_iota(jnp.int32, (1, columns), 1)
    return [
        jnp.where((lane >= j * HD) & (lane < (j + 1) * HD), scale, 0.0).astype(LOW)
        for j in range(columns // HD)
    ]


def gelu_pair(hidden):
    square = hidden * hidden
    tanh = jnp.tanh(GELU_A * hidden * (1.0 + GELU_B * square))
    half = 0.5 * (1.0 + tanh)
    slope = half + hidden * (0.5 * GELU_A) * (1.0 - tanh * tanh) * (1.0 + 3.0 * GELU_B * square)
    return hidden * half, slope


class Sizes:
    def __init__(self, rows, width, shards, columns, units, length):
        self.rows, self.width, self.shards = rows, width, shards
        self.columns, self.units, self.length = columns, units, length
        self.sequences = rows // length
        self.heads = columns // HD
        self.out_row = 3 * columns
        self.up_row = 4 * columns
        self.down_row = 4 * columns + width
        self.block_rows = 4 * columns + width + units


def norm_rows(sz, x_ref, gain, shift, n_ref, chunk=128):
    @pl.loop(0, sz.rows, step=chunk)
    def _(start):
        at = pl.ds(pl.multiple_of(start, chunk), chunk)
        normal, _ = standardize(x_ref[at, :].astype(F32))
        n_ref[at, :] = (normal * gain + shift).astype(LOW)


def forward_attention(sz, shard, w_ref, b_query, b_value, n_ref, t_ref, p_ref, m_ref):
    cols, length = sz.columns, sz.length
    normed = n_ref[...]
    q_ref, k_ref, v_ref, o_ref = (t_ref.at[shard, i] for i in range(4))
    q_ref[...] = (dot(normed, w_ref[shard, 0:cols, :], NT) + b_query).astype(LOW)
    k_ref[...] = dot(normed, w_ref[shard, cols : 2 * cols, :], NT).astype(LOW)
    v_ref[...] = (dot(normed, w_ref[shard, 2 * cols : 3 * cols, :], NT) + b_value).astype(LOW)
    scaled = head_masks(cols, HD**-0.5)
    masks = head_masks(cols, 1.0)
    for seq in range(sz.sequences):
        at = slice(seq * length, (seq + 1) * length)
        queries, keys, values = q_ref[at, :], k_ref[at, :], v_ref[at, :]
        mixture = jnp.zeros((length, cols), F32)
        for head in range(sz.heads):
            scores = dot(queries * scaled[head], keys, NT)
            exponent = jnp.exp(scores - jnp.max(scores, -1, keepdims=True))
            weights = (exponent / jnp.sum(exponent, -1, keepdims=True)).astype(LOW)
            p_ref[shard, seq * sz.heads + head] = weights
            mixture += dot(weights, values * masks[head], NN)
        o_ref[at, :] = mixture.astype(LOW)
    m_ref[...] += dot(o_ref[...], w_ref[shard, sz.out_row : sz.out_row + cols, :], NN)


def forward_up(sz, shard, w_ref, b_up, n2_ref, as_ref):
    hidden = dot(n2_ref[...], w_ref[shard, sz.up_row : sz.up_row + sz.width, :], NN) + b_up
    active, slope = gelu_pair(hidden)
    as_ref[shard, 0] = active.astype(LOW)
    as_ref[shard, 1] = slope.astype(LOW)


def forward_down(sz, shard, w_ref, as_ref, y_ref):
    y_ref[...] += dot(as_ref[shard, 0], w_ref[shard, sz.down_row : sz.down_row + sz.units, :], NN)


def backward_mlp(sz, w_ref, as_ref, low_ref, n2_ref, du_ref, dn_ref, down_ref, up_ref, sum_row):
    low = low_ref[...]
    grad_active = dot(low, w_ref[sz.width : sz.width + sz.units, :], NT)
    du_ref[...] = (grad_active * as_ref[1].astype(F32)).astype(LOW)
    sum_row[...] = jnp.sum(du_ref[...].astype(F32), 0, keepdims=True)
    if down_ref is not None:
        down_ref[...] = dot(as_ref[0], low, TN).astype(LOW)
    up_ref[...] = dot(n2_ref[...], du_ref[...], TN).astype(LOW)
    dn_ref[...] += dot(du_ref[...], w_ref[0 : sz.width, :], NT)


def norm_back_rows(sz, x_ref, gain, dn_ref, g_ref, out_ref, gain_row, shift_row, sum_row, low_ref, chunk=128):
    for row in (gain_row, shift_row, sum_row):
        if row is not None:
            row[...] = jnp.zeros_like(row)

    @pl.loop(0, sz.rows, step=chunk)
    def _(start):
        at = pl.ds(pl.multiple_of(start, chunk), chunk)
        normal, inverse = standardize(x_ref[at, :])
        dn = dn_ref[at, :]
        dy = dn * gain
        part = inverse * (
            dy - jnp.mean(dy, -1, keepdims=True) - normal * jnp.mean(dy * normal, -1, keepdims=True)
        )
        total = g_ref[at, :].astype(F32) + part
        out_ref[at, :] = total
        if low_ref is not None:
            low_ref[at, :] = total.astype(LOW)
        gain_row[...] += jnp.sum(dn * normal, 0, keepdims=True)
        shift_row[...] += jnp.sum(dn, 0, keepdims=True)
        if sum_row is not None:
            sum_row[...] += jnp.sum(total, 0, keepdims=True)


def backward_attention(sz, w_ref, t_ref, p_ref, dml_ref, n_ref, do_ref, dq_ref, dk_ref, dv_ref, dn_ref, g_ref, query_row, value_row):
    cols, length = sz.columns, sz.length
    low = dml_ref[...]
    q_ref, k_ref, v_ref, o_ref = (t_ref.at[i] for i in range(4))
    w_out = w_ref[sz.out_row : sz.out_row + cols, :]
    do_ref[...] = dot(low, w_out, NT).astype(LOW)
    g_ref[sz.out_row : sz.out_row + cols, :] = dot(o_ref[...], low, TN).astype(LOW)
    scaled = head_masks(cols, HD**-0.5)
    masks = head_masks(cols, 1.0)
    for seq in range(sz.sequences):
        at = slice(seq * length, (seq + 1) * length)
        queries, keys, values = q_ref[at, :], k_ref[at, :], v_ref[at, :]
        grad_o = do_ref[at, :]
        dq = jnp.zeros((length, cols), F32)
        dk = jnp.zeros((length, cols), F32)
        dv = jnp.zeros((length, cols), F32)
        for head in range(sz.heads):
            weights = p_ref[seq * sz.heads + head]
            grad_head = grad_o * masks[head]
            dp = dot(grad_head, values, NT)
            dv += dot(weights, grad_head, TN)
            wide = weights.astype(F32)
            ds = (wide * (dp - jnp.sum(wide * dp, -1, keepdims=True))).astype(LOW)
            dq += dot(ds, keys * scaled[head], NN)
            dk += dot(ds, queries * scaled[head], TN)
        dq_ref[at, :] = dq.astype(LOW)
        dk_ref[at, :] = dk.astype(LOW)
        dv_ref[at, :] = dv.astype(LOW)
    normed = n_ref[...]
    query_row[...] = jnp.sum(dq_ref[...].astype(F32), 0, keepdims=True)
    value_row[...] = jnp.sum(dv_ref[...].astype(F32), 0, keepdims=True)
    for i, part in enumerate((dq_ref, dk_ref, dv_ref)):
        g_ref[i * cols : (i + 1) * cols, :] = dot(part[...], normed, TN).astype(LOW)
        dn_ref[...] += dot(part[...], w_ref[i * cols : (i + 1) * cols, :], NN)


def saved_shapes(sz):
    s, r, c = sz.shards, sz.rows, sz.columns
    return [
        ((r, sz.width), LOW),
        ((s, 4, r, c), LOW),
        ((s, sz.sequences * sz.heads, sz.length, sz.length), LOW),
        ((r, sz.width), F32),
        ((r, sz.width), LOW),
        ((s, 2, r, sz.units), LOW),
    ]


def structs(shapes):
    return [jax.ShapeDtypeStruct(s, d) for s, d in shapes]


def vmems(shapes):
    return [pltpu.VMEM(s, d) for s, d in shapes]


class Place:
    def __init__(self, heads, zs=None):
        self.clip, self.y, self.z = (lax.axis_index(n) for n in ("clip", "tube", "head"))
        self.heads = heads
        self.core, self.x = lax.rem(self.clip, 2), lax.div(self.clip, 2)
        c, x, y = self.core, self.x, self.y
        self.first = (c + 2 * (x + (1 - c) * (1 - 2 * x)), y + c * (1 - 2 * y), self.z)
        self.second = (c + 2 * (x + c * (1 - 2 * x)), y + (1 - c) * (1 - 2 * y), self.z)
        self.other = (1 - c + 2 * x, y, self.z)
        self.i = (1 - c) * x + c * y
        self.j = (1 - c) * y + c * x
        self.along_x = (c + 2 * (1 - x), y, self.z)

    def head(self, step):
        return (self.clip, self.y, lax.rem(self.z + step + self.heads, self.heads))

    def across(self, step):
        return (self.clip, 1 - self.y, lax.rem(self.z + step + self.heads, self.heads))

    def clip_peers(self):
        return [self.head(d) for d in range(1, self.heads)] + [self.across(d) for d in range(self.heads)]

    def all_peers(self):
        return [self.along_x, self.other] + self.clip_peers()


def greet(peers):
    barrier = pltpu.get_barrier_semaphore()
    for peer in peers:
        pl.semaphore_signal(barrier, inc=1, device_id=peer, device_id_type=MESH)
    pl.semaphore_wait(barrier, len(peers))


class Moves:
    def __init__(self, send_sem, recv_sem):
        self.send_sem, self.recv_sem, self.count, self.sent = send_sem, recv_sem, 0, {}

    def reserve(self):
        self.count += 1
        return self.count - 1

    def one(self, n, src, dst, target):
        return pltpu.make_async_remote_copy(
            src, dst, self.send_sem.at[n], self.recv_sem.at[n], device_id=target, device_id_type=MESH
        )

    def phase(self, copies):
        made = []
        for src, dst, landing, target in copies:
            n = self.count
            self.count += 1
            made.append((src, dst, landing, target, n))
        return made

    def start(self, made):
        for src, dst, _, target, n in made:
            copy = pltpu.make_async_remote_copy(
                src, dst, self.send_sem.at[n], self.recv_sem.at[n], device_id=target, device_id_type=MESH
            )
            copy.start()
            self.sent[n] = copy

    def arrive(self, made):
        for src, _, landing, target, n in made:
            pltpu.make_async_remote_copy(
                src, landing, self.send_sem.at[n], self.recv_sem.at[n], device_id=target, device_id_type=MESH
            ).wait_recv()

    def left(self, made):
        for *_, n in made:
            if n in self.sent:
                self.sent.pop(n).wait_send()

    def finish(self):
        for copy in self.sent.values():
            copy.wait_send()
        self.sent = {}


def piece_list(sz, blocks):
    out = []
    for b in range(blocks):
        for kind, start in ((ATTN, 0), (UP, sz.up_row), (DOWN, sz.down_row)):
            parts = 2 if (b, kind) == (0, ATTN) else 1
            size = sz.width // parts
            out += [(b, kind, start + i * size, size) for i in range(parts)]
    return out


def gather_phases(place, moves, full, offset, rows):
    q = rows // 8
    c, i, j, z, heads = place.core, place.i, place.j, place.z, place.heads

    def at(ref, head, start, size):
        return ref.at[head, pl.ds(pl.multiple_of(offset + start * q, q), size * q), :]

    def other(d):
        return lax.rem(z + d, heads)

    mine = 4 * c + 2 * j + i
    near = 4 * c + 2 * j + (1 - i)
    pair = 4 * c + 2 * j
    pair_far = 4 * c + 2 * (1 - j)
    steps = range(1, heads)
    return [
        moves.phase(
            [(at(full, z, mine, 1), at(full, z, mine, 1), at(full, lax.rem(z + heads - d, heads), mine, 1), place.head(d)) for d in steps]
        ),
        moves.phase(
            [(at(full, other(d), mine, 1), at(full, other(d), mine, 1), at(full, other(d), near, 1), place.first) for d in steps]
        ),
        moves.phase(
            [(at(full, other(d), pair, 2), at(full, other(d), pair, 2), at(full, other(d), pair_far, 2), place.second) for d in steps]
        ),
        moves.phase(
            [(at(full, other(d), 4 * c, 4), at(full, other(d), 4 * c, 4), at(full, other(d), 4 * (1 - c), 4), place.other) for d in steps]
        ),
    ]


def masked_rows(rows, marks_ref):
    patches = marks_ref.shape[-1]
    marks = marks_ref[...].astype(F32).reshape(rows // patches, patches).astype(LOW)
    group = lax.div(lax.broadcasted_iota(jnp.int32, (rows, rows // patches), 0), patches)
    spread = (group == lax.broadcasted_iota(jnp.int32, (rows, rows // patches), 1)).astype(F32).astype(LOW)
    wide = dot(spread, marks, NN)
    lane = lax.broadcasted_iota(jnp.int32, (rows, patches), 1)
    mine = lane == lax.rem(lax.broadcasted_iota(jnp.int32, (rows, patches), 0), patches)
    return jnp.sum(jnp.where(mine, wide, 0.0), -1, keepdims=True) > 0.5


class Saves:
    def __init__(self, sem):
        self.sem, self.count = sem, 0

    def start(self, src, dst):
        copy = pltpu.make_async_copy(src, dst, self.sem.at[self.count])
        self.count += 1
        copy.start()
        return copy


def forward_kernel(sz, blocks, frame_share, tube_share, *refs):
    (w_qkv, w_out, w_up, w_down, tokens, marks, b_qv, b_up, embed, gains, shifts, b_out, b_down), refs = refs[:13], refs[13:]
    fulls, refs = refs[:blocks], refs[blocks:]
    saved, refs = [refs[7 * b : 7 * b + 7] for b in range(blocks)], refs[7 * blocks :]
    (frame_marks,), refs = refs[:1], refs[1:]
    w = refs[:blocks]
    (
        frames, bqv, bup, x, n, t, p, m, n2, act, y, y_low, second, send_sem, recv_sem, local_sem, save_sem,
    ) = refs[blocks:]
    heads, block_rows, length = sz.shards, sz.block_rows, sz.length
    place = Place(heads)
    moves = Moves(send_sem, recv_sem)
    local, saves = Saves(local_sem), Saves(save_sem)

    def settle(copies):
        for copy in copies:
            copy.wait()

    yy, z = place.y, place.z
    tubes = tokens.shape[1]
    greet(place.all_peers())

    owned = pl.ds((2 * z + yy) * frame_share, frame_share)
    asked = pl.ds((2 * z + 1 - yy) * frame_share, frame_share)
    here, there = pl.ds(yy * tubes, tubes), pl.ds((1 - yy) * tubes, tubes)
    exchange = moves.phase(
        [
            (src.at[asked], dst.at[:, here], dst.at[:, there], place.across(0))
            for src, dst in ((tokens, frames), (marks, frame_marks))
        ]
        + [
            (src, dst.at[z], dst.at[lax.rem(z + heads - d, heads)], place.head(d))
            for src, dst in ((b_qv, bqv), (b_up, bup))
            for d in range(1, heads)
        ]
    )
    spread = moves.phase(
        [
            (
                y_low.at[:, pl.ds((heads * ty + tz) * tube_share, tube_share)],
                second.at[pl.ds((2 * z + yy) * frame_share, frame_share)],
                second.at[pl.ds((2 * fz + ty) * frame_share, frame_share)],
                target,
            )
            for ty, tz, fz, target in [
                (yy, lax.rem(z + d, heads), lax.rem(z + heads - d, heads), place.head(d)) for d in range(1, heads)
            ]
            + [
                (1 - yy, lax.rem(z + d, heads), lax.rem(z + heads - d, heads), place.across(d)) for d in range(heads)
            ]
        ]
    )
    pieces = piece_list(sz, blocks)
    work = [gather_phases(place, moves, w[b], start, size) for b, _, start, size in pieces]
    moves.start(exchange)
    own_parts = {}
    for b in range(blocks):
        mine = w[b].at[z]
        own_parts[b, ATTN] = [
            local.start(w_qkv.at[b], mine.at[pl.ds(0, sz.out_row)]),
            local.start(w_out.at[b], mine.at[pl.ds(sz.out_row, sz.columns)]),
        ]
        own_parts[b, UP] = [local.start(w_up.at[b], mine.at[pl.ds(sz.up_row, sz.width)])]
        own_parts[b, DOWN] = [local.start(w_down.at[b], mine.at[pl.ds(sz.down_row, sz.units)])]

    def begin_piece(piece):
        b, kind, _, _ = pieces[piece]
        settle(own_parts.pop((b, kind), ()))
        moves.start(work[piece][0])
    owns = [
        local.start(tokens.at[owned], frames.at[:, here]),
        local.start(marks.at[owned], frame_marks.at[:, here]),
        local.start(b_qv, bqv.at[z]),
        local.start(b_up, bup.at[z]),
    ]

    def save(b, index, src, part=None):
        dst = saved[b][index]
        return saves.start(src, dst if part is None else dst.at[part])

    def begin_block(b):
        norm_rows(sz, x, gains[b, 0:1, :], shifts[b, 0:1, :], n)
        m[...] = x[...] + b_out[b : b + 1, :]
        return [save(b, 0, x), save(b, 1, n)]

    def attention(b, s):
        forward_attention(sz, s, w[b], bqv[s, b, 0:1, :], bqv[s, b, 1:2, :], n, t, p, m)
        return [save(b, 2, t.at[s], s), save(b, 3, p.at[s], s)]

    def middle(b):
        norm_rows(sz, m, gains[b, 1:2, :], shifts[b, 1:2, :], n2)
        y[...] = m[...] + b_down[b : b + 1, :]
        return [save(b, 4, m), save(b, 5, n2)]

    def up(b, s):
        forward_up(sz, s, w[b], bup[s, b : b + 1, :], n2, act)
        return [save(b, 6, act.at[s], s)]

    def down(b, s):
        forward_down(sz, s, w[b], act, y)

    def keep(piece):
        b, _, start, size = pieces[piece]
        at = pl.ds(start, size)
        return [saves.start(w[b].at[:, at], fulls[b].at[:, at])]

    kept, early = [], []
    wide = [None] * blocks

    def first_input():
        settle(owns)
        moves.arrive(exchange)
        tok = frames[...].astype(F32).reshape(sz.rows, sz.width)
        x[...] = jnp.where(masked_rows(sz.rows, frame_marks), embed[...].reshape(1, sz.width), tok)
        early.extend(begin_block(0))

    def second_input():
        moves.arrive(spread)
        wide[1].wait()
        settle(early)
        for j in range(tube_share):
            x[j * length : (j + 1) * length, :] = second[:, j].astype(F32).reshape(length, sz.width)
        kept.extend(begin_block(1))

    def spread_first():
        y_low[...] = y[...].astype(LOW).reshape(y_low.shape)
        moves.start(spread)
        wide[1] = local.start(
            y_low.at[:, pl.ds((heads * yy + z) * tube_share, tube_share)],
            second.at[pl.ds((2 * z + yy) * frame_share, frame_share)],
        )

    def advance(piece, phase):
        moves.arrive(work[piece][phase])
        if phase < 3:
            moves.start(work[piece][phase + 1])
        else:
            kept.extend(keep(piece))

    steps = {(FIRST_INPUT,): first_input, (SPREAD,): spread_first, (SECOND_INPUT,): second_input}
    for piece in range(len(work)):
        steps[SEND, piece] = functools.partial(begin_piece, piece)
        for phase in range(4):
            steps[PASS, piece, phase] = functools.partial(advance, piece, phase)
    for b in range(blocks):
        held = kept if b else early
        run = lambda f, *args, held=held: held.extend(f(*args) or ())
        steps[MIDDLE, b] = functools.partial(run, middle, b)
        for s in range(heads):
            steps[ATTEND, b, s] = functools.partial(run, attention, b, s)
            steps[EXPAND, b, s] = functools.partial(run, up, b, s)
            steps[CONTRACT, b, s] = functools.partial(run, down, b, s)
    for step in FORWARD_ORDER:
        steps[step]()
    moves.finish()
    settle(kept)


def run_forward(sz, blocks, frame_share, tube_share, weights, tokens, marks, b_qv, b_up, embed, gains, shifts, b_out, b_down):
    heads, width, rows = sz.shards, sz.width, sz.rows
    tubes, patches = 2 * tokens.shape[1], tokens.shape[2]
    frames = tokens.shape[0]
    saved = [((rows, width), F32)] + saved_shapes(sz)
    whole_frames = (frame_share, tubes, patches)
    count = len(piece_list(sz, blocks)) * 4 * (heads - 1) + 2 + 2 * (heads - 1) + 2 * heads - 1
    hbm, vmem = pl.BlockSpec(memory_space=pl.ANY), pl.BlockSpec(memory_space=pltpu.VMEM)
    full = ((heads, sz.block_rows, width), LOW)
    mixed = (frames, tube_share, patches, width)
    out = pl.pallas_call(
        lambda *refs: forward_kernel(sz, blocks, frame_share, tube_share, *refs),
        name="forward_both",
        out_shape=structs([full] * blocks + saved * blocks + [(whole_frames, jnp.int32)]),
        in_specs=[hbm] * 8 + [vmem] * 5,
        out_specs=[hbm] * (blocks + 7 * blocks) + [vmem],
        scratch_shapes=vmems(
            [full] * blocks
            + [
                (whole_frames + (width,), LOW),
                ((heads,) + b_qv.shape, F32),
                ((heads,) + b_up.shape, F32),
            ]
            + saved
            + [
                ((rows, width), F32),
                (whole_frames + (width,), LOW),
                (mixed, LOW),
            ]
        )
        + [
            pltpu.SemaphoreType.DMA((count,)),
            pltpu.SemaphoreType.DMA((count,)),
            pltpu.SemaphoreType.DMA((16,)),
            pltpu.SemaphoreType.DMA((64,)),
        ],
        compiler_params=pltpu.CompilerParams(
            collective_id=0, has_side_effects=True, vmem_limit_bytes=62 * 2**20
        ),
    )(*weights, tokens, marks, b_qv, b_up, embed, gains, shifts, b_out, b_down)
    fulls, out = out[:blocks], out[blocks:]
    saved = [out[7 * b : 7 * b + 7] for b in range(blocks)]
    return fulls, saved, out[-1]


class Line:
    def __init__(self, place, send_sem, recv_sem, region, own=None):
        self.place, self.send_sem, self.recv_sem, self.region = place, send_sem, recv_sem, region
        self.own = own
        self.steps = place.heads - 1

    def moves(self, step):
        z, last = self.place.z, self.place.heads - 1
        return [
            ((z >= step) & (z < last), z - step, 1, z > step, z - 1 - step, 2 * step),
            ((z <= last - step) & (z > 0), z + step, -1, z < last - step, z + 1 + step, 2 * step + 1),
        ]

    def copy(self, block, way, n):
        return pltpu.make_async_remote_copy(
            self.own if n < 2 and self.own is not None else self.region(block),
            self.region(block),
            self.send_sem.at[n],
            self.recv_sem.at[n],
            device_id=self.place.head(way),
            device_id_type=MESH,
        )

    def start(self, step):
        for sends, block, way, _, _, n in self.moves(step):
            pl.when(sends)(lambda block=block, way=way, n=n: self.copy(block, way, n).start())

    def arrive(self, step):
        for _, _, way, gets, block, n in self.moves(step):
            pl.when(gets)(lambda block=block, way=way, n=n: self.copy(block, way, n).wait_recv())

    def finish(self):
        for step in range(self.steps):
            for sends, block, way, _, _, n in self.moves(step):
                pl.when(sends)(lambda block=block, way=way, n=n: self.copy(block, way, n).wait_send())


class Reduction:
    def __init__(self, place, moves, grads, out, out_row, rows, bufs, final_buf, final_sem):
        q = rows // 8
        self.q, self.place, self.moves, self.grads = q, place, moves, grads
        self.core_buf, self.first_buf, self.second_buf, self.head_buf = bufs
        self.final_buf, self.final_sem = final_buf, final_sem
        c, i, j, z, heads = place.core, place.i, place.j, place.z, place.heads
        cut = lambda start, size: pl.ds(pl.multiple_of(start * q, q), size * q)
        row = lambda start, size: out.at[pl.ds(pl.multiple_of(out_row + start * q, q), size * q), :]
        self.kept, self.given = cut(4 * c, 4), cut(4 * (1 - c), 4)
        self.part, self.subpart = cut(2 * i, 2), cut(j, 1)
        shards = range(heads)
        self.core = moves.phase(
            [(grads.at[s % 2, self.given, :], self.core_buf.at[s], self.core_buf.at[s], place.other) for s in shards]
        )
        self.first = moves.phase(
            [(self.core_buf.at[s, cut(2 * (1 - i), 2), :], self.first_buf.at[s], self.first_buf.at[s], place.first) for s in shards]
        )
        self.second = moves.phase(
            [(self.first_buf.at[s, cut(1 - j, 1), :], self.second_buf.at[s], self.second_buf.at[s], place.second) for s in shards]
        )
        self.to_right = moves.reserve()
        self.to_left = moves.reserve()
        a, mine = 4 * c, 2 * i + j
        self.share_second = moves.phase([(final_buf, row(a + mine, 1), row(a + 2 * i + 1 - j, 1), place.second)])
        self.share_first = moves.phase([(row(a + 2 * i, 2), row(a + 2 * i, 2), row(a + 2 * (1 - i), 2), place.first)])
        self.share_core = moves.phase([(row(a, 4), row(a, 4), row(4 - a, 4), place.other)])
        self.keep = pltpu.make_async_copy(final_buf, row(a + mine, 1), final_sem)

    def give(self, s):
        self.moves.start([self.core[s]])

    def step_first(self, s):
        self.moves.arrive([self.core[s]])
        self.core_buf[s] = self.core_buf[s] + self.grads[s % 2, self.kept, :]
        self.moves.start([self.first[s]])

    def step_second(self, free_sem=None):
        for s in range(self.place.heads):
            self.moves.arrive([self.first[s]])
            self.first_buf[s] = self.first_buf[s] + self.core_buf[s, self.part, :]
            self.moves.start([self.second[s]])
        if free_sem is not None:
            self.moves.left(self.first)
            pl.semaphore_signal(free_sem, inc=1, device_id=self.place.other, device_id_type=MESH)

    def step_heads(self):
        for s in range(self.place.heads):
            self.moves.arrive([self.second[s]])
            self.second_buf[s] = self.second_buf[s] + self.first_buf[s, self.subpart, :]
        last = self.place.heads - 1
        pl.when(self.place.z == 0)(functools.partial(self.send_right, 0))
        pl.when(self.place.z == last)(functools.partial(self.send_left, last))

    def right_copy(self, z):
        return self.moves.one(
            self.to_right, self.second_buf.at[z + 1 :], self.head_buf.at[z + 2 :], self.place.head(1)
        )

    def left_copy(self, z):
        return self.moves.one(self.to_left, self.second_buf.at[:z], self.head_buf.at[:z], self.place.head(-1))

    def send_right(self, z):
        self.right_copy(z).start()

    def send_left(self, z):
        self.left_copy(z).start()

    def from_left(self, z):
        self.right_copy(z - 1).wait_recv()
        for s in range(z + 1, self.place.heads):
            self.second_buf[s] = self.second_buf[s] + self.head_buf[s + 1]
        if z < self.place.heads - 1:
            self.send_right(z)

    def from_right(self, z):
        self.left_copy(z + 1).wait_recv()
        for s in range(z):
            self.second_buf[s] = self.second_buf[s] + self.head_buf[s]
        if z > 0:
            self.send_left(z)

    def step_pass(self, hop):
        heads = self.place.heads
        pl.when(self.place.z == hop)(functools.partial(self.from_left, hop))
        pl.when(self.place.z == heads - 1 - hop)(functools.partial(self.from_right, heads - 1 - hop))

    def step_share(self):
        z, last = self.place.z, self.place.heads - 1
        self.step_pass(last)

        @pl.when(z == 0)
        def _():
            self.final_buf[...] = self.second_buf[0] + self.head_buf[0]

        @pl.when(z == last)
        def _():
            self.final_buf[...] = self.second_buf[last] + self.head_buf[last + 1]

        @pl.when((z > 0) & (z < last))
        def _():
            total = self.second_buf[z].astype(F32) + self.head_buf[z].astype(F32)
            self.final_buf[...] = (total + self.head_buf[z + 1].astype(F32)).astype(LOW)

        self.keep.start()
        self.moves.start(self.share_second)

    def finish(self):
        last = self.place.heads - 1
        for z in range(last + 1):
            if z < last:
                pl.when(self.place.z == z)(lambda z=z: self.right_copy(z).wait_send())
            if z > 0:
                pl.when(self.place.z == z)(lambda z=z: self.left_copy(z).wait_send())

    def step_share_first(self):
        self.keep.wait()
        self.moves.arrive(self.share_second)
        self.moves.start(self.share_first)

    def step_share_core(self):
        self.moves.arrive(self.share_first)
        self.moves.start(self.share_core)

    def end(self):
        self.moves.arrive(self.share_core)


SMALL_ROWS = 48
GAIN_ROW, SHIFT_ROW, BOUT_ROW, BDOWN_ROW, BUP_ROW, BQV_ROW = 1, 5, 9, 11, 16, 24


def backward_kernel(sz, blocks, frame_share, tube_share, *refs):
    fulls, refs = refs[:blocks], refs[blocks:]
    saved, refs = [refs[7 * b : 7 * b + 7] for b in range(blocks)], refs[7 * blocks :]
    (cotangent, marks, gains, b_down), refs = refs[:4], refs[4:]
    (out_result, out_tokens, out_grads, out_small), refs = refs[:4], refs[4:]
    (
        wm, act, wa, t, p, m, n2, n, x, low, dn, dm, du, do, dq, dk, dv, cot, dx_low, back, result,
        grads, core_buf, first_buf, second_buf, head_buf, final_buf, small, small_in, small_heads, small_last,
        send_sem, recv_sem, line_sem, load_sem, copy_sem, final_sem, free_sem,
    ) = refs
    heads, width, length = sz.shards, sz.width, sz.length
    place = Place(heads)
    moves = Moves(send_sem, recv_sem)
    loads = Saves(copy_sem)
    yy, z = place.y, place.z
    tubes = cotangent.shape[1]

    def step_loads(b, kind, s):
        slot = s % 2
        if kind == MLP_BACK:
            pairs = [(fulls[b].at[s, pl.ds(sz.up_row, 2 * width), :], wm.at[slot]), (saved[b][6].at[s], act.at[slot])]
            base = 0
        else:
            pairs = [
                (fulls[b].at[s, pl.ds(0, sz.up_row), :], wa.at[slot]),
                (saved[b][2].at[s], t.at[slot]),
                (saved[b][3].at[s], p.at[slot]),
            ]
            base = 4
        return [
            pltpu.make_async_copy(src, dst, load_sem.at[base + slot * len(pairs) + i]) for i, (src, dst) in enumerate(pairs)
        ]

    steps = [(b, kind, s) for b in (1, 0) for kind in (MLP_BACK, ATTN_BACK) for s in range(heads)]

    def fetch(i):
        if i < len(steps):
            for copy in step_loads(*steps[i]):
                copy.start()

    def ready(i):
        for copy in step_loads(*steps[i]):
            copy.wait()
        fetch(i + 1)

    first_load = loads.start(cotangent.at[:, pl.ds(z * tube_share, tube_share)], cot)
    fetch(0)
    norm_loads = {1: [loads.start(saved[1][4], m), loads.start(saved[1][5], n2)]}
    later_loads = {1: [loads.start(saved[1][1], n), loads.start(saved[1][0], x)]}
    small[...] = jnp.zeros_like(small)
    greet(place.all_peers())

    red = {}
    for b in (1, 0):
        for k in (DOWN, UP, ATTN):
            base = b * sz.block_rows + (sz.down_row, sz.up_row, 0)[k]
            red[b, k] = Reduction(
                place,
                moves,
                grads.at[k],
                out_grads,
                base,
                width,
                (core_buf.at[k], first_buf.at[b, k], second_buf.at[b, k], head_buf.at[b, k]),
                final_buf.at[b, k],
                final_sem.at[b * 3 + k],
            )
    tube_region = lambda block: out_result.at[:, pl.ds(block * tube_share, tube_share)]
    line = Line(place, line_sem.at[0], line_sem.at[1], tube_region, result)
    spread = moves.phase(
        [
            (
                dx_low.at[pl.ds((2 * tz + ty) * frame_share, frame_share)],
                back.at[:, pl.ds((heads * yy + z) * tube_share, tube_share)],
                back.at[:, pl.ds((heads * ty + fz) * tube_share, tube_share)],
                target,
            )
            for ty, tz, fz, target in [
                (yy, lax.rem(z + d, heads), lax.rem(z + heads - d, heads), place.head(d)) for d in range(1, heads)
            ]
            + [
                (1 - yy, lax.rem(z + d, heads), lax.rem(z + heads - d, heads), place.across(d)) for d in range(heads)
            ]
        ]
    )

    first_load.wait()
    frames = cot.shape[0]
    for j in range(tube_share):
        low[j * length : (j + 1) * length, :] = cot[:, j].reshape(length, width)
    own_result = []

    def send_result():
        for j in range(tube_share):
            at = slice(j * length, (j + 1) * length)
            result[:, j] = dm[at, :].astype(LOW).reshape(frames, length // frames, width)
        line.start(0)
        own_result.append(loads.start(result, tube_region(z)))

    def mlp_start():
        begin_mlp(1)
        grads[DOWN, 0] = dot(act[0, 0], low[...], TN).astype(LOW)
        red[1, DOWN].give(0)

    def row(r, columns=None):
        return small.at[r : r + 1, :] if columns is None else small.at[r : r + 1, 0:columns]

    def begin_mlp(b):
        row(BDOWN_ROW + b)[...] = jnp.sum(low[...].astype(F32), 0, keepdims=True)
        dn[...] = jnp.zeros_like(dn)
        for copy in norm_loads[b]:
            copy.wait()
        if b:
            dm[...] = m[...] + b_down[b : b + 1, :]
        ready((1 - b) * 2 * heads)

    def mlp(b, s):
        if s:
            ready((1 - b) * 2 * heads + s)
        elif b == 0:
            begin_mlp(b)
        for k in (DOWN, UP):
            if s >= 2:
                moves.left([red[b, k].core[s - 2]])
            elif b == 0:
                moves.left([red[1, k].core[s + heads - 2]])
        first = (b, s) == (1, 0)
        slot = s % 2
        backward_mlp(
            sz, wm.at[slot], act.at[slot], low, n2, du, dn, None if first else grads.at[DOWN, slot], grads.at[UP, slot],
            row(BUP_ROW + b * heads + s),
        )
        for k in (UP,) if first else (DOWN, UP):
            if s == 0 and b == 0:
                pl.semaphore_wait(free_sem.at[k], 1)
            red[b, k].give(s)
        if b:
            dm[...] += dot(act[slot, 0], wm[slot, width : width + sz.units, :], NN)

    def mlp_norm(b):
        norm_back_rows(
            sz, m, gains[b, 1:2, :], dn, low, dm, row(GAIN_ROW + 2 * b + 1), row(SHIFT_ROW + 2 * b + 1), row(BOUT_ROW + b), low
        )
        if b:
            norm_loads[0] = [loads.start(saved[0][4], m), loads.start(saved[0][5], n2)]

    def attention(b, s):
        if s == 0:
            dn[...] = jnp.zeros_like(dn)
            for copy in later_loads[b]:
                copy.wait()
        ready((1 - b) * 2 * heads + heads + s)
        if s >= 2:
            moves.left([red[b, ATTN].core[s - 2]])
        elif b == 0:
            moves.left([red[1, ATTN].core[s + heads - 2]])
        r = BQV_ROW + 2 * (b * heads + s)
        backward_attention(
            sz, wa.at[s % 2], t.at[s % 2], p.at[s % 2], low, n, do, dq, dk, dv, dn, grads.at[ATTN, s % 2],
            row(r, sz.columns), row(r + 1, sz.columns),
        )
        if s == 0 and b == 0:
            pl.semaphore_wait(free_sem.at[ATTN], 1)
        red[b, ATTN].give(s)

    own_spread = []

    def attention_norm(b):
        norm_back_rows(
            sz, x, gains[b, 0:1, :], dn, dm, dm, row(GAIN_ROW + 2 * b), row(SHIFT_ROW + 2 * b), None, None
        )
        if b:
            later_loads[0] = [loads.start(saved[0][1], n), loads.start(saved[0][0], x)]
            for j in range(tube_share):
                dx_low[:, j] = dm[j * length : (j + 1) * length, :].astype(LOW).reshape(frames, length // frames, width)
            moves.start(spread)
            own_spread.append(
                loads.start(
                    dx_low.at[pl.ds((2 * z + yy) * frame_share, frame_share)],
                    back.at[:, pl.ds((heads * yy + z) * tube_share, tube_share)],
                )
            )
            return
        mark = masked_rows(sz.rows, marks)
        grad = dm[...]
        row(0)[...] = jnp.sum(jnp.where(mark, grad, 0.0), 0, keepdims=True)
        back[...] = jnp.where(mark, 0.0, grad).astype(LOW).reshape(back.shape)
        moves.start(cross)
        own_copy = loads.start(back.at[:, here], own_frames(z))
        moves.start(small_steps[0])
        own_copy.wait()
        own_line.start(0)

    def second_upstream():
        moves.arrive(spread)
        for copy in own_spread:
            copy.wait()
        low[...] = back[...].reshape(sz.rows, width)

    here, there = pl.ds(yy * tubes, tubes), pl.ds((1 - yy) * tubes, tubes)
    own_frames = lambda block: out_tokens.at[pl.ds((2 * block + yy) * frame_share, frame_share)]
    far_frames = lambda block: out_tokens.at[pl.ds((2 * block + 1 - yy) * frame_share, frame_share)]
    cross = moves.phase([(back.at[:, there], own_frames(z), far_frames(z), place.across(0))])
    own_line = Line(place, line_sem.at[2], line_sem.at[3], own_frames)
    far_line = Line(place, line_sem.at[4], line_sem.at[5], far_frames)

    def start_far():
        moves.arrive(cross)
        far_line.start(0)

    half = SMALL_ROWS // 2
    part = pl.ds(pl.multiple_of(place.core * half, half), half)
    far_part = pl.ds(pl.multiple_of((1 - place.core) * half, half), half)
    small_steps = [
        moves.phase([(small, small_in.at[i], small_in.at[i], target)])
        for i, target in enumerate((place.other, place.first, place.second))
    ]
    small_z = moves.phase(
        [(small.at[part], small_heads.at[d - 1], small_heads.at[d - 1], place.head(d)) for d in range(1, heads)]
    )
    small_end = moves.phase([(small_last.at[part], small_last.at[part], small_last.at[far_part], place.other)])

    def add_small(i):
        moves.arrive(small_steps[i])
        moves.left(small_steps[i])
        small[...] += small_in[i]
        moves.start(small_steps[i + 1] if i + 1 < len(small_steps) else small_z)

    def add_small_heads():
        moves.arrive(small_z)
        total = small[part, :]
        for d in range(heads - 1):
            total += small_heads[d]
        small_last[part, :] = total
        moves.start(small_end)

    def end_small():
        moves.arrive(small_end)
        out_small[...] = small_last[...]

    def pass_on(way, step):
        way.arrive(step)
        if step + 1 < way.steps:
            way.start(step + 1)

    todo = {(UPSTREAM,): second_upstream, (MLP_START,): mlp_start, (SEND_RESULT,): send_result, (FAR_START,): start_far, (SMALL, 3): add_small_heads, (SMALL, 4): end_small}
    for i in range(3):
        todo[SMALL, i] = functools.partial(add_small, i)
    for name, way in ((RESULT_LINE, line), (OWN_LINE, own_line), (FAR_LINE, far_line)):
        for step in range(way.steps):
            todo[name, step] = functools.partial(pass_on, way, step)
    for b in range(blocks):
        todo[MLP_NORM, b] = functools.partial(mlp_norm, b)
        todo[ATTN_NORM, b] = functools.partial(attention_norm, b)
        for s in range(heads):
            todo[MLP_BACK, b, s] = functools.partial(mlp, b, s)
            todo[ATTN_BACK, b, s] = functools.partial(attention, b, s)
        for k in (DOWN, UP, ATTN):
            each = red[b, k]
            for s in range(heads):
                todo[ADD_CORE, b, k, s] = functools.partial(each.step_first, s)
            todo[ADD_FIRST, b, k] = functools.partial(each.step_second, free_sem.at[k] if b else None)
            todo[ADD_SECOND, b, k] = each.step_heads
            for hop in range(1, heads - 1):
                todo[PASS_HEADS, b, k, hop] = functools.partial(each.step_pass, hop)
            todo[ADD_HEADS, b, k] = each.step_share
            todo[SHARE_FIRST, b, k] = each.step_share_first
            todo[SHARE_CORE, b, k] = each.step_share_core
            todo[ARRIVED, b, k] = each.end
    for step in BACKWARD_ORDER:
        todo[step]()
    for copy in own_result:
        copy.wait()
    for each in (line, own_line, far_line, *red.values()):
        each.finish()
    moves.finish()


def run_backward(sz, blocks, frame_share, tube_share, fulls, saved, cotangent, marks, gains, b_down):
    heads, width, rows, cols = sz.shards, sz.width, sz.rows, sz.columns
    frames, tubes, patches = cotangent.shape[:3]
    hbm, vmem = pl.BlockSpec(memory_space=pl.ANY), pl.BlockSpec(memory_space=pltpu.VMEM)
    q = width // 8
    local = (frame_share, 2 * tubes, patches, width)
    mixed = (frames, tube_share, patches, width)
    kinds = 3 * blocks
    count = kinds * (3 * heads + 3 + 2) + 2 * heads - 1 + 1 + 4 + heads - 1
    flat = [array for per in saved for array in per]
    return pl.pallas_call(
        lambda *refs: backward_kernel(sz, blocks, frame_share, tube_share, *refs),
        name="backward_both",
        out_shape=structs(
            [
                (cotangent.shape, LOW),
                (cotangent.shape, LOW),
                ((blocks * sz.block_rows, width), LOW),
                ((SMALL_ROWS, width), F32),
            ]
        ),
        in_specs=[hbm] * (blocks + len(flat) + 1) + [vmem] * 3,
        out_specs=[hbm] * 3 + [vmem],
        scratch_shapes=vmems(
            [
                ((2, 2 * width, width), LOW),
                ((2, 2, rows, sz.units), LOW),
                ((2, sz.up_row, width), LOW),
                ((2, 4, rows, cols), LOW),
                ((2, sz.sequences * sz.heads, sz.length, sz.length), LOW),
                ((rows, width), F32),
                ((rows, width), LOW),
                ((rows, width), LOW),
                ((rows, width), F32),
                ((rows, width), LOW),
                ((rows, width), F32),
                ((rows, width), F32),
                ((rows, sz.units), LOW),
                ((rows, cols), LOW),
                ((rows, cols), LOW),
                ((rows, cols), LOW),
                ((rows, cols), LOW),
                (mixed, LOW),
                (mixed, LOW),
                (local, LOW),
                (mixed, LOW),
                ((3, 2, width, width), LOW),
                ((3, heads, 4 * q, width), LOW),
                ((blocks, 3, heads, 2 * q, width), LOW),
                ((blocks, 3, heads, q, width), LOW),
                ((blocks, 3, heads + 1, q, width), LOW),
                ((blocks, 3, q, width), LOW),
                ((SMALL_ROWS, width), F32),
                ((3, SMALL_ROWS, width), F32),
                ((heads - 1, SMALL_ROWS // 2, width), F32),
                ((SMALL_ROWS, width), F32),
            ]
        )
        + [
            pltpu.SemaphoreType.DMA((count,)),
            pltpu.SemaphoreType.DMA((count,)),
            pltpu.SemaphoreType.DMA((6, 2 * (heads - 1))),
            pltpu.SemaphoreType.DMA((10,)),
            pltpu.SemaphoreType.DMA((24,)),
            pltpu.SemaphoreType.DMA((kinds,)),
            pltpu.SemaphoreType.REGULAR((3,)),
        ],
        compiler_params=pltpu.CompilerParams(
            collective_id=1, has_side_effects=True, vmem_limit_bytes=63 * 2**20
        ),
    )(*fulls, *flat, cotangent, marks, gains, b_down)


def finish(sz, blocks, output, tokens, whole, small):
    heads, width, cols, units = sz.shards, sz.width, sz.columns, sz.units
    parts = 4

    def kernel(o_in, t_in, a_in, c_in, u_in, d_in, small, o_out, t_out, embed, gain, shift, a, bqv, c, bout, u, bup, d, bdown):
        for src, dst in ((o_in, o_out), (t_in, t_out)):
            dst[...] = src[...]
        for src, dst in ((a_in, a), (c_in, c), (u_in, u), (d_in, d)):
            dst[...] = src[...].astype(F32)

        @pl.when((pl.program_id(0) == 0) & (pl.program_id(1) == 0))
        def _():
            head = lax.axis_index("head")
            embed[...] = small[0, :]
            for b in range(blocks):
                for norm in range(2):
                    gain[b, norm : norm + 1, :] = small[GAIN_ROW + 2 * b + norm : GAIN_ROW + 2 * b + norm + 1, :]
                    shift[b, norm : norm + 1, :] = small[SHIFT_ROW + 2 * b + norm : SHIFT_ROW + 2 * b + norm + 1, :]
                bout[b : b + 1, :] = small[BOUT_ROW + b : BOUT_ROW + b + 1, :]
                bdown[b : b + 1, :] = small[BDOWN_ROW + b : BDOWN_ROW + b + 1, :]
                bup[b : b + 1, :] = small[pl.ds(BUP_ROW + b * heads + head, 1), :]
                for i in range(2):
                    bqv[b, i : i + 1, :] = small[pl.ds(BQV_ROW + 2 * (b * heads + head) + i, 1), 0:cols]

    def rows(size, first):
        return pl.BlockSpec((1, size // parts, width), lambda b, i: (b, first * parts // size + i, 0))

    def kept(*shape):
        return pl.BlockSpec(shape, lambda b, i: (0,) * len(shape))

    share = output.shape[0] // (blocks * parts)
    cut = pl.BlockSpec((share,) + output.shape[1:], lambda b, i: (b * parts + i, 0, 0, 0))
    pair, triple = (blocks, width), (blocks, 2, width)
    sizes = (3 * cols, cols, width, units)
    shapes = [(output.shape, LOW), (output.shape, LOW)] + [
        (s, F32)
        for s in (
            (width,),
            triple,
            triple,
            (blocks, sizes[0], width),
            (blocks, 2, cols),
            (blocks, sizes[1], width),
            pair,
            (blocks, sizes[2], width),
            pair,
            (blocks, sizes[3], width),
            pair,
        )
    ]
    out = [rows(size, 0) for size in sizes]
    return pl.pallas_call(
        kernel,
        name="finish",
        grid=(blocks, parts),
        out_shape=structs(shapes),
        in_specs=[
            cut,
            cut,
            rows(sizes[0], 0),
            rows(sizes[1], sz.out_row),
            rows(sizes[2], sz.up_row),
            rows(sizes[3], sz.down_row),
            kept(SMALL_ROWS, width),
        ],
        out_specs=[
            cut,
            cut,
            kept(width),
            kept(*triple),
            kept(*triple),
            out[0],
            kept(blocks, 2, cols),
            out[1],
            kept(*pair),
            out[2],
            kept(*pair),
            out[3],
            kept(*pair),
        ],
        compiler_params=pltpu.CompilerParams(vmem_limit_bytes=62 * 2**20),
    )(output, tokens, whole, whole, whole, whole, small)


def fits_local(arrays, clip_size, tube_size, head_size):
    clips, frames, tubes = arrays[0].shape[:3]
    width = arrays[0].shape[-1]
    columns, units = arrays[5].shape[3] // head_size, arrays[9].shape[2] // head_size
    devices = tube_size * head_size
    return (
        (clips, clip_size, tube_size) == (4, 4, 2)
        and frames % devices == 0
        and frames == tubes
        and head_size % 2 == 0
        and width == 4 * columns == units
        and width % 384 == 0
        and columns % HD == 0
    )


def on_device_local(
    tokens,
    token_mask,
    mask_embed,
    norm_gains,
    norm_shifts,
    w_qkv,
    b_qv,
    w_out,
    b_out,
    w_up,
    b_up,
    w_down,
    b_down,
    cotangent,
):
    _, frames, tubes, patches, width = tokens.shape
    tube_size, heads = lax.axis_size("tube"), lax.axis_size("head")
    head = lax.axis_index("head")
    blocks, columns, units = w_qkv.shape[0], w_qkv.shape[-1], w_up.shape[-1]
    frame_share = frames // (tube_size * heads)
    tube_share = tubes // heads
    rows = frame_share * tube_size * tubes * patches
    sz = Sizes(rows, width, heads, columns, units, rows // frame_share)

    full, saved, mark_frames = run_forward(
        sz,
        blocks,
        frame_share,
        tube_share,
        (w_qkv.transpose(0, 2, 3, 1).reshape(blocks, 3 * columns, width), w_out, w_up, w_down),
        tokens[0],
        token_mask[0],
        b_qv,
        b_up,
        mask_embed,
        norm_gains,
        norm_shifts,
        b_out,
        b_down,
    )
    output, grad_tokens, whole, small = run_backward(
        sz, blocks, frame_share, tube_share, full, saved, cotangent[0], mark_frames, norm_gains, b_down
    )
    out = finish(sz, blocks, output, grad_tokens, whole.reshape(blocks, sz.block_rows, width), small)
    output, grad_tokens, embed, gains, shifts, qkv_grad, bqv, out_grad, bout, up_grad, bup, down_grad, bdown = out
    qkv_grad = qkv_grad.reshape(blocks, 3, columns, width).transpose(0, 3, 1, 2)
    return (
        output[None],
        grad_tokens[None],
        embed,
        gains,
        shifts,
        qkv_grad,
        bqv,
        out_grad,
        bout,
        up_grad,
        bup,
        down_grad,
        bdown,
    )


def solution(mesh):
    sizes = [mesh.shape[name] for name in ("clip", "tube", "head")]

    def run(*arrays):
        on_device = on_device_local if fits_local(arrays, *sizes) else on_device_sums
        return on_mesh(on_device, mesh)(*arrays)

    return run


def on_mesh(on_device, mesh):
    return jax.shard_map(
        on_device,
        mesh=mesh,
        in_specs=(
            P("clip", None, "tube", None, None),
            P("clip", None, "tube", None),
            P(),
            P(),
            P(),
            P(None, None, None, "head"),
            P(None, None, "head"),
            P(None, "head", None),
            P(),
            P(None, None, "head"),
            P(None, "head"),
            P(None, "head", None),
            P(),
            P("clip", None, "tube", None, None),
        ),
        out_specs=(
            P("clip", None, "tube", None, None),
            P("clip", None, "tube", None, None),
            P(),
            P(),
            P(),
            P(None, None, None, "head"),
            P(None, None, "head"),
            P(None, "head", None),
            P(),
            P(None, None, "head"),
            P(None, "head"),
            P(None, "head", None),
            P(),
        ),
        check_vma=False,
    )
```

```python
import functools

import jax
import jax.numpy as jnp
from jax import lax
from jax.experimental import pallas as pl
from jax.experimental.pallas import tpu as pltpu
from jax.sharding import PartitionSpec as P

F32 = jnp.float32
LOW = jnp.bfloat16
MESH = pl.DeviceIdType.MESH

HD = 64


EPS = 1e-05


def norm_forward(values, gain_vector, shift_vector):
    centre = values - jnp.mean(values, -1, keepdims=True)
    inverse = lax.rsqrt(jnp.mean(centre * centre, -1, keepdims=True) + EPS)
    normal = centre * inverse
    return (normal * gain_vector + shift_vector, normal, inverse)


def norm_backward(grad_out, normal, inverse, gain_vector):
    grad_normal = grad_out * gain_vector
    grad_in = inverse * (
        grad_normal
        - jnp.mean(grad_normal, -1, keepdims=True)
        - normal * jnp.mean(grad_normal * normal, -1, keepdims=True)
    )
    return (grad_in, jnp.sum(grad_out * normal, 0), jnp.sum(grad_out, 0))


def row_total(partial_sum):
    return lax.psum(partial_sum.astype(jnp.bfloat16), "head").astype(jnp.float32)


def input_total(partial_sum):
    return lax.psum(partial_sum.astype(jnp.bfloat16), "head").astype(jnp.float32)


def split_heads(tensor, batch_count, length):
    return tensor.reshape(batch_count, length, tensor.shape[-1] // HD, HD)


def attend(queries, key_rows, value_rows):
    scores = jnp.einsum(
        "bshe,bthe->bhst", queries, key_rows, preferred_element_type=jnp.float32
    ) * HD ** (-0.5)
    maximum = jnp.max(scores, -1, keepdims=True)
    exponent = jnp.exp(scores - maximum)
    denominator = jnp.sum(exponent, -1, keepdims=True)
    weights_soft = (exponent / denominator).astype(jnp.bfloat16)
    mixture = jnp.einsum(
        "bhst,bthe->bshe", weights_soft, value_rows, preferred_element_type=jnp.float32
    )
    return (mixture.astype(jnp.bfloat16), maximum + jnp.log(denominator))


def attend_back(queries, key_rows, value_rows, log_total, grad_mixture):
    scaling = HD ** (-0.5)
    scores = (
        jnp.einsum("bshe,bthe->bhst", queries, key_rows, preferred_element_type=jnp.float32)
        * scaling
    )
    weights_soft = jnp.exp(scores - log_total)
    grad_weights = jnp.einsum(
        "bshe,bthe->bhst", grad_mixture, value_rows, preferred_element_type=jnp.float32
    )
    grad_values = jnp.einsum(
        "bhst,bshe->bthe",
        weights_soft.astype(jnp.bfloat16),
        grad_mixture,
        preferred_element_type=jnp.float32,
    )
    grad_scores = (
        weights_soft * (grad_weights - jnp.sum(weights_soft * grad_weights, -1, keepdims=True))
    ).astype(jnp.bfloat16)
    grad_queries = (
        jnp.einsum("bhst,bthe->bshe", grad_scores, key_rows, preferred_element_type=jnp.float32)
        * scaling
    )
    grad_keys = (
        jnp.einsum("bhst,bshe->bthe", grad_scores, queries, preferred_element_type=jnp.float32)
        * scaling
    )
    return (grad_queries, grad_keys, grad_values)


def mixer_forward(block_kind, queries, key_rows, value_rows):
    clip_count, frame_count, tube_count, patch_count, columns = queries.shape
    if block_kind == 1:
        reorder = (0, 2, 1, 3, 4)
        pieces = [
            split_heads(
                tensor.transpose(reorder), clip_count * tube_count, frame_count * patch_count
            )
            for tensor in (queries, key_rows, value_rows)
        ]
        mixture, log_total = attend(pieces[0], pieces[1], pieces[2])
        mixture = mixture.reshape(
            clip_count, tube_count, frame_count, patch_count, columns
        ).transpose(reorder)
        return (mixture, (pieces, log_total))
    key_all, value_all = (
        lax.all_gather(key_rows, "tube", axis=2, tiled=True),
        lax.all_gather(value_rows, "tube", axis=2, tiled=True),
    )
    tube_all = key_all.shape[2]
    pieces = [
        split_heads(queries, clip_count * frame_count, tube_count * patch_count),
        split_heads(key_all, clip_count * frame_count, tube_all * patch_count),
        split_heads(value_all, clip_count * frame_count, tube_all * patch_count),
    ]
    mixture, log_total = attend(pieces[0], pieces[1], pieces[2])
    return (
        mixture.reshape(clip_count, frame_count, tube_count, patch_count, columns),
        (pieces, log_total),
    )


def mixer_backward(block_kind, retained, grad_mixture):
    pieces, log_total = retained
    clip_count, frame_count, tube_count, patch_count, columns = grad_mixture.shape
    if block_kind == 1:
        reorder = (0, 2, 1, 3, 4)
        moved = split_heads(
            grad_mixture.transpose(reorder), clip_count * tube_count, frame_count * patch_count
        )
        gradients = attend_back(pieces[0], pieces[1], pieces[2], log_total, moved)
        return [
            grad.astype(jnp.bfloat16)
            .reshape(clip_count, tube_count, frame_count, patch_count, columns)
            .transpose(reorder)
            for grad in gradients
        ]
    gradients = attend_back(
        pieces[0],
        pieces[1],
        pieces[2],
        log_total,
        split_heads(grad_mixture, clip_count * frame_count, tube_count * patch_count),
    )
    tube_all = pieces[1].shape[1] // patch_count
    grad_keys = gradients[1].reshape(clip_count, frame_count, tube_all, patch_count, columns)
    grad_values = gradients[2].reshape(clip_count, frame_count, tube_all, patch_count, columns)
    grad_keys, grad_values = (
        lax.psum_scatter(
            grad_keys.astype(jnp.bfloat16), "tube", scatter_dimension=2, tiled=True
        ).astype(jnp.float32),
        lax.psum_scatter(
            grad_values.astype(jnp.bfloat16), "tube", scatter_dimension=2, tiled=True
        ).astype(jnp.float32),
    )
    grad_queries = (
        gradients[0]
        .astype(jnp.bfloat16)
        .reshape(clip_count, frame_count, tube_count, patch_count, columns)
    )
    return [grad_queries, grad_keys.astype(jnp.bfloat16), grad_values.astype(jnp.bfloat16)]


def block_forward(block_kind, residual, layout, weights):
    gains, shifts, w_qkv, b_qv, w_out, b_out, w_up, b_up, w_down, b_down = weights
    columns = w_qkv.shape[-1]
    grid_shape = layout[:-1] + (columns,)
    normed_share, first_normal, first_inverse = norm_forward(residual, gains[0], shifts[0])
    normed = normed_share.astype(jnp.bfloat16)
    projected = jnp.einsum("rd,dcj->rcj", normed, w_qkv, preferred_element_type=jnp.float32)
    queries = (projected[:, 0] + b_qv[0]).astype(jnp.bfloat16).reshape(grid_shape)
    key_rows = projected[:, 1].astype(jnp.bfloat16).reshape(grid_shape)
    value_rows = (projected[:, 2] + b_qv[1]).astype(jnp.bfloat16).reshape(grid_shape)
    mixture, retained = mixer_forward(block_kind, queries, key_rows, value_rows)
    mixture = mixture.reshape(-1, columns)
    middle = (
        residual + row_total(jnp.dot(mixture, w_out, preferred_element_type=jnp.float32)) + b_out
    )
    second_share, second_normal, second_inverse = norm_forward(middle, gains[1], shifts[1])
    normed_two = second_share.astype(jnp.bfloat16)
    hidden = jnp.dot(normed_two, w_up, preferred_element_type=jnp.float32) + b_up
    active = jax.nn.gelu(hidden).astype(jnp.bfloat16)
    stored = (
        normed,
        first_normal,
        first_inverse,
        retained,
        mixture,
        normed_two,
        second_normal,
        second_inverse,
        hidden,
    )
    return (middle, active, stored)


def block_output(middle, active, w_down, b_down):
    return middle + row_total(jnp.dot(active, w_down, preferred_element_type=jnp.float32)) + b_down


def block_backward(block_kind, residual, layout, weights, grad_rows):
    gains, shifts, w_qkv, b_qv, w_out, b_out, w_up, b_up, w_down, b_down = weights
    middle, active, stored = block_forward(block_kind, residual, layout, weights)
    (
        normed,
        first_normal,
        first_inverse,
        retained,
        mixture,
        normed_two,
        second_normal,
        second_inverse,
        hidden,
    ) = stored
    columns = w_qkv.shape[-1]
    grad_low = grad_rows.astype(jnp.bfloat16)
    grad_wdown = jnp.dot(active.T, grad_low, preferred_element_type=jnp.float32)
    grad_bdown = jnp.sum(grad_rows, 0)
    grad_active = jnp.dot(grad_low, w_down.T, preferred_element_type=jnp.float32)
    gelu_pull = jax.vjp(jax.nn.gelu, hidden)[1]
    grad_hidden = gelu_pull(grad_active)[0].astype(jnp.bfloat16)
    grad_bup = jnp.sum(grad_hidden.astype(jnp.float32), 0)
    grad_wup = jnp.dot(normed_two.T, grad_hidden, preferred_element_type=jnp.float32)
    grad_normed_two = input_total(jnp.dot(grad_hidden, w_up.T, preferred_element_type=jnp.float32))
    grad_norm, grad_gain_two, grad_shift_two = norm_backward(
        grad_normed_two, second_normal, second_inverse, gains[1]
    )
    grad_middle = grad_rows + grad_norm
    grad_bout = jnp.sum(grad_middle, 0)
    grad_mid_low = grad_middle.astype(jnp.bfloat16)
    grad_wout = jnp.dot(mixture.T, grad_mid_low, preferred_element_type=jnp.float32)
    grad_mixture = jnp.dot(grad_mid_low, w_out.T, preferred_element_type=jnp.float32).astype(
        jnp.bfloat16
    )
    grad_parts = mixer_backward(
        block_kind, retained, grad_mixture.reshape(layout[:-1] + (columns,))
    )
    grad_flat = [grad.reshape(-1, columns) for grad in grad_parts]
    grad_project = jnp.stack(grad_flat, 1)
    grad_bqv = jnp.stack(
        [jnp.sum(grad_flat[0].astype(jnp.float32), 0), jnp.sum(grad_flat[2].astype(jnp.float32), 0)]
    )
    grad_wqkv = jnp.einsum("rd,rcj->dcj", normed, grad_project, preferred_element_type=jnp.float32)
    grad_normed = input_total(
        jnp.einsum("rcj,dcj->rd", grad_project, w_qkv, preferred_element_type=jnp.float32)
    )
    grad_input, grad_gain_one, grad_shift_one = norm_backward(
        grad_normed, first_normal, first_inverse, gains[0]
    )
    gradients = (
        jnp.stack([grad_gain_one, grad_gain_two]),
        jnp.stack([grad_shift_one, grad_shift_two]),
        grad_wqkv,
        grad_bqv,
        grad_wout,
        grad_bout,
        grad_wup,
        grad_bup,
        grad_wdown,
        grad_bdown,
    )
    return (grad_middle + grad_input, gradients)


def on_device_sums(
    tokens,
    token_mask,
    mask_embed,
    norm_gains,
    norm_shifts,
    w_qkv,
    b_qv,
    w_out,
    b_out,
    w_up,
    b_up,
    w_down,
    b_down,
    cotangent,
):
    layout = tokens.shape
    width = layout[-1]
    masked = (token_mask == 1).reshape(-1, 1)
    initial = jnp.where(masked, mask_embed[None, :], tokens.reshape(-1, width).astype(jnp.float32))
    upstream = cotangent.reshape(-1, width).astype(jnp.float32)

    def weights_of(block_kind):
        return (
            norm_gains[block_kind],
            norm_shifts[block_kind],
            w_qkv[block_kind],
            b_qv[block_kind],
            w_out[block_kind],
            b_out[block_kind],
            w_up[block_kind],
            b_up[block_kind],
            w_down[block_kind],
            b_down[block_kind],
        )

    middle, active, unused_first = block_forward(0, initial, layout, weights_of(0))
    second = block_output(middle, active, w_down[0], b_down[0])
    middle, active, unused_second = block_forward(1, second, layout, weights_of(1))
    output_rows = block_output(middle, active, w_down[1], b_down[1])
    grad_second, grads_later = block_backward(1, second, layout, weights_of(1), upstream)
    grad_initial, grads_earlier = block_backward(0, initial, layout, weights_of(0), grad_second)
    stacked = [
        jnp.stack([first_grad, later_grad])
        for first_grad, later_grad in zip(grads_earlier, grads_later)
    ]
    grad_embed = jnp.sum(jnp.where(masked, grad_initial, 0.0), 0)
    output_low = output_rows.astype(jnp.bfloat16)
    grad_low = jnp.where(masked, 0.0, grad_initial).astype(jnp.bfloat16)
    shares = (
        lax.psum_scatter(stacked[2], ("clip", "tube"), scatter_dimension=1, tiled=True),
        lax.psum_scatter(stacked[4], ("clip", "tube"), scatter_dimension=2, tiled=True),
        lax.psum_scatter(stacked[6], ("clip", "tube"), scatter_dimension=1, tiled=True),
        lax.psum_scatter(stacked[8], ("clip", "tube"), scatter_dimension=2, tiled=True),
    )
    whole = (
        lax.all_gather(shares[0].astype(jnp.bfloat16), ("clip", "tube"), axis=1, tiled=True).astype(
            jnp.float32
        ),
        lax.all_gather(shares[1].astype(jnp.bfloat16), ("clip", "tube"), axis=2, tiled=True).astype(
            jnp.float32
        ),
        lax.all_gather(shares[2].astype(jnp.bfloat16), ("clip", "tube"), axis=1, tiled=True).astype(
            jnp.float32
        ),
        lax.all_gather(shares[3].astype(jnp.bfloat16), ("clip", "tube"), axis=2, tiled=True).astype(
            jnp.float32
        ),
    )
    column_part = (
        grad_embed,
        stacked[0],
        stacked[1],
        stacked[5],
        stacked[9],
        stacked[3],
        stacked[7],
    )
    small = lax.psum(
        (
            column_part[0],
            column_part[1],
            column_part[2],
            column_part[3],
            column_part[4],
            column_part[5],
            column_part[6],
        ),
        ("clip", "tube"),
    )
    embed_grad, gain_grad, shift_grad, bout_grad, bdown_grad = (
        small[0],
        small[1],
        small[2],
        small[3],
        small[4],
    )
    bqv_grad, bup_grad = (small[5], small[6])
    return (
        output_low.reshape(layout),
        grad_low.reshape(layout),
        embed_grad,
        gain_grad,
        shift_grad,
        whole[0],
        bqv_grad,
        whole[1],
        bout_grad,
        whole[2],
        bup_grad,
        whole[3],
        bdown_grad,
    )


DOWN, UP, ATTN = range(3)
SEND, PASS, FIRST_INPUT, SECOND_INPUT, SPREAD, ATTEND, MIDDLE, EXPAND, CONTRACT = range(9)
FORWARD_ORDER = (
    (SEND, 0), (PASS, 0, 0), (SEND, 1), (FIRST_INPUT,), (PASS, 0, 1), (PASS, 1, 0), (SEND, 2), (PASS, 1, 1),
    (PASS, 0, 2), (PASS, 0, 3), (PASS, 1, 2), (PASS, 2, 0), (SEND, 3), (PASS, 1, 3), (ATTEND, 0, 0), (ATTEND, 0, 1),
    (ATTEND, 0, 2), (PASS, 2, 1), (ATTEND, 0, 3), (MIDDLE, 0), (PASS, 3, 0), (SEND, 4), (PASS, 2, 2), (PASS, 3, 1),
    (PASS, 2, 3), (EXPAND, 0, 0), (PASS, 4, 0), (SEND, 5), (EXPAND, 0, 1), (EXPAND, 0, 2), (EXPAND, 0, 3),
    (PASS, 3, 2), (PASS, 4, 1), (PASS, 5, 0), (SEND, 6), (PASS, 3, 3), (CONTRACT, 0, 0), (CONTRACT, 0, 1),
    (CONTRACT, 0, 2), (CONTRACT, 0, 3), (SPREAD,), (PASS, 5, 1), (PASS, 4, 2), (PASS, 4, 3), (PASS, 6, 0),
    (SECOND_INPUT,), (ATTEND, 1, 0), (PASS, 6, 1), (PASS, 5, 2), (ATTEND, 1, 1), (ATTEND, 1, 2), (PASS, 5, 3),
    (ATTEND, 1, 3), (MIDDLE, 1), (EXPAND, 1, 0), (PASS, 6, 2), (EXPAND, 1, 1), (EXPAND, 1, 2), (EXPAND, 1, 3),
    (PASS, 6, 3),
)
MLP_BACK, MLP_NORM, ATTN_BACK, ATTN_NORM, UPSTREAM, RESULT_LINE, OWN_LINE, FAR_START, FAR_LINE, SMALL = range(10)
ADD_CORE, ADD_FIRST, ADD_SECOND, PASS_HEADS, ADD_HEADS, SHARE_FIRST, SHARE_CORE, ARRIVED, MLP_START, SEND_RESULT = range(10, 20)
BACKWARD_ORDER = (
    (MLP_START,), (MLP_BACK, 1, 0), (ADD_CORE, 1, DOWN, 0), (MLP_BACK, 1, 1), (ADD_CORE, 1, UP, 0), (MLP_BACK, 1, 2),
    (ADD_CORE, 1, DOWN, 1), (ADD_CORE, 1, UP, 1), (MLP_BACK, 1, 3), (ADD_CORE, 1, UP, 2), (ADD_CORE, 1, DOWN, 2),
    (SEND_RESULT,), (MLP_NORM, 1), (ATTN_BACK, 1, 0), (ADD_CORE, 1, UP, 3), (ADD_CORE, 1, DOWN, 3), (ATTN_BACK, 1, 1),
    (ADD_CORE, 1, ATTN, 0), (ATTN_BACK, 1, 2), (ADD_CORE, 1, ATTN, 1), (ATTN_BACK, 1, 3), (ADD_CORE, 1, ATTN, 2),
    (ATTN_NORM, 1), (ADD_CORE, 1, ATTN, 3), (RESULT_LINE, 0), (ADD_FIRST, 1, DOWN), (ADD_FIRST, 1, ATTN),
    (ADD_FIRST, 1, UP), (UPSTREAM,), (MLP_BACK, 0, 0), (MLP_BACK, 0, 1), (ADD_SECOND, 1, DOWN),
    (ADD_CORE, 0, DOWN, 0), (ADD_CORE, 0, UP, 0), (MLP_BACK, 0, 2), (ADD_CORE, 0, DOWN, 1), (ADD_SECOND, 1, ATTN),
    (ADD_CORE, 0, UP, 1), (MLP_BACK, 0, 3), (MLP_NORM, 0), (ATTN_BACK, 0, 0), (ADD_CORE, 0, UP, 3),
    (ADD_SECOND, 1, UP), (PASS_HEADS, 1, DOWN, 1), (ADD_CORE, 0, DOWN, 2), (ADD_CORE, 0, UP, 2), (RESULT_LINE, 1),
    (ADD_CORE, 0, DOWN, 3), (ATTN_BACK, 0, 1), (ADD_CORE, 0, ATTN, 0), (ATTN_BACK, 0, 2), (PASS_HEADS, 1, ATTN, 1),
    (ADD_CORE, 0, ATTN, 1), (ATTN_BACK, 0, 3), (PASS_HEADS, 1, UP, 1), (ATTN_NORM, 0), (ADD_FIRST, 0, UP),
    (ADD_CORE, 0, ATTN, 2), (PASS_HEADS, 1, ATTN, 2), (PASS_HEADS, 1, DOWN, 2), (FAR_START,), (ADD_CORE, 0, ATTN, 3),
    (OWN_LINE, 0), (ADD_FIRST, 0, DOWN), (PASS_HEADS, 1, UP, 2), (ADD_SECOND, 0, UP), (SMALL, 0),
    (ADD_HEADS, 1, ATTN), (ADD_FIRST, 0, ATTN), (FAR_LINE, 0), (ADD_SECOND, 0, DOWN), (SHARE_FIRST, 1, ATTN),
    (PASS_HEADS, 0, UP, 1), (OWN_LINE, 1), (ADD_HEADS, 1, DOWN), (ADD_SECOND, 0, ATTN), (ADD_HEADS, 1, UP),
    (PASS_HEADS, 0, DOWN, 1), (SHARE_FIRST, 1, DOWN), (PASS_HEADS, 0, UP, 2), (SMALL, 1), (SHARE_FIRST, 1, UP),
    (PASS_HEADS, 0, ATTN, 1), (PASS_HEADS, 0, DOWN, 2), (SMALL, 2), (ADD_HEADS, 0, UP), (ADD_HEADS, 0, DOWN),
    (SHARE_CORE, 1, ATTN), (OWN_LINE, 2), (SHARE_FIRST, 0, UP), (PASS_HEADS, 0, ATTN, 2), (SHARE_FIRST, 0, DOWN),
    (SHARE_CORE, 1, DOWN), (FAR_LINE, 1), (ADD_HEADS, 0, ATTN), (SMALL, 3), (SHARE_FIRST, 0, ATTN),
    (SHARE_CORE, 1, UP), (SHARE_CORE, 0, DOWN), (ARRIVED, 1, DOWN), (SMALL, 4), (ARRIVED, 1, UP), (ARRIVED, 1, ATTN),
    (SHARE_CORE, 0, UP), (SHARE_CORE, 0, ATTN), (ARRIVED, 0, DOWN), (ARRIVED, 0, UP), (FAR_LINE, 2), (RESULT_LINE, 2),
    (ARRIVED, 0, ATTN),
)

GELU_A = 0.7978845608028654
GELU_B = 0.044715


def dot(left, right, dims):
    return lax.dot_general(left, right, (dims, ((), ())), preferred_element_type=F32)


NN, NT, TN = ((1,), (0,)), ((1,), (1,)), ((0,), (0,))


def standardize(values):
    centre = values - jnp.mean(values, -1, keepdims=True)
    inverse = lax.rsqrt(jnp.mean(centre * centre, -1, keepdims=True) + EPS)
    return centre * inverse, inverse


def head_masks(columns, scale):
    lane = lax.broadcasted_iota(jnp.int32, (1, columns), 1)
    return [
        jnp.where((lane >= j * HD) & (lane < (j + 1) * HD), scale, 0.0).astype(LOW)
        for j in range(columns // HD)
    ]


def gelu_pair(hidden):
    square = hidden * hidden
    tanh = jnp.tanh(GELU_A * hidden * (1.0 + GELU_B * square))
    half = 0.5 * (1.0 + tanh)
    slope = half + hidden * (0.5 * GELU_A) * (1.0 - tanh * tanh) * (1.0 + 3.0 * GELU_B * square)
    return hidden * half, slope


class Sizes:
    def __init__(self, rows, width, shards, columns, units, length):
        self.rows, self.width, self.shards = rows, width, shards
        self.columns, self.units, self.length = columns, units, length
        self.sequences = rows // length
        self.heads = columns // HD
        self.out_row = 3 * columns
        self.up_row = 4 * columns
        self.down_row = 4 * columns + width
        self.block_rows = 4 * columns + width + units


def norm_rows(sz, x_ref, gain, shift, n_ref, chunk=128):
    @pl.loop(0, sz.rows, step=chunk)
    def _(start):
        at = pl.ds(pl.multiple_of(start, chunk), chunk)
        normal, _ = standardize(x_ref[at, :].astype(F32))
        n_ref[at, :] = (normal * gain + shift).astype(LOW)


def forward_attention(sz, shard, w_ref, b_query, b_value, n_ref, t_ref, p_ref, m_ref):
    cols, length = sz.columns, sz.length
    normed = n_ref[...]
    q_ref, k_ref, v_ref, o_ref = (t_ref.at[shard, i] for i in range(4))
    q_ref[...] = (dot(normed, w_ref[shard, 0:cols, :], NT) + b_query).astype(LOW)
    k_ref[...] = dot(normed, w_ref[shard, cols : 2 * cols, :], NT).astype(LOW)
    v_ref[...] = (dot(normed, w_ref[shard, 2 * cols : 3 * cols, :], NT) + b_value).astype(LOW)
    scaled = head_masks(cols, HD**-0.5)
    masks = head_masks(cols, 1.0)
    for seq in range(sz.sequences):
        at = slice(seq * length, (seq + 1) * length)
        queries, keys, values = q_ref[at, :], k_ref[at, :], v_ref[at, :]
        mixture = jnp.zeros((length, cols), F32)
        for head in range(sz.heads):
            scores = dot(queries * scaled[head], keys, NT)
            exponent = jnp.exp(scores - jnp.max(scores, -1, keepdims=True))
            weights = (exponent / jnp.sum(exponent, -1, keepdims=True)).astype(LOW)
            p_ref[shard, seq * sz.heads + head] = weights
            mixture += dot(weights, values * masks[head], NN)
        o_ref[at, :] = mixture.astype(LOW)
    m_ref[...] += dot(o_ref[...], w_ref[shard, sz.out_row : sz.out_row + cols, :], NN)


def forward_up(sz, shard, w_ref, b_up, n2_ref, as_ref):
    hidden = dot(n2_ref[...], w_ref[shard, sz.up_row : sz.up_row + sz.width, :], NN) + b_up
    active, slope = gelu_pair(hidden)
    as_ref[shard, 0] = active.astype(LOW)
    as_ref[shard, 1] = slope.astype(LOW)


def forward_down(sz, shard, w_ref, as_ref, y_ref):
    y_ref[...] += dot(as_ref[shard, 0], w_ref[shard, sz.down_row : sz.down_row + sz.units, :], NN)


def backward_mlp(sz, w_ref, as_ref, low_ref, n2_ref, du_ref, dn_ref, down_ref, up_ref, sum_row):
    low = low_ref[...]
    grad_active = dot(low, w_ref[sz.width : sz.width + sz.units, :], NT)
    du_ref[...] = (grad_active * as_ref[1].astype(F32)).astype(LOW)
    sum_row[...] = jnp.sum(du_ref[...].astype(F32), 0, keepdims=True)
    if down_ref is not None:
        down_ref[...] = dot(as_ref[0], low, TN).astype(LOW)
    up_ref[...] = dot(n2_ref[...], du_ref[...], TN).astype(LOW)
    dn_ref[...] += dot(du_ref[...], w_ref[0 : sz.width, :], NT)


def norm_back_rows(sz, x_ref, gain, dn_ref, g_ref, out_ref, gain_row, shift_row, sum_row, low_ref, chunk=128):
    for row in (gain_row, shift_row, sum_row):
        if row is not None:
            row[...] = jnp.zeros_like(row)

    @pl.loop(0, sz.rows, step=chunk)
    def _(start):
        at = pl.ds(pl.multiple_of(start, chunk), chunk)
        normal, inverse = standardize(x_ref[at, :])
        dn = dn_ref[at, :]
        dy = dn * gain
        part = inverse * (
            dy - jnp.mean(dy, -1, keepdims=True) - normal * jnp.mean(dy * normal, -1, keepdims=True)
        )
        total = g_ref[at, :].astype(F32) + part
        out_ref[at, :] = total
        if low_ref is not None:
            low_ref[at, :] = total.astype(LOW)
        gain_row[...] += jnp.sum(dn * normal, 0, keepdims=True)
        shift_row[...] += jnp.sum(dn, 0, keepdims=True)
        if sum_row is not None:
            sum_row[...] += jnp.sum(total, 0, keepdims=True)


def backward_attention(sz, w_ref, t_ref, p_ref, dml_ref, n_ref, do_ref, dq_ref, dk_ref, dv_ref, dn_ref, g_ref, query_row, value_row):
    cols, length = sz.columns, sz.length
    low = dml_ref[...]
    q_ref, k_ref, v_ref, o_ref = (t_ref.at[i] for i in range(4))
    w_out = w_ref[sz.out_row : sz.out_row + cols, :]
    do_ref[...] = dot(low, w_out, NT).astype(LOW)
    g_ref[sz.out_row : sz.out_row + cols, :] = dot(o_ref[...], low, TN).astype(LOW)
    scaled = head_masks(cols, HD**-0.5)
    masks = head_masks(cols, 1.0)
    for seq in range(sz.sequences):
        at = slice(seq * length, (seq + 1) * length)
        queries, keys, values = q_ref[at, :], k_ref[at, :], v_ref[at, :]
        grad_o = do_ref[at, :]
        dq = jnp.zeros((length, cols), F32)
        dk = jnp.zeros((length, cols), F32)
        dv = jnp.zeros((length, cols), F32)
        for head in range(sz.heads):
            weights = p_ref[seq * sz.heads + head]
            grad_head = grad_o * masks[head]
            dp = dot(grad_head, values, NT)
            dv += dot(weights, grad_head, TN)
            wide = weights.astype(F32)
            ds = (wide * (dp - jnp.sum(wide * dp, -1, keepdims=True))).astype(LOW)
            dq += dot(ds, keys * scaled[head], NN)
            dk += dot(ds, queries * scaled[head], TN)
        dq_ref[at, :] = dq.astype(LOW)
        dk_ref[at, :] = dk.astype(LOW)
        dv_ref[at, :] = dv.astype(LOW)
    normed = n_ref[...]
    query_row[...] = jnp.sum(dq_ref[...].astype(F32), 0, keepdims=True)
    value_row[...] = jnp.sum(dv_ref[...].astype(F32), 0, keepdims=True)
    for i, part in enumerate((dq_ref, dk_ref, dv_ref)):
        g_ref[i * cols : (i + 1) * cols, :] = dot(part[...], normed, TN).astype(LOW)
        dn_ref[...] += dot(part[...], w_ref[i * cols : (i + 1) * cols, :], NN)


def saved_shapes(sz):
    s, r, c = sz.shards, sz.rows, sz.columns
    return [
        ((r, sz.width), LOW),
        ((s, 4, r, c), LOW),
        ((s, sz.sequences * sz.heads, sz.length, sz.length), LOW),
        ((r, sz.width), F32),
        ((r, sz.width), LOW),
        ((s, 2, r, sz.units), LOW),
    ]


def structs(shapes):
    return [jax.ShapeDtypeStruct(s, d) for s, d in shapes]


def vmems(shapes):
    return [pltpu.VMEM(s, d) for s, d in shapes]


class Place:
    def __init__(self, heads, zs=None):
        self.clip, self.y, self.z = (lax.axis_index(n) for n in ("clip", "tube", "head"))
        self.heads = heads
        self.core, self.x = lax.rem(self.clip, 2), lax.div(self.clip, 2)
        c, x, y = self.core, self.x, self.y
        self.first = (c + 2 * (x + (1 - c) * (1 - 2 * x)), y + c * (1 - 2 * y), self.z)
        self.second = (c + 2 * (x + c * (1 - 2 * x)), y + (1 - c) * (1 - 2 * y), self.z)
        self.other = (1 - c + 2 * x, y, self.z)
        self.i = (1 - c) * x + c * y
        self.j = (1 - c) * y + c * x
        self.along_x = (c + 2 * (1 - x), y, self.z)

    def head(self, step):
        return (self.clip, self.y, lax.rem(self.z + step + self.heads, self.heads))

    def across(self, step):
        return (self.clip, 1 - self.y, lax.rem(self.z + step + self.heads, self.heads))

    def clip_peers(self):
        return [self.head(d) for d in range(1, self.heads)] + [self.across(d) for d in range(self.heads)]

    def all_peers(self):
        return [self.along_x, self.other] + self.clip_peers()


def greet(peers):
    barrier = pltpu.get_barrier_semaphore()
    for peer in peers:
        pl.semaphore_signal(barrier, inc=1, device_id=peer, device_id_type=MESH)
    pl.semaphore_wait(barrier, len(peers))


class Moves:
    def __init__(self, send_sem, recv_sem):
        self.send_sem, self.recv_sem, self.count, self.sent = send_sem, recv_sem, 0, {}

    def reserve(self):
        self.count += 1
        return self.count - 1

    def one(self, n, src, dst, target):
        return pltpu.make_async_remote_copy(
            src, dst, self.send_sem.at[n], self.recv_sem.at[n], device_id=target, device_id_type=MESH
        )

    def phase(self, copies):
        made = []
        for src, dst, landing, target in copies:
            n = self.count
            self.count += 1
            made.append((src, dst, landing, target, n))
        return made

    def start(self, made):
        for src, dst, _, target, n in made:
            copy = pltpu.make_async_remote_copy(
                src, dst, self.send_sem.at[n], self.recv_sem.at[n], device_id=target, device_id_type=MESH
            )
            copy.start()
            self.sent[n] = copy

    def arrive(self, made):
        for src, _, landing, target, n in made:
            pltpu.make_async_remote_copy(
                src, landing, self.send_sem.at[n], self.recv_sem.at[n], device_id=target, device_id_type=MESH
            ).wait_recv()

    def left(self, made):
        for *_, n in made:
            if n in self.sent:
                self.sent.pop(n).wait_send()

    def finish(self):
        for copy in self.sent.values():
            copy.wait_send()
        self.sent = {}


def piece_list(sz, blocks):
    out = []
    for b in range(blocks):
        for kind, start in ((ATTN, 0), (UP, sz.up_row), (DOWN, sz.down_row)):
            parts = 2 if (b, kind) == (0, ATTN) else 1
            size = sz.width // parts
            out += [(b, kind, start + i * size, size) for i in range(parts)]
    return out


def gather_phases(place, moves, full, offset, rows):
    q = rows // 8
    c, i, j, z, heads = place.core, place.i, place.j, place.z, place.heads

    def at(ref, head, start, size):
        return ref.at[head, pl.ds(pl.multiple_of(offset + start * q, q), size * q), :]

    def other(d):
        return lax.rem(z + d, heads)

    mine = 4 * c + 2 * j + i
    near = 4 * c + 2 * j + (1 - i)
    pair = 4 * c + 2 * j
    pair_far = 4 * c + 2 * (1 - j)
    steps = range(1, heads)
    return [
        moves.phase(
            [(at(full, z, mine, 1), at(full, z, mine, 1), at(full, lax.rem(z + heads - d, heads), mine, 1), place.head(d)) for d in steps]
        ),
        moves.phase(
            [(at(full, other(d), mine, 1), at(full, other(d), mine, 1), at(full, other(d), near, 1), place.first) for d in steps]
        ),
        moves.phase(
            [(at(full, other(d), pair, 2), at(full, other(d), pair, 2), at(full, other(d), pair_far, 2), place.second) for d in steps]
        ),
        moves.phase(
            [(at(full, other(d), 4 * c, 4), at(full, other(d), 4 * c, 4), at(full, other(d), 4 * (1 - c), 4), place.other) for d in steps]
        ),
    ]


def masked_rows(rows, marks_ref):
    patches = marks_ref.shape[-1]
    marks = marks_ref[...].astype(F32).reshape(rows // patches, patches).astype(LOW)
    group = lax.div(lax.broadcasted_iota(jnp.int32, (rows, rows // patches), 0), patches)
    spread = (group == lax.broadcasted_iota(jnp.int32, (rows, rows // patches), 1)).astype(F32).astype(LOW)
    wide = dot(spread, marks, NN)
    lane = lax.broadcasted_iota(jnp.int32, (rows, patches), 1)
    mine = lane == lax.rem(lax.broadcasted_iota(jnp.int32, (rows, patches), 0), patches)
    return jnp.sum(jnp.where(mine, wide, 0.0), -1, keepdims=True) > 0.5


class Saves:
    def __init__(self, sem):
        self.sem, self.count = sem, 0

    def start(self, src, dst):
        copy = pltpu.make_async_copy(src, dst, self.sem.at[self.count])
        self.count += 1
        copy.start()
        return copy


def forward_kernel(sz, blocks, frame_share, tube_share, *refs):
    (w_qkv, w_out, w_up, w_down, tokens, marks, b_qv, b_up, embed, gains, shifts, b_out, b_down), refs = refs[:13], refs[13:]
    fulls, refs = refs[:blocks], refs[blocks:]
    saved, refs = [refs[7 * b : 7 * b + 7] for b in range(blocks)], refs[7 * blocks :]
    (frame_marks,), refs = refs[:1], refs[1:]
    w = refs[:blocks]
    (
        frames, bqv, bup, x, n, t, p, m, n2, act, y, y_low, second, send_sem, recv_sem, local_sem, save_sem,
    ) = refs[blocks:]
    heads, block_rows, length = sz.shards, sz.block_rows, sz.length
    place = Place(heads)
    moves = Moves(send_sem, recv_sem)
    local, saves = Saves(local_sem), Saves(save_sem)

    def settle(copies):
        for copy in copies:
            copy.wait()

    yy, z = place.y, place.z
    tubes = tokens.shape[1]
    greet(place.all_peers())

    owned = pl.ds((2 * z + yy) * frame_share, frame_share)
    asked = pl.ds((2 * z + 1 - yy) * frame_share, frame_share)
    here, there = pl.ds(yy * tubes, tubes), pl.ds((1 - yy) * tubes, tubes)
    exchange = moves.phase(
        [
            (src.at[asked], dst.at[:, here], dst.at[:, there], place.across(0))
            for src, dst in ((tokens, frames), (marks, frame_marks))
        ]
        + [
            (src, dst.at[z], dst.at[lax.rem(z + heads - d, heads)], place.head(d))
            for src, dst in ((b_qv, bqv), (b_up, bup))
            for d in range(1, heads)
        ]
    )
    spread = moves.phase(
        [
            (
                y_low.at[:, pl.ds((heads * ty + tz) * tube_share, tube_share)],
                second.at[pl.ds((2 * z + yy) * frame_share, frame_share)],
                second.at[pl.ds((2 * fz + ty) * frame_share, frame_share)],
                target,
            )
            for ty, tz, fz, target in [
                (yy, lax.rem(z + d, heads), lax.rem(z + heads - d, heads), place.head(d)) for d in range(1, heads)
            ]
            + [
                (1 - yy, lax.rem(z + d, heads), lax.rem(z + heads - d, heads), place.across(d)) for d in range(heads)
            ]
        ]
    )
    pieces = piece_list(sz, blocks)
    work = [gather_phases(place, moves, w[b], start, size) for b, _, start, size in pieces]
    moves.start(exchange)
    own_parts = {}
    for b in range(blocks):
        mine = w[b].at[z]
        own_parts[b, ATTN] = [
            local.start(w_qkv.at[b], mine.at[pl.ds(0, sz.out_row)]),
            local.start(w_out.at[b], mine.at[pl.ds(sz.out_row, sz.columns)]),
        ]
        own_parts[b, UP] = [local.start(w_up.at[b], mine.at[pl.ds(sz.up_row, sz.width)])]
        own_parts[b, DOWN] = [local.start(w_down.at[b], mine.at[pl.ds(sz.down_row, sz.units)])]

    def begin_piece(piece):
        b, kind, _, _ = pieces[piece]
        settle(own_parts.pop((b, kind), ()))
        moves.start(work[piece][0])
    owns = [
        local.start(tokens.at[owned], frames.at[:, here]),
        local.start(marks.at[owned], frame_marks.at[:, here]),
        local.start(b_qv, bqv.at[z]),
        local.start(b_up, bup.at[z]),
    ]

    def save(b, index, src, part=None):
        dst = saved[b][index]
        return saves.start(src, dst if part is None else dst.at[part])

    def begin_block(b):
        norm_rows(sz, x, gains[b, 0:1, :], shifts[b, 0:1, :], n)
        m[...] = x[...] + b_out[b : b + 1, :]
        return [save(b, 0, x), save(b, 1, n)]

    def attention(b, s):
        forward_attention(sz, s, w[b], bqv[s, b, 0:1, :], bqv[s, b, 1:2, :], n, t, p, m)
        return [save(b, 2, t.at[s], s), save(b, 3, p.at[s], s)]

    def middle(b):
        norm_rows(sz, m, gains[b, 1:2, :], shifts[b, 1:2, :], n2)
        y[...] = m[...] + b_down[b : b + 1, :]
        return [save(b, 4, m), save(b, 5, n2)]

    def up(b, s):
        forward_up(sz, s, w[b], bup[s, b : b + 1, :], n2, act)
        return [save(b, 6, act.at[s], s)]

    def down(b, s):
        forward_down(sz, s, w[b], act, y)

    def keep(piece):
        b, _, start, size = pieces[piece]
        at = pl.ds(start, size)
        return [saves.start(w[b].at[:, at], fulls[b].at[:, at])]

    kept, early = [], []
    wide = [None] * blocks

    def first_input():
        settle(owns)
        moves.arrive(exchange)
        tok = frames[...].astype(F32).reshape(sz.rows, sz.width)
        x[...] = jnp.where(masked_rows(sz.rows, frame_marks), embed[...].reshape(1, sz.width), tok)
        early.extend(begin_block(0))

    def second_input():
        moves.arrive(spread)
        wide[1].wait()
        settle(early)
        for j in range(tube_share):
            x[j * length : (j + 1) * length, :] = second[:, j].astype(F32).reshape(length, sz.width)
        kept.extend(begin_block(1))

    def spread_first():
        y_low[...] = y[...].astype(LOW).reshape(y_low.shape)
        moves.start(spread)
        wide[1] = local.start(
            y_low.at[:, pl.ds((heads * yy + z) * tube_share, tube_share)],
            second.at[pl.ds((2 * z + yy) * frame_share, frame_share)],
        )

    def advance(piece, phase):
        moves.arrive(work[piece][phase])
        if phase < 3:
            moves.start(work[piece][phase + 1])
        else:
            kept.extend(keep(piece))

    steps = {(FIRST_INPUT,): first_input, (SPREAD,): spread_first, (SECOND_INPUT,): second_input}
    for piece in range(len(work)):
        steps[SEND, piece] = functools.partial(begin_piece, piece)
        for phase in range(4):
            steps[PASS, piece, phase] = functools.partial(advance, piece, phase)
    for b in range(blocks):
        held = kept if b else early
        run = lambda f, *args, held=held: held.extend(f(*args) or ())
        steps[MIDDLE, b] = functools.partial(run, middle, b)
        for s in range(heads):
            steps[ATTEND, b, s] = functools.partial(run, attention, b, s)
            steps[EXPAND, b, s] = functools.partial(run, up, b, s)
            steps[CONTRACT, b, s] = functools.partial(run, down, b, s)
    for step in FORWARD_ORDER:
        steps[step]()
    moves.finish()
    settle(kept)


def run_forward(sz, blocks, frame_share, tube_share, weights, tokens, marks, b_qv, b_up, embed, gains, shifts, b_out, b_down):
    heads, width, rows = sz.shards, sz.width, sz.rows
    tubes, patches = 2 * tokens.shape[1], tokens.shape[2]
    frames = tokens.shape[0]
    saved = [((rows, width), F32)] + saved_shapes(sz)
    whole_frames = (frame_share, tubes, patches)
    count = len(piece_list(sz, blocks)) * 4 * (heads - 1) + 2 + 2 * (heads - 1) + 2 * heads - 1
    hbm, vmem = pl.BlockSpec(memory_space=pl.ANY), pl.BlockSpec(memory_space=pltpu.VMEM)
    full = ((heads, sz.block_rows, width), LOW)
    mixed = (frames, tube_share, patches, width)
    out = pl.pallas_call(
        lambda *refs: forward_kernel(sz, blocks, frame_share, tube_share, *refs),
        name="forward_both",
        out_shape=structs([full] * blocks + saved * blocks + [(whole_frames, jnp.int32)]),
        in_specs=[hbm] * 8 + [vmem] * 5,
        out_specs=[hbm] * (blocks + 7 * blocks) + [vmem],
        scratch_shapes=vmems(
            [full] * blocks
            + [
                (whole_frames + (width,), LOW),
                ((heads,) + b_qv.shape, F32),
                ((heads,) + b_up.shape, F32),
            ]
            + saved
            + [
                ((rows, width), F32),
                (whole_frames + (width,), LOW),
                (mixed, LOW),
            ]
        )
        + [
            pltpu.SemaphoreType.DMA((count,)),
            pltpu.SemaphoreType.DMA((count,)),
            pltpu.SemaphoreType.DMA((16,)),
            pltpu.SemaphoreType.DMA((64,)),
        ],
        compiler_params=pltpu.CompilerParams(
            collective_id=0, has_side_effects=True, vmem_limit_bytes=62 * 2**20
        ),
    )(*weights, tokens, marks, b_qv, b_up, embed, gains, shifts, b_out, b_down)
    fulls, out = out[:blocks], out[blocks:]
    saved = [out[7 * b : 7 * b + 7] for b in range(blocks)]
    return fulls, saved, out[-1]


class Line:
    def __init__(self, place, send_sem, recv_sem, region, own=None):
        self.place, self.send_sem, self.recv_sem, self.region = place, send_sem, recv_sem, region
        self.own = own
        self.steps = place.heads - 1

    def moves(self, step):
        z, last = self.place.z, self.place.heads - 1
        return [
            ((z >= step) & (z < last), z - step, 1, z > step, z - 1 - step, 2 * step),
            ((z <= last - step) & (z > 0), z + step, -1, z < last - step, z + 1 + step, 2 * step + 1),
        ]

    def copy(self, block, way, n):
        return pltpu.make_async_remote_copy(
            self.own if n < 2 and self.own is not None else self.region(block),
            self.region(block),
            self.send_sem.at[n],
            self.recv_sem.at[n],
            device_id=self.place.head(way),
            device_id_type=MESH,
        )

    def start(self, step):
        for sends, block, way, _, _, n in self.moves(step):
            pl.when(sends)(lambda block=block, way=way, n=n: self.copy(block, way, n).start())

    def arrive(self, step):
        for _, _, way, gets, block, n in self.moves(step):
            pl.when(gets)(lambda block=block, way=way, n=n: self.copy(block, way, n).wait_recv())

    def finish(self):
        for step in range(self.steps):
            for sends, block, way, _, _, n in self.moves(step):
                pl.when(sends)(lambda block=block, way=way, n=n: self.copy(block, way, n).wait_send())


class Reduction:
    def __init__(self, place, moves, grads, out, out_row, rows, bufs, final_buf, final_sem):
        q = rows // 8
        self.q, self.place, self.moves, self.grads = q, place, moves, grads
        self.core_buf, self.first_buf, self.second_buf, self.head_buf = bufs
        self.final_buf, self.final_sem = final_buf, final_sem
        c, i, j, z, heads = place.core, place.i, place.j, place.z, place.heads
        cut = lambda start, size: pl.ds(pl.multiple_of(start * q, q), size * q)
        row = lambda start, size: out.at[pl.ds(pl.multiple_of(out_row + start * q, q), size * q), :]
        self.kept, self.given = cut(4 * c, 4), cut(4 * (1 - c), 4)
        self.part, self.subpart = cut(2 * i, 2), cut(j, 1)
        shards = range(heads)
        self.core = moves.phase(
            [(grads.at[s % 2, self.given, :], self.core_buf.at[s], self.core_buf.at[s], place.other) for s in shards]
        )
        self.first = moves.phase(
            [(self.core_buf.at[s, cut(2 * (1 - i), 2), :], self.first_buf.at[s], self.first_buf.at[s], place.first) for s in shards]
        )
        self.second = moves.phase(
            [(self.first_buf.at[s, cut(1 - j, 1), :], self.second_buf.at[s], self.second_buf.at[s], place.second) for s in shards]
        )
        self.to_right = moves.reserve()
        self.to_left = moves.reserve()
        a, mine = 4 * c, 2 * i + j
        self.share_second = moves.phase([(final_buf, row(a + mine, 1), row(a + 2 * i + 1 - j, 1), place.second)])
        self.share_first = moves.phase([(row(a + 2 * i, 2), row(a + 2 * i, 2), row(a + 2 * (1 - i), 2), place.first)])
        self.share_core = moves.phase([(row(a, 4), row(a, 4), row(4 - a, 4), place.other)])
        self.keep = pltpu.make_async_copy(final_buf, row(a + mine, 1), final_sem)

    def give(self, s):
        self.moves.start([self.core[s]])

    def step_first(self, s):
        self.moves.arrive([self.core[s]])
        self.core_buf[s] = self.core_buf[s] + self.grads[s % 2, self.kept, :]
        self.moves.start([self.first[s]])

    def step_second(self, free_sem=None):
        for s in range(self.place.heads):
            self.moves.arrive([self.first[s]])
            self.first_buf[s] = self.first_buf[s] + self.core_buf[s, self.part, :]
            self.moves.start([self.second[s]])
        if free_sem is not None:
            self.moves.left(self.first)
            pl.semaphore_signal(free_sem, inc=1, device_id=self.place.other, device_id_type=MESH)

    def step_heads(self):
        for s in range(self.place.heads):
            self.moves.arrive([self.second[s]])
            self.second_buf[s] = self.second_buf[s] + self.first_buf[s, self.subpart, :]
        last = self.place.heads - 1
        pl.when(self.place.z == 0)(functools.partial(self.send_right, 0))
        pl.when(self.place.z == last)(functools.partial(self.send_left, last))

    def right_copy(self, z):
        return self.moves.one(
            self.to_right, self.second_buf.at[z + 1 :], self.head_buf.at[z + 2 :], self.place.head(1)
        )

    def left_copy(self, z):
        return self.moves.one(self.to_left, self.second_buf.at[:z], self.head_buf.at[:z], self.place.head(-1))

    def send_right(self, z):
        self.right_copy(z).start()

    def send_left(self, z):
        self.left_copy(z).start()

    def from_left(self, z):
        self.right_copy(z - 1).wait_recv()
        for s in range(z + 1, self.place.heads):
            self.second_buf[s] = self.second_buf[s] + self.head_buf[s + 1]
        if z < self.place.heads - 1:
            self.send_right(z)

    def from_right(self, z):
        self.left_copy(z + 1).wait_recv()
        for s in range(z):
            self.second_buf[s] = self.second_buf[s] + self.head_buf[s]
        if z > 0:
            self.send_left(z)

    def step_pass(self, hop):
        heads = self.place.heads
        pl.when(self.place.z == hop)(functools.partial(self.from_left, hop))
        pl.when(self.place.z == heads - 1 - hop)(functools.partial(self.from_right, heads - 1 - hop))

    def step_share(self):
        z, last = self.place.z, self.place.heads - 1
        self.step_pass(last)

        @pl.when(z == 0)
        def _():
            self.final_buf[...] = self.second_buf[0] + self.head_buf[0]

        @pl.when(z == last)
        def _():
            self.final_buf[...] = self.second_buf[last] + self.head_buf[last + 1]

        @pl.when((z > 0) & (z < last))
        def _():
            total = self.second_buf[z].astype(F32) + self.head_buf[z].astype(F32)
            self.final_buf[...] = (total + self.head_buf[z + 1].astype(F32)).astype(LOW)

        self.keep.start()
        self.moves.start(self.share_second)

    def finish(self):
        last = self.place.heads - 1
        for z in range(last + 1):
            if z < last:
                pl.when(self.place.z == z)(lambda z=z: self.right_copy(z).wait_send())
            if z > 0:
                pl.when(self.place.z == z)(lambda z=z: self.left_copy(z).wait_send())

    def step_share_first(self):
        self.keep.wait()
        self.moves.arrive(self.share_second)
        self.moves.start(self.share_first)

    def step_share_core(self):
        self.moves.arrive(self.share_first)
        self.moves.start(self.share_core)

    def end(self):
        self.moves.arrive(self.share_core)


SMALL_ROWS = 48
GAIN_ROW, SHIFT_ROW, BOUT_ROW, BDOWN_ROW, BUP_ROW, BQV_ROW = 1, 5, 9, 11, 16, 24


def backward_kernel(sz, blocks, frame_share, tube_share, *refs):
    fulls, refs = refs[:blocks], refs[blocks:]
    saved, refs = [refs[7 * b : 7 * b + 7] for b in range(blocks)], refs[7 * blocks :]
    (cotangent, marks, gains, b_down), refs = refs[:4], refs[4:]
    (out_result, out_tokens, out_grads, out_small), refs = refs[:4], refs[4:]
    (
        wm, act, wa, t, p, m, n2, n, x, low, dn, dm, du, do, dq, dk, dv, cot, dx_low, back, result,
        grads, core_buf, first_buf, second_buf, head_buf, final_buf, small, small_in, small_heads, small_last,
        send_sem, recv_sem, line_sem, load_sem, copy_sem, final_sem, free_sem,
    ) = refs
    heads, width, length = sz.shards, sz.width, sz.length
    place = Place(heads)
    moves = Moves(send_sem, recv_sem)
    loads = Saves(copy_sem)
    yy, z = place.y, place.z
    tubes = cotangent.shape[1]

    def step_loads(b, kind, s):
        slot = s % 2
        if kind == MLP_BACK:
            pairs = [(fulls[b].at[s, pl.ds(sz.up_row, 2 * width), :], wm.at[slot]), (saved[b][6].at[s], act.at[slot])]
            base = 0
        else:
            pairs = [
                (fulls[b].at[s, pl.ds(0, sz.up_row), :], wa.at[slot]),
                (saved[b][2].at[s], t.at[slot]),
                (saved[b][3].at[s], p.at[slot]),
            ]
            base = 4
        return [
            pltpu.make_async_copy(src, dst, load_sem.at[base + slot * len(pairs) + i]) for i, (src, dst) in enumerate(pairs)
        ]

    steps = [(b, kind, s) for b in (1, 0) for kind in (MLP_BACK, ATTN_BACK) for s in range(heads)]

    def fetch(i):
        if i < len(steps):
            for copy in step_loads(*steps[i]):
                copy.start()

    def ready(i):
        for copy in step_loads(*steps[i]):
            copy.wait()
        fetch(i + 1)

    first_load = loads.start(cotangent.at[:, pl.ds(z * tube_share, tube_share)], cot)
    fetch(0)
    norm_loads = {1: [loads.start(saved[1][4], m), loads.start(saved[1][5], n2)]}
    later_loads = {1: [loads.start(saved[1][1], n), loads.start(saved[1][0], x)]}
    small[...] = jnp.zeros_like(small)
    greet(place.all_peers())

    red = {}
    for b in (1, 0):
        for k in (DOWN, UP, ATTN):
            base = b * sz.block_rows + (sz.down_row, sz.up_row, 0)[k]
            red[b, k] = Reduction(
                place,
                moves,
                grads.at[k],
                out_grads,
                base,
                width,
                (core_buf.at[k], first_buf.at[b, k], second_buf.at[b, k], head_buf.at[b, k]),
                final_buf.at[b, k],
                final_sem.at[b * 3 + k],
            )
    tube_region = lambda block: out_result.at[:, pl.ds(block * tube_share, tube_share)]
    line = Line(place, line_sem.at[0], line_sem.at[1], tube_region, result)
    spread = moves.phase(
        [
            (
                dx_low.at[pl.ds((2 * tz + ty) * frame_share, frame_share)],
                back.at[:, pl.ds((heads * yy + z) * tube_share, tube_share)],
                back.at[:, pl.ds((heads * ty + fz) * tube_share, tube_share)],
                target,
            )
            for ty, tz, fz, target in [
                (yy, lax.rem(z + d, heads), lax.rem(z + heads - d, heads), place.head(d)) for d in range(1, heads)
            ]
            + [
                (1 - yy, lax.rem(z + d, heads), lax.rem(z + heads - d, heads), place.across(d)) for d in range(heads)
            ]
        ]
    )

    first_load.wait()
    frames = cot.shape[0]
    for j in range(tube_share):
        low[j * length : (j + 1) * length, :] = cot[:, j].reshape(length, width)
    own_result = []

    def send_result():
        for j in range(tube_share):
            at = slice(j * length, (j + 1) * length)
            result[:, j] = dm[at, :].astype(LOW).reshape(frames, length // frames, width)
        line.start(0)
        own_result.append(loads.start(result, tube_region(z)))

    def mlp_start():
        begin_mlp(1)
        grads[DOWN, 0] = dot(act[0, 0], low[...], TN).astype(LOW)
        red[1, DOWN].give(0)

    def row(r, columns=None):
        return small.at[r : r + 1, :] if columns is None else small.at[r : r + 1, 0:columns]

    def begin_mlp(b):
        row(BDOWN_ROW + b)[...] = jnp.sum(low[...].astype(F32), 0, keepdims=True)
        dn[...] = jnp.zeros_like(dn)
        for copy in norm_loads[b]:
            copy.wait()
        if b:
            dm[...] = m[...] + b_down[b : b + 1, :]
        ready((1 - b) * 2 * heads)

    def mlp(b, s):
        if s:
            ready((1 - b) * 2 * heads + s)
        elif b == 0:
            begin_mlp(b)
        for k in (DOWN, UP):
            if s >= 2:
                moves.left([red[b, k].core[s - 2]])
            elif b == 0:
                moves.left([red[1, k].core[s + heads - 2]])
        first = (b, s) == (1, 0)
        slot = s % 2
        backward_mlp(
            sz, wm.at[slot], act.at[slot], low, n2, du, dn, None if first else grads.at[DOWN, slot], grads.at[UP, slot],
            row(BUP_ROW + b * heads + s),
        )
        for k in (UP,) if first else (DOWN, UP):
            if s == 0 and b == 0:
                pl.semaphore_wait(free_sem.at[k], 1)
            red[b, k].give(s)
        if b:
            dm[...] += dot(act[slot, 0], wm[slot, width : width + sz.units, :], NN)

    def mlp_norm(b):
        norm_back_rows(
            sz, m, gains[b, 1:2, :], dn, low, dm, row(GAIN_ROW + 2 * b + 1), row(SHIFT_ROW + 2 * b + 1), row(BOUT_ROW + b), low
        )
        if b:
            norm_loads[0] = [loads.start(saved[0][4], m), loads.start(saved[0][5], n2)]

    def attention(b, s):
        if s == 0:
            dn[...] = jnp.zeros_like(dn)
            for copy in later_loads[b]:
                copy.wait()
        ready((1 - b) * 2 * heads + heads + s)
        if s >= 2:
            moves.left([red[b, ATTN].core[s - 2]])
        elif b == 0:
            moves.left([red[1, ATTN].core[s + heads - 2]])
        r = BQV_ROW + 2 * (b * heads + s)
        backward_attention(
            sz, wa.at[s % 2], t.at[s % 2], p.at[s % 2], low, n, do, dq, dk, dv, dn, grads.at[ATTN, s % 2],
            row(r, sz.columns), row(r + 1, sz.columns),
        )
        if s == 0 and b == 0:
            pl.semaphore_wait(free_sem.at[ATTN], 1)
        red[b, ATTN].give(s)

    own_spread = []

    def attention_norm(b):
        norm_back_rows(
            sz, x, gains[b, 0:1, :], dn, dm, dm, row(GAIN_ROW + 2 * b), row(SHIFT_ROW + 2 * b), None, None
        )
        if b:
            later_loads[0] = [loads.start(saved[0][1], n), loads.start(saved[0][0], x)]
            for j in range(tube_share):
                dx_low[:, j] = dm[j * length : (j + 1) * length, :].astype(LOW).reshape(frames, length // frames, width)
            moves.start(spread)
            own_spread.append(
                loads.start(
                    dx_low.at[pl.ds((2 * z + yy) * frame_share, frame_share)],
                    back.at[:, pl.ds((heads * yy + z) * tube_share, tube_share)],
                )
            )
            return
        mark = masked_rows(sz.rows, marks)
        grad = dm[...]
        row(0)[...] = jnp.sum(jnp.where(mark, grad, 0.0), 0, keepdims=True)
        back[...] = jnp.where(mark, 0.0, grad).astype(LOW).reshape(back.shape)
        moves.start(cross)
        own_copy = loads.start(back.at[:, here], own_frames(z))
        moves.start(small_steps[0])
        own_copy.wait()
        own_line.start(0)

    def second_upstream():
        moves.arrive(spread)
        for copy in own_spread:
            copy.wait()
        low[...] = back[...].reshape(sz.rows, width)

    here, there = pl.ds(yy * tubes, tubes), pl.ds((1 - yy) * tubes, tubes)
    own_frames = lambda block: out_tokens.at[pl.ds((2 * block + yy) * frame_share, frame_share)]
    far_frames = lambda block: out_tokens.at[pl.ds((2 * block + 1 - yy) * frame_share, frame_share)]
    cross = moves.phase([(back.at[:, there], own_frames(z), far_frames(z), place.across(0))])
    own_line = Line(place, line_sem.at[2], line_sem.at[3], own_frames)
    far_line = Line(place, line_sem.at[4], line_sem.at[5], far_frames)

    def start_far():
        moves.arrive(cross)
        far_line.start(0)

    half = SMALL_ROWS // 2
    part = pl.ds(pl.multiple_of(place.core * half, half), half)
    far_part = pl.ds(pl.multiple_of((1 - place.core) * half, half), half)
    small_steps = [
        moves.phase([(small, small_in.at[i], small_in.at[i], target)])
        for i, target in enumerate((place.other, place.first, place.second))
    ]
    small_z = moves.phase(
        [(small.at[part], small_heads.at[d - 1], small_heads.at[d - 1], place.head(d)) for d in range(1, heads)]
    )
    small_end = moves.phase([(small_last.at[part], small_last.at[part], small_last.at[far_part], place.other)])

    def add_small(i):
        moves.arrive(small_steps[i])
        moves.left(small_steps[i])
        small[...] += small_in[i]
        moves.start(small_steps[i + 1] if i + 1 < len(small_steps) else small_z)

    def add_small_heads():
        moves.arrive(small_z)
        total = small[part, :]
        for d in range(heads - 1):
            total += small_heads[d]
        small_last[part, :] = total
        moves.start(small_end)

    def end_small():
        moves.arrive(small_end)
        out_small[...] = small_last[...]

    def pass_on(way, step):
        way.arrive(step)
        if step + 1 < way.steps:
            way.start(step + 1)

    todo = {(UPSTREAM,): second_upstream, (MLP_START,): mlp_start, (SEND_RESULT,): send_result, (FAR_START,): start_far, (SMALL, 3): add_small_heads, (SMALL, 4): end_small}
    for i in range(3):
        todo[SMALL, i] = functools.partial(add_small, i)
    for name, way in ((RESULT_LINE, line), (OWN_LINE, own_line), (FAR_LINE, far_line)):
        for step in range(way.steps):
            todo[name, step] = functools.partial(pass_on, way, step)
    for b in range(blocks):
        todo[MLP_NORM, b] = functools.partial(mlp_norm, b)
        todo[ATTN_NORM, b] = functools.partial(attention_norm, b)
        for s in range(heads):
            todo[MLP_BACK, b, s] = functools.partial(mlp, b, s)
            todo[ATTN_BACK, b, s] = functools.partial(attention, b, s)
        for k in (DOWN, UP, ATTN):
            each = red[b, k]
            for s in range(heads):
                todo[ADD_CORE, b, k, s] = functools.partial(each.step_first, s)
            todo[ADD_FIRST, b, k] = functools.partial(each.step_second, free_sem.at[k] if b else None)
            todo[ADD_SECOND, b, k] = each.step_heads
            for hop in range(1, heads - 1):
                todo[PASS_HEADS, b, k, hop] = functools.partial(each.step_pass, hop)
            todo[ADD_HEADS, b, k] = each.step_share
            todo[SHARE_FIRST, b, k] = each.step_share_first
            todo[SHARE_CORE, b, k] = each.step_share_core
            todo[ARRIVED, b, k] = each.end
    for step in BACKWARD_ORDER:
        todo[step]()
    for copy in own_result:
        copy.wait()
    for each in (line, own_line, far_line, *red.values()):
        each.finish()
    moves.finish()


def run_backward(sz, blocks, frame_share, tube_share, fulls, saved, cotangent, marks, gains, b_down):
    heads, width, rows, cols = sz.shards, sz.width, sz.rows, sz.columns
    frames, tubes, patches = cotangent.shape[:3]
    hbm, vmem = pl.BlockSpec(memory_space=pl.ANY), pl.BlockSpec(memory_space=pltpu.VMEM)
    q = width // 8
    local = (frame_share, 2 * tubes, patches, width)
    mixed = (frames, tube_share, patches, width)
    kinds = 3 * blocks
    count = kinds * (3 * heads + 3 + 2) + 2 * heads - 1 + 1 + 4 + heads - 1
    flat = [array for per in saved for array in per]
    return pl.pallas_call(
        lambda *refs: backward_kernel(sz, blocks, frame_share, tube_share, *refs),
        name="backward_both",
        out_shape=structs(
            [
                (cotangent.shape, LOW),
                (cotangent.shape, LOW),
                ((blocks * sz.block_rows, width), LOW),
                ((SMALL_ROWS, width), F32),
            ]
        ),
        in_specs=[hbm] * (blocks + len(flat) + 1) + [vmem] * 3,
        out_specs=[hbm] * 3 + [vmem],
        scratch_shapes=vmems(
            [
                ((2, 2 * width, width), LOW),
                ((2, 2, rows, sz.units), LOW),
                ((2, sz.up_row, width), LOW),
                ((2, 4, rows, cols), LOW),
                ((2, sz.sequences * sz.heads, sz.length, sz.length), LOW),
                ((rows, width), F32),
                ((rows, width), LOW),
                ((rows, width), LOW),
                ((rows, width), F32),
                ((rows, width), LOW),
                ((rows, width), F32),
                ((rows, width), F32),
                ((rows, sz.units), LOW),
                ((rows, cols), LOW),
                ((rows, cols), LOW),
                ((rows, cols), LOW),
                ((rows, cols), LOW),
                (mixed, LOW),
                (mixed, LOW),
                (local, LOW),
                (mixed, LOW),
                ((3, 2, width, width), LOW),
                ((3, heads, 4 * q, width), LOW),
                ((blocks, 3, heads, 2 * q, width), LOW),
                ((blocks, 3, heads, q, width), LOW),
                ((blocks, 3, heads + 1, q, width), LOW),
                ((blocks, 3, q, width), LOW),
                ((SMALL_ROWS, width), F32),
                ((3, SMALL_ROWS, width), F32),
                ((heads - 1, SMALL_ROWS // 2, width), F32),
                ((SMALL_ROWS, width), F32),
            ]
        )
        + [
            pltpu.SemaphoreType.DMA((count,)),
            pltpu.SemaphoreType.DMA((count,)),
            pltpu.SemaphoreType.DMA((6, 2 * (heads - 1))),
            pltpu.SemaphoreType.DMA((10,)),
            pltpu.SemaphoreType.DMA((24,)),
            pltpu.SemaphoreType.DMA((kinds,)),
            pltpu.SemaphoreType.REGULAR((3,)),
        ],
        compiler_params=pltpu.CompilerParams(
            collective_id=1, has_side_effects=True, vmem_limit_bytes=63 * 2**20
        ),
    )(*fulls, *flat, cotangent, marks, gains, b_down)


def finish(sz, blocks, output, tokens, whole, small):
    heads, width, cols, units = sz.shards, sz.width, sz.columns, sz.units
    parts = 4

    def kernel(o_in, t_in, a_in, c_in, u_in, d_in, small, o_out, t_out, embed, gain, shift, a, bqv, c, bout, u, bup, d, bdown):
        for src, dst in ((o_in, o_out), (t_in, t_out)):
            dst[...] = src[...]
        for src, dst in ((a_in, a), (c_in, c), (u_in, u), (d_in, d)):
            dst[...] = src[...].astype(F32)

        @pl.when((pl.program_id(0) == 0) & (pl.program_id(1) == 0))
        def _():
            head = lax.axis_index("head")
            embed[...] = small[0, :]
            for b in range(blocks):
                for norm in range(2):
                    gain[b, norm : norm + 1, :] = small[GAIN_ROW + 2 * b + norm : GAIN_ROW + 2 * b + norm + 1, :]
                    shift[b, norm : norm + 1, :] = small[SHIFT_ROW + 2 * b + norm : SHIFT_ROW + 2 * b + norm + 1, :]
                bout[b : b + 1, :] = small[BOUT_ROW + b : BOUT_ROW + b + 1, :]
                bdown[b : b + 1, :] = small[BDOWN_ROW + b : BDOWN_ROW + b + 1, :]
                bup[b : b + 1, :] = small[pl.ds(BUP_ROW + b * heads + head, 1), :]
                for i in range(2):
                    bqv[b, i : i + 1, :] = small[pl.ds(BQV_ROW + 2 * (b * heads + head) + i, 1), 0:cols]

    def rows(size, first):
        return pl.BlockSpec((1, size // parts, width), lambda b, i: (b, first * parts // size + i, 0))

    def kept(*shape):
        return pl.BlockSpec(shape, lambda b, i: (0,) * len(shape))

    share = output.shape[0] // (blocks * parts)
    cut = pl.BlockSpec((share,) + output.shape[1:], lambda b, i: (b * parts + i, 0, 0, 0))
    pair, triple = (blocks, width), (blocks, 2, width)
    sizes = (3 * cols, cols, width, units)
    shapes = [(output.shape, LOW), (output.shape, LOW)] + [
        (s, F32)
        for s in (
            (width,),
            triple,
            triple,
            (blocks, sizes[0], width),
            (blocks, 2, cols),
            (blocks, sizes[1], width),
            pair,
            (blocks, sizes[2], width),
            pair,
            (blocks, sizes[3], width),
            pair,
        )
    ]
    out = [rows(size, 0) for size in sizes]
    return pl.pallas_call(
        kernel,
        name="finish",
        grid=(blocks, parts),
        out_shape=structs(shapes),
        in_specs=[
            cut,
            cut,
            rows(sizes[0], 0),
            rows(sizes[1], sz.out_row),
            rows(sizes[2], sz.up_row),
            rows(sizes[3], sz.down_row),
            kept(SMALL_ROWS, width),
        ],
        out_specs=[
            cut,
            cut,
            kept(width),
            kept(*triple),
            kept(*triple),
            out[0],
            kept(blocks, 2, cols),
            out[1],
            kept(*pair),
            out[2],
            kept(*pair),
            out[3],
            kept(*pair),
        ],
        compiler_params=pltpu.CompilerParams(vmem_limit_bytes=62 * 2**20),
    )(output, tokens, whole, whole, whole, whole, small)


def fits_local(arrays, clip_size, tube_size, head_size):
    clips, frames, tubes = arrays[0].shape[:3]
    width = arrays[0].shape[-1]
    columns, units = arrays[5].shape[3] // head_size, arrays[9].shape[2] // head_size
    devices = tube_size * head_size
    return (
        (clips, clip_size, tube_size) == (4, 4, 2)
        and frames % devices == 0
        and frames == tubes
        and head_size % 2 == 0
        and width == 4 * columns == units
        and width % 384 == 0
        and columns % HD == 0
    )


def on_device_local(
    tokens,
    token_mask,
    mask_embed,
    norm_gains,
    norm_shifts,
    w_qkv,
    b_qv,
    w_out,
    b_out,
    w_up,
    b_up,
    w_down,
    b_down,
    cotangent,
):
    _, frames, tubes, patches, width = tokens.shape
    tube_size, heads = lax.axis_size("tube"), lax.axis_size("head")
    head = lax.axis_index("head")
    blocks, columns, units = w_qkv.shape[0], w_qkv.shape[-1], w_up.shape[-1]
    frame_share = frames // (tube_size * heads)
    tube_share = tubes // heads
    rows = frame_share * tube_size * tubes * patches
    sz = Sizes(rows, width, heads, columns, units, rows // frame_share)

    full, saved, mark_frames = run_forward(
        sz,
        blocks,
        frame_share,
        tube_share,
        (w_qkv.transpose(0, 2, 3, 1).reshape(blocks, 3 * columns, width), w_out, w_up, w_down),
        tokens[0],
        token_mask[0],
        b_qv,
        b_up,
        mask_embed,
        norm_gains,
        norm_shifts,
        b_out,
        b_down,
    )
    output, grad_tokens, whole, small = run_backward(
        sz, blocks, frame_share, tube_share, full, saved, cotangent[0], mark_frames, norm_gains, b_down
    )
    out = finish(sz, blocks, output, grad_tokens, whole.reshape(blocks, sz.block_rows, width), small)
    output, grad_tokens, embed, gains, shifts, qkv_grad, bqv, out_grad, bout, up_grad, bup, down_grad, bdown = out
    qkv_grad = qkv_grad.reshape(blocks, 3, columns, width).transpose(0, 3, 1, 2)
    return (
        output[None],
        grad_tokens[None],
        embed,
        gains,
        shifts,
        qkv_grad,
        bqv,
        out_grad,
        bout,
        up_grad,
        bup,
        down_grad,
        bdown,
    )


def solution(mesh):
    sizes = [mesh.shape[name] for name in ("clip", "tube", "head")]

    def run(*arrays):
        on_device = on_device_local if fits_local(arrays, *sizes) else on_device_sums
        return on_mesh(on_device, mesh)(*arrays)

    return run


def on_mesh(on_device, mesh):
    return jax.shard_map(
        on_device,
        mesh=mesh,
        in_specs=(
            P("clip", None, "tube", None, None),
            P("clip", None, "tube", None),
            P(),
            P(),
            P(),
            P(None, None, None, "head"),
            P(None, None, "head"),
            P(None, "head", None),
            P(),
            P(None, None, "head"),
            P(None, "head"),
            P(None, "head", None),
            P(),
            P("clip", None, "tube", None, None),
        ),
        out_specs=(
            P("clip", None, "tube", None, None),
            P("clip", None, "tube", None, None),
            P(),
            P(),
            P(),
            P(None, None, None, "head"),
            P(None, None, "head"),
            P(None, "head", None),
            P(),
            P(None, None, "head"),
            P(None, "head"),
            P(None, "head", None),
            P(),
        ),
        check_vma=False,
    )
```
